32 devices in a mesh: dp: 8 (over y, x, core), tensor: 4 (over z).
Axes of the slice: x: 2, y: 2, z: 4, core: 2. Of those that a mesh axis runs over, the one named last changes fastest.
Arguments:
- tokens: bfloat16 [2048, 1152], P('dp'), may hold values from -6 to 6
- conditioning: bfloat16 [3, 1152], replicated, may hold values from -6 to 6
- latent_len: int32 [3], replicated, may hold values from 1 to 1024, 2048 in all
- w_ada: bfloat16 [1152, 6, 1152], P('dp', None, 'tensor'), may hold values from -0.1875 to 0.1875
- b_ada: bfloat16 [6, 1152], P(None, 'tensor'), may hold values from -1.75 to 1.75
- w_qkv: bfloat16 [1152, 3, 1152], P('dp', None, 'tensor'), may hold values from -0.1875 to 0.1875
- b_qv: bfloat16 [2, 1152], P(None, 'tensor'), may hold values from -1.75 to 1.75
- w_proj: bfloat16 [1152, 1152], P('tensor', 'dp'), may hold values from -1.5 to 1.5
- b_proj: bfloat16 [1152], replicated, may hold values from -1.75 to 1.75
- w_fc1: bfloat16 [1152, 4608], P('dp', 'tensor'), may hold values from -0.1875 to 0.1875
- b_fc1: bfloat16 [4608], P('tensor'), may hold values from -1.75 to 1.75
- w_fc2: bfloat16 [4608, 1152], P('tensor', 'dp'), may hold values from -0.09375 to 0.09375
- b_fc2: bfloat16 [1152], replicated, may hold values from -1.75 to 1.75
- cotangent: bfloat16 [2048, 1152], P('dp'), may hold values from -6 to 6
Outputs:
- block_out: bfloat16 [2048, 1152], P('dp')
- grad_tokens: float32 [2048, 1152], P('dp')
- grad_cond: float32 [3, 1152], replicated
- grad_w_ada: float32 [1152, 6, 1152], P('dp', None, 'tensor')
- grad_b_ada: float32 [6, 1152], P(None, 'tensor')
- grad_w_qkv: float32 [1152, 3, 1152], P('dp', None, 'tensor')
- grad_b_qv: float32 [2, 1152], P(None, 'tensor')
- grad_w_proj: float32 [1152, 1152], P('tensor', 'dp')
- grad_b_proj: float32 [1152], replicated
- grad_w_fc1: float32 [1152, 4608], P('dp', 'tensor')
- grad_b_fc1: float32 [4608], P('tensor')
- grad_w_fc2: float32 [4608, 1152], P('tensor', 'dp')
- grad_b_fc2: float32 [1152], replicated
The draws below stay inside these ranges and needn't reach their ends.
Inputs may be any that keep to these rules, and one draw needn't show every extreme that they name: `latent_len`: the 3 latents lie end to end and fill all 2048 tokens; the longest has exactly 1024 tokens.
All inputs are finite; a program needn't handle non-finite values.
Results may differ from the reference program's by a relative error of at most 0.012.
The reference program's roundings to bfloat16 on the way count: a program that leaves them out, or rounds other values in their place, can miss the bound.
Values may be sent and summed in bfloat16 or wider, within the bound.
No kernel may reach another device: no remote copies, remote signals or barrier semaphores. Data moves between devices by JAX's collectives and lax.ppermute only.
A program may use at most 192 MiB of HBM per device.

```python
import math
import jax
import jax.numpy as jnp
import numpy as np
from jax import lax

D = 1152
H = 16
DH = 72
FF = 4608
SEQ = 1024
TOKENS = 2048
LATENTS = 3


def levels(stream_key, extent, split, least, high):
    def one(dim, parts):
        draws = jax.random.uniform(jax.random.fold_in(jax.random.fold_in(stream_key, 6), dim), (parts,), jnp.float32, least / len(split), high / len(split))
        return jnp.repeat(jnp.exp(draws), extent[dim] // parts).reshape((-1,) + (1,) * (len(extent) - dim - 1))

    loudness = one(*split[0])
    for cut in split[1:]:
        loudness = loudness * one(*cut)
    return loudness


def length_profile(number_of, total, limit, lean):
    portions = [(1 << 20) // math.isqrt(rank ** lean) + 1 for rank in range(2, number_of + 1)]
    spare, holding = total - limit - (number_of - 1), [1] * (number_of - 1)
    while spare > 0:
        movable = [i for i in range(number_of - 1) if holding[i] < limit]
        mass, budget = sum([portions[i] for i in movable]), spare
        for i in movable:
            extra = min(limit - holding[i], max(1, budget * portions[i] // mass), spare)
            holding[i] = holding[i] + extra
            spare = spare - extra
    return np.array([limit] + holding)


def uneven(key, count, total, reach, skew):
    if count == 2:
        one = jax.random.randint(key, (), max(1, total - reach), min(reach, total - 1) + 1)
        return jnp.stack([one, total - one])
    tallies = jnp.asarray(length_profile(count, total, reach, skew), jnp.int32)
    couples = (count - 1) // 2
    source_of, sink = tallies[1:1 + 2 * couples:2], tallies[2:2 + 2 * couples:2]
    room = jnp.minimum(source_of - 1, reach - sink)
    passed = jax.random.randint(jax.random.fold_in(key, 1), (couples,), 0, 1 << 20) % (room + 1)
    tallies = tallies.at[1:1 + 2 * couples:2].set(source_of - passed).at[2:2 + 2 * couples:2].set(sink + passed)
    return tallies[jax.random.permutation(jax.random.fold_in(key, 2), count)]


def bell_draw(own_key, dims, scale, most, shards=(), kind=jnp.bfloat16):
    drawn = scale * jax.random.normal(own_key, dims, jnp.float32)
    if shards:
        drawn = drawn * levels(own_key, dims, shards, -0.22, 0.18)
    return jnp.clip(drawn, -most, most).astype(kind)


def setup_inputs(seed: int = 0) -> dict:
    key_of = jax.random.split(jax.random.key(seed), 15)
    return {
        "tokens": bell_draw(key_of[0], (TOKENS, D), 1.0, 6.0, ((0, 8),)),
        "conditioning": bell_draw(key_of[1], (LATENTS, D), 1.0, 6.0),
        "latent_len": uneven(key_of[2], LATENTS, TOKENS, SEQ, 2).astype(jnp.int32),
        "w_ada": bell_draw(key_of[3], (D, 6, D), D ** -0.5, 0.1875, ((0, 8), (2, 4))),
        "b_ada": bell_draw(key_of[4], (6, D), 0.3, 1.75, ((1, 4),)),
        "w_qkv": bell_draw(key_of[5], (D, 3, D), D ** -0.5, 0.1875, ((0, 8), (2, 4))),
        "b_qv": bell_draw(key_of[6], (2, D), 0.3, 1.75, ((1, 4),)),
        "w_proj": bell_draw(key_of[7], (D, D), (D * 16 // SEQ) ** -0.5, 1.5, ((0, 4), (1, 8))),
        "b_proj": bell_draw(key_of[8], (D,), 0.3, 1.75),
        "w_fc1": bell_draw(key_of[9], (D, FF), D ** -0.5, 0.1875, ((0, 8), (1, 4))),
        "b_fc1": bell_draw(key_of[10], (FF,), 0.3, 1.75, ((0, 4),)),
        "w_fc2": bell_draw(key_of[11], (FF, D), FF ** -0.5, 0.09375, ((0, 4), (1, 8))),
        "b_fc2": bell_draw(key_of[12], (D,), 0.3, 1.75),
        "cotangent": bell_draw(key_of[13], (TOKENS, D), 1.0, 6.0, ((0, 8),)),
    }


@jax.custom_vjp
def low(v):
    return lax.optimization_barrier(v.astype(jnp.bfloat16)).astype(jnp.float32)

@jax.custom_vjp
def low_back(v):
    return v

def low_keep(v):
    return (low(v), None)

def low_pass(kept, grad):
    return (grad,)

def back_keep(v):
    return (v, None)

def back_low(kept, grad):
    return (low(grad),)
low.defvjp(low_keep, low_pass)
low_back.defvjp(back_keep, back_low)
NORM_EPS = 1e-06
HIGHEST_PRECISION = lax.Precision.HIGHEST

def layer_norm(values):
    average = lax.optimization_barrier(jnp.mean(values, axis=-1, keepdims=True))
    centred = values - average
    spread = lax.optimization_barrier(jnp.mean(centred * centred, axis=-1, keepdims=True))
    return centred * lax.rsqrt(spread + NORM_EPS)

def modulated(values, shift_part, scales):
    return layer_norm(values) * (1.0 + scales) + shift_part

def latent_index(latent_len, positions, token_total):
    latent_ends = jnp.cumsum(latent_len, dtype=jnp.int32)
    found_ids = lax.optimization_barrier(jnp.sum((positions[:, None] >= latent_ends[None, :]).astype(jnp.int32), axis=1, dtype=jnp.int32))
    inside = (positions >= 0) & (positions < token_total)
    return jnp.where(inside, found_ids, -1).astype(jnp.int32)

def forward(tokens, conditioning, w_ada, b_ada, w_qkv, b_qv, w_proj, b_proj, w_fc1, b_fc1, w_fc2, b_fc2, latent_ids):
    token_total = tokens.shape[0]
    activated = low(jax.nn.silu(conditioning))
    modulation = jnp.einsum('ld,dkf->lkf', activated, w_ada, precision=HIGHEST_PRECISION) + b_ada[None]
    per_token = low_back(modulation[latent_ids])
    hidden_one = low(modulated(tokens, per_token[:, 0], per_token[:, 1]))
    bias_three = jnp.stack([b_qv[0], jnp.zeros_like(b_qv[0]), b_qv[1]])
    projected = jnp.einsum('td,dkf->tkf', hidden_one, w_qkv, precision=HIGHEST_PRECISION) + bias_three[None]
    projected = low(low_back(projected))
    queries = projected[:, 0].reshape(token_total, H, DH)
    key_rows = projected[:, 1].reshape(token_total, H, DH)
    value_rows = projected[:, 2].reshape(token_total, H, DH)
    padded_keys = jnp.pad(key_rows, ((SEQ, SEQ), (0, 0), (0, 0)))
    padded_values = jnp.pad(value_rows, ((SEQ, SEQ), (0, 0), (0, 0)))
    padded_ids = jnp.pad(latent_ids, (SEQ, SEQ), constant_values=-1)
    block_rows = min(512, token_total)
    window = block_rows + 2 * SEQ
    score_scale = 1.0 / math.sqrt(DH)

    def attend(block_start):
        query_block = lax.dynamic_slice_in_dim(queries, block_start, block_rows, 0)
        query_ids = lax.dynamic_slice_in_dim(latent_ids, block_start, block_rows, 0)
        key_block = lax.dynamic_slice_in_dim(padded_keys, block_start, window, 0)
        value_block = lax.dynamic_slice_in_dim(padded_values, block_start, window, 0)
        key_ids = lax.dynamic_slice_in_dim(padded_ids, block_start, window, 0)
        scores = jnp.einsum('qhe,khe->hqk', query_block, key_block, precision=HIGHEST_PRECISION) * score_scale
        scores = low_back(scores)
        allowed = (query_ids[:, None] == key_ids[None, :])[None]
        scores = jnp.where(allowed, scores, -1e+30)
        largest = lax.optimization_barrier(jnp.max(scores, axis=-1, keepdims=True))
        weights_raw = jnp.exp(scores - largest)
        probabilities = weights_raw / lax.optimization_barrier(jnp.sum(weights_raw, axis=-1, keepdims=True))
        return jnp.einsum('hqk,khe->qhe', low(probabilities), value_block, precision=HIGHEST_PRECISION)
    starts = jnp.arange(token_total // block_rows, dtype=jnp.int32) * block_rows
    attended = lax.map(jax.checkpoint(attend), starts)
    attended = low(low_back(attended.reshape(token_total, H * DH)))
    attn_out = low_back(jnp.dot(attended, w_proj, precision=HIGHEST_PRECISION) + b_proj)
    residual_mid = tokens + per_token[:, 2] * attn_out
    hidden_two = low(modulated(residual_mid, per_token[:, 3], per_token[:, 4]))
    pre_act = low_back(jnp.dot(hidden_two, w_fc1, precision=HIGHEST_PRECISION) + b_fc1)
    gelu_out = low(jax.nn.gelu(pre_act, approximate=True))
    mlp_out = low_back(jnp.dot(gelu_out, w_fc2, precision=HIGHEST_PRECISION) + b_fc2)
    return residual_mid + per_token[:, 5] * mlp_out

def reference(tokens, conditioning, latent_len, w_ada, b_ada, w_qkv, b_qv, w_proj, b_proj, w_fc1, b_fc1, w_fc2, b_fc2, cotangent):
    token_total = tokens.shape[0]
    positions = jnp.arange(token_total, dtype=jnp.int32)
    latent_ids = latent_index(latent_len, positions, token_total)
    floats = [member.astype(jnp.float32) for member in (tokens, conditioning, w_ada, b_ada, w_qkv, b_qv, w_proj, b_proj, w_fc1, b_fc1, w_fc2, b_fc2)]

    def wrapped(*params):
        return forward(*params, latent_ids)
    result, pull_back = jax.vjp(wrapped, *floats)
    gradients = pull_back(cotangent.astype(jnp.float32))
    return (result.astype(jnp.bfloat16), gradients[0], gradients[1], gradients[2], gradients[3], gradients[4], gradients[5], gradients[6], gradients[7], gradients[8], gradients[9], gradients[10], gradients[11])
```

```python
import math

import jax
import jax.numpy as jnp
from jax import lax
from jax.experimental import pallas as pl
from jax.experimental.pallas import tpu as pltpu
from jax.sharding import PartitionSpec as P

DH = 72
SEQ = 1024
NORM_EPS = 1e-06
NEGATIVE = -1e30
SCALE = 1.0 / math.sqrt(DH)
VMEM_BYTES = 40 * 1024 * 1024
BF16 = jnp.bfloat16
F32 = jnp.float32


def swap(block, axis, bits):
    route = [(i, i ^ bits) for i in range(lax.axis_size(axis))]
    return lax.ppermute(block, axis, route)


def exchange(blocks, axis):
    return lax.all_to_all(blocks, axis, 0, 0, tiled=True)


def gather(block, axis, count):
    return exchange(jnp.broadcast_to(block[None], (count,) + block.shape), axis)


def gather_rows(block):
    count = lax.axis_size("dp")
    if count > 8:
        return lax.all_gather(block, "dp", axis=0, tiled=True)
    me = lax.axis_index("dp")
    held = [block] + [swap(block, "dp", bits) for bits in range(2, count, 2)]
    other = swap(jnp.stack(held), "dp", 1)
    full = jnp.zeros((count,) + block.shape, block.dtype)
    for step in range(count // 2):
        full = lax.dynamic_update_index_in_dim(full, held[step], me ^ (2 * step), 0)
        full = lax.dynamic_update_index_in_dim(full, other[step], me ^ (2 * step + 1), 0)
    return full.reshape((count * block.shape[0],) + block.shape[1:])


def scatter_rows(partial):
    count = lax.axis_size("dp")
    share = partial.shape[0] // count
    if count > 8:
        return lax.psum_scatter(partial.astype(F32), "dp", scatter_dimension=0, tiled=True)
    me = lax.axis_index("dp")
    core = me % 2
    blocks = partial.reshape(count // 2, 2, share, partial.shape[1])
    theirs = lax.dynamic_index_in_dim(blocks, 1 - core, 1, keepdims=False)
    ours = lax.dynamic_index_in_dim(blocks, core, 1, keepdims=False)
    both = (ours.astype(F32) + swap(theirs, "dp", 1).astype(F32)).astype(BF16)
    chip = me // 2
    total = lax.dynamic_index_in_dim(both, chip, 0, keepdims=False).astype(F32)
    for step in range(1, count // 2):
        sent = lax.dynamic_index_in_dim(both, chip ^ step, 0, keepdims=False)
        total = total + swap(sent, "dp", 2 * step).astype(F32)
    return total


def sum_shares(partial, axis):
    count = lax.axis_size(axis)
    blocks = partial.astype(BF16).reshape((count, partial.shape[0] // count) + partial.shape[1:])
    return jnp.sum(exchange(blocks, axis).astype(F32), axis=0)


def gather_shares(share, axis):
    count = lax.axis_size(axis)
    parts = gather(share, axis, count)
    return parts.reshape((count * share.shape[0],) + share.shape[1:])


def tile_range(meta_ref, latents, tile, core):
    lane = lax.broadcasted_iota(jnp.int32, (1, 256), 1)
    first = tile * 512 + core * 128
    last = first + 383
    place = first + lane + jnp.where(lane >= 128, 128, 0)
    begin = jnp.zeros((1, 256), jnp.int32)
    finish = jnp.zeros((1, 256), jnp.int32)
    low = jnp.int32(0)
    high = jnp.int32(0)
    start = jnp.int32(0)
    for number in range(latents):
        end = start + meta_ref[1 + number]
        inside = (place >= start) & (place < end)
        begin = jnp.where(inside, start, begin)
        finish = jnp.where(inside, end, finish)
        low = jnp.where((first >= start) & (first < end), start, low)
        high = jnp.where((last >= start) & (last < end), end, high)
        start = end
    return begin, finish, low // 256, (high + 255) // 256


def pair(ref, tile, start):
    left = ref[2 * tile, :, start : start + 128]
    right = ref[2 * tile + 1, :, start : start + 128]
    return jnp.concatenate([left, right], axis=1)


def key_mask(block, begin, finish):
    place = block * 256 + lax.broadcasted_iota(jnp.int32, (256, 256), 0)
    return (place >= begin) & (place < finish)


def forward_kernel(latents, meta_ref, packed_ref, out_ref, exact_ref, log_ref, keys, scores):
    blocks = packed_ref.shape[0]
    core = meta_ref[0]
    for block in range(blocks):
        keys[block] = packed_ref[block, :, :256].astype(F32).T.astype(BF16)
    for tile in range(blocks // 2):
        begin, finish, low, high = tile_range(meta_ref, latents, tile, core)
        query = pair(packed_ref, tile, 512)

        def score(block, largest):
            raw = jnp.dot(keys[block], query, preferred_element_type=F32) * SCALE
            raw = jnp.where(key_mask(block, begin, finish), raw, NEGATIVE)
            scores[block] = raw
            return jnp.maximum(largest, jnp.max(raw, axis=0, keepdims=True))

        largest = lax.fori_loop(low, high, score, jnp.full((1, 256), NEGATIVE, F32))

        def mix(block, carry):
            total, mixed = carry
            weights = jnp.exp(scores[block] - largest)
            total = total + jnp.sum(weights, axis=0, keepdims=True)
            values = packed_ref[block, :, 256:512]
            mixed = mixed + jnp.dot(values, weights.astype(BF16), preferred_element_type=F32)
            return total, mixed

        total, mixed = lax.fori_loop(
            low, high, mix, (jnp.zeros((1, 256), F32), jnp.zeros((DH, 256), F32))
        )
        mixed = mixed / total
        log_total = largest + jnp.log(total)
        for half in range(2):
            part = mixed[:, half * 128 : half * 128 + 128]
            exact_ref[2 * tile + half] = part
            out_ref[2 * tile + half] = part.astype(BF16)
            log_ref[2 * tile + half] = log_total[:, half * 128 : half * 128 + 128]


def backward_kernel(
    latents, meta_ref, packed_ref, grad_ref, exact_ref, log_ref, out_ref, keys, values, d_keys, d_values
):
    blocks = packed_ref.shape[0]
    core = meta_ref[0]
    for block in range(blocks):
        keys[block] = packed_ref[block, :, :256].astype(F32).T.astype(BF16)
        values[block] = packed_ref[block, :, 256:512].astype(F32).T.astype(BF16)
    d_keys[...] = jnp.zeros_like(d_keys)
    d_values[...] = jnp.zeros_like(d_values)
    by_query = (((1,), (1,)), ((), ()))
    for tile in range(blocks // 2):
        begin, finish, low, high = tile_range(meta_ref, latents, tile, core)
        query = pair(packed_ref, tile, 512)
        grad = pair(grad_ref, tile, 0)
        inner = jnp.sum(grad.astype(F32) * pair(exact_ref, tile, 0), axis=0, keepdims=True)
        log_total = pair(log_ref, tile, 0)

        def step(block, d_query):
            raw = jnp.dot(keys[block], query, preferred_element_type=F32) * SCALE
            probs = jnp.where(key_mask(block, begin, finish), jnp.exp(raw - log_total), 0.0)
            d_probs = jnp.dot(values[block], grad, preferred_element_type=F32)
            d_scores = (probs * (d_probs - inner)).astype(BF16)
            d_values[block] += lax.dot_general(
                grad, probs.astype(BF16), by_query, preferred_element_type=F32
            )
            d_keys[block] += lax.dot_general(query, d_scores, by_query, preferred_element_type=F32)
            key_rows = packed_ref[block, :, :256]
            return d_query + jnp.dot(key_rows, d_scores, preferred_element_type=F32)

        d_query = lax.fori_loop(low, high, step, jnp.zeros((DH, 256), F32)) * SCALE
        for half in range(2):
            part = d_query[:, half * 128 : half * 128 + 128]
            out_ref[2 * tile + half, :, 512:640] = part.astype(BF16)
    for block in range(blocks):
        out_ref[block, :, :256] = (d_keys[block] * SCALE).astype(BF16)
        out_ref[block, :, 256:512] = d_values[block].astype(BF16)


def attend_forward(meta, packed):
    blocks = packed.shape[0]
    shape = jax.ShapeDtypeStruct
    return pl.pallas_call(
        lambda *refs: forward_kernel(meta.shape[0] - 1, *refs),
        out_shape=(
            shape((blocks, DH, 128), BF16),
            shape((blocks, DH, 128), F32),
            shape((blocks, 1, 128), F32),
        ),
        in_specs=[
            pl.BlockSpec(memory_space=pltpu.SMEM),
            pl.BlockSpec(memory_space=pltpu.VMEM),
        ],
        out_specs=tuple([pl.BlockSpec(memory_space=pltpu.VMEM)] * 3),
        scratch_shapes=[
            pltpu.VMEM((blocks, 256, DH), BF16),
            pltpu.VMEM((blocks, 256, 256), F32),
        ],
        compiler_params=pltpu.CompilerParams(vmem_limit_bytes=VMEM_BYTES),
        cost_estimate=pl.CostEstimate(flops=10**9, bytes_accessed=4 * 10**6, transcendentals=10**6),
        name="attend_forward",
    )(meta, packed)


def attend_backward(meta, packed, grad, exact, log_total):
    blocks = packed.shape[0]
    return pl.pallas_call(
        lambda *refs: backward_kernel(meta.shape[0] - 1, *refs),
        out_shape=jax.ShapeDtypeStruct(packed.shape, BF16),
        in_specs=[pl.BlockSpec(memory_space=pltpu.SMEM)]
        + [pl.BlockSpec(memory_space=pltpu.VMEM)] * 4,
        out_specs=pl.BlockSpec(memory_space=pltpu.VMEM),
        scratch_shapes=[
            pltpu.VMEM((blocks, 256, DH), BF16),
            pltpu.VMEM((blocks, 256, DH), BF16),
            pltpu.VMEM((blocks, DH, 256), F32),
            pltpu.VMEM((blocks, DH, 256), F32),
        ],
        compiler_params=pltpu.CompilerParams(vmem_limit_bytes=VMEM_BYTES),
        cost_estimate=pl.CostEstimate(flops=3 * 10**9, bytes_accessed=4 * 10**6, transcendentals=10**6),
        name="attend_backward",
    )(meta, packed, grad, exact, log_total)


class HeadSplit:
    def __init__(self, latent_len, rows):
        self.rows = rows
        self.meta = jnp.concatenate([lax.axis_index("dp").astype(jnp.int32)[None] % 2, latent_len])

    def forward(self, projected):
        heads, rows = projected.shape[1], self.rows
        query = projected[0].reshape(heads, DH, 2, rows // 2).transpose(0, 2, 1, 3)
        key = jnp.broadcast_to(projected[1][:, None], (heads, 2, DH, rows))
        value = jnp.broadcast_to(projected[2][:, None], (heads, 2, DH, rows))
        packed = jnp.concatenate([key, value, query], axis=3)
        self.packed = exchange(packed.reshape(heads * 2, DH, rows * 5 // 2), "dp")
        out, self.exact, self.log_total = attend_forward(self.meta, self.packed)
        return self.unsplit(exchange(out, "dp")).reshape(heads * DH, rows)

    def unsplit(self, parts):
        heads = parts.shape[0] // 2
        parts = parts.reshape(heads, 2, DH, self.rows // 2).transpose(0, 2, 1, 3)
        return parts.reshape(heads, DH, self.rows)

    def backward(self, d_attended):
        rows = self.rows
        heads = d_attended.shape[0] // DH
        grad = d_attended.reshape(heads, DH, 2, rows // 2).transpose(0, 2, 1, 3)
        grad = exchange(grad.reshape(heads * 2, DH, rows // 2), "dp")
        out = attend_backward(self.meta, self.packed, grad, self.exact, self.log_total)
        parts = exchange(out, "dp")
        d_query = self.unsplit(parts[:, :, 2 * rows :])
        halves = parts.reshape(heads, 2, DH, rows * 5 // 2)[..., : 2 * rows].astype(F32)
        d_key_value = (halves[:, 0] + halves[:, 1]).astype(BF16)
        return jnp.stack([d_query, d_key_value[..., :rows], d_key_value[..., rows:]])


class Window:
    def __init__(self, latent_len, rows):
        self.rows = rows
        self.reach = (SEQ - 2) // rows + 1
        total = rows * lax.axis_size("dp")
        first = lax.axis_index("dp") * rows
        own = latent_index(latent_len, first, rows, total)
        ids = [
            latent_index(latent_len, first + offset * rows, rows, total)
            for offset in range(-self.reach, self.reach + 1)
        ]
        self.allowed = own[:, None] == jnp.concatenate(ids)[None, :]

    def from_behind(self, block, distance):
        devices = range(lax.axis_size("dp"))
        return lax.ppermute(
            block, "dp", [(i - distance, i) for i in devices if i - distance in devices]
        )

    def head_scores(self, query, key):
        raw = jnp.einsum("eq,ek->qk", query, key, preferred_element_type=F32) * SCALE
        return jnp.where(self.allowed, raw, NEGATIVE)

    def forward(self, projected):
        key_value = projected[1:]
        pieces = [
            key_value if offset == 0 else self.from_behind(key_value, -offset)
            for offset in range(-self.reach, self.reach + 1)
        ]
        window = jnp.concatenate(pieces, axis=3)
        self.operands = (projected[0], window[0], window[1])

        def one(operands):
            query, key, value = operands
            scores = self.head_scores(query, key)
            largest = jnp.max(scores, axis=1, keepdims=True)
            weights = jnp.exp(scores - largest)
            totals = jnp.sum(weights, axis=1, keepdims=True)
            probs = (weights / totals).astype(BF16)
            mixed = jnp.einsum("qk,ek->eq", probs, value, preferred_element_type=F32)
            return mixed.astype(BF16), (largest + jnp.log(totals))[:, 0]

        out, self.log_total = lax.map(one, self.operands)
        return out.reshape(-1, self.rows)

    def backward(self, d_attended):
        rows, reach = self.rows, self.reach
        grads = d_attended.reshape(-1, DH, rows)

        def one(operands):
            query, key, value, grad, log_total = operands
            probs = jnp.exp(self.head_scores(query, key) - log_total[:, None])
            d_value = jnp.einsum("qk,eq->ek", probs.astype(BF16), grad, preferred_element_type=F32)
            d_probs = jnp.einsum("eq,ek->qk", grad, value, preferred_element_type=F32)
            inner = jnp.sum(probs * d_probs, axis=1, keepdims=True)
            d_scores = (probs * (d_probs - inner)).astype(BF16)
            d_query = jnp.einsum("qk,ek->eq", d_scores, key, preferred_element_type=F32) * SCALE
            d_key = jnp.einsum("qk,eq->ek", d_scores, query, preferred_element_type=F32) * SCALE
            return d_query, d_key, d_value

        d_query, d_key, d_value = lax.map(one, self.operands + (grads, self.log_total))
        d_window = jnp.stack([d_key, d_value])
        d_key_value = d_window[..., reach * rows : (reach + 1) * rows]
        for offset in range(-reach, reach + 1):
            if offset != 0:
                block = d_window[..., (offset + reach) * rows : (offset + reach + 1) * rows]
                d_key_value = d_key_value + self.from_behind(block, offset)
        return jnp.concatenate([d_query[None], d_key_value]).astype(BF16)


def latent_index(latent_len, first_row, row_count, token_total):
    positions = first_row + jnp.arange(row_count, dtype=jnp.int32)
    ends = jnp.cumsum(latent_len, dtype=jnp.int32)
    found = jnp.sum((positions[:, None] >= ends[None, :]).astype(jnp.int32), axis=1, dtype=jnp.int32)
    return jnp.where((positions >= 0) & (positions < token_total), found, -1)


def normed(values):
    average = jnp.mean(values, axis=-1, keepdims=True)
    centred = values - average
    spread = jnp.mean(centred * centred, axis=-1, keepdims=True)
    inverse = lax.rsqrt(spread + NORM_EPS)
    return centred * inverse, inverse


def norm_back(unit, inverse, grad):
    along = jnp.mean(grad * unit, axis=-1, keepdims=True)
    return inverse * (grad - jnp.mean(grad, axis=-1, keepdims=True) - unit * along)


def pick(rows_by_latent, ids):
    out = jnp.zeros((ids.shape[0], rows_by_latent.shape[1]), F32)
    for number in range(rows_by_latent.shape[0]):
        out = jnp.where(ids[:, None] == number, rows_by_latent[number][None], out)
    return out


def gelu_pair(value):
    root = math.sqrt(2.0 / math.pi)
    bend = jnp.tanh(root * (value + 0.044715 * value * value * value))
    slope = root * (1.0 + 3.0 * 0.044715 * value * value)
    gelu = 0.5 * value * (1.0 + bend)
    return gelu, 0.5 * (1.0 + bend) + 0.5 * value * (1.0 - bend * bend) * slope


def local(
    tokens,
    conditioning,
    latent_len,
    w_ada,
    b_ada,
    w_qkv,
    b_qv,
    w_proj,
    b_proj,
    w_fc1,
    b_fc1,
    w_fc2,
    b_fc2,
    cotangent,
):
    rows, width = tokens.shape
    share_width = w_qkv.shape[0]
    features = w_qkv.shape[2]
    units = w_fc1.shape[1]
    heads = features // DH
    latents = conditioning.shape[0]
    n_dp, n_tensor = lax.axis_size("dp"), lax.axis_size("tensor")
    my_dp, my_tensor = lax.axis_index("dp"), lax.axis_index("tensor")
    total = rows * n_dp
    share = rows // n_tensor

    full_qkv = gather_rows(w_qkv.reshape(share_width, 3 * features))
    full_late = gather_rows(jnp.concatenate([w_fc1, w_fc2.T, w_proj.T], axis=1))
    full_fc1 = full_late[:, :units]
    full_fc2 = full_late[:, units : 2 * units]
    full_proj = full_late[:, 2 * units :]

    cond = conditioning.astype(F32)
    gate = 1.0 / (1.0 + jnp.exp(-cond))
    activated = (cond * gate).astype(BF16)
    own_activated = lax.dynamic_slice_in_dim(activated, my_dp * share_width, share_width, 1)
    flat_ada = w_ada.reshape(share_width, 6 * features)
    mod_part = jnp.dot(own_activated, flat_ada, preferred_element_type=F32)
    mod_mine = jnp.sum(gather(mod_part, "dp", n_dp), axis=0) + b_ada.astype(F32).reshape(1, -1)
    modulation = gather(mod_mine, "tensor", n_tensor)
    modulation = modulation.reshape(n_tensor, latents, 6, features).transpose(2, 1, 0, 3)
    modulation = modulation.reshape(6, latents, width)

    ids = latent_index(latent_len, my_dp * rows, rows, total)
    own_ids = lax.dynamic_slice_in_dim(ids, my_tensor * share, share, 0)

    def own(values):
        return lax.dynamic_slice_in_dim(values, my_tensor * share, share, 0)

    unit_one, inverse_one = normed(tokens.astype(F32))
    hidden_one = (unit_one * (1.0 + pick(modulation[1], ids)) + pick(modulation[0], ids)).astype(BF16)
    bias = jnp.concatenate([b_qv[0], jnp.zeros_like(b_qv[0]), b_qv[1]]).astype(F32)
    projected = lax.dot_general(
        full_qkv, hidden_one, (((0,), (1,)), ((), ())), preferred_element_type=F32
    )
    projected = (projected + bias[:, None]).astype(BF16).reshape(3, heads, DH, rows)
    split = HeadSplit if 2 * heads == n_dp else Window
    attention = split(latent_len, rows)
    attended = attention.forward(projected)
    attn_part = lax.dot_general(
        attended, full_proj, (((0,), (1,)), ((), ())), preferred_element_type=F32
    )
    attn_out = sum_shares(attn_part, "tensor") + b_proj.astype(F32)
    own_tokens = own(tokens).astype(F32)
    gate_one = pick(modulation[2], own_ids)
    residual_mid = own_tokens + gate_one * attn_out
    unit_two, inverse_two = normed(residual_mid)
    scale_two = 1.0 + pick(modulation[4], own_ids)
    hidden_two_own = (unit_two * scale_two + pick(modulation[3], own_ids)).astype(BF16)
    hidden_two = gather_shares(hidden_two_own, "tensor")

    d_mlp = (cotangent.astype(F32) * pick(modulation[5], ids)).astype(BF16)
    d_gelu = jnp.dot(d_mlp, full_fc2, preferred_element_type=F32)
    pre_act = jnp.dot(hidden_two, full_fc1, preferred_element_type=F32) + b_fc1.astype(F32)
    gelu_out, gelu_slope = gelu_pair(pre_act)
    gelu_out = gelu_out.astype(BF16)
    d_pre_wide = d_gelu * gelu_slope
    d_pre = d_pre_wide.astype(BF16)
    by_last = (((1,), (1,)), ((), ()))
    by_token = (((0,), (0,)), ((), ()))
    d_two_part = lax.dot_general(d_pre, full_fc1, by_last, preferred_element_type=F32)
    d_hidden_two = sum_shares(d_two_part, "tensor")
    own_cotangent = own(cotangent).astype(F32)
    d_mid = own_cotangent + norm_back(unit_two, inverse_two, d_hidden_two * scale_two)
    d_attn_own = (d_mid * gate_one).astype(BF16)
    d_attn = gather_shares(d_attn_own, "tensor")

    mlp_part = lax.dot_general(gelu_out, full_fc2, by_last, preferred_element_type=F32)
    mlp_out = sum_shares(mlp_part, "tensor") + b_fc2.astype(F32)
    gate_two = pick(modulation[5], own_ids)
    result = gather_shares((residual_mid + gate_two * mlp_out).astype(BF16), "tensor")

    d_attended = lax.dot_general(
        full_proj, d_attn, (((0,), (1,)), ((), ())), preferred_element_type=F32
    ).astype(BF16)
    d_projected = attention.backward(d_attended).reshape(3 * features, rows)
    d_one_part = lax.dot_general(
        d_projected, full_qkv, (((0,), (1,)), ((), ())), preferred_element_type=F32
    )
    d_hidden_one = sum_shares(d_one_part, "tensor")
    own_unit, own_inverse = own(unit_one), own(inverse_one)
    scale_one = 1.0 + pick(modulation[1], own_ids)
    grad_own = d_mid + norm_back(own_unit, own_inverse, d_hidden_one * scale_one)
    grad_tokens = gather_shares(grad_own.astype(BF16), "tensor").astype(F32)

    grad_fc1 = lax.dot_general(hidden_two, d_pre, by_token, preferred_element_type=F32)
    grad_fc2 = lax.dot_general(d_mlp, gelu_out, by_token, preferred_element_type=F32)
    grad_proj = lax.dot_general(
        d_attn, attended, (((0,), (1,)), ((), ())), preferred_element_type=F32
    )
    grad_late = jnp.concatenate(
        [grad_fc1.astype(BF16), grad_fc2.astype(BF16), grad_proj.astype(BF16)], axis=1
    )
    grad_late = scatter_rows(grad_late)
    grad_qkv = lax.dot_general(
        hidden_one, d_projected, (((0,), (1,)), ((), ())), preferred_element_type=F32
    )
    grad_qkv = scatter_rows(grad_qkv.astype(BF16)).reshape(share_width, 3, features)

    d_float = d_projected.astype(F32).reshape(3, features, rows)
    bias_part = jnp.concatenate(
        [
            jnp.sum(d_mlp.astype(F32), axis=0),
            jnp.sum(d_attn.astype(F32), axis=0),
            jnp.sum(d_pre.astype(F32), axis=0),
            jnp.sum(d_float[0], axis=1),
            jnp.sum(d_float[2], axis=1),
        ]
    )
    bias_total = jnp.sum(gather(bias_part, "dp", n_dp), axis=0)

    d_token = jnp.stack(
        [
            d_hidden_one,
            d_hidden_one * own_unit,
            d_mid * attn_out,
            d_hidden_two,
            d_hidden_two * unit_two,
            own_cotangent * mlp_out,
        ],
        axis=1,
    ).astype(BF16)
    one_hot = (jnp.arange(latents, dtype=jnp.int32)[:, None] == own_ids[None, :]).astype(BF16)
    d_mod_part = jnp.dot(one_hot, d_token.reshape(share, 6 * width), preferred_element_type=F32)
    d_mod_part = d_mod_part.reshape(latents * 6, n_tensor, features).transpose(1, 0, 2)
    d_mod_mine = jnp.sum(exchange(d_mod_part, "tensor"), axis=0)
    d_mod = jnp.sum(gather(d_mod_mine, "dp", n_dp), axis=0).reshape(latents, 6 * features)
    grad_b_ada = jnp.sum(d_mod, axis=0).reshape(6, features)
    grad_w_ada = lax.dot_general(
        own_activated.astype(F32), d_mod, by_token, precision=lax.Precision.HIGHEST
    ).reshape(share_width, 6, features)
    high = d_mod.astype(BF16)
    low = (d_mod - high.astype(F32)).astype(BF16)
    d_active = lax.dot_general(
        jnp.concatenate([high, low]), flat_ada, by_last, preferred_element_type=F32
    )
    d_active = d_active[:latents] + d_active[latents:]
    d_active = jnp.sum(gather(d_active, "tensor", n_tensor), axis=0)
    d_active = gather(d_active, "dp", n_dp).transpose(1, 0, 2).reshape(latents, width)
    grad_cond = d_active * (gate * (1.0 + cond * (1.0 - gate)))

    return (
        result,
        grad_tokens,
        grad_cond,
        grad_w_ada,
        grad_b_ada,
        grad_qkv,
        bias_total[2 * width + units :].reshape(2, features),
        grad_late[:, 2 * units :].T,
        bias_total[width : 2 * width],
        grad_late[:, :units],
        bias_total[2 * width : 2 * width + units],
        grad_late[:, units : 2 * units].T,
        bias_total[:width],
    )


def solution(mesh):
    in_specs = (
        P("dp", None),
        P(),
        P(),
        P("dp", None, "tensor"),
        P(None, "tensor"),
        P("dp", None, "tensor"),
        P(None, "tensor"),
        P("tensor", "dp"),
        P(),
        P("dp", "tensor"),
        P("tensor"),
        P("tensor", "dp"),
        P(),
        P("dp", None),
    )
    out_specs = (
        P("dp", None),
        P("dp", None),
        P(),
        P("dp", None, "tensor"),
        P(None, "tensor"),
        P("dp", None, "tensor"),
        P(None, "tensor"),
        P("tensor", "dp"),
        P(),
        P("dp", "tensor"),
        P("tensor"),
        P("tensor", "dp"),
        P(),
    )
    return jax.shard_map(local, mesh=mesh, in_specs=in_specs, out_specs=out_specs, check_vma=False)
```

```python
import math

import jax
import jax.numpy as jnp
from jax import lax
from jax.experimental import pallas as pl
from jax.experimental.pallas import tpu as pltpu
from jax.sharding import PartitionSpec as P

DH = 72
SEQ = 1024
NORM_EPS = 1e-06
NEGATIVE = -1e30
SCALE = 1.0 / math.sqrt(DH)
VMEM_BYTES = 40 * 1024 * 1024
BF16 = jnp.bfloat16
F32 = jnp.float32


def swap(block, axis, bits):
    route = [(i, i ^ bits) for i in range(lax.axis_size(axis))]
    return lax.ppermute(block, axis, route)


def exchange(blocks, axis):
    return lax.all_to_all(blocks, axis, 0, 0, tiled=True)


def gather(block, axis, count):
    return exchange(jnp.broadcast_to(block[None], (count,) + block.shape), axis)


def after(value, *others):
    return lax.optimization_barrier((value,) + others)[0]


def choose(core, first, second):
    return jnp.where(core == 0, first, second), jnp.where(core == 0, second, first)


def gather_pair_now(first, second):
    count = lax.axis_size("dp")
    both = jnp.stack([first, second])
    blocks = jnp.broadcast_to(both[None], (count // 2,) + both.shape)
    mine = exchange(blocks.reshape((count,) + first.shape), "dp").reshape(-1, first.shape[1])
    return mine, swap(mine, "dp", 1)


def gather_pair_beside(first, second):
    count = lax.axis_size("dp")
    core, chip = lax.axis_index("dp") % 2, lax.axis_index("dp") // 2
    keep, send = choose(core, first, second)
    theirs = swap(send, "dp", 1)
    rows = jnp.concatenate(choose(core, keep, theirs))
    full = jnp.zeros((count // 2,) + rows.shape, rows.dtype)
    for step in range(count // 2):
        part = swap(rows, "dp", 2 * step) if step else rows
        full = lax.dynamic_update_index_in_dim(full, part, chip ^ step, 0)
    mine = full.reshape(-1, rows.shape[1])
    return mine, swap(mine, "dp", 1)


def scatter_pair(mine, other):
    count = lax.axis_size("dp")
    core, chip = lax.axis_index("dp") % 2, lax.axis_index("dp") // 2
    total = (mine + swap(other.astype(BF16), "dp", 1).astype(F32)).astype(BF16)
    blocks = total.reshape(count // 2, total.shape[0] // (count // 2), total.shape[1])
    rows = lax.dynamic_index_in_dim(blocks, chip, 0, keepdims=False).astype(F32)
    for step in range(1, count // 2):
        sent = lax.dynamic_index_in_dim(blocks, chip ^ step, 0, keepdims=False)
        rows = rows + swap(sent, "dp", 2 * step).astype(F32)
    half = rows.shape[0] // 2
    keep, send = choose(core, rows[:half], rows[half:])
    return choose(core, keep, swap(send, "dp", 1))


def sum_beside(partial, axis):
    count, me = lax.axis_size(axis), lax.axis_index(axis)
    blocks = partial.astype(BF16).reshape((count, partial.shape[0] // count) + partial.shape[1:])
    total = lax.dynamic_index_in_dim(blocks, me, 0, keepdims=False).astype(F32)
    for bits in range(1, count):
        sent = lax.dynamic_index_in_dim(blocks, me ^ bits, 0, keepdims=False)
        total = total + swap(sent, axis, bits).astype(F32)
    return total


def gather_beside(share, axis):
    count, me = lax.axis_size(axis), lax.axis_index(axis)
    parts = jnp.stack([share] + [swap(share, axis, bits) for bits in range(1, count)])
    ordered = [lax.dynamic_index_in_dim(parts, me ^ place, 0, keepdims=False) for place in range(count)]
    return jnp.concatenate(ordered)


def sum_shares(partial, axis):
    count = lax.axis_size(axis)
    blocks = partial.astype(BF16).reshape((count, partial.shape[0] // count) + partial.shape[1:])
    return jnp.sum(exchange(blocks, axis).astype(F32), axis=0)


def gather_shares(share, axis):
    count = lax.axis_size(axis)
    parts = gather(share, axis, count)
    return parts.reshape((count * share.shape[0],) + share.shape[1:])


def tile_range(meta_ref, latents, tile, core):
    lane = lax.broadcasted_iota(jnp.int32, (1, 256), 1)
    first = tile * 512 + core * 128
    last = first + 383
    place = first + lane + jnp.where(lane >= 128, 128, 0)
    begin = jnp.zeros((1, 256), jnp.int32)
    finish = jnp.zeros((1, 256), jnp.int32)
    low = jnp.int32(0)
    high = jnp.int32(0)
    start = jnp.int32(0)
    for number in range(latents):
        end = start + meta_ref[1 + number]
        inside = (place >= start) & (place < end)
        begin = jnp.where(inside, start, begin)
        finish = jnp.where(inside, end, finish)
        low = jnp.where((first >= start) & (first < end), start, low)
        high = jnp.where((last >= start) & (last < end), end, high)
        start = end
    return begin, finish, low // 256, (high + 255) // 256


def pair(ref, tile, start):
    left = ref[2 * tile, :, start : start + 128]
    right = ref[2 * tile + 1, :, start : start + 128]
    return jnp.concatenate([left, right], axis=1)


def key_mask(block, begin, finish):
    place = block * 256 + lax.broadcasted_iota(jnp.int32, (256, 256), 0)
    return (place >= begin) & (place < finish)


def forward_kernel(latents, meta_ref, packed_ref, out_ref, exact_ref, log_ref, keys, scores):
    blocks = packed_ref.shape[0]
    core = meta_ref[0]
    for block in range(blocks):
        keys[block] = packed_ref[block, :, :256].astype(F32).T.astype(BF16)
    for tile in range(blocks // 2):
        begin, finish, low, high = tile_range(meta_ref, latents, tile, core)
        query = pair(packed_ref, tile, 512)

        def score(block, largest):
            raw = jnp.dot(keys[block], query, preferred_element_type=F32) * SCALE
            raw = jnp.where(key_mask(block, begin, finish), raw, NEGATIVE)
            scores[block] = raw
            return jnp.maximum(largest, jnp.max(raw, axis=0, keepdims=True))

        largest = lax.fori_loop(low, high, score, jnp.full((1, 256), NEGATIVE, F32))

        def mix(block, carry):
            total, mixed = carry
            weights = jnp.exp(scores[block] - largest)
            total = total + jnp.sum(weights, axis=0, keepdims=True)
            values = packed_ref[block, :, 256:512]
            mixed = mixed + jnp.dot(values, weights.astype(BF16), preferred_element_type=F32)
            return total, mixed

        total, mixed = lax.fori_loop(
            low, high, mix, (jnp.zeros((1, 256), F32), jnp.zeros((DH, 256), F32))
        )
        mixed = mixed / total
        log_total = largest + jnp.log(total)
        for half in range(2):
            part = mixed[:, half * 128 : half * 128 + 128]
            exact_ref[2 * tile + half] = part
            out_ref[2 * tile + half] = part.astype(BF16)
            log_ref[2 * tile + half] = log_total[:, half * 128 : half * 128 + 128]


def backward_kernel(
    latents, meta_ref, packed_ref, grad_ref, exact_ref, log_ref, out_ref, keys, values, d_keys, d_values
):
    blocks = packed_ref.shape[0]
    core = meta_ref[0]
    for block in range(blocks):
        keys[block] = packed_ref[block, :, :256].astype(F32).T.astype(BF16)
        values[block] = packed_ref[block, :, 256:512].astype(F32).T.astype(BF16)
    d_keys[...] = jnp.zeros_like(d_keys)
    d_values[...] = jnp.zeros_like(d_values)
    by_query = (((1,), (1,)), ((), ()))
    for tile in range(blocks // 2):
        begin, finish, low, high = tile_range(meta_ref, latents, tile, core)
        query = pair(packed_ref, tile, 512)
        grad = pair(grad_ref, tile, 0)
        inner = jnp.sum(grad.astype(F32) * pair(exact_ref, tile, 0), axis=0, keepdims=True)
        log_total = pair(log_ref, tile, 0)

        def step(block, d_query):
            raw = jnp.dot(keys[block], query, preferred_element_type=F32) * SCALE
            probs = jnp.where(key_mask(block, begin, finish), jnp.exp(raw - log_total), 0.0)
            d_probs = jnp.dot(values[block], grad, preferred_element_type=F32)
            d_scores = (probs * (d_probs - inner)).astype(BF16)
            d_values[block] += lax.dot_general(
                grad, probs.astype(BF16), by_query, preferred_element_type=F32
            )
            d_keys[block] += lax.dot_general(query, d_scores, by_query, preferred_element_type=F32)
            key_rows = packed_ref[block, :, :256]
            return d_query + jnp.dot(key_rows, d_scores, preferred_element_type=F32)

        d_query = lax.fori_loop(low, high, step, jnp.zeros((DH, 256), F32)) * SCALE
        for half in range(2):
            part = d_query[:, half * 128 : half * 128 + 128]
            out_ref[2 * tile + half, :, 512:640] = part.astype(BF16)
    for block in range(blocks):
        out_ref[block, :, :256] = (d_keys[block] * SCALE).astype(BF16)
        out_ref[block, :, 256:512] = d_values[block].astype(BF16)


def attend_forward(meta, packed):
    blocks = packed.shape[0]
    shape = jax.ShapeDtypeStruct
    return pl.pallas_call(
        lambda *refs: forward_kernel(meta.shape[0] - 1, *refs),
        out_shape=(
            shape((blocks, DH, 128), BF16),
            shape((blocks, DH, 128), F32),
            shape((blocks, 1, 128), F32),
        ),
        in_specs=[
            pl.BlockSpec(memory_space=pltpu.SMEM),
            pl.BlockSpec(memory_space=pltpu.VMEM),
        ],
        out_specs=tuple([pl.BlockSpec(memory_space=pltpu.VMEM)] * 3),
        scratch_shapes=[
            pltpu.VMEM((blocks, 256, DH), BF16),
            pltpu.VMEM((blocks, 256, 256), F32),
        ],
        compiler_params=pltpu.CompilerParams(vmem_limit_bytes=VMEM_BYTES),
        cost_estimate=pl.CostEstimate(flops=10**9, bytes_accessed=4 * 10**6, transcendentals=10**6),
        name="attend_forward",
    )(meta, packed)


def attend_backward(meta, packed, grad, exact, log_total):
    blocks = packed.shape[0]
    return pl.pallas_call(
        lambda *refs: backward_kernel(meta.shape[0] - 1, *refs),
        out_shape=jax.ShapeDtypeStruct(packed.shape, BF16),
        in_specs=[pl.BlockSpec(memory_space=pltpu.SMEM)]
        + [pl.BlockSpec(memory_space=pltpu.VMEM)] * 4,
        out_specs=pl.BlockSpec(memory_space=pltpu.VMEM),
        scratch_shapes=[
            pltpu.VMEM((blocks, 256, DH), BF16),
            pltpu.VMEM((blocks, 256, DH), BF16),
            pltpu.VMEM((blocks, DH, 256), F32),
            pltpu.VMEM((blocks, DH, 256), F32),
        ],
        compiler_params=pltpu.CompilerParams(vmem_limit_bytes=VMEM_BYTES),
        cost_estimate=pl.CostEstimate(flops=3 * 10**9, bytes_accessed=4 * 10**6, transcendentals=10**6),
        name="attend_backward",
    )(meta, packed, grad, exact, log_total)


class HeadSplit:
    def __init__(self, latent_len, rows):
        self.rows = rows
        self.meta = jnp.concatenate([lax.axis_index("dp").astype(jnp.int32)[None] % 2, latent_len])

    def forward(self, projected):
        heads, rows = projected.shape[1], self.rows
        query = projected[0].reshape(heads, DH, 2, rows // 2).transpose(0, 2, 1, 3)
        key = jnp.broadcast_to(projected[1][:, None], (heads, 2, DH, rows))
        value = jnp.broadcast_to(projected[2][:, None], (heads, 2, DH, rows))
        packed = jnp.concatenate([key, value, query], axis=3)
        self.packed = exchange(packed.reshape(heads * 2, DH, rows * 5 // 2), "dp")
        out, self.exact, self.log_total = attend_forward(self.meta, self.packed)
        return self.unsplit(exchange(out, "dp")).reshape(heads * DH, rows)

    def unsplit(self, parts):
        heads = parts.shape[0] // 2
        parts = parts.reshape(heads, 2, DH, self.rows // 2).transpose(0, 2, 1, 3)
        return parts.reshape(heads, DH, self.rows)

    def backward(self, d_attended):
        rows = self.rows
        heads = d_attended.shape[0] // DH
        grad = d_attended.reshape(heads, DH, 2, rows // 2).transpose(0, 2, 1, 3)
        grad = exchange(grad.reshape(heads * 2, DH, rows // 2), "dp")
        out = attend_backward(self.meta, self.packed, grad, self.exact, self.log_total)
        parts = exchange(out, "dp")
        d_query = self.unsplit(parts[:, :, 2 * rows :])
        halves = parts.reshape(heads, 2, DH, rows * 5 // 2)[..., : 2 * rows].astype(F32)
        d_key_value = (halves[:, 0] + halves[:, 1]).astype(BF16)
        return jnp.stack([d_query, d_key_value[..., :rows], d_key_value[..., rows:]])


class Window:
    def __init__(self, latent_len, rows):
        self.rows = rows
        self.reach = (SEQ - 2) // rows + 1
        total = rows * lax.axis_size("dp")
        first = lax.axis_index("dp") * rows
        own = latent_index(latent_len, first, rows, total)
        ids = [
            latent_index(latent_len, first + offset * rows, rows, total)
            for offset in range(-self.reach, self.reach + 1)
        ]
        self.allowed = own[:, None] == jnp.concatenate(ids)[None, :]

    def from_behind(self, block, distance):
        devices = range(lax.axis_size("dp"))
        return lax.ppermute(
            block, "dp", [(i - distance, i) for i in devices if i - distance in devices]
        )

    def head_scores(self, query, key):
        raw = jnp.einsum("eq,ek->qk", query, key, preferred_element_type=F32) * SCALE
        return jnp.where(self.allowed, raw, NEGATIVE)

    def forward(self, projected):
        key_value = projected[1:]
        pieces = [
            key_value if offset == 0 else self.from_behind(key_value, -offset)
            for offset in range(-self.reach, self.reach + 1)
        ]
        window = jnp.concatenate(pieces, axis=3)
        self.operands = (projected[0], window[0], window[1])

        def one(operands):
            query, key, value = operands
            scores = self.head_scores(query, key)
            largest = jnp.max(scores, axis=1, keepdims=True)
            weights = jnp.exp(scores - largest)
            totals = jnp.sum(weights, axis=1, keepdims=True)
            probs = (weights / totals).astype(BF16)
            mixed = jnp.einsum("qk,ek->eq", probs, value, preferred_element_type=F32)
            return mixed.astype(BF16), (largest + jnp.log(totals))[:, 0]

        out, self.log_total = lax.map(one, self.operands)
        return out.reshape(-1, self.rows)

    def backward(self, d_attended):
        rows, reach = self.rows, self.reach
        grads = d_attended.reshape(-1, DH, rows)

        def one(operands):
            query, key, value, grad, log_total = operands
            probs = jnp.exp(self.head_scores(query, key) - log_total[:, None])
            d_value = jnp.einsum("qk,eq->ek", probs.astype(BF16), grad, preferred_element_type=F32)
            d_probs = jnp.einsum("eq,ek->qk", grad, value, preferred_element_type=F32)
            inner = jnp.sum(probs * d_probs, axis=1, keepdims=True)
            d_scores = (probs * (d_probs - inner)).astype(BF16)
            d_query = jnp.einsum("qk,ek->eq", d_scores, key, preferred_element_type=F32) * SCALE
            d_key = jnp.einsum("qk,eq->ek", d_scores, query, preferred_element_type=F32) * SCALE
            return d_query, d_key, d_value

        d_query, d_key, d_value = lax.map(one, self.operands + (grads, self.log_total))
        d_window = jnp.stack([d_key, d_value])
        d_key_value = d_window[..., reach * rows : (reach + 1) * rows]
        for offset in range(-reach, reach + 1):
            if offset != 0:
                block = d_window[..., (offset + reach) * rows : (offset + reach + 1) * rows]
                d_key_value = d_key_value + self.from_behind(block, offset)
        return jnp.concatenate([d_query[None], d_key_value]).astype(BF16)


def latent_index(latent_len, first_row, row_count, token_total):
    positions = first_row + jnp.arange(row_count, dtype=jnp.int32)
    ends = jnp.cumsum(latent_len, dtype=jnp.int32)
    found = jnp.sum((positions[:, None] >= ends[None, :]).astype(jnp.int32), axis=1, dtype=jnp.int32)
    return jnp.where((positions >= 0) & (positions < token_total), found, -1)


def normed(values):
    average = jnp.mean(values, axis=-1, keepdims=True)
    centred = values - average
    spread = jnp.mean(centred * centred, axis=-1, keepdims=True)
    inverse = lax.rsqrt(spread + NORM_EPS)
    return centred * inverse, inverse


def norm_back(unit, inverse, grad):
    along = jnp.mean(grad * unit, axis=-1, keepdims=True)
    return inverse * (grad - jnp.mean(grad, axis=-1, keepdims=True) - unit * along)


def pick(rows_by_latent, ids):
    out = jnp.zeros((ids.shape[0], rows_by_latent.shape[1]), F32)
    for number in range(rows_by_latent.shape[0]):
        out = jnp.where(ids[:, None] == number, rows_by_latent[number][None], out)
    return out


def gelu_pair(value):
    root = math.sqrt(2.0 / math.pi)
    bend = jnp.tanh(root * (value + 0.044715 * value * value * value))
    slope = root * (1.0 + 3.0 * 0.044715 * value * value)
    gelu = 0.5 * value * (1.0 + bend)
    return gelu, 0.5 * (1.0 + bend) + 0.5 * value * (1.0 - bend * bend) * slope


def local(
    tokens,
    conditioning,
    latent_len,
    w_ada,
    b_ada,
    w_qkv,
    b_qv,
    w_proj,
    b_proj,
    w_fc1,
    b_fc1,
    w_fc2,
    b_fc2,
    cotangent,
):
    rows, width = tokens.shape
    share_width = w_qkv.shape[0]
    features = w_qkv.shape[2]
    units = w_fc1.shape[1]
    heads = features // DH
    latents = conditioning.shape[0]
    n_dp, n_tensor = lax.axis_size("dp"), lax.axis_size("tensor")
    my_dp, my_tensor = lax.axis_index("dp"), lax.axis_index("tensor")
    total = rows * n_dp
    share = rows // n_tensor

    core = my_dp % 2
    qk = w_qkv[:, :2].reshape(share_width, 2 * features)
    vp = jnp.concatenate([w_qkv[:, 2], w_proj.T], axis=1)
    early_mine, early_other = gather_pair_now(qk, vp)
    full_vp = choose(core, early_other, early_mine)[0]

    cond = conditioning.astype(F32)
    gate = 1.0 / (1.0 + jnp.exp(-cond))
    activated = (cond * gate).astype(BF16)
    own_activated = lax.dynamic_slice_in_dim(activated, my_dp * share_width, share_width, 1)
    flat_ada = w_ada.reshape(share_width, 6 * features)
    mod_part = jnp.dot(own_activated, flat_ada, preferred_element_type=F32)
    mod_mine = jnp.sum(gather(mod_part, "dp", n_dp), axis=0) + b_ada.astype(F32).reshape(1, -1)
    modulation = gather(mod_mine, "tensor", n_tensor)
    modulation = modulation.reshape(n_tensor, latents, 6, features).transpose(2, 1, 0, 3)
    modulation = modulation.reshape(6, latents, width)

    ids = latent_index(latent_len, my_dp * rows, rows, total)
    own_ids = lax.dynamic_slice_in_dim(ids, my_tensor * share, share, 0)

    def own(values):
        return lax.dynamic_slice_in_dim(values, my_tensor * share, share, 0)

    unit_one, inverse_one = normed(tokens.astype(F32))
    hidden_one = (unit_one * (1.0 + pick(modulation[1], ids)) + pick(modulation[0], ids)).astype(BF16)
    by_hidden = (((0,), (1,)), ((), ()))
    by_last = (((1,), (1,)), ((), ()))
    by_token = (((0,), (0,)), ((), ()))
    blank = jnp.zeros((features, rows), BF16)
    bias = jnp.concatenate([b_qv[0], jnp.zeros_like(b_qv[0]), b_qv[1]]).astype(F32)
    from_mine = lax.dot_general(early_mine, hidden_one, by_hidden, preferred_element_type=F32)
    from_other = lax.dot_general(early_other, hidden_one, by_hidden, preferred_element_type=F32)
    projected = jnp.concatenate(choose(core, from_mine, from_other))[: 3 * features]
    projected = (projected + bias[:, None]).astype(BF16).reshape(3, heads, DH, rows)
    split = HeadSplit if 2 * heads == n_dp else Window
    attention = split(latent_len, rows)
    attended = attention.forward(projected)
    attended_low = jnp.concatenate([blank, attended])
    attn_part = lax.dot_general(attended_low, full_vp, (((0,), (1,)), ((), ())), preferred_element_type=F32)
    late_mine, late_other = gather_pair_beside(after(w_fc1, attended), after(w_fc2.T, attended))
    full_fc1, full_fc2 = choose(core, late_mine, late_other)
    attn_out = sum_shares(attn_part, "tensor") + b_proj.astype(F32)
    own_tokens = own(tokens).astype(F32)
    gate_one = pick(modulation[2], own_ids)
    residual_mid = own_tokens + gate_one * attn_out
    unit_two, inverse_two = normed(residual_mid)
    scale_two = 1.0 + pick(modulation[4], own_ids)
    hidden_two_own = (unit_two * scale_two + pick(modulation[3], own_ids)).astype(BF16)
    hidden_two = gather_shares(hidden_two_own, "tensor")

    d_mlp = (cotangent.astype(F32) * pick(modulation[5], ids)).astype(BF16)
    d_gelu = jnp.dot(d_mlp, full_fc2, preferred_element_type=F32)
    pre_act = jnp.dot(hidden_two, full_fc1, preferred_element_type=F32) + b_fc1.astype(F32)
    gelu_out, gelu_slope = gelu_pair(pre_act)
    gelu_out = gelu_out.astype(BF16)
    d_pre_wide = d_gelu * gelu_slope
    d_pre = d_pre_wide.astype(BF16)
    d_two_part = lax.dot_general(d_pre, full_fc1, by_last, preferred_element_type=F32)
    d_hidden_two = sum_shares(d_two_part, "tensor")
    own_cotangent = own(cotangent).astype(F32)
    d_mid = own_cotangent + norm_back(unit_two, inverse_two, d_hidden_two * scale_two)
    d_attn_own = (d_mid * gate_one).astype(BF16)
    d_attn = gather_shares(d_attn_own, "tensor")

    left_mine, left_other = choose(core, hidden_two, d_mlp)
    right_mine, right_other = choose(core, d_pre, gelu_out)
    grad_fc1, grad_fc2 = scatter_pair(
        lax.dot_general(left_mine, right_mine, by_token, preferred_element_type=F32),
        lax.dot_general(left_other, right_other, by_token, preferred_element_type=F32),
    )

    mlp_part = lax.dot_general(
        after(gelu_out, d_attn), full_fc2, by_last, preferred_element_type=F32
    )
    mlp_out = sum_beside(mlp_part, "tensor") + b_fc2.astype(F32)
    gate_two = pick(modulation[5], own_ids)
    result = gather_beside((residual_mid + gate_two * mlp_out).astype(BF16), "tensor")

    d_attended = lax.dot_general(full_vp, d_attn, by_hidden, preferred_element_type=F32)
    d_attended = d_attended[features:].astype(BF16)
    d_projected = attention.backward(d_attended).reshape(3 * features, rows)
    d_qk = d_projected[: 2 * features]
    d_value = d_projected[2 * features :]
    d_mine, d_other = choose(core, d_qk, jnp.concatenate([d_value, blank]))
    d_one_part = lax.dot_general(
        d_mine, early_mine, (((0,), (1,)), ((), ())), preferred_element_type=F32
    ) + lax.dot_general(d_other, early_other, (((0,), (1,)), ((), ())), preferred_element_type=F32)
    d_hidden_one = sum_shares(d_one_part, "tensor")
    own_unit, own_inverse = own(unit_one), own(inverse_one)
    scale_one = 1.0 + pick(modulation[1], own_ids)
    grad_own = d_mid + norm_back(own_unit, own_inverse, d_hidden_one * scale_one)
    grad_tokens = gather_beside(grad_own.astype(BF16), "tensor").astype(F32)

    left = jnp.concatenate([hidden_one, d_attn])
    right_qk = jnp.concatenate([d_qk, jnp.zeros_like(d_qk)], axis=1)
    right_vp = jnp.concatenate(
        [jnp.concatenate([d_value, blank]), attended_low], axis=1
    )
    right_mine, right_other = choose(core, right_qk, right_vp)
    by_rows = (((0,), (1,)), ((), ()))
    grad_qk, grad_vp = scatter_pair(
        lax.dot_general(left, right_mine, by_rows, preferred_element_type=F32),
        lax.dot_general(left, right_other, by_rows, preferred_element_type=F32),
    )
    grad_qkv = jnp.concatenate([grad_qk, grad_vp[:, :features]], axis=1)
    grad_qkv = grad_qkv.reshape(share_width, 3, features)

    d_float = d_projected.astype(F32).reshape(3, features, rows)
    bias_part = jnp.concatenate(
        [
            jnp.sum(d_mlp.astype(F32), axis=0),
            jnp.sum(d_attn.astype(F32), axis=0),
            jnp.sum(d_pre.astype(F32), axis=0),
            jnp.sum(d_float[0], axis=1),
            jnp.sum(d_float[2], axis=1),
        ]
    )
    bias_rows = bias_part.reshape(-1, features)

    one_hot = (jnp.arange(latents, dtype=jnp.int32)[:, None] == own_ids[None, :]).astype(BF16)

    def by_latent(parts):
        joined = jnp.concatenate([part.astype(BF16) for part in parts], axis=1)
        sums = jnp.dot(one_hot, joined, preferred_element_type=F32)
        return sums.reshape(latents, len(parts), n_tensor, features)

    d_mod_last = by_latent(
        [d_mid * attn_out, d_hidden_two, d_hidden_two * unit_two, own_cotangent * mlp_out]
    )
    d_mod_first = by_latent([d_hidden_one, d_hidden_one * own_unit])
    d_mod_part = jnp.concatenate([d_mod_first, d_mod_last], axis=1).transpose(2, 0, 1, 3)
    d_mod_part = d_mod_part.reshape(n_tensor, latents * 6, features)
    d_mod_mine = jnp.sum(exchange(d_mod_part, "tensor"), axis=0)
    sums = jnp.sum(gather(jnp.concatenate([d_mod_mine, bias_rows]), "dp", n_dp), axis=0)
    d_mod = sums[: 6 * latents].reshape(latents, 6 * features)
    bias_total = sums[6 * latents :].reshape(-1)
    grad_b_ada = jnp.sum(d_mod, axis=0).reshape(6, features)
    grad_w_ada = lax.dot_general(
        own_activated.astype(F32), d_mod, by_token, precision=lax.Precision.HIGHEST
    ).reshape(share_width, 6, features)
    high = d_mod.astype(BF16)
    low = (d_mod - high.astype(F32)).astype(BF16)
    d_active = lax.dot_general(
        jnp.concatenate([high, low]), flat_ada, by_last, preferred_element_type=F32
    )
    d_active = d_active[:latents] + d_active[latents:]
    d_active = gather(d_active, ("dp", "tensor"), n_dp * n_tensor)
    d_active = jnp.sum(d_active.reshape(n_dp, n_tensor, latents, share_width), axis=1)
    d_active = d_active.transpose(1, 0, 2).reshape(latents, width)
    grad_cond = d_active * (gate * (1.0 + cond * (1.0 - gate)))

    return (
        result,
        grad_tokens,
        grad_cond,
        grad_w_ada,
        grad_b_ada,
        grad_qkv,
        bias_total[2 * width + units :].reshape(2, features),
        grad_vp[:, features:].T,
        bias_total[width : 2 * width],
        grad_fc1,
        bias_total[2 * width : 2 * width + units],
        grad_fc2.T,
        bias_total[:width],
    )


def solution(mesh):
    in_specs = (
        P("dp", None),
        P(),
        P(),
        P("dp", None, "tensor"),
        P(None, "tensor"),
        P("dp", None, "tensor"),
        P(None, "tensor"),
        P("tensor", "dp"),
        P(),
        P("dp", "tensor"),
        P("tensor"),
        P("tensor", "dp"),
        P(),
        P("dp", None),
    )
    out_specs = (
        P("dp", None),
        P("dp", None),
        P(),
        P("dp", None, "tensor"),
        P(None, "tensor"),
        P("dp", None, "tensor"),
        P(None, "tensor"),
        P("tensor", "dp"),
        P(),
        P("dp", "tensor"),
        P("tensor"),
        P("tensor", "dp"),
        P(),
    )
    return jax.shard_map(local, mesh=mesh, in_specs=in_specs, out_specs=out_specs, check_vma=False)
```

```python
import math

import jax
import jax.numpy as jnp
from jax import lax
from jax.experimental import pallas as pl
from jax.experimental.pallas import tpu as pltpu
from jax.sharding import PartitionSpec as P

DH = 72
SEQ = 1024
NORM_EPS = 1e-06
NEGATIVE = -1e30
SCALE = 1.0 / math.sqrt(DH)
VMEM_BYTES = 40 * 1024 * 1024
BF16 = jnp.bfloat16
F32 = jnp.float32


def swap(block, axis, bits):
    route = [(i, i ^ bits) for i in range(lax.axis_size(axis))]
    return lax.ppermute(block, axis, route)


def exchange(blocks, axis):
    return lax.all_to_all(blocks, axis, 0, 0, tiled=True)


def gather(block, axis, count):
    return exchange(jnp.broadcast_to(block[None], (count,) + block.shape), axis)


def after(value, *others):
    return lax.optimization_barrier((value,) + others)[0]


def choose(core, first, second):
    return jnp.where(core == 0, first, second), jnp.where(core == 0, second, first)


def pair_rows(first, second):
    core = lax.axis_index("dp") % 2
    keep, send = choose(core, first, second)
    return jnp.concatenate(choose(core, keep, swap(send, "dp", 1)))


def chip_parts(rows):
    count = lax.axis_size("dp") // 2
    return [rows] + [swap(rows, "dp", 2 * step) for step in range(1, count)]


def assemble(parts):
    chip = lax.axis_index("dp") // 2
    full = jnp.zeros((len(parts),) + parts[0].shape, parts[0].dtype)
    for step, part in enumerate(parts):
        full = lax.dynamic_update_index_in_dim(full, part, chip ^ step, 0)
    mine = full.reshape(-1, parts[0].shape[1])
    return mine, swap(mine, "dp", 1)


def pair_total(mine, other):
    count = lax.axis_size("dp") // 2
    total = (mine + swap(other.astype(BF16), "dp", 1).astype(F32)).astype(BF16)
    return total.reshape(count, total.shape[0] // count, total.shape[1])


def chip_share(blocks, step):
    chip = lax.axis_index("dp") // 2
    sent = lax.dynamic_index_in_dim(blocks, chip ^ step, 0, keepdims=False)
    return swap(sent, "dp", 2 * step) if step else sent


def finish_pair(parts):
    core = lax.axis_index("dp") % 2
    rows = sum(part.astype(F32) for part in parts)
    half = rows.shape[0] // 2
    keep, send = choose(core, rows[:half], rows[half:])
    return choose(core, keep, swap(send, "dp", 1))


def sum_beside(partial, axis):
    count, me = lax.axis_size(axis), lax.axis_index(axis)
    blocks = partial.astype(BF16).reshape((count, partial.shape[0] // count) + partial.shape[1:])
    total = lax.dynamic_index_in_dim(blocks, me, 0, keepdims=False).astype(F32)
    for bits in range(1, count):
        sent = lax.dynamic_index_in_dim(blocks, me ^ bits, 0, keepdims=False)
        total = total + swap(sent, axis, bits).astype(F32)
    return total


def gather_beside(share, axis):
    count, me = lax.axis_size(axis), lax.axis_index(axis)
    parts = jnp.stack([share] + [swap(share, axis, bits) for bits in range(1, count)])
    ordered = [lax.dynamic_index_in_dim(parts, me ^ place, 0, keepdims=False) for place in range(count)]
    return jnp.concatenate(ordered)


def exchange_shares(partial, axis):
    count = lax.axis_size(axis)
    blocks = partial.reshape((count, partial.shape[0] // count) + partial.shape[1:])
    return exchange(blocks, axis)


def sum_shares(partial, axis):
    return jnp.sum(exchange_shares(partial, axis).astype(F32), axis=0)


def gather_shares(share, axis):
    count = lax.axis_size(axis)
    parts = gather(share, axis, count)
    return parts.reshape((count * share.shape[0],) + share.shape[1:])


def tile_range(meta_ref, latents, tile, core):
    lane = lax.broadcasted_iota(jnp.int32, (1, 256), 1)
    first = tile * 512 + core * 128
    last = first + 383
    place = first + lane + jnp.where(lane >= 128, 128, 0)
    begin = jnp.zeros((1, 256), jnp.int32)
    finish = jnp.zeros((1, 256), jnp.int32)
    low = jnp.int32(0)
    high = jnp.int32(0)
    start = jnp.int32(0)
    for number in range(latents):
        end = start + meta_ref[1 + number]
        inside = (place >= start) & (place < end)
        begin = jnp.where(inside, start, begin)
        finish = jnp.where(inside, end, finish)
        low = jnp.where((first >= start) & (first < end), start, low)
        high = jnp.where((last >= start) & (last < end), end, high)
        start = end
    return begin, finish, low // 256, (high + 255) // 256


def pair(ref, tile, start):
    left = ref[2 * tile, :, start : start + 128]
    right = ref[2 * tile + 1, :, start : start + 128]
    return jnp.concatenate([left, right], axis=1)


def key_mask(block, begin, finish):
    place = block * 256 + lax.broadcasted_iota(jnp.int32, (256, 256), 0)
    return (place >= begin) & (place < finish)


def forward_kernel(latents, meta_ref, packed_ref, out_ref, exact_ref, log_ref, keys, scores):
    blocks = packed_ref.shape[0]
    core = meta_ref[0]
    for block in range(blocks):
        keys[block] = packed_ref[block, :, :256].astype(F32).T.astype(BF16)
    for tile in range(blocks // 2):
        begin, finish, low, high = tile_range(meta_ref, latents, tile, core)
        query = pair(packed_ref, tile, 512)

        def score(block, largest):
            raw = jnp.dot(keys[block], query, preferred_element_type=F32) * SCALE
            raw = jnp.where(key_mask(block, begin, finish), raw, NEGATIVE)
            scores[block] = raw
            return jnp.maximum(largest, jnp.max(raw, axis=0, keepdims=True))

        largest = lax.fori_loop(low, high, score, jnp.full((1, 256), NEGATIVE, F32))

        def mix(block, carry):
            total, mixed = carry
            weights = jnp.exp(scores[block] - largest)
            total = total + jnp.sum(weights, axis=0, keepdims=True)
            values = packed_ref[block, :, 256:512]
            mixed = mixed + jnp.dot(values, weights.astype(BF16), preferred_element_type=F32)
            return total, mixed

        total, mixed = lax.fori_loop(
            low, high, mix, (jnp.zeros((1, 256), F32), jnp.zeros((DH, 256), F32))
        )
        mixed = mixed / total
        log_total = largest + jnp.log(total)
        for half in range(2):
            part = mixed[:, half * 128 : half * 128 + 128]
            exact_ref[2 * tile + half] = part
            out_ref[2 * tile + half] = part.astype(BF16)
            log_ref[2 * tile + half] = log_total[:, half * 128 : half * 128 + 128]


def backward_kernel(
    latents, meta_ref, packed_ref, grad_ref, exact_ref, log_ref, out_ref, keys, values, d_keys, d_values
):
    blocks = packed_ref.shape[0]
    core = meta_ref[0]
    for block in range(blocks):
        keys[block] = packed_ref[block, :, :256].astype(F32).T.astype(BF16)
        values[block] = packed_ref[block, :, 256:512].astype(F32).T.astype(BF16)
    d_keys[...] = jnp.zeros_like(d_keys)
    d_values[...] = jnp.zeros_like(d_values)
    by_query = (((1,), (1,)), ((), ()))
    for tile in range(blocks // 2):
        begin, finish, low, high = tile_range(meta_ref, latents, tile, core)
        query = pair(packed_ref, tile, 512)
        grad = pair(grad_ref, tile, 0)
        inner = jnp.sum(grad.astype(F32) * pair(exact_ref, tile, 0), axis=0, keepdims=True)
        log_total = pair(log_ref, tile, 0)

        def step(block, d_query):
            raw = jnp.dot(keys[block], query, preferred_element_type=F32) * SCALE
            probs = jnp.where(key_mask(block, begin, finish), jnp.exp(raw - log_total), 0.0)
            d_probs = jnp.dot(values[block], grad, preferred_element_type=F32)
            d_scores = (probs * (d_probs - inner)).astype(BF16)
            d_values[block] += lax.dot_general(
                grad, probs.astype(BF16), by_query, preferred_element_type=F32
            )
            d_keys[block] += lax.dot_general(query, d_scores, by_query, preferred_element_type=F32)
            key_rows = packed_ref[block, :, :256]
            return d_query + jnp.dot(key_rows, d_scores, preferred_element_type=F32)

        d_query = lax.fori_loop(low, high, step, jnp.zeros((DH, 256), F32)) * SCALE
        for half in range(2):
            part = d_query[:, half * 128 : half * 128 + 128]
            out_ref[2 * tile + half, :, 512:640] = part.astype(BF16)
    for block in range(blocks):
        out_ref[block, :, :256] = (d_keys[block] * SCALE).astype(BF16)
        out_ref[block, :, 256:512] = d_values[block].astype(BF16)


def attend_forward(meta, packed):
    blocks = packed.shape[0]
    shape = jax.ShapeDtypeStruct
    return pl.pallas_call(
        lambda *refs: forward_kernel(meta.shape[0] - 1, *refs),
        out_shape=(
            shape((blocks, DH, 128), BF16),
            shape((blocks, DH, 128), F32),
            shape((blocks, 1, 128), F32),
        ),
        in_specs=[
            pl.BlockSpec(memory_space=pltpu.SMEM),
            pl.BlockSpec(memory_space=pltpu.VMEM),
        ],
        out_specs=tuple([pl.BlockSpec(memory_space=pltpu.VMEM)] * 3),
        scratch_shapes=[
            pltpu.VMEM((blocks, 256, DH), BF16),
            pltpu.VMEM((blocks, 256, 256), F32),
        ],
        compiler_params=pltpu.CompilerParams(vmem_limit_bytes=VMEM_BYTES),
        cost_estimate=pl.CostEstimate(flops=10**9, bytes_accessed=4 * 10**6, transcendentals=10**6),
        name="attend_forward",
    )(meta, packed)


def attend_backward(meta, packed, grad, exact, log_total):
    blocks = packed.shape[0]
    return pl.pallas_call(
        lambda *refs: backward_kernel(meta.shape[0] - 1, *refs),
        out_shape=jax.ShapeDtypeStruct(packed.shape, BF16),
        in_specs=[pl.BlockSpec(memory_space=pltpu.SMEM)]
        + [pl.BlockSpec(memory_space=pltpu.VMEM)] * 4,
        out_specs=pl.BlockSpec(memory_space=pltpu.VMEM),
        scratch_shapes=[
            pltpu.VMEM((blocks, 256, DH), BF16),
            pltpu.VMEM((blocks, 256, DH), BF16),
            pltpu.VMEM((blocks, DH, 256), F32),
            pltpu.VMEM((blocks, DH, 256), F32),
        ],
        compiler_params=pltpu.CompilerParams(vmem_limit_bytes=VMEM_BYTES),
        cost_estimate=pl.CostEstimate(flops=3 * 10**9, bytes_accessed=4 * 10**6, transcendentals=10**6),
        name="attend_backward",
    )(meta, packed, grad, exact, log_total)


class HeadSplit:
    def __init__(self, latent_len, rows):
        self.rows = rows
        self.meta = jnp.concatenate([lax.axis_index("dp").astype(jnp.int32)[None] % 2, latent_len])

    def forward(self, projected, beside):
        heads, rows = projected.shape[1], self.rows
        query = projected[0].reshape(heads, DH, 2, rows // 2).transpose(0, 2, 1, 3)
        key = jnp.broadcast_to(projected[1][:, None], (heads, 2, DH, rows))
        value = jnp.broadcast_to(projected[2][:, None], (heads, 2, DH, rows))
        packed = jnp.concatenate([key, value, query], axis=3)
        packed = exchange(packed.reshape(heads * 2, DH, rows * 5 // 2), "dp")
        self.packed = after(packed, beside)
        out, self.exact, self.log_total = attend_forward(self.meta, self.packed)
        return self.unsplit(exchange(out, "dp")).reshape(heads * DH, rows)

    def unsplit(self, parts):
        heads = parts.shape[0] // 2
        parts = parts.reshape(heads, 2, DH, self.rows // 2).transpose(0, 2, 1, 3)
        return parts.reshape(heads, DH, self.rows)

    def backward(self, d_attended, beside):
        rows = self.rows
        heads = d_attended.shape[0] // DH
        grad = d_attended.reshape(heads, DH, 2, rows // 2).transpose(0, 2, 1, 3)
        grad = exchange(grad.reshape(heads * 2, DH, rows // 2), "dp")
        out = attend_backward(self.meta, self.packed, grad, self.exact, self.log_total)
        parts = after(exchange(out, "dp"), beside)
        d_query = self.unsplit(parts[:, :, 2 * rows :])
        halves = parts.reshape(heads, 2, DH, rows * 5 // 2)[..., : 2 * rows].astype(F32)
        d_key_value = (halves[:, 0] + halves[:, 1]).astype(BF16)
        return jnp.stack([d_query, d_key_value[..., :rows], d_key_value[..., rows:]])


class Window:
    def __init__(self, latent_len, rows):
        self.rows = rows
        self.reach = (SEQ - 2) // rows + 1
        total = rows * lax.axis_size("dp")
        first = lax.axis_index("dp") * rows
        own = latent_index(latent_len, first, rows, total)
        ids = [
            latent_index(latent_len, first + offset * rows, rows, total)
            for offset in range(-self.reach, self.reach + 1)
        ]
        self.allowed = own[:, None] == jnp.concatenate(ids)[None, :]

    def from_behind(self, block, distance):
        devices = range(lax.axis_size("dp"))
        return lax.ppermute(
            block, "dp", [(i - distance, i) for i in devices if i - distance in devices]
        )

    def head_scores(self, query, key):
        raw = jnp.einsum("eq,ek->qk", query, key, preferred_element_type=F32) * SCALE
        return jnp.where(self.allowed, raw, NEGATIVE)

    def forward(self, projected, beside):
        key_value = projected[1:]
        pieces = [
            key_value if offset == 0 else self.from_behind(key_value, -offset)
            for offset in range(-self.reach, self.reach + 1)
        ]
        window = jnp.concatenate(pieces, axis=3)
        self.operands = (projected[0], window[0], window[1])

        def one(operands):
            query, key, value = operands
            scores = self.head_scores(query, key)
            largest = jnp.max(scores, axis=1, keepdims=True)
            weights = jnp.exp(scores - largest)
            totals = jnp.sum(weights, axis=1, keepdims=True)
            probs = (weights / totals).astype(BF16)
            mixed = jnp.einsum("qk,ek->eq", probs, value, preferred_element_type=F32)
            return mixed.astype(BF16), (largest + jnp.log(totals))[:, 0]

        out, self.log_total = lax.map(one, self.operands)
        return out.reshape(-1, self.rows)

    def backward(self, d_attended, beside):
        rows, reach = self.rows, self.reach
        grads = d_attended.reshape(-1, DH, rows)

        def one(operands):
            query, key, value, grad, log_total = operands
            probs = jnp.exp(self.head_scores(query, key) - log_total[:, None])
            d_value = jnp.einsum("qk,eq->ek", probs.astype(BF16), grad, preferred_element_type=F32)
            d_probs = jnp.einsum("eq,ek->qk", grad, value, preferred_element_type=F32)
            inner = jnp.sum(probs * d_probs, axis=1, keepdims=True)
            d_scores = (probs * (d_probs - inner)).astype(BF16)
            d_query = jnp.einsum("qk,ek->eq", d_scores, key, preferred_element_type=F32) * SCALE
            d_key = jnp.einsum("qk,eq->ek", d_scores, query, preferred_element_type=F32) * SCALE
            return d_query, d_key, d_value

        d_query, d_key, d_value = lax.map(one, self.operands + (grads, self.log_total))
        d_window = jnp.stack([d_key, d_value])
        d_key_value = d_window[..., reach * rows : (reach + 1) * rows]
        for offset in range(-reach, reach + 1):
            if offset != 0:
                block = d_window[..., (offset + reach) * rows : (offset + reach + 1) * rows]
                d_key_value = d_key_value + self.from_behind(block, offset)
        return jnp.concatenate([d_query[None], d_key_value]).astype(BF16)


def latent_index(latent_len, first_row, row_count, token_total):
    positions = first_row + jnp.arange(row_count, dtype=jnp.int32)
    ends = jnp.cumsum(latent_len, dtype=jnp.int32)
    found = jnp.sum((positions[:, None] >= ends[None, :]).astype(jnp.int32), axis=1, dtype=jnp.int32)
    return jnp.where((positions >= 0) & (positions < token_total), found, -1)


def normed(values):
    average = jnp.mean(values, axis=-1, keepdims=True)
    centred = values - average
    spread = jnp.mean(centred * centred, axis=-1, keepdims=True)
    inverse = lax.rsqrt(spread + NORM_EPS)
    return centred * inverse, inverse


def norm_back(unit, inverse, grad):
    along = jnp.mean(grad * unit, axis=-1, keepdims=True)
    return inverse * (grad - jnp.mean(grad, axis=-1, keepdims=True) - unit * along)


def pick(rows_by_latent, ids):
    out = jnp.zeros((ids.shape[0], rows_by_latent.shape[1]), F32)
    for number in range(rows_by_latent.shape[0]):
        out = jnp.where(ids[:, None] == number, rows_by_latent[number][None], out)
    return out


def gelu_pair(value):
    root = math.sqrt(2.0 / math.pi)
    bend = jnp.tanh(root * (value + 0.044715 * value * value * value))
    slope = root * (1.0 + 3.0 * 0.044715 * value * value)
    gelu = 0.5 * value * (1.0 + bend)
    return gelu, 0.5 * (1.0 + bend) + 0.5 * value * (1.0 - bend * bend) * slope


def local(
    tokens,
    conditioning,
    latent_len,
    w_ada,
    b_ada,
    w_qkv,
    b_qv,
    w_proj,
    b_proj,
    w_fc1,
    b_fc1,
    w_fc2,
    b_fc2,
    cotangent,
):
    rows, width = tokens.shape
    share_width = w_qkv.shape[0]
    features = w_qkv.shape[2]
    units = w_fc1.shape[1]
    heads = features // DH
    latents = conditioning.shape[0]
    n_dp, n_tensor = lax.axis_size("dp"), lax.axis_size("tensor")
    my_dp, my_tensor = lax.axis_index("dp"), lax.axis_index("tensor")
    total = rows * n_dp
    share = rows // n_tensor

    core = my_dp % 2
    qk = w_qkv[:, :2].reshape(share_width, 2 * features)
    vp = jnp.concatenate([w_qkv[:, 2], w_proj.T], axis=1)
    early_mine, early_other = assemble(chip_parts(pair_rows(qk, vp)))

    cond = conditioning.astype(F32)
    gate = 1.0 / (1.0 + jnp.exp(-cond))
    activated = (cond * gate).astype(BF16)
    own_activated = lax.dynamic_slice_in_dim(activated, my_dp * share_width, share_width, 1)
    flat_ada = w_ada.reshape(share_width, 6 * features)
    mod_part = jnp.dot(own_activated, flat_ada, preferred_element_type=F32)
    mod_mine = jnp.sum(gather(mod_part, "dp", n_dp), axis=0) + b_ada.astype(F32).reshape(1, -1)
    modulation = gather(mod_mine, "tensor", n_tensor)
    modulation = modulation.reshape(n_tensor, latents, 6, features).transpose(2, 1, 0, 3)
    modulation = modulation.reshape(6, latents, width)

    ids = latent_index(latent_len, my_dp * rows, rows, total)
    own_ids = lax.dynamic_slice_in_dim(ids, my_tensor * share, share, 0)

    def own(values):
        return lax.dynamic_slice_in_dim(values, my_tensor * share, share, 0)

    unit_one, inverse_one = normed(tokens.astype(F32))
    hidden_one = (unit_one * (1.0 + pick(modulation[1], ids)) + pick(modulation[0], ids)).astype(BF16)
    by_last = (((1,), (1,)), ((), ()))
    by_token = (((0,), (0,)), ((), ()))
    by_rows = (((0,), (1,)), ((), ()))
    bias = jnp.concatenate([b_qv[0], jnp.zeros_like(b_qv[0]), b_qv[1]]).astype(F32)
    bias = jnp.concatenate([bias, jnp.zeros((features,), F32)]).reshape(2, 2 * features)
    bias_mine, bias_other = choose(core, bias[0], bias[1])
    from_mine = jnp.dot(hidden_one, early_mine, preferred_element_type=F32) + bias_mine
    from_other = jnp.dot(hidden_one, early_other, preferred_element_type=F32) + bias_other
    joined = choose(core, from_mine.astype(BF16).T, from_other.astype(BF16).T)
    projected = jnp.concatenate(joined)[: 3 * features].reshape(3, heads, DH, rows)
    full_proj = choose(core, early_other, early_mine)[0][:, features:]
    full_proj = after(full_proj, projected)
    late_rows = pair_rows(after(w_fc1, projected), after(w_fc2.T, projected))
    split = HeadSplit if 2 * heads == n_dp else Window
    attention = split(latent_len, rows)
    attended = attention.forward(projected, (full_proj, late_rows))
    attn_part = lax.dot_general(attended, full_proj, by_rows, preferred_element_type=F32).astype(BF16)
    late_parts = chip_parts(after(late_rows, attn_part))
    attn_out = sum_shares(attn_part, "tensor") + b_proj.astype(F32)
    own_tokens = own(tokens).astype(F32)
    gate_one = pick(modulation[2], own_ids)
    residual_mid = own_tokens + gate_one * attn_out
    unit_two, inverse_two = normed(residual_mid)
    scale_two = 1.0 + pick(modulation[4], own_ids)
    hidden_two_own = (unit_two * scale_two + pick(modulation[3], own_ids)).astype(BF16)
    hidden_two = gather_shares(hidden_two_own, "tensor")
    late_mine, late_other = assemble(after(late_parts, hidden_two_own))

    d_mlp = (cotangent.astype(F32) * pick(modulation[5], ids)).astype(BF16)
    left_mine, left_other = choose(core, hidden_two, d_mlp)
    from_mine = jnp.dot(left_mine, late_mine, preferred_element_type=F32)
    from_other = jnp.dot(left_other, late_other, preferred_element_type=F32)
    pre_act, d_gelu = choose(core, from_mine, from_other)
    gelu_out, gelu_slope = gelu_pair(pre_act + b_fc1.astype(F32))
    gelu_out = gelu_out.astype(BF16)
    d_pre = (d_gelu * gelu_slope).astype(BF16)
    right_mine, right_other = choose(core, d_pre, gelu_out)
    back_mine = lax.dot_general(right_mine, late_mine, by_last, preferred_element_type=F32)
    back_other = lax.dot_general(right_other, late_other, by_last, preferred_element_type=F32)
    d_two_part, mlp_part = choose(core, back_mine.astype(BF16), back_other.astype(BF16))
    d_hidden_two = exchange_shares(d_two_part, "tensor")

    right_mine, right_other = after((right_mine, right_other), d_two_part)
    sent = lax.dot_general(left_other, right_other, by_token, preferred_element_type=F32)
    kept = lax.dot_general(left_mine, right_mine, by_token, preferred_element_type=F32)
    late_total = pair_total(kept, sent)
    d_hidden_two, late_total = lax.optimization_barrier((d_hidden_two, late_total))
    late_grads = [chip_share(late_total, step) for step in range(n_dp // 2 - 1)]

    d_hidden_two = jnp.sum(d_hidden_two.astype(F32), axis=0)
    own_cotangent = own(cotangent).astype(F32)
    d_mid = own_cotangent + norm_back(unit_two, inverse_two, d_hidden_two * scale_two)
    d_attn_own = (d_mid * gate_one).astype(BF16)
    d_attn = after(gather_shares(d_attn_own, "tensor"), late_grads)

    d_attended = jnp.dot(d_attn, full_proj, preferred_element_type=F32).astype(BF16).T
    mlp_out = sum_beside(after(mlp_part, d_attended), "tensor") + b_fc2.astype(F32)
    gate_two = pick(modulation[5], own_ids)
    result_own = (residual_mid + gate_two * mlp_out).astype(BF16)
    d_projected = attention.backward(d_attended, result_own).reshape(3 * features, rows)
    result = gather_beside(result_own, "tensor")
    blank = jnp.zeros((features, rows), BF16)
    d_qk = d_projected[: 2 * features]
    d_value = d_projected[2 * features :]
    d_mine, d_other = choose(core, d_qk, jnp.concatenate([d_value, blank]))
    d_one_part = lax.dot_general(
        d_mine, early_mine, by_rows, preferred_element_type=F32
    ) + lax.dot_general(d_other, early_other, by_rows, preferred_element_type=F32)
    d_one_part = d_one_part.astype(BF16)
    d_hidden_one = exchange_shares(d_one_part, "tensor")

    left = jnp.concatenate([hidden_one, d_attn])
    right_qk = jnp.concatenate([d_qk, jnp.zeros_like(d_qk)], axis=1)
    right_vp = jnp.concatenate(
        [jnp.concatenate([d_value, blank]), jnp.concatenate([blank, attended])], axis=1
    )
    right_mine, right_other = choose(core, right_qk, right_vp)
    right_mine, right_other = after((right_mine, right_other), d_one_part)
    sent = lax.dot_general(left, right_other, by_rows, preferred_element_type=F32)
    kept = lax.dot_general(left, right_mine, by_rows, preferred_element_type=F32)
    early_total = pair_total(kept, sent)
    late_last = chip_share(after(late_total, d_one_part), n_dp // 2 - 1)
    d_hidden_one, early_total = lax.optimization_barrier((d_hidden_one, early_total))
    early_grads = [chip_share(early_total, step) for step in range(n_dp // 2)]

    d_hidden_one = jnp.sum(d_hidden_one.astype(F32), axis=0)
    own_unit, own_inverse = own(unit_one), own(inverse_one)
    scale_one = 1.0 + pick(modulation[1], own_ids)
    grad_own = d_mid + norm_back(own_unit, own_inverse, d_hidden_one * scale_one)

    d_float = d_projected.astype(F32).reshape(3, features, rows)
    bias_part = jnp.concatenate(
        [
            jnp.sum(d_mlp.astype(F32), axis=0),
            jnp.sum(d_attn.astype(F32), axis=0),
            jnp.sum(d_pre.astype(F32), axis=0),
            jnp.sum(d_float[0], axis=1),
            jnp.sum(d_float[2], axis=1),
        ]
    )
    bias_rows = bias_part.reshape(-1, features)

    one_hot = (jnp.arange(latents, dtype=jnp.int32)[:, None] == own_ids[None, :]).astype(BF16)

    def by_latent(parts):
        joined = jnp.concatenate([part.astype(BF16) for part in parts], axis=1)
        sums = jnp.dot(one_hot, joined, preferred_element_type=F32)
        return sums.reshape(latents, len(parts), n_tensor, features)

    d_mod_last = by_latent(
        [d_mid * attn_out, d_hidden_two, d_hidden_two * unit_two, own_cotangent * mlp_out]
    )
    d_mod_first = by_latent([d_hidden_one, d_hidden_one * own_unit])
    d_mod_part = jnp.concatenate([d_mod_first, d_mod_last], axis=1).transpose(2, 0, 1, 3)
    d_mod_part = d_mod_part.reshape(n_tensor, latents * 6, features)
    grad_tokens = gather_beside(after(grad_own.astype(BF16), d_mod_part), "tensor").astype(F32)
    d_mod_mine = jnp.sum(exchange(d_mod_part, "tensor"), axis=0)
    sums = jnp.sum(gather(jnp.concatenate([d_mod_mine, bias_rows]), "dp", n_dp), axis=0)
    d_mod = sums[: 6 * latents].reshape(latents, 6 * features)
    bias_total = sums[6 * latents :].reshape(-1)
    grad_b_ada = jnp.sum(d_mod, axis=0).reshape(6, features)
    grad_w_ada = lax.dot_general(
        own_activated.astype(F32), d_mod, by_token, precision=lax.Precision.HIGHEST
    ).reshape(share_width, 6, features)
    high = d_mod.astype(BF16)
    low = (d_mod - high.astype(F32)).astype(BF16)
    d_active = lax.dot_general(
        jnp.concatenate([high, low]), flat_ada, by_last, preferred_element_type=F32
    )
    d_active = d_active[:latents] + d_active[latents:]
    d_active = gather(d_active, ("dp", "tensor"), n_dp * n_tensor)
    d_active = jnp.sum(d_active.reshape(n_dp, n_tensor, latents, share_width), axis=1)
    d_active = d_active.transpose(1, 0, 2).reshape(latents, width)
    grad_cond = d_active * (gate * (1.0 + cond * (1.0 - gate)))

    grad_fc1, grad_fc2 = finish_pair(late_grads + [late_last])
    grad_qk, grad_vp = finish_pair(early_grads)
    grad_qkv = jnp.concatenate([grad_qk, grad_vp[:, :features]], axis=1)
    grad_qkv = grad_qkv.reshape(share_width, 3, features)

    return (
        result,
        grad_tokens,
        grad_cond,
        grad_w_ada,
        grad_b_ada,
        grad_qkv,
        bias_total[2 * width + units :].reshape(2, features),
        grad_vp[:, features:].T,
        bias_total[width : 2 * width],
        grad_fc1,
        bias_total[2 * width : 2 * width + units],
        grad_fc2.T,
        bias_total[:width],
    )


def solution(mesh):
    in_specs = (
        P("dp", None),
        P(),
        P(),
        P("dp", None, "tensor"),
        P(None, "tensor"),
        P("dp", None, "tensor"),
        P(None, "tensor"),
        P("tensor", "dp"),
        P(),
        P("dp", "tensor"),
        P("tensor"),
        P("tensor", "dp"),
        P(),
        P("dp", None),
    )
    out_specs = (
        P("dp", None),
        P("dp", None),
        P(),
        P("dp", None, "tensor"),
        P(None, "tensor"),
        P("dp", None, "tensor"),
        P(None, "tensor"),
        P("tensor", "dp"),
        P(),
        P("dp", "tensor"),
        P("tensor"),
        P("tensor", "dp"),
        P(),
    )
    return jax.shard_map(local, mesh=mesh, in_specs=in_specs, out_specs=out_specs, check_vma=False)
```

```python
import math

import jax
import jax.numpy as jnp
from jax import lax
from jax.experimental import pallas as pl
from jax.experimental.pallas import tpu as pltpu
from jax.sharding import PartitionSpec as P

DH = 72
SEQ = 1024
NORM_EPS = 1e-06
NEGATIVE = -1e30
SCALE = 1.0 / math.sqrt(DH)
VMEM_BYTES = 40 * 1024 * 1024
BF16 = jnp.bfloat16
F32 = jnp.float32


def swap(block, axis, bits):
    route = [(i, i ^ bits) for i in range(lax.axis_size(axis))]
    return lax.ppermute(block, axis, route)


def exchange(blocks, axis):
    return lax.all_to_all(blocks, axis, 0, 0, tiled=True)


def gather(block, axis, count):
    return exchange(jnp.broadcast_to(block[None], (count,) + block.shape), axis)


def after(value, *others):
    return lax.optimization_barrier((value,) + others)[0]


def choose(core, first, second):
    return jnp.where(core == 0, first, second), jnp.where(core == 0, second, first)


def pair_rows(first, second):
    core = lax.axis_index("dp") % 2
    keep, send = choose(core, first, second)
    return jnp.concatenate(choose(core, keep, swap(send, "dp", 1)))


def chip_parts(rows):
    count = lax.axis_size("dp") // 2
    return [rows] + [swap(rows, "dp", 2 * step) for step in range(1, count)]


def assemble(parts):
    chip = lax.axis_index("dp") // 2
    full = jnp.zeros((len(parts),) + parts[0].shape, parts[0].dtype)
    for step, part in enumerate(parts):
        full = lax.dynamic_update_index_in_dim(full, part, chip ^ step, 0)
    mine = full.reshape(-1, parts[0].shape[1])
    return mine, swap(mine, "dp", 1)


def pair_total(mine, other):
    count = lax.axis_size("dp") // 2
    total = (mine + swap(other.astype(BF16), "dp", 1).astype(F32)).astype(BF16)
    return total.reshape(count, total.shape[0] // count, total.shape[1])


def chip_share(blocks, step):
    chip = lax.axis_index("dp") // 2
    sent = lax.dynamic_index_in_dim(blocks, chip ^ step, 0, keepdims=False)
    return swap(sent, "dp", 2 * step) if step else sent


def finish_pair(parts):
    core = lax.axis_index("dp") % 2
    rows = sum(part.astype(F32) for part in parts)
    half = rows.shape[0] // 2
    keep, send = choose(core, rows[:half], rows[half:])
    return choose(core, keep, swap(send, "dp", 1))


def parts_beside(partial, axis):
    count, me = lax.axis_size(axis), lax.axis_index(axis)
    blocks = partial.reshape((count, partial.shape[0] // count) + partial.shape[1:])
    parts = [lax.dynamic_index_in_dim(blocks, me, 0, keepdims=False)]
    for bits in range(1, count):
        sent = lax.dynamic_index_in_dim(blocks, me ^ bits, 0, keepdims=False)
        parts.append(swap(sent, axis, bits))
    return parts


def gather_beside(share, axis):
    count, me = lax.axis_size(axis), lax.axis_index(axis)
    parts = jnp.stack([share] + [swap(share, axis, bits) for bits in range(1, count)])
    ordered = [lax.dynamic_index_in_dim(parts, me ^ place, 0, keepdims=False) for place in range(count)]
    return jnp.concatenate(ordered)


def exchange_shares(partial, axis):
    count = lax.axis_size(axis)
    blocks = partial.reshape((count, partial.shape[0] // count) + partial.shape[1:])
    return exchange(blocks, axis)


def tile_range(meta_ref, latents, tile, core):
    lane = lax.broadcasted_iota(jnp.int32, (1, 256), 1)
    first = tile * 512 + core * 128
    last = first + 383
    place = first + lane + jnp.where(lane >= 128, 128, 0)
    begin = jnp.zeros((1, 256), jnp.int32)
    finish = jnp.zeros((1, 256), jnp.int32)
    low = jnp.int32(0)
    high = jnp.int32(0)
    start = jnp.int32(0)
    for number in range(latents):
        end = start + meta_ref[1 + number]
        inside = (place >= start) & (place < end)
        begin = jnp.where(inside, start, begin)
        finish = jnp.where(inside, end, finish)
        low = jnp.where((first >= start) & (first < end), start, low)
        high = jnp.where((last >= start) & (last < end), end, high)
        start = end
    return begin, finish, low // 256, (high + 255) // 256


def pair(ref, tile, start):
    left = ref[2 * tile, :, start : start + 128]
    right = ref[2 * tile + 1, :, start : start + 128]
    return jnp.concatenate([left, right], axis=1)


def key_mask(block, begin, finish):
    place = block * 256 + lax.broadcasted_iota(jnp.int32, (256, 256), 0)
    return (place >= begin) & (place < finish)


def forward_kernel(latents, meta_ref, packed_ref, out_ref, exact_ref, log_ref, keys, scores):
    blocks = packed_ref.shape[0]
    core = meta_ref[0]
    for block in range(blocks):
        keys[block] = packed_ref[block, :, :256].astype(F32).T.astype(BF16)
    for tile in range(blocks // 2):
        begin, finish, low, high = tile_range(meta_ref, latents, tile, core)
        query = pair(packed_ref, tile, 512)

        def score(block, largest):
            raw = jnp.dot(keys[block], query, preferred_element_type=F32) * SCALE
            raw = jnp.where(key_mask(block, begin, finish), raw, NEGATIVE)
            scores[block] = raw
            return jnp.maximum(largest, jnp.max(raw, axis=0, keepdims=True))

        largest = lax.fori_loop(low, high, score, jnp.full((1, 256), NEGATIVE, F32))

        def mix(block, carry):
            total, mixed = carry
            weights = jnp.exp(scores[block] - largest)
            total = total + jnp.sum(weights, axis=0, keepdims=True)
            values = packed_ref[block, :, 256:512]
            mixed = mixed + jnp.dot(values, weights.astype(BF16), preferred_element_type=F32)
            return total, mixed

        total, mixed = lax.fori_loop(
            low, high, mix, (jnp.zeros((1, 256), F32), jnp.zeros((DH, 256), F32))
        )
        mixed = mixed / total
        log_total = largest + jnp.log(total)
        for half in range(2):
            part = mixed[:, half * 128 : half * 128 + 128]
            exact_ref[2 * tile + half] = part
            out_ref[2 * tile + half] = part.astype(BF16)
            log_ref[2 * tile + half] = log_total[:, half * 128 : half * 128 + 128]


def backward_kernel(
    latents, meta_ref, packed_ref, grad_ref, exact_ref, log_ref, out_ref, keys, values, d_keys, d_values
):
    blocks = packed_ref.shape[0]
    core = meta_ref[0]
    for block in range(blocks):
        keys[block] = packed_ref[block, :, :256].astype(F32).T.astype(BF16)
        values[block] = packed_ref[block, :, 256:512].astype(F32).T.astype(BF16)
    d_keys[...] = jnp.zeros_like(d_keys)
    d_values[...] = jnp.zeros_like(d_values)
    by_query = (((1,), (1,)), ((), ()))
    for tile in range(blocks // 2):
        begin, finish, low, high = tile_range(meta_ref, latents, tile, core)
        query = pair(packed_ref, tile, 512)
        grad = pair(grad_ref, tile, 0)
        inner = jnp.sum(grad.astype(F32) * pair(exact_ref, tile, 0), axis=0, keepdims=True)
        log_total = pair(log_ref, tile, 0)

        def step(block, d_query):
            raw = jnp.dot(keys[block], query, preferred_element_type=F32) * SCALE
            probs = jnp.where(key_mask(block, begin, finish), jnp.exp(raw - log_total), 0.0)
            d_probs = jnp.dot(values[block], grad, preferred_element_type=F32)
            d_scores = (probs * (d_probs - inner)).astype(BF16)
            d_values[block] += lax.dot_general(
                grad, probs.astype(BF16), by_query, preferred_element_type=F32
            )
            d_keys[block] += lax.dot_general(query, d_scores, by_query, preferred_element_type=F32)
            key_rows = packed_ref[block, :, :256]
            return d_query + jnp.dot(key_rows, d_scores, preferred_element_type=F32)

        d_query = lax.fori_loop(low, high, step, jnp.zeros((DH, 256), F32)) * SCALE
        for half in range(2):
            part = d_query[:, half * 128 : half * 128 + 128]
            out_ref[2 * tile + half, :, 512:640] = part.astype(BF16)
    for block in range(blocks):
        out_ref[block, :, :256] = (d_keys[block] * SCALE).astype(BF16)
        out_ref[block, :, 256:512] = d_values[block].astype(BF16)


def attend_forward(meta, packed):
    blocks = packed.shape[0]
    shape = jax.ShapeDtypeStruct
    return pl.pallas_call(
        lambda *refs: forward_kernel(meta.shape[0] - 1, *refs),
        out_shape=(
            shape((blocks, DH, 128), BF16),
            shape((blocks, DH, 128), F32),
            shape((blocks, 1, 128), F32),
        ),
        in_specs=[
            pl.BlockSpec(memory_space=pltpu.SMEM),
            pl.BlockSpec(memory_space=pltpu.VMEM),
        ],
        out_specs=tuple([pl.BlockSpec(memory_space=pltpu.VMEM)] * 3),
        scratch_shapes=[
            pltpu.VMEM((blocks, 256, DH), BF16),
            pltpu.VMEM((blocks, 256, 256), F32),
        ],
        compiler_params=pltpu.CompilerParams(vmem_limit_bytes=VMEM_BYTES),
        cost_estimate=pl.CostEstimate(flops=10**9, bytes_accessed=4 * 10**6, transcendentals=10**6),
        name="attend_forward",
    )(meta, packed)


def attend_backward(meta, packed, grad, exact, log_total):
    blocks = packed.shape[0]
    return pl.pallas_call(
        lambda *refs: backward_kernel(meta.shape[0] - 1, *refs),
        out_shape=jax.ShapeDtypeStruct(packed.shape, BF16),
        in_specs=[pl.BlockSpec(memory_space=pltpu.SMEM)]
        + [pl.BlockSpec(memory_space=pltpu.VMEM)] * 4,
        out_specs=pl.BlockSpec(memory_space=pltpu.VMEM),
        scratch_shapes=[
            pltpu.VMEM((blocks, 256, DH), BF16),
            pltpu.VMEM((blocks, 256, DH), BF16),
            pltpu.VMEM((blocks, DH, 256), F32),
            pltpu.VMEM((blocks, DH, 256), F32),
        ],
        compiler_params=pltpu.CompilerParams(vmem_limit_bytes=VMEM_BYTES),
        cost_estimate=pl.CostEstimate(flops=3 * 10**9, bytes_accessed=4 * 10**6, transcendentals=10**6),
        name="attend_backward",
    )(meta, packed, grad, exact, log_total)


class HeadSplit:
    def __init__(self, latent_len, rows):
        self.rows = rows
        self.meta = jnp.concatenate([lax.axis_index("dp").astype(jnp.int32)[None] % 2, latent_len])

    def forward(self, packed, beside):
        self.packed = after(exchange(packed, "dp"), beside)
        out, self.exact, self.log_total = attend_forward(self.meta, self.packed)
        return self.unsplit(exchange(out, "dp")).reshape(-1, self.rows)

    def unsplit(self, parts):
        heads = parts.shape[0] // 2
        parts = parts.reshape(heads, 2, DH, self.rows // 2).transpose(0, 2, 1, 3)
        return parts.reshape(heads, DH, self.rows)

    def backward(self, grad, beside):
        grad = exchange(grad, "dp")
        out = attend_backward(self.meta, self.packed, grad, self.exact, self.log_total)
        return after(exchange(out, "dp"), beside)


class Window:
    def __init__(self, latent_len, rows):
        self.rows = rows
        self.reach = (SEQ - 2) // rows + 1
        total = rows * lax.axis_size("dp")
        first = lax.axis_index("dp") * rows
        own = latent_index(latent_len, first, rows, total)
        ids = [
            latent_index(latent_len, first + offset * rows, rows, total)
            for offset in range(-self.reach, self.reach + 1)
        ]
        self.allowed = own[:, None] == jnp.concatenate(ids)[None, :]

    def from_behind(self, block, distance):
        devices = range(lax.axis_size("dp"))
        return lax.ppermute(
            block, "dp", [(i - distance, i) for i in devices if i - distance in devices]
        )

    def head_scores(self, query, key):
        raw = jnp.einsum("eq,ek->qk", query, key, preferred_element_type=F32) * SCALE
        return jnp.where(self.allowed, raw, NEGATIVE)

    def forward(self, packed, beside):
        rows = self.rows
        split = packed.reshape(-1, 2, DH, rows * 5 // 2)
        query = jnp.concatenate([split[:, 0, :, 2 * rows :], split[:, 1, :, 2 * rows :]], axis=2)
        projected = jnp.stack([query, split[:, 0, :, :rows], split[:, 0, :, rows : 2 * rows]])
        key_value = projected[1:]
        pieces = [
            key_value if offset == 0 else self.from_behind(key_value, -offset)
            for offset in range(-self.reach, self.reach + 1)
        ]
        window = jnp.concatenate(pieces, axis=3)
        self.operands = (projected[0], window[0], window[1])

        def one(operands):
            query, key, value = operands
            scores = self.head_scores(query, key)
            largest = jnp.max(scores, axis=1, keepdims=True)
            weights = jnp.exp(scores - largest)
            totals = jnp.sum(weights, axis=1, keepdims=True)
            probs = (weights / totals).astype(BF16)
            mixed = jnp.einsum("qk,ek->eq", probs, value, preferred_element_type=F32)
            return mixed.astype(BF16), (largest + jnp.log(totals))[:, 0]

        out, self.log_total = lax.map(one, self.operands)
        return out.reshape(-1, self.rows)

    def backward(self, grad, beside):
        rows, reach = self.rows, self.reach
        halves = grad.reshape(-1, 2, DH, rows // 2)
        grads = jnp.concatenate([halves[:, 0], halves[:, 1]], axis=2)

        def one(operands):
            query, key, value, grad, log_total = operands
            probs = jnp.exp(self.head_scores(query, key) - log_total[:, None])
            d_value = jnp.einsum("qk,eq->ek", probs.astype(BF16), grad, preferred_element_type=F32)
            d_probs = jnp.einsum("eq,ek->qk", grad, value, preferred_element_type=F32)
            inner = jnp.sum(probs * d_probs, axis=1, keepdims=True)
            d_scores = (probs * (d_probs - inner)).astype(BF16)
            d_query = jnp.einsum("qk,ek->eq", d_scores, key, preferred_element_type=F32) * SCALE
            d_key = jnp.einsum("qk,eq->ek", d_scores, query, preferred_element_type=F32) * SCALE
            return d_query, d_key, d_value

        d_query, d_key, d_value = lax.map(one, self.operands + (grads, self.log_total))
        d_window = jnp.stack([d_key, d_value])
        d_key_value = d_window[..., reach * rows : (reach + 1) * rows]
        for offset in range(-reach, reach + 1):
            if offset != 0:
                block = d_window[..., (offset + reach) * rows : (offset + reach + 1) * rows]
                d_key_value = d_key_value + self.from_behind(block, offset)
        wide = jnp.concatenate([d_key_value[0], d_key_value[1]], axis=2)
        wide = jnp.stack([wide, jnp.zeros_like(wide)], axis=1)
        halves = d_query.reshape(-1, DH, 2, rows // 2).transpose(0, 2, 1, 3)
        packed = jnp.concatenate([wide, halves], axis=3).astype(BF16)
        return packed.reshape(-1, DH, rows * 5 // 2)


META = 4


def vmem(count):
    return [pl.BlockSpec(memory_space=pltpu.VMEM)] * count


def call(body, name, meta, arrays, outs, scratch=(), anywhere=0):
    return pl.pallas_call(
        body,
        out_shape=tuple(jax.ShapeDtypeStruct(shape, kind) for shape, kind in outs),
        in_specs=[pl.BlockSpec(memory_space=pltpu.SMEM)]
        + [pl.BlockSpec(memory_space=pl.ANY)] * anywhere
        + vmem(len(arrays) - anywhere),
        out_specs=tuple(vmem(len(outs))),
        scratch_shapes=list(scratch),
        compiler_params=pltpu.CompilerParams(vmem_limit_bytes=VMEM_BYTES),
        cost_estimate=pl.CostEstimate(flops=1, bytes_accessed=1, transcendentals=0),
        name=name,
    )(meta, *arrays)


def row_masks(meta_ref, latents, first, rows):
    place = first + lax.broadcasted_iota(jnp.int32, (rows, 1), 0)
    ids = jnp.zeros((rows, 1), jnp.int32)
    end = jnp.int32(0)
    for number in range(latents - 1):
        end = end + meta_ref[META + number]
        ids = ids + (place >= end).astype(jnp.int32)
    return [(ids == number).astype(F32) for number in range(latents)]


def rows_of(mod_ref, masks, feature):
    out = masks[0] * mod_ref[feature : feature + 1, :]
    for number in range(1, len(masks)):
        row = number * 6 + feature
        out = out + masks[number] * mod_ref[row : row + 1, :]
    return out


def latent_sums(out_ref, masks, values, feature, features):
    rounded = values.astype(BF16).astype(F32)
    for number, mask in enumerate(masks):
        row = number * features + feature
        out_ref[row : row + 1, :] = jnp.sum(mask * rounded, axis=0, keepdims=True)


def own_rows(meta_ref, ref, share):
    start = pl.multiple_of(meta_ref[2] * share, share)
    return ref[pl.ds(start, share), :].astype(F32)


def on_core(meta_ref, body, mine, other):
    @pl.when(meta_ref[0] == 0)
    def _():
        body(mine, other)

    @pl.when(meta_ref[0] != 0)
    def _():
        body(other, mine)


def project_kernel(
    latents, meta_ref, tokens_ref, cot_ref, mod_ref, bias_ref, mine_ref, other_ref,
    hidden_ref, d_mlp_ref, packed_ref,
):
    rows, width = tokens_ref.shape
    masks = row_masks(meta_ref, latents, meta_ref[1], rows)
    unit, _ = normed(tokens_ref[...].astype(F32))
    hidden = unit * (1.0 + rows_of(mod_ref, masks, 1)) + rows_of(mod_ref, masks, 0)
    hidden_ref[...] = hidden.astype(BF16)
    d_mlp_ref[...] = (cot_ref[...].astype(F32) * rows_of(mod_ref, masks, 5)).astype(BF16)
    heads = packed_ref.shape[0] // 2
    features = heads * DH

    def body(qk_ref, vp_ref):
        left = hidden_ref[...]
        both = jnp.dot(left, qk_ref[...], preferred_element_type=F32) + bias_ref[0:1, :]
        both = both.T
        value = jnp.dot(left, vp_ref[...], preferred_element_type=F32) + bias_ref[1:2, :]
        value = value.T
        for head in range(heads):
            start = head * DH
            query = both[start : start + DH].astype(BF16)
            key = both[features + start : features + start + DH].astype(BF16)
            val = value[start : start + DH].astype(BF16)
            for half in range(2):
                packed_ref[2 * head + half, :, :rows] = key
                packed_ref[2 * head + half, :, rows : 2 * rows] = val
                packed_ref[2 * head + half, :, 2 * rows :] = query[
                    :, half * (rows // 2) : (half + 1) * (rows // 2)
                ]

    on_core(meta_ref, body, mine_ref, other_ref)


def middle_kernel(
    latents, meta_ref, parts_ref, tokens_ref, mod_ref, bias_ref, sent_ref, attn_ref, mid_ref
):
    copies, share, width = parts_ref.shape
    masks = row_masks(meta_ref, latents, meta_ref[1] + meta_ref[2] * share, share)
    attn = bias_ref[...].astype(F32)
    for part in range(copies):
        attn = attn + parts_ref[part].astype(F32)
    attn_ref[...] = attn
    mid = own_rows(meta_ref, tokens_ref, share) + rows_of(mod_ref, masks, 2) * attn
    mid_ref[...] = mid
    unit, _ = normed(mid)
    hidden = unit * (1.0 + rows_of(mod_ref, masks, 4)) + rows_of(mod_ref, masks, 3)
    for part in range(copies):
        sent_ref[part] = hidden.astype(BF16)


def mlp_kernel(count, meta_ref, *refs):
    mine_parts, other_parts = refs[:count], refs[count : 2 * count]
    hidden_ref, d_mlp_ref, bias_ref = refs[2 * count : 2 * count + 3]
    d_two_ref, mlp_ref, gelu_ref, d_pre_ref, d_bias_ref = refs[2 * count + 3 : 2 * count + 8]
    mine_ref, other_ref, d_two_sum, mlp_sum, sems = refs[2 * count + 8 :]
    block = mine_parts[0].shape[0]
    copies = []
    for place, (parts, whole) in enumerate(((mine_parts, mine_ref), (other_parts, other_ref))):
        for step, part in enumerate(parts):
            start = pl.multiple_of((meta_ref[3] ^ step) * block, 16)
            copies.append(
                pltpu.make_async_copy(
                    part, whole.at[pl.ds(start, block), :], sems.at[place * count + step]
                )
            )
    for copy in copies:
        copy.start()
    for copy in copies:
        copy.wait()
    d_two_sum[...] = jnp.zeros_like(d_two_sum)
    mlp_sum[...] = jnp.zeros_like(mlp_sum)
    tile = 384
    by_last = (((1,), (1,)), ((), ()))

    def body(fc1_ref, fc2_ref):
        def step(number, carry):
            units = pl.ds(pl.multiple_of(number * tile, tile), tile)
            fc1, fc2 = fc1_ref[:, units], fc2_ref[:, units]
            pre = jnp.dot(hidden_ref[...], fc1, preferred_element_type=F32)
            gelu, slope = gelu_pair(pre + bias_ref[:, units].astype(F32))
            grad = jnp.dot(d_mlp_ref[...], fc2, preferred_element_type=F32)
            d_pre = (grad * slope).astype(BF16)
            gelu = gelu.astype(BF16)
            gelu_ref[:, units] = gelu
            d_pre_ref[:, units] = d_pre
            d_bias_ref[:, units] = jnp.sum(d_pre.astype(F32), axis=0, keepdims=True)
            d_two_sum[...] += lax.dot_general(d_pre, fc1, by_last, preferred_element_type=F32)
            mlp_sum[...] += lax.dot_general(gelu, fc2, by_last, preferred_element_type=F32)
            return carry

        lax.fori_loop(0, fc1_ref.shape[1] // tile, step, 0)

    on_core(meta_ref, body, mine_ref, other_ref)
    d_two_ref[...] = d_two_sum[...].astype(BF16)
    mlp_ref[...] = mlp_sum[...].astype(BF16)


def middle_back_kernel(
    latents, meta_ref, parts_ref, mid_in_ref, attn_ref, cot_ref, mod_ref, sent_ref, d_mid_ref, sums_ref
):
    copies, share, width = parts_ref.shape
    masks = row_masks(meta_ref, latents, meta_ref[1] + meta_ref[2] * share, share)
    d_hidden = parts_ref[0].astype(F32)
    for part in range(1, copies):
        d_hidden = d_hidden + parts_ref[part].astype(F32)
    unit, inverse = normed(mid_in_ref[...])
    d_mid = own_rows(meta_ref, cot_ref, share) + norm_back(
        unit, inverse, d_hidden * (1.0 + rows_of(mod_ref, masks, 4))
    )
    d_mid_ref[...] = d_mid
    d_attn = (d_mid * rows_of(mod_ref, masks, 2)).astype(BF16)
    for part in range(copies):
        sent_ref[part] = d_attn
    latent_sums(sums_ref, masks, d_mid * attn_ref[...], 0, 3)
    latent_sums(sums_ref, masks, d_hidden, 1, 3)
    latent_sums(sums_ref, masks, d_hidden * unit, 2, 3)


def result_kernel(
    latents, count, meta_ref, *refs
):
    parts = refs[:count]
    mid_ref, cot_ref, mod_ref, bias_ref, result_ref, sums_ref = refs[count:]
    share = result_ref.shape[0]
    masks = row_masks(meta_ref, latents, meta_ref[1] + meta_ref[2] * share, share)
    mlp = bias_ref[...].astype(F32)
    for part in parts:
        mlp = mlp + part[...].astype(F32)
    result_ref[...] = (mid_ref[...] + rows_of(mod_ref, masks, 5) * mlp).astype(BF16)
    latent_sums(sums_ref, masks, own_rows(meta_ref, cot_ref, share) * mlp, 0, 1)


def spread_kernel(meta_ref, d_attn_ref, proj_ref, packed_ref, d_bias_ref):
    grad = jnp.dot(d_attn_ref[...], proj_ref[...], preferred_element_type=F32).T
    half = grad.shape[1] // 2
    for place in range(packed_ref.shape[0]):
        start = place // 2 * DH
        side = place % 2 * half
        packed_ref[place] = grad[start : start + DH, side : side + half].astype(BF16)
    d_bias_ref[...] = jnp.sum(d_attn_ref[...].astype(F32), axis=0, keepdims=True)


def unspread_kernel(meta_ref, parts_ref, mine_ref, other_ref, d_one_ref, d_qk_ref, d_vp_ref):
    heads = parts_ref.shape[0] // 2
    rows = d_one_ref.shape[0]
    query, key, value = [], [], []
    for head in range(heads):
        left = parts_ref[2 * head].astype(F32)
        right = parts_ref[2 * head + 1].astype(F32)
        both = left[:, : 2 * rows] + right[:, : 2 * rows]
        key.append(both[:, :rows])
        value.append(both[:, rows:])
        query.append(jnp.concatenate([left[:, 2 * rows :], right[:, 2 * rows :]], axis=1))
    d_qk_ref[...] = jnp.concatenate(query + key, axis=0).T.astype(BF16)
    blank = jnp.zeros((heads * DH, rows), F32)
    d_vp_ref[...] = jnp.concatenate(value + [blank], axis=0).T.astype(BF16)
    tile = 384
    by_last = (((1,), (1,)), ((), ()))

    def body(qk_ref, vp_ref):
        def step(number, carry):
            columns = pl.ds(pl.multiple_of(number * tile, tile), tile)
            total = lax.dot_general(d_qk_ref[...], qk_ref[columns, :], by_last, preferred_element_type=F32)
            total += lax.dot_general(d_vp_ref[...], vp_ref[columns, :], by_last, preferred_element_type=F32)
            d_one_ref[:, columns] = total.astype(BF16)
            return carry

        lax.fori_loop(0, qk_ref.shape[0] // tile, step, 0)

    on_core(meta_ref, body, mine_ref, other_ref)


def first_back_kernel(
    latents, meta_ref, parts_ref, tokens_ref, d_mid_ref, mod_ref, mid_sums_ref, last_sums_ref,
    grad_ref, sent_ref, first_sums,
):
    copies, share, width = parts_ref.shape
    masks = row_masks(meta_ref, latents, meta_ref[1] + meta_ref[2] * share, share)
    d_hidden = parts_ref[0].astype(F32)
    for part in range(1, copies):
        d_hidden = d_hidden + parts_ref[part].astype(F32)
    unit, inverse = normed(own_rows(meta_ref, tokens_ref, share))
    grad = d_mid_ref[...] + norm_back(unit, inverse, d_hidden * (1.0 + rows_of(mod_ref, masks, 1)))
    grad_ref[...] = grad.astype(BF16)
    latent_sums(first_sums, masks, d_hidden, 0, 2)
    latent_sums(first_sums, masks, d_hidden * unit, 1, 2)
    columns = width // copies
    for number in range(latents):
        for feature in range(6):
            if feature < 2:
                row = first_sums[number * 2 + feature : number * 2 + feature + 1, :]
            elif feature < 5:
                place = number * 3 + feature - 2
                row = mid_sums_ref[place : place + 1, :]
            else:
                row = last_sums_ref[number : number + 1, :]
            place = number * 6 + feature
            for part in range(copies):
                sent_ref[part, place : place + 1, :] = row[:, part * columns : (part + 1) * columns]


def latent_index(latent_len, first_row, row_count, token_total):
    positions = first_row + jnp.arange(row_count, dtype=jnp.int32)
    ends = jnp.cumsum(latent_len, dtype=jnp.int32)
    found = jnp.sum((positions[:, None] >= ends[None, :]).astype(jnp.int32), axis=1, dtype=jnp.int32)
    return jnp.where((positions >= 0) & (positions < token_total), found, -1)


def normed(values):
    average = jnp.mean(values, axis=-1, keepdims=True)
    centred = values - average
    spread = jnp.mean(centred * centred, axis=-1, keepdims=True)
    inverse = lax.rsqrt(spread + NORM_EPS)
    return centred * inverse, inverse


def norm_back(unit, inverse, grad):
    along = jnp.mean(grad * unit, axis=-1, keepdims=True)
    return inverse * (grad - jnp.mean(grad, axis=-1, keepdims=True) - unit * along)


def gelu_pair(value):
    root = math.sqrt(2.0 / math.pi)
    bend = jnp.tanh(root * (value + 0.044715 * value * value * value))
    slope = root * (1.0 + 3.0 * 0.044715 * value * value)
    gelu = 0.5 * value * (1.0 + bend)
    return gelu, 0.5 * (1.0 + bend) + 0.5 * value * (1.0 - bend * bend) * slope


def local(
    tokens,
    conditioning,
    latent_len,
    w_ada,
    b_ada,
    w_qkv,
    b_qv,
    w_proj,
    b_proj,
    w_fc1,
    b_fc1,
    w_fc2,
    b_fc2,
    cotangent,
):
    rows, width = tokens.shape
    share_width = w_qkv.shape[0]
    features = w_qkv.shape[2]
    units = w_fc1.shape[1]
    heads = features // DH
    latents = conditioning.shape[0]
    n_dp, n_tensor = lax.axis_size("dp"), lax.axis_size("tensor")
    my_dp, my_tensor = lax.axis_index("dp"), lax.axis_index("tensor")
    share = rows // n_tensor

    core = my_dp % 2
    qk = w_qkv[:, :2].reshape(share_width, 2 * features)
    vp = jnp.concatenate([w_qkv[:, 2], w_proj.T], axis=1)
    early_parts = chip_parts(pair_rows(qk, vp))

    cond = conditioning.astype(F32)
    gate = 1.0 / (1.0 + jnp.exp(-cond))
    activated = (cond * gate).astype(BF16)
    own_activated = lax.dynamic_slice_in_dim(activated, my_dp * share_width, share_width, 1)
    flat_ada = w_ada.reshape(share_width, 6 * features)
    mod_part = jnp.dot(own_activated, flat_ada, preferred_element_type=F32)
    mod_part = mod_part.reshape(latents * 6, features)
    mod_mine = jnp.sum(gather(mod_part, "dp", n_dp), axis=0)
    mod_mine = mod_mine + jnp.tile(b_ada.astype(F32), (latents, 1))
    modulation = gather(mod_mine, "tensor", n_tensor).transpose(1, 0, 2).reshape(6 * latents, width)

    mod_rows, early_parts = lax.optimization_barrier((modulation, early_parts))
    early_mine, early_other = assemble(early_parts)
    meta = jnp.stack([core, my_dp * rows, my_tensor, my_dp // 2]).astype(jnp.int32)
    meta = jnp.concatenate([meta, latent_len])
    by_last = (((1,), (1,)), ((), ()))
    by_token = (((0,), (0,)), ((), ()))
    by_rows = (((0,), (1,)), ((), ()))
    bias = jnp.concatenate([b_qv[0], jnp.zeros_like(b_qv[0]), b_qv[1], jnp.zeros_like(b_qv[0])])
    hidden_one, d_mlp, packed = call(
        lambda *refs: project_kernel(latents, *refs),
        "project",
        meta,
        (tokens, cotangent, mod_rows, bias.astype(F32).reshape(2, -1), early_mine, early_other),
        (((rows, width), BF16), ((rows, width), BF16), ((2 * heads, DH, rows * 5 // 2), BF16)),
    )
    full_proj = choose(core, after(early_other, packed), early_mine)[0][:, features:]
    late_rows = pair_rows(after(w_fc1, packed), after(w_fc2.T, packed))
    split = HeadSplit if 2 * heads == n_dp else Window
    attention = split(latent_len, rows)
    attended = attention.forward(packed, (full_proj, late_rows))
    attn_part = lax.dot_general(attended, full_proj, by_rows, preferred_element_type=F32).astype(BF16)
    late_parts = chip_parts(after(late_rows, attended))
    attn_parts = exchange_shares(attn_part, "tensor")
    hidden_blocks, attn_out, residual_mid = call(
        lambda *refs: middle_kernel(latents, *refs),
        "middle",
        meta,
        (attn_parts, tokens, mod_rows, b_proj.reshape(1, -1)),
        (((n_tensor, share, width), BF16), ((share, width), F32), ((share, width), F32)),
    )
    hidden_two = exchange(hidden_blocks, "tensor").reshape(rows, width)

    late_parts = after(late_parts, hidden_two)
    mlp_meta = meta
    if len(late_parts) > 4:
        late_mine, late_other = assemble(late_parts)
        late_parts, swapped = [late_mine], [late_other]
        mlp_meta = meta.at[3].set(0)
    else:
        swapped = [swap(part, "dp", 1) for part in late_parts]
    count = len(late_parts)
    d_two_part, mlp_part, gelu_out, d_pre, d_bias_fc1 = call(
        lambda *refs: mlp_kernel(count, *refs),
        "mlp",
        mlp_meta,
        (*late_parts, *swapped, hidden_two, d_mlp, b_fc1.reshape(1, -1)),
        (((rows, width), BF16), ((rows, width), BF16), ((rows, units), BF16), ((rows, units), BF16))
        + (((1, units), F32),),
        [pltpu.VMEM((width, units), BF16)] * 2
        + [pltpu.VMEM((rows, width), F32)] * 2
        + [pltpu.SemaphoreType.DMA((2 * count,))],
        2 * count,
    )
    d_two_parts = exchange_shares(d_two_part, "tensor")

    left_mine, left_other = choose(core, hidden_two, d_mlp)
    right_mine, right_other = choose(core, d_pre, gelu_out)
    sent = lax.dot_general(left_other, right_other, by_token, preferred_element_type=F32)
    kept = lax.dot_general(left_mine, right_mine, by_token, preferred_element_type=F32)
    late_total = pair_total(kept, sent)
    d_two_parts, late_total = lax.optimization_barrier((d_two_parts, late_total))
    late_grads = [chip_share(late_total, step) for step in range(n_dp // 2 - 1)]

    d_attn_blocks, d_mid, mid_sums = call(
        lambda *refs: middle_back_kernel(latents, *refs),
        "middle_back",
        meta,
        (d_two_parts, residual_mid, attn_out, cotangent, mod_rows),
        (((n_tensor, share, width), BF16), ((share, width), F32), ((3 * latents, width), F32)),
    )
    d_attn = exchange(d_attn_blocks, "tensor").reshape(rows, width)

    d_spread, d_bias_proj = call(
        spread_kernel,
        "spread",
        meta,
        (d_attn, full_proj),
        (((2 * heads, DH, rows // 2), BF16), ((1, width), F32)),
    )
    mlp_parts = parts_beside(after(mlp_part, d_spread), "tensor")
    result_own, last_sums = call(
        lambda *refs: result_kernel(latents, n_tensor, *refs),
        "result",
        meta,
        (*mlp_parts, residual_mid, cotangent, mod_rows, b_fc2.reshape(1, -1)),
        (((share, width), BF16), ((latents, width), F32)),
    )
    d_packed = attention.backward(d_spread, (result_own, late_grads))
    result = gather_beside(result_own, "tensor")
    d_one_part, d_qk, d_vp = call(
        unspread_kernel,
        "unspread",
        meta,
        (d_packed, early_mine, early_other),
        (((rows, width), BF16), ((rows, 2 * features), BF16), ((rows, 2 * features), BF16)),
    )
    d_one_parts = exchange_shares(d_one_part, "tensor")

    left = jnp.concatenate([hidden_one, d_attn])
    blank = jnp.zeros((features, rows), BF16)
    right_qk = jnp.concatenate([d_qk, jnp.zeros_like(d_qk)])
    right_vp = jnp.concatenate([d_vp, jnp.concatenate([blank, attended]).T])
    right_mine, right_other = choose(core, right_qk, right_vp)
    sent = lax.dot_general(left, right_other, by_token, preferred_element_type=F32)
    kept = lax.dot_general(left, right_mine, by_token, preferred_element_type=F32)
    early_total = pair_total(kept, sent)
    late_last = chip_share(after(late_total, d_one_part), n_dp // 2 - 1)
    d_one_parts, early_total = lax.optimization_barrier((d_one_parts, early_total))
    early_grads = [chip_share(early_total, step) for step in range(n_dp // 2)]

    grad_own, d_mod_part = call(
        lambda *refs: first_back_kernel(latents, *refs),
        "first_back",
        meta,
        (d_one_parts, tokens, d_mid, mod_rows, mid_sums, last_sums),
        (((share, width), BF16), ((n_tensor, 6 * latents, features), F32)),
        [pltpu.VMEM((2 * latents, width), F32)],
    )
    bias_part = jnp.concatenate(
        [
            jnp.sum(d_mlp.astype(F32), axis=0),
            d_bias_proj[0],
            d_bias_fc1[0],
            jnp.sum(d_qk[:, :features].astype(F32), axis=0),
            jnp.sum(d_vp[:, :features].astype(F32), axis=0),
        ]
    )
    bias_rows = bias_part.reshape(-1, features)
    d_mod_mine = jnp.sum(exchange(d_mod_part, "tensor"), axis=0)
    grad_tokens = gather_beside(after(grad_own, d_mod_mine), "tensor").astype(F32)
    sums = jnp.sum(gather(jnp.concatenate([d_mod_mine, bias_rows]), "dp", n_dp), axis=0)
    d_mod = sums[: 6 * latents].reshape(latents, 6 * features)
    bias_total = sums[6 * latents :].reshape(-1)
    grad_b_ada = jnp.sum(d_mod, axis=0).reshape(6, features)
    grad_w_ada = lax.dot_general(
        own_activated.astype(F32), d_mod, by_token, precision=lax.Precision.HIGHEST
    ).reshape(share_width, 6, features)
    high = d_mod.astype(BF16)
    low = (d_mod - high.astype(F32)).astype(BF16)
    d_active = lax.dot_general(
        jnp.concatenate([high, low]), flat_ada, by_last, preferred_element_type=F32
    )
    d_active = d_active[:latents] + d_active[latents:]
    d_active = gather(d_active, ("dp", "tensor"), n_dp * n_tensor)
    d_active = jnp.sum(d_active.reshape(n_dp, n_tensor, latents, share_width), axis=1)
    d_active = d_active.transpose(1, 0, 2).reshape(latents, width)
    grad_cond = d_active * (gate * (1.0 + cond * (1.0 - gate)))

    grad_fc1, grad_fc2 = finish_pair(late_grads + [late_last])
    grad_qk, grad_vp = finish_pair(after(early_grads, d_active))
    grad_qkv = jnp.concatenate([grad_qk, grad_vp[:, :features]], axis=1)
    grad_qkv = grad_qkv.reshape(share_width, 3, features)

    return (
        result,
        grad_tokens,
        grad_cond,
        grad_w_ada,
        grad_b_ada,
        grad_qkv,
        bias_total[2 * width + units :].reshape(2, features),
        grad_vp[:, features:].T,
        bias_total[width : 2 * width],
        grad_fc1,
        bias_total[2 * width : 2 * width + units],
        grad_fc2.T,
        bias_total[:width],
    )


def solution(mesh):
    in_specs = (
        P("dp", None),
        P(),
        P(),
        P("dp", None, "tensor"),
        P(None, "tensor"),
        P("dp", None, "tensor"),
        P(None, "tensor"),
        P("tensor", "dp"),
        P(),
        P("dp", "tensor"),
        P("tensor"),
        P("tensor", "dp"),
        P(),
        P("dp", None),
    )
    out_specs = (
        P("dp", None),
        P("dp", None),
        P(),
        P("dp", None, "tensor"),
        P(None, "tensor"),
        P("dp", None, "tensor"),
        P(None, "tensor"),
        P("tensor", "dp"),
        P(),
        P("dp", "tensor"),
        P("tensor"),
        P("tensor", "dp"),
        P(),
    )
    return jax.shard_map(local, mesh=mesh, in_specs=in_specs, out_specs=out_specs, check_vma=False)
```

```python
import math

import jax
import jax.numpy as jnp
from jax import lax
from jax.experimental import pallas as pl
from jax.experimental.pallas import tpu as pltpu
from jax.sharding import PartitionSpec as P

DH = 72
SEQ = 1024
NORM_EPS = 1e-06
NEGATIVE = -1e30
SCALE = 1.0 / math.sqrt(DH)
MIB = 1024 * 1024
BF16 = jnp.bfloat16
F32 = jnp.float32


def swap(block, axis, bits):
    route = [(i, i ^ bits) for i in range(lax.axis_size(axis))]
    return lax.ppermute(block, axis, route)


def exchange(blocks, axis):
    return lax.all_to_all(blocks, axis, 0, 0, tiled=True)


def gather(block, axis, count):
    return exchange(jnp.broadcast_to(block[None], (count,) + block.shape), axis)


def after(value, *others):
    return lax.optimization_barrier((value,) + others)[0]


def choose(core, first, second):
    return jnp.where(core == 0, first, second), jnp.where(core == 0, second, first)


def pair_rows(first, second):
    core = lax.axis_index("dp") % 2
    keep, send = choose(core, first, second)
    return jnp.concatenate(choose(core, keep, swap(send, "dp", 1)))


def chip_parts(rows):
    count = lax.axis_size("dp") // 2
    return [rows] + [swap(rows, "dp", 2 * step) for step in range(1, count)]


def gather_chips(rows):
    count = lax.axis_size("dp")
    groups = [list(range(core, count, 2)) for core in range(2)]
    return lax.all_gather(rows, "dp", axis=0, tiled=True, axis_index_groups=groups)


def sum_chips(blocks):
    if len(blocks) == 1:
        count, chip = lax.axis_size("dp") // 2, lax.axis_index("dp") // 2
        rows = blocks[0].reshape((count, -1) + blocks[0].shape[1:])
        blocks = [
            lax.dynamic_index_in_dim(rows, chip ^ step, 0, keepdims=False) for step in range(count)
        ]
    return [swap(block, "dp", 2 * step) if step else block for step, block in enumerate(blocks)]


def finish_pair(parts):
    core = lax.axis_index("dp") % 2
    rows = sum(part.astype(F32) for part in parts)
    half = rows.shape[0] // 2
    keep, send = choose(core, rows[:half], rows[half:])
    return choose(core, keep, swap(send, "dp", 1))


def parts_beside(partial, axis):
    count, me = lax.axis_size(axis), lax.axis_index(axis)
    blocks = partial.reshape((count, partial.shape[0] // count) + partial.shape[1:])
    parts = [lax.dynamic_index_in_dim(blocks, me, 0, keepdims=False)]
    for bits in range(1, count):
        sent = lax.dynamic_index_in_dim(blocks, me ^ bits, 0, keepdims=False)
        parts.append(swap(sent, axis, bits))
    return parts


def gather_beside(share, axis):
    count, me = lax.axis_size(axis), lax.axis_index(axis)
    parts = jnp.stack([share] + [swap(share, axis, bits) for bits in range(1, count)])
    ordered = [lax.dynamic_index_in_dim(parts, me ^ place, 0, keepdims=False) for place in range(count)]
    return jnp.concatenate(ordered)


def exchange_shares(partial, axis):
    count = lax.axis_size(axis)
    blocks = partial.reshape((count, partial.shape[0] // count) + partial.shape[1:])
    return exchange(blocks, axis)


def tile_range(meta_ref, latents, tile, core):
    lane = lax.broadcasted_iota(jnp.int32, (1, 256), 1)
    first = tile * 512 + core * 128
    last = first + 383
    place = first + lane + jnp.where(lane >= 128, 128, 0)
    begin = jnp.zeros((1, 256), jnp.int32)
    finish = jnp.zeros((1, 256), jnp.int32)
    low = jnp.int32(0)
    high = jnp.int32(0)
    start = jnp.int32(0)
    for number in range(latents):
        end = start + meta_ref[1 + number]
        inside = (place >= start) & (place < end)
        begin = jnp.where(inside, start, begin)
        finish = jnp.where(inside, end, finish)
        low = jnp.where((first >= start) & (first < end), start, low)
        high = jnp.where((last >= start) & (last < end), end, high)
        start = end
    return begin, finish, low // 256, (high + 255) // 256


def pair(ref, tile, start):
    left = ref[2 * tile, :, start : start + 128]
    right = ref[2 * tile + 1, :, start : start + 128]
    return jnp.concatenate([left, right], axis=1)


def key_mask(block, begin, finish):
    place = block * 256 + lax.broadcasted_iota(jnp.int32, (256, 256), 0)
    return (place >= begin) & (place < finish)


def forward_kernel(latents, meta_ref, packed_ref, out_ref, exact_ref, log_ref, keys, scores):
    blocks = packed_ref.shape[0]
    core = meta_ref[0]
    for block in range(blocks):
        keys[block] = packed_ref[block, :, :256].astype(F32).T.astype(BF16)
    for tile in range(blocks // 2):
        begin, finish, low, high = tile_range(meta_ref, latents, tile, core)
        query = pair(packed_ref, tile, 512)

        def score(block, largest):
            raw = jnp.dot(keys[block], query, preferred_element_type=F32) * SCALE
            raw = jnp.where(key_mask(block, begin, finish), raw, NEGATIVE)
            scores[block] = raw
            return jnp.maximum(largest, jnp.max(raw, axis=0, keepdims=True))

        largest = lax.fori_loop(low, high, score, jnp.full((1, 256), NEGATIVE, F32))

        def mix(block, carry):
            total, mixed = carry
            weights = jnp.exp(scores[block] - largest)
            total = total + jnp.sum(weights, axis=0, keepdims=True)
            values = packed_ref[block, :, 256:512]
            mixed = mixed + jnp.dot(values, weights.astype(BF16), preferred_element_type=F32)
            return total, mixed

        total, mixed = lax.fori_loop(
            low, high, mix, (jnp.zeros((1, 256), F32), jnp.zeros((DH, 256), F32))
        )
        mixed = mixed / total
        log_total = largest + jnp.log(total)
        for half in range(2):
            part = mixed[:, half * 128 : half * 128 + 128]
            exact_ref[2 * tile + half] = part
            out_ref[2 * tile + half] = part.astype(BF16)
            log_ref[2 * tile + half] = log_total[:, half * 128 : half * 128 + 128]


def backward_kernel(
    latents, meta_ref, packed_ref, grad_ref, exact_ref, log_ref, out_ref, keys, values, d_keys, d_values
):
    blocks = packed_ref.shape[0]
    core = meta_ref[0]
    for block in range(blocks):
        keys[block] = packed_ref[block, :, :256].astype(F32).T.astype(BF16)
        values[block] = packed_ref[block, :, 256:512].astype(F32).T.astype(BF16)
    d_keys[...] = jnp.zeros_like(d_keys)
    d_values[...] = jnp.zeros_like(d_values)
    by_query = (((1,), (1,)), ((), ()))
    for tile in range(blocks // 2):
        begin, finish, low, high = tile_range(meta_ref, latents, tile, core)
        query = pair(packed_ref, tile, 512)
        grad = pair(grad_ref, tile, 0)
        inner = jnp.sum(grad.astype(F32) * pair(exact_ref, tile, 0), axis=0, keepdims=True)
        log_total = pair(log_ref, tile, 0)

        def step(block, d_query):
            raw = jnp.dot(keys[block], query, preferred_element_type=F32) * SCALE
            probs = jnp.where(key_mask(block, begin, finish), jnp.exp(raw - log_total), 0.0)
            d_probs = jnp.dot(values[block], grad, preferred_element_type=F32)
            d_scores = (probs * (d_probs - inner)).astype(BF16)
            d_values[block] += lax.dot_general(
                grad, probs.astype(BF16), by_query, preferred_element_type=F32
            )
            d_keys[block] += lax.dot_general(query, d_scores, by_query, preferred_element_type=F32)
            key_rows = packed_ref[block, :, :256]
            return d_query + jnp.dot(key_rows, d_scores, preferred_element_type=F32)

        d_query = lax.fori_loop(low, high, step, jnp.zeros((DH, 256), F32)) * SCALE
        for half in range(2):
            part = d_query[:, half * 128 : half * 128 + 128]
            out_ref[2 * tile + half, :, 512:640] = part.astype(BF16)
    for block in range(blocks):
        out_ref[block, :, :256] = (d_keys[block] * SCALE).astype(BF16)
        out_ref[block, :, 256:512] = d_values[block].astype(BF16)


def attend_forward(meta, packed):
    blocks = packed.shape[0]
    shape = jax.ShapeDtypeStruct
    return pl.pallas_call(
        lambda *refs: forward_kernel(meta.shape[0] - 1, *refs),
        out_shape=(
            shape((blocks, DH, 128), BF16),
            shape((blocks, DH, 128), F32),
            shape((blocks, 1, 128), F32),
        ),
        in_specs=[
            pl.BlockSpec(memory_space=pltpu.SMEM),
            pl.BlockSpec(memory_space=pltpu.VMEM),
        ],
        out_specs=tuple([pl.BlockSpec(memory_space=pltpu.VMEM)] * 3),
        scratch_shapes=[
            pltpu.VMEM((blocks, 256, DH), BF16),
            pltpu.VMEM((blocks, 256, 256), F32),
        ],
        compiler_params=pltpu.CompilerParams(vmem_limit_bytes=10 * MIB),
        cost_estimate=pl.CostEstimate(flops=10**9, bytes_accessed=4 * 10**6, transcendentals=10**6),
        name="attend_forward",
    )(meta, packed)


def attend_backward(meta, packed, grad, exact, log_total):
    blocks = packed.shape[0]
    return pl.pallas_call(
        lambda *refs: backward_kernel(meta.shape[0] - 1, *refs),
        out_shape=jax.ShapeDtypeStruct(packed.shape, BF16),
        in_specs=[pl.BlockSpec(memory_space=pltpu.SMEM)]
        + [pl.BlockSpec(memory_space=pltpu.VMEM)] * 4,
        out_specs=pl.BlockSpec(memory_space=pltpu.VMEM),
        scratch_shapes=[
            pltpu.VMEM((blocks, 256, DH), BF16),
            pltpu.VMEM((blocks, 256, DH), BF16),
            pltpu.VMEM((blocks, DH, 256), F32),
            pltpu.VMEM((blocks, DH, 256), F32),
        ],
        compiler_params=pltpu.CompilerParams(vmem_limit_bytes=10 * MIB),
        cost_estimate=pl.CostEstimate(flops=3 * 10**9, bytes_accessed=4 * 10**6, transcendentals=10**6),
        name="attend_backward",
    )(meta, packed, grad, exact, log_total)


class HeadSplit:
    def __init__(self, latent_len, rows):
        self.rows = rows
        self.meta = jnp.concatenate([lax.axis_index("dp").astype(jnp.int32)[None] % 2, latent_len])

    def forward(self, packed, beside):
        self.packed = after(exchange(packed, "dp"), beside)
        out, self.exact, self.log_total = attend_forward(self.meta, self.packed)
        return exchange(out, "dp")

    def backward(self, grad, beside):
        grad = exchange(grad, "dp")
        out = attend_backward(self.meta, self.packed, grad, self.exact, self.log_total)
        return exchange(after(out, beside), "dp")


class Window:
    def __init__(self, latent_len, rows):
        self.rows = rows
        self.reach = (SEQ - 2) // rows + 1
        total = rows * lax.axis_size("dp")
        first = lax.axis_index("dp") * rows
        own = latent_index(latent_len, first, rows, total)
        ids = [
            latent_index(latent_len, first + offset * rows, rows, total)
            for offset in range(-self.reach, self.reach + 1)
        ]
        self.allowed = own[:, None] == jnp.concatenate(ids)[None, :]

    def from_behind(self, block, distance):
        devices = range(lax.axis_size("dp"))
        return lax.ppermute(
            block, "dp", [(i - distance, i) for i in devices if i - distance in devices]
        )

    def head_scores(self, query, key):
        raw = jnp.einsum("eq,ek->qk", query, key, preferred_element_type=F32) * SCALE
        return jnp.where(self.allowed, raw, NEGATIVE)

    def forward(self, packed, beside):
        rows = self.rows
        split = packed.reshape(-1, 2, DH, rows * 5 // 2)
        query = jnp.concatenate([split[:, 0, :, 2 * rows :], split[:, 1, :, 2 * rows :]], axis=2)
        projected = jnp.stack([query, split[:, 0, :, :rows], split[:, 0, :, rows : 2 * rows]])
        key_value = projected[1:]
        pieces = [
            key_value if offset == 0 else self.from_behind(key_value, -offset)
            for offset in range(-self.reach, self.reach + 1)
        ]
        window = jnp.concatenate(pieces, axis=3)
        self.operands = (projected[0], window[0], window[1])

        def one(operands):
            query, key, value = operands
            scores = self.head_scores(query, key)
            largest = jnp.max(scores, axis=1, keepdims=True)
            weights = jnp.exp(scores - largest)
            totals = jnp.sum(weights, axis=1, keepdims=True)
            probs = (weights / totals).astype(BF16)
            mixed = jnp.einsum("qk,ek->eq", probs, value, preferred_element_type=F32)
            return mixed.astype(BF16), (largest + jnp.log(totals))[:, 0]

        out, self.log_total = lax.map(one, self.operands)
        out = out.reshape(-1, DH, 2, rows // 2).transpose(0, 2, 1, 3)
        return out.reshape(-1, DH, rows // 2)

    def backward(self, grad, beside):
        rows, reach = self.rows, self.reach
        halves = grad.reshape(-1, 2, DH, rows // 2)
        grads = jnp.concatenate([halves[:, 0], halves[:, 1]], axis=2)

        def one(operands):
            query, key, value, grad, log_total = operands
            probs = jnp.exp(self.head_scores(query, key) - log_total[:, None])
            d_value = jnp.einsum("qk,eq->ek", probs.astype(BF16), grad, preferred_element_type=F32)
            d_probs = jnp.einsum("eq,ek->qk", grad, value, preferred_element_type=F32)
            inner = jnp.sum(probs * d_probs, axis=1, keepdims=True)
            d_scores = (probs * (d_probs - inner)).astype(BF16)
            d_query = jnp.einsum("qk,ek->eq", d_scores, key, preferred_element_type=F32) * SCALE
            d_key = jnp.einsum("qk,eq->ek", d_scores, query, preferred_element_type=F32) * SCALE
            return d_query, d_key, d_value

        d_query, d_key, d_value = lax.map(one, self.operands + (grads, self.log_total))
        d_window = jnp.stack([d_key, d_value])
        d_key_value = d_window[..., reach * rows : (reach + 1) * rows]
        for offset in range(-reach, reach + 1):
            if offset != 0:
                block = d_window[..., (offset + reach) * rows : (offset + reach + 1) * rows]
                d_key_value = d_key_value + self.from_behind(block, offset)
        wide = jnp.concatenate([d_key_value[0], d_key_value[1]], axis=2)
        wide = jnp.stack([wide, jnp.zeros_like(wide)], axis=1)
        halves = d_query.reshape(-1, DH, 2, rows // 2).transpose(0, 2, 1, 3)
        packed = jnp.concatenate([wide, halves], axis=3).astype(BF16)
        return packed.reshape(-1, DH, rows * 5 // 2)


META = 4


def vmem(count):
    return [pl.BlockSpec(memory_space=pltpu.VMEM)] * count


def call(body, name, meta, arrays, outs, scratch=(), anywhere=0, limit=8):
    return pl.pallas_call(
        body,
        out_shape=tuple(jax.ShapeDtypeStruct(shape, kind) for shape, kind in outs),
        in_specs=[pl.BlockSpec(memory_space=pltpu.SMEM)]
        + [pl.BlockSpec(memory_space=pl.ANY)] * anywhere
        + vmem(len(arrays) - anywhere),
        out_specs=tuple(vmem(len(outs))),
        scratch_shapes=list(scratch),
        compiler_params=pltpu.CompilerParams(vmem_limit_bytes=limit * MIB),
        cost_estimate=pl.CostEstimate(flops=1, bytes_accessed=1, transcendentals=0),
        name=name,
    )(meta, *arrays)


def row_masks(meta_ref, latents, first, rows):
    place = first + lax.broadcasted_iota(jnp.int32, (rows, 1), 0)
    ids = jnp.zeros((rows, 1), jnp.int32)
    end = jnp.int32(0)
    for number in range(latents - 1):
        end = end + meta_ref[META + number]
        ids = ids + (place >= end).astype(jnp.int32)
    return [(ids == number).astype(F32) for number in range(latents)]


def rows_of(mod_ref, masks, feature):
    out = masks[0] * mod_ref[feature : feature + 1, :]
    for number in range(1, len(masks)):
        row = number * 6 + feature
        out = out + masks[number] * mod_ref[row : row + 1, :]
    return out


def latent_sums(out_ref, masks, values, feature, features):
    rounded = values.astype(BF16).astype(F32)
    for number, mask in enumerate(masks):
        row = number * features + feature
        out_ref[row : row + 1, :] = jnp.sum(mask * rounded, axis=0, keepdims=True)


def own_rows(meta_ref, ref, share):
    start = pl.multiple_of(meta_ref[2] * share, share)
    return ref[pl.ds(start, share), :].astype(F32)


def on_core(meta_ref, body, mine, other):
    @pl.when(meta_ref[0] == 0)
    def _():
        body(mine, other)

    @pl.when(meta_ref[0] != 0)
    def _():
        body(other, mine)


def place_rows(meta_ref, parts, whole, sems):
    block = parts[0].shape[0]
    copies = []
    for step, part in enumerate(parts):
        start = pl.multiple_of((meta_ref[3] ^ step) * block, 16)
        copies.append(
            pltpu.make_async_copy(part, whole.at[pl.ds(start, block), :], sems.at[step])
        )
    return copies


def place_pair(meta_ref, mine, other, first_ref, second_ref, sems):
    def body(first, second):
        copies = place_rows(meta_ref, first, first_ref, sems.at[0])
        copies += place_rows(meta_ref, second, second_ref, sems.at[1])
        for copy in copies:
            copy.start()
        for copy in copies:
            copy.wait()

    on_core(meta_ref, body, mine, other)


def project_kernel(latents, count, meta_ref, *refs):
    mine, other = refs[:count], refs[count : 2 * count]
    tokens_ref, cot_ref, mod_ref, bias_ref = refs[2 * count : 2 * count + 4]
    hidden_ref, d_mlp_ref, packed_ref, qk_ref, vp_ref, sems = refs[2 * count + 4 :]
    rows, width = tokens_ref.shape
    place_pair(meta_ref, mine, other, qk_ref, vp_ref, sems)
    masks = row_masks(meta_ref, latents, meta_ref[1], rows)
    unit, _ = normed(tokens_ref[...].astype(F32))
    hidden = unit * (1.0 + rows_of(mod_ref, masks, 1)) + rows_of(mod_ref, masks, 0)
    hidden_ref[...] = hidden.astype(BF16)
    d_mlp_ref[...] = (cot_ref[...].astype(F32) * rows_of(mod_ref, masks, 5)).astype(BF16)
    heads = packed_ref.shape[0] // 2
    features = heads * DH
    left = hidden_ref[...]
    both = jnp.dot(left, qk_ref[...], preferred_element_type=F32) + bias_ref[0:1, :]
    both = both.T
    value = jnp.dot(left, vp_ref[...], preferred_element_type=F32) + bias_ref[1:2, :]
    value = value.T
    for head in range(heads):
        start = head * DH
        query = both[start : start + DH].astype(BF16)
        key = both[features + start : features + start + DH].astype(BF16)
        val = value[start : start + DH].astype(BF16)
        for half in range(2):
            packed_ref[2 * head + half, :, :rows] = key
            packed_ref[2 * head + half, :, rows : 2 * rows] = val
            packed_ref[2 * head + half, :, 2 * rows :] = query[
                :, half * (rows // 2) : (half + 1) * (rows // 2)
            ]


def attend_out_kernel(meta_ref, parts_ref, vp_ref, part_ref, attended_ref):
    heads = parts_ref.shape[0] // 2
    rows = part_ref.shape[0]
    stacked = [jnp.zeros((heads * DH, rows), F32)]
    for head in range(heads):
        left = parts_ref[2 * head].astype(F32)
        right = parts_ref[2 * head + 1].astype(F32)
        stacked.append(jnp.concatenate([left, right], axis=1))
    attended_ref[...] = jnp.concatenate(stacked, axis=0).T.astype(BF16)
    part_ref[...] = lax.dot_general(
        attended_ref[...], vp_ref[...], (((1,), (1,)), ((), ())), preferred_element_type=F32
    ).astype(BF16)


def middle_kernel(
    latents, meta_ref, parts_ref, tokens_ref, mod_ref, bias_ref, sent_ref, attn_ref, mid_ref
):
    copies, share, width = parts_ref.shape
    masks = row_masks(meta_ref, latents, meta_ref[1] + meta_ref[2] * share, share)
    attn = bias_ref[...].astype(F32)
    for part in range(copies):
        attn = attn + parts_ref[part].astype(F32)
    attn_ref[...] = attn
    mid = own_rows(meta_ref, tokens_ref, share) + rows_of(mod_ref, masks, 2) * attn
    mid_ref[...] = mid
    unit, _ = normed(mid)
    hidden = unit * (1.0 + rows_of(mod_ref, masks, 4)) + rows_of(mod_ref, masks, 3)
    for part in range(copies):
        sent_ref[part] = hidden.astype(BF16)


def mlp_kernel(
    meta_ref, mine_ref, other_ref, hidden_ref, d_mlp_ref, bias_ref,
    d_two_ref, mlp_ref, gelu_ref, d_pre_ref, d_bias_ref,
    fc1_ref, fc2_ref, d_two_sum, mlp_sum, sems,
):
    def load(first, second):
        copies = [
            pltpu.make_async_copy(first, fc1_ref, sems.at[0]),
            pltpu.make_async_copy(second, fc2_ref, sems.at[1]),
        ]
        for copy in copies:
            copy.start()
        for copy in copies:
            copy.wait()

    on_core(meta_ref, load, mine_ref, other_ref)
    d_two_sum[...] = jnp.zeros_like(d_two_sum)
    mlp_sum[...] = jnp.zeros_like(mlp_sum)
    tile = 384
    by_last = (((1,), (1,)), ((), ()))

    def step(number, carry):
        units = pl.ds(pl.multiple_of(number * tile, tile), tile)
        fc1, fc2 = fc1_ref[:, units], fc2_ref[:, units]
        pre = jnp.dot(hidden_ref[...], fc1, preferred_element_type=F32)
        gelu, slope = gelu_pair(pre + bias_ref[:, units].astype(F32))
        grad = jnp.dot(d_mlp_ref[...], fc2, preferred_element_type=F32)
        d_pre = (grad * slope).astype(BF16)
        gelu = gelu.astype(BF16)
        gelu_ref[:, units] = gelu
        d_pre_ref[:, units] = d_pre
        d_bias_ref[:, units] = jnp.sum(d_pre.astype(F32), axis=0, keepdims=True)
        d_two_sum[...] += lax.dot_general(d_pre, fc1, by_last, preferred_element_type=F32)
        mlp_sum[...] += lax.dot_general(gelu, fc2, by_last, preferred_element_type=F32)
        return carry

    lax.fori_loop(0, fc1_ref.shape[1] // tile, step, 0)
    d_two_ref[...] = d_two_sum[...].astype(BF16)
    mlp_ref[...] = mlp_sum[...].astype(BF16)


def middle_back_kernel(
    latents, meta_ref, parts_ref, mid_in_ref, attn_ref, cot_ref, mod_ref, sent_ref, d_mid_ref, sums_ref
):
    copies, share, width = parts_ref.shape
    masks = row_masks(meta_ref, latents, meta_ref[1] + meta_ref[2] * share, share)
    d_hidden = parts_ref[0].astype(F32)
    for part in range(1, copies):
        d_hidden = d_hidden + parts_ref[part].astype(F32)
    unit, inverse = normed(mid_in_ref[...])
    d_mid = own_rows(meta_ref, cot_ref, share) + norm_back(
        unit, inverse, d_hidden * (1.0 + rows_of(mod_ref, masks, 4))
    )
    d_mid_ref[...] = d_mid
    d_attn = (d_mid * rows_of(mod_ref, masks, 2)).astype(BF16)
    for part in range(copies):
        sent_ref[part] = d_attn
    latent_sums(sums_ref, masks, d_mid * attn_ref[...], 0, 3)
    latent_sums(sums_ref, masks, d_hidden, 1, 3)
    latent_sums(sums_ref, masks, d_hidden * unit, 2, 3)


def result_kernel(
    latents, count, meta_ref, *refs
):
    parts = refs[:count]
    mid_ref, cot_ref, mod_ref, bias_ref, result_ref, sums_ref = refs[count:]
    share = result_ref.shape[0]
    masks = row_masks(meta_ref, latents, meta_ref[1] + meta_ref[2] * share, share)
    mlp = bias_ref[...].astype(F32)
    for part in parts:
        mlp = mlp + part[...].astype(F32)
    result_ref[...] = (mid_ref[...] + rows_of(mod_ref, masks, 5) * mlp).astype(BF16)
    latent_sums(sums_ref, masks, own_rows(meta_ref, cot_ref, share) * mlp, 0, 1)


def spread_kernel(meta_ref, d_attn_ref, vp_ref, packed_ref, d_bias_ref):
    grad = jnp.dot(d_attn_ref[...], vp_ref[...], preferred_element_type=F32).T
    half = grad.shape[1] // 2
    features = grad.shape[0] // 2
    for place in range(packed_ref.shape[0]):
        start = features + place // 2 * DH
        side = place % 2 * half
        packed_ref[place] = grad[start : start + DH, side : side + half].astype(BF16)
    d_bias_ref[...] = jnp.sum(d_attn_ref[...].astype(F32), axis=0, keepdims=True)


def unspread_kernel(meta_ref, parts_ref, qk_ref, vp_ref, d_one_ref, d_qk_ref, d_vp_ref):
    heads = parts_ref.shape[0] // 2
    rows = d_one_ref.shape[0]
    query, key, value = [], [], []
    for head in range(heads):
        left = parts_ref[2 * head].astype(F32)
        right = parts_ref[2 * head + 1].astype(F32)
        both = left[:, : 2 * rows] + right[:, : 2 * rows]
        key.append(both[:, :rows])
        value.append(both[:, rows:])
        query.append(jnp.concatenate([left[:, 2 * rows :], right[:, 2 * rows :]], axis=1))
    d_qk_ref[...] = jnp.concatenate(query + key, axis=0).T.astype(BF16)
    blank = jnp.zeros((heads * DH, rows), F32)
    d_vp_ref[...] = jnp.concatenate(value + [blank], axis=0).T.astype(BF16)
    tile = 384
    by_last = (((1,), (1,)), ((), ()))

    def step(number, carry):
        columns = pl.ds(pl.multiple_of(number * tile, tile), tile)
        total = lax.dot_general(d_qk_ref[...], qk_ref[columns, :], by_last, preferred_element_type=F32)
        total += lax.dot_general(d_vp_ref[...], vp_ref[columns, :], by_last, preferred_element_type=F32)
        d_one_ref[:, columns] = total.astype(BF16)
        return carry

    lax.fori_loop(0, qk_ref.shape[0] // tile, step, 0)


def weight_kernel(first_pairs, second_pairs, meta_ref, *refs):
    operands = 1 + max(max(pair) for pair in first_pairs + second_pairs)
    ins, outs, total = refs[:operands], refs[operands:-1], refs[-1]
    tile = 384

    def body(pairs):
        def step(number, carry):
            columns = pl.ds(pl.multiple_of(number * tile, tile), tile)
            block = jnp.zeros((tile, total.shape[1]), F32)
            for left, right in pairs:
                block += lax.dot_general(
                    ins[left][:, columns], ins[right][...], (((0,), (0,)), ((), ())),
                    preferred_element_type=F32,
                )
            total[columns, :] = block.astype(BF16)
            return carry

        lax.fori_loop(0, total.shape[0] // tile, step, 0)

    on_core(meta_ref, lambda pairs, _: body(pairs), first_pairs, second_pairs)
    rows = outs[0].shape[0]
    for step, out in enumerate(outs):
        start = pl.multiple_of((meta_ref[3] ^ step) * rows, 16)
        out[...] = total[pl.ds(start, rows), :]


def first_back_kernel(
    latents, meta_ref, parts_ref, tokens_ref, d_mid_ref, mod_ref, mid_sums_ref, last_sums_ref,
    grad_ref, sent_ref, first_sums,
):
    copies, share, width = parts_ref.shape
    masks = row_masks(meta_ref, latents, meta_ref[1] + meta_ref[2] * share, share)
    d_hidden = parts_ref[0].astype(F32)
    for part in range(1, copies):
        d_hidden = d_hidden + parts_ref[part].astype(F32)
    unit, inverse = normed(own_rows(meta_ref, tokens_ref, share))
    grad = d_mid_ref[...] + norm_back(unit, inverse, d_hidden * (1.0 + rows_of(mod_ref, masks, 1)))
    grad_ref[...] = grad.astype(BF16)
    latent_sums(first_sums, masks, d_hidden, 0, 2)
    latent_sums(first_sums, masks, d_hidden * unit, 1, 2)
    columns = width // copies
    for number in range(latents):
        for feature in range(6):
            if feature < 2:
                row = first_sums[number * 2 + feature : number * 2 + feature + 1, :]
            elif feature < 5:
                place = number * 3 + feature - 2
                row = mid_sums_ref[place : place + 1, :]
            else:
                row = last_sums_ref[number : number + 1, :]
            place = number * 6 + feature
            for part in range(copies):
                sent_ref[part, place : place + 1, :] = row[:, part * columns : (part + 1) * columns]


def latent_index(latent_len, first_row, row_count, token_total):
    positions = first_row + jnp.arange(row_count, dtype=jnp.int32)
    ends = jnp.cumsum(latent_len, dtype=jnp.int32)
    found = jnp.sum((positions[:, None] >= ends[None, :]).astype(jnp.int32), axis=1, dtype=jnp.int32)
    return jnp.where((positions >= 0) & (positions < token_total), found, -1)


def normed(values):
    average = jnp.mean(values, axis=-1, keepdims=True)
    centred = values - average
    spread = jnp.mean(centred * centred, axis=-1, keepdims=True)
    inverse = lax.rsqrt(spread + NORM_EPS)
    return centred * inverse, inverse


def norm_back(unit, inverse, grad):
    along = jnp.mean(grad * unit, axis=-1, keepdims=True)
    return inverse * (grad - jnp.mean(grad, axis=-1, keepdims=True) - unit * along)


def gelu_pair(value):
    root = math.sqrt(2.0 / math.pi)
    bend = jnp.tanh(root * (value + 0.044715 * value * value * value))
    slope = root * (1.0 + 3.0 * 0.044715 * value * value)
    gelu = 0.5 * value * (1.0 + bend)
    return gelu, 0.5 * (1.0 + bend) + 0.5 * value * (1.0 - bend * bend) * slope


def local(
    tokens,
    conditioning,
    latent_len,
    w_ada,
    b_ada,
    w_qkv,
    b_qv,
    w_proj,
    b_proj,
    w_fc1,
    b_fc1,
    w_fc2,
    b_fc2,
    cotangent,
):
    rows, width = tokens.shape
    share_width = w_qkv.shape[0]
    features = w_qkv.shape[2]
    units = w_fc1.shape[1]
    heads = features // DH
    latents = conditioning.shape[0]
    n_dp, n_tensor = lax.axis_size("dp"), lax.axis_size("tensor")
    my_dp, my_tensor = lax.axis_index("dp"), lax.axis_index("tensor")
    share = rows // n_tensor

    core = my_dp % 2
    qk = w_qkv[:, :2].reshape(share_width, 2 * features)
    vp = jnp.concatenate([w_qkv[:, 2], w_proj.T], axis=1)
    early_rows = pair_rows(qk, vp)

    cond = conditioning.astype(F32)
    gate = 1.0 / (1.0 + jnp.exp(-cond))
    activated = (cond * gate).astype(BF16)
    own_activated = lax.dynamic_slice_in_dim(activated, my_dp * share_width, share_width, 1)
    flat_ada = w_ada.reshape(share_width, 6 * features)
    mod_part = jnp.dot(own_activated, flat_ada, preferred_element_type=F32)
    mod_part = mod_part.reshape(latents * 6, features)
    mod_mine = jnp.sum(gather(mod_part, "dp", n_dp), axis=0)
    mod_mine = mod_mine + jnp.tile(b_ada.astype(F32), (latents, 1))
    few_chips = n_dp // 2 <= 4
    early_rows = after(early_rows, mod_mine)
    early_parts = chip_parts(early_rows) if few_chips else [gather_chips(early_rows)]
    modulation = gather(mod_mine, "tensor", n_tensor).transpose(1, 0, 2).reshape(6 * latents, width)

    mod_rows, early_parts = lax.optimization_barrier((modulation, early_parts))
    early_parts += [swap(part, "dp", 1) for part in early_parts]
    count = len(early_parts) // 2
    meta = jnp.stack([core, my_dp * rows, my_tensor, my_dp // 2]).astype(jnp.int32)
    meta = jnp.concatenate([meta, latent_len])
    place_meta = meta if few_chips else meta.at[3].set(0)
    by_last = (((1,), (1,)), ((), ()))
    by_token = (((0,), (0,)), ((), ()))
    bias = jnp.concatenate([b_qv[0], jnp.zeros_like(b_qv[0]), b_qv[1], jnp.zeros_like(b_qv[0])])
    hidden_one, d_mlp, packed, full_qk, full_vp = call(
        lambda *refs: project_kernel(latents, count, *refs),
        "project",
        place_meta,
        (*early_parts, tokens, cotangent, mod_rows, bias.astype(F32).reshape(2, -1)),
        (((rows, width), BF16), ((rows, width), BF16), ((2 * heads, DH, rows * 5 // 2), BF16))
        + (((width, 2 * features), BF16),) * 2,
        [pltpu.SemaphoreType.DMA((2, count))],
        2 * count,
        12,
    )
    late_rows = pair_rows(after(w_fc1, packed), after(w_fc2.T, packed))
    hidden_other = swap(after(hidden_one, packed), "dp", 1)
    split = HeadSplit if 2 * heads == n_dp else Window
    attention = split(latent_len, rows)
    attended_parts = attention.forward(packed, late_rows)
    late_mine = gather_chips(after(late_rows, attended_parts))
    attn_part, attended = call(
        attend_out_kernel,
        "attend_out",
        meta,
        (attended_parts, full_vp),
        (((rows, width), BF16), ((rows, 2 * features), BF16)),
    )
    attn_parts = exchange_shares(attn_part, "tensor")
    hidden_blocks, attn_out, residual_mid = call(
        lambda *refs: middle_kernel(latents, *refs),
        "middle",
        meta,
        (attn_parts, tokens, mod_rows, b_proj.reshape(1, -1)),
        (((n_tensor, share, width), BF16), ((share, width), F32), ((share, width), F32)),
    )
    hidden_two = exchange(hidden_blocks, "tensor").reshape(rows, width)

    late_other = swap(after(late_mine, hidden_two), "dp", 1)
    d_two_part, mlp_part, gelu_out, d_pre, d_bias_fc1 = call(
        mlp_kernel,
        "mlp",
        meta,
        (late_mine, late_other, hidden_two, d_mlp, b_fc1.reshape(1, -1)),
        (((rows, width), BF16), ((rows, width), BF16), ((rows, units), BF16), ((rows, units), BF16))
        + (((1, units), F32),),
        [pltpu.VMEM((width, units), BF16)] * 2
        + [pltpu.VMEM((rows, width), F32)] * 2
        + [pltpu.SemaphoreType.DMA((2,))],
        2,
        16,
    )
    d_two_parts = exchange_shares(d_two_part, "tensor")

    chips = n_dp // 2 if few_chips else 1
    left_other = swap(choose(core, after(d_mlp, d_two_part), hidden_two)[0], "dp", 1)
    right_other = swap(choose(core, after(gelu_out, d_two_part), d_pre)[0], "dp", 1)
    late_blocks = call(
        lambda *refs: weight_kernel([(0, 2), (4, 5)], [(1, 3), (4, 5)], *refs),
        "late_weights",
        place_meta,
        (hidden_two, d_mlp, d_pre, gelu_out, left_other, right_other),
        (((width // chips, units), BF16),) * chips,
        [pltpu.VMEM((width, units), BF16)],
        0,
        12,
    )
    d_two_parts, late_blocks = lax.optimization_barrier((d_two_parts, late_blocks))
    late_grads = sum_chips(late_blocks)

    d_attn_blocks, d_mid, mid_sums = call(
        lambda *refs: middle_back_kernel(latents, *refs),
        "middle_back",
        meta,
        (d_two_parts, residual_mid, attn_out, cotangent, mod_rows),
        (((n_tensor, share, width), BF16), ((share, width), F32), ((3 * latents, width), F32)),
    )
    d_attn = exchange(d_attn_blocks, "tensor").reshape(rows, width)

    d_spread, d_bias_proj = call(
        spread_kernel,
        "spread",
        meta,
        (d_attn, full_vp),
        (((2 * heads, DH, rows // 2), BF16), ((1, width), F32)),
    )
    mlp_parts = parts_beside(after(mlp_part, d_spread), "tensor")
    d_attn_other = swap(after(d_attn, d_spread), "dp", 1)
    attended_other = swap(after(attended, d_spread), "dp", 1)
    d_packed = attention.backward(d_spread, mlp_parts)
    mlp_parts = after(mlp_parts, d_packed)
    result_own, last_sums = call(
        lambda *refs: result_kernel(latents, n_tensor, *refs),
        "result",
        meta,
        (*mlp_parts, residual_mid, cotangent, mod_rows, b_fc2.reshape(1, -1)),
        (((share, width), BF16), ((latents, width), F32)),
    )
    d_one_part, d_qk, d_vp = call(
        unspread_kernel,
        "unspread",
        meta,
        (d_packed, full_qk, full_vp),
        (((rows, width), BF16), ((rows, 2 * features), BF16), ((rows, 2 * features), BF16)),
    )
    d_one_parts = exchange_shares(d_one_part, "tensor")
    result = gather_beside(after(result_own, d_one_part), "tensor")

    late_grads = late_grads[:-1] + [after(late_grads[-1], d_one_part)]
    right_other = swap(choose(core, after(d_vp, d_one_part), d_qk)[0], "dp", 1)
    early_blocks = call(
        lambda *refs: weight_kernel(
            [(0, 2), (5, 7)], [(0, 3), (1, 4), (5, 7), (6, 8)], *refs
        ),
        "early_weights",
        place_meta,
        (hidden_one, d_attn, d_qk, d_vp, attended, hidden_other, d_attn_other, right_other, attended_other),
        (((width // chips, 2 * features), BF16),) * chips,
        [pltpu.VMEM((width, 2 * features), BF16)],
        0,
        12,
    )
    d_one_parts, early_blocks = lax.optimization_barrier((d_one_parts, early_blocks))
    early_grads = sum_chips(early_blocks)

    grad_own, d_mod_part = call(
        lambda *refs: first_back_kernel(latents, *refs),
        "first_back",
        meta,
        (d_one_parts, tokens, d_mid, mod_rows, mid_sums, last_sums),
        (((share, width), BF16), ((n_tensor, 6 * latents, features), F32)),
        [pltpu.VMEM((2 * latents, width), F32)],
    )
    bias_part = jnp.concatenate(
        [
            jnp.sum(d_mlp.astype(F32), axis=0),
            d_bias_proj[0],
            d_bias_fc1[0],
            jnp.sum(d_qk[:, :features].astype(F32), axis=0),
            jnp.sum(d_vp[:, :features].astype(F32), axis=0),
        ]
    )
    bias_rows = bias_part.reshape(-1, features)
    d_mod_mine = jnp.sum(exchange(d_mod_part, "tensor"), axis=0)
    grad_tokens = gather_beside(after(grad_own, d_mod_mine), "tensor").astype(F32)
    sums = jnp.sum(gather(jnp.concatenate([d_mod_mine, bias_rows]), "dp", n_dp), axis=0)
    d_mod = sums[: 6 * latents].reshape(latents, 6 * features)
    bias_total = sums[6 * latents :].reshape(-1)
    grad_b_ada = jnp.sum(d_mod, axis=0).reshape(6, features)
    grad_w_ada = lax.dot_general(
        own_activated.astype(F32), d_mod, by_token, precision=lax.Precision.HIGHEST
    ).reshape(share_width, 6, features)
    high = d_mod.astype(BF16)
    low = (d_mod - high.astype(F32)).astype(BF16)
    d_active = lax.dot_general(
        jnp.concatenate([high, low]), flat_ada, by_last, preferred_element_type=F32
    )
    d_active = d_active[:latents] + d_active[latents:]
    d_active = gather(d_active, ("dp", "tensor"), n_dp * n_tensor)
    d_active = jnp.sum(d_active.reshape(n_dp, n_tensor, latents, share_width), axis=1)
    d_active = d_active.transpose(1, 0, 2).reshape(latents, width)
    grad_cond = d_active * (gate * (1.0 + cond * (1.0 - gate)))

    grad_fc1, grad_fc2 = finish_pair(late_grads)
    grad_qk, grad_vp = finish_pair(after(early_grads, d_active))
    grad_qkv = jnp.concatenate([grad_qk, grad_vp[:, :features]], axis=1)
    grad_qkv = grad_qkv.reshape(share_width, 3, features)

    return (
        result,
        grad_tokens,
        grad_cond,
        grad_w_ada,
        grad_b_ada,
        grad_qkv,
        bias_total[2 * width + units :].reshape(2, features),
        grad_vp[:, features:].T,
        bias_total[width : 2 * width],
        grad_fc1,
        bias_total[2 * width : 2 * width + units],
        grad_fc2.T,
        bias_total[:width],
    )


def solution(mesh):
    in_specs = (
        P("dp", None),
        P(),
        P(),
        P("dp", None, "tensor"),
        P(None, "tensor"),
        P("dp", None, "tensor"),
        P(None, "tensor"),
        P("tensor", "dp"),
        P(),
        P("dp", "tensor"),
        P("tensor"),
        P("tensor", "dp"),
        P(),
        P("dp", None),
    )
    out_specs = (
        P("dp", None),
        P("dp", None),
        P(),
        P("dp", None, "tensor"),
        P(None, "tensor"),
        P("dp", None, "tensor"),
        P(None, "tensor"),
        P("tensor", "dp"),
        P(),
        P("dp", "tensor"),
        P("tensor"),
        P("tensor", "dp"),
        P(),
    )
    return jax.shard_map(local, mesh=mesh, in_specs=in_specs, out_specs=out_specs, check_vma=False)
```

```python
import math

import jax
import jax.numpy as jnp
from jax import lax
from jax.experimental import pallas as pl
from jax.experimental.pallas import tpu as pltpu
from jax.sharding import PartitionSpec as P

DH = 72
SEQ = 1024
NORM_EPS = 1e-06
NEGATIVE = -1e30
SCALE = 1.0 / math.sqrt(DH)
VMEM_BYTES = 58 * 1024 * 1024
BF16 = jnp.bfloat16
F32 = jnp.float32


def swap(block, axis, bits):
    route = [(i, i ^ bits) for i in range(lax.axis_size(axis))]
    return lax.ppermute(block, axis, route)


def exchange(blocks, axis):
    return lax.all_to_all(blocks, axis, 0, 0, tiled=True)


def gather(block, axis, count):
    return exchange(jnp.broadcast_to(block[None], (count,) + block.shape), axis)


def gate(value, *others):
    return pl.pallas_call(
        lambda *refs: None,
        out_shape=jax.ShapeDtypeStruct(value.shape, value.dtype),
        in_specs=[pl.BlockSpec(memory_space=pl.ANY)] * (1 + len(others)),
        out_specs=pl.BlockSpec(memory_space=pl.ANY),
        input_output_aliases={0: 0},
        cost_estimate=pl.CostEstimate(flops=1, bytes_accessed=1, transcendentals=0),
        name="gate",
    )(value, *others)


def choose(core, first, second):
    return jnp.where(core == 0, first, second), jnp.where(core == 0, second, first)


def pair_rows(first, second):
    core = lax.axis_index("dp") % 2
    keep, send = choose(core, first, second)
    return jnp.concatenate(choose(core, keep, swap(send, "dp", 1)))


def chip_parts(rows):
    count = lax.axis_size("dp") // 2
    return [rows] + [swap(rows, "dp", 2 * step) for step in range(1, count)]


def gather_chips(rows):
    count = lax.axis_size("dp")
    groups = [list(range(core, count, 2)) for core in range(2)]
    return lax.all_gather(rows, "dp", axis=0, tiled=True, axis_index_groups=groups)


def sum_chips(blocks):
    if len(blocks) == 1:
        count, chip = lax.axis_size("dp") // 2, lax.axis_index("dp") // 2
        rows = blocks[0].reshape((count, -1) + blocks[0].shape[1:])
        blocks = [
            lax.dynamic_index_in_dim(rows, chip ^ step, 0, keepdims=False) for step in range(count)
        ]
    return [swap(block, "dp", 2 * step) if step else block for step, block in enumerate(blocks)]


def finish_pair(parts):
    core = lax.axis_index("dp") % 2
    rows = sum(part.astype(F32) for part in parts)
    half = rows.shape[0] // 2
    keep, send = choose(core, rows[:half], rows[half:])
    return choose(core, keep, swap(send, "dp", 1))


def gather_beside(share, axis):
    count, me = lax.axis_size(axis), lax.axis_index(axis)
    parts = jnp.stack([share] + [swap(share, axis, bits) for bits in range(1, count)])
    ordered = [lax.dynamic_index_in_dim(parts, me ^ place, 0, keepdims=False) for place in range(count)]
    return jnp.concatenate(ordered)


def exchange_shares(partial, axis):
    count = lax.axis_size(axis)
    blocks = partial.reshape((count, partial.shape[0] // count) + partial.shape[1:])
    return exchange(blocks, axis)


def tile_range(meta_ref, latents, tile, core):
    lane = lax.broadcasted_iota(jnp.int32, (1, 256), 1)
    first = tile * 512 + core * 128
    last = first + 383
    place = first + lane + jnp.where(lane >= 128, 128, 0)
    begin = jnp.zeros((1, 256), jnp.int32)
    finish = jnp.zeros((1, 256), jnp.int32)
    low = jnp.int32(0)
    high = jnp.int32(0)
    start = jnp.int32(0)
    for number in range(latents):
        end = start + meta_ref[1 + number]
        inside = (place >= start) & (place < end)
        begin = jnp.where(inside, start, begin)
        finish = jnp.where(inside, end, finish)
        low = jnp.where((first >= start) & (first < end), start, low)
        high = jnp.where((last >= start) & (last < end), end, high)
        start = end
    return begin, finish, low // 256, (high + 255) // 256


def pair(ref, tile, start):
    left = ref[2 * tile, :, start : start + 128]
    right = ref[2 * tile + 1, :, start : start + 128]
    return jnp.concatenate([left, right], axis=1)


def key_mask(block, begin, finish):
    place = block * 256 + lax.broadcasted_iota(jnp.int32, (256, 256), 0)
    return (place >= begin) & (place < finish)


def forward_kernel(latents, meta_ref, packed_ref, out_ref, exact_ref, log_ref, keys, scores):
    blocks = packed_ref.shape[0]
    core = meta_ref[0]
    for block in range(blocks):
        keys[block] = packed_ref[block, :, :256].astype(F32).T.astype(BF16)
    for tile in range(blocks // 2):
        begin, finish, low, high = tile_range(meta_ref, latents, tile, core)
        query = pair(packed_ref, tile, 512)

        def score(block, largest):
            raw = jnp.dot(keys[block], query, preferred_element_type=F32) * SCALE
            raw = jnp.where(key_mask(block, begin, finish), raw, NEGATIVE)
            scores[block] = raw
            return jnp.maximum(largest, jnp.max(raw, axis=0, keepdims=True))

        largest = lax.fori_loop(low, high, score, jnp.full((1, 256), NEGATIVE, F32))

        def mix(block, carry):
            total, mixed = carry
            weights = jnp.exp(scores[block] - largest)
            total = total + jnp.sum(weights, axis=0, keepdims=True)
            values = packed_ref[block, :, 256:512]
            mixed = mixed + jnp.dot(values, weights.astype(BF16), preferred_element_type=F32)
            return total, mixed

        total, mixed = lax.fori_loop(
            low, high, mix, (jnp.zeros((1, 256), F32), jnp.zeros((DH, 256), F32))
        )
        mixed = mixed / total
        log_total = largest + jnp.log(total)
        for half in range(2):
            part = mixed[:, half * 128 : half * 128 + 128]
            exact_ref[2 * tile + half] = part
            out_ref[2 * tile + half] = part.astype(BF16)
            log_ref[2 * tile + half] = log_total[:, half * 128 : half * 128 + 128]


def backward_kernel(
    latents, meta_ref, packed_ref, grad_ref, exact_ref, log_ref, out_ref, keys, values, d_keys, d_values
):
    blocks = packed_ref.shape[0]
    core = meta_ref[0]
    for block in range(blocks):
        keys[block] = packed_ref[block, :, :256].astype(F32).T.astype(BF16)
        values[block] = packed_ref[block, :, 256:512].astype(F32).T.astype(BF16)
    d_keys[...] = jnp.zeros_like(d_keys)
    d_values[...] = jnp.zeros_like(d_values)
    by_query = (((1,), (1,)), ((), ()))
    for tile in range(blocks // 2):
        begin, finish, low, high = tile_range(meta_ref, latents, tile, core)
        query = pair(packed_ref, tile, 512)
        grad = pair(grad_ref, tile, 0)
        inner = jnp.sum(grad.astype(F32) * pair(exact_ref, tile, 0), axis=0, keepdims=True)
        log_total = pair(log_ref, tile, 0)

        def step(block, d_query):
            raw = jnp.dot(keys[block], query, preferred_element_type=F32) * SCALE
            probs = jnp.where(key_mask(block, begin, finish), jnp.exp(raw - log_total), 0.0)
            d_probs = jnp.dot(values[block], grad, preferred_element_type=F32)
            d_scores = (probs * (d_probs - inner)).astype(BF16)
            d_values[block] += lax.dot_general(
                grad, probs.astype(BF16), by_query, preferred_element_type=F32
            )
            d_keys[block] += lax.dot_general(query, d_scores, by_query, preferred_element_type=F32)
            key_rows = packed_ref[block, :, :256]
            return d_query + jnp.dot(key_rows, d_scores, preferred_element_type=F32)

        d_query = lax.fori_loop(low, high, step, jnp.zeros((DH, 256), F32)) * SCALE
        for half in range(2):
            part = d_query[:, half * 128 : half * 128 + 128]
            out_ref[2 * tile + half, :, 512:640] = part.astype(BF16)
    for block in range(blocks):
        out_ref[block, :, :256] = (d_keys[block] * SCALE).astype(BF16)
        out_ref[block, :, 256:512] = d_values[block].astype(BF16)


def attend_forward(meta, packed):
    blocks = packed.shape[0]
    shape = jax.ShapeDtypeStruct
    return pl.pallas_call(
        lambda *refs: forward_kernel(meta.shape[0] - 1, *refs),
        out_shape=(
            shape((blocks, DH, 128), BF16),
            shape((blocks, DH, 128), F32),
            shape((blocks, 1, 128), F32),
        ),
        in_specs=[
            pl.BlockSpec(memory_space=pltpu.SMEM),
            pl.BlockSpec(memory_space=pltpu.VMEM),
        ],
        out_specs=tuple([pl.BlockSpec(memory_space=pltpu.VMEM)] * 3),
        scratch_shapes=[
            pltpu.VMEM((blocks, 256, DH), BF16),
            pltpu.VMEM((blocks, 256, 256), F32),
        ],
        compiler_params=pltpu.CompilerParams(vmem_limit_bytes=VMEM_BYTES),
        cost_estimate=pl.CostEstimate(flops=10**9, bytes_accessed=4 * 10**6, transcendentals=10**6),
        name="attend_forward",
    )(meta, packed)


def attend_backward(meta, packed, grad, exact, log_total):
    blocks = packed.shape[0]
    return pl.pallas_call(
        lambda *refs: backward_kernel(meta.shape[0] - 1, *refs),
        out_shape=jax.ShapeDtypeStruct(packed.shape, BF16),
        in_specs=[pl.BlockSpec(memory_space=pltpu.SMEM)]
        + [pl.BlockSpec(memory_space=pltpu.VMEM)] * 4,
        out_specs=pl.BlockSpec(memory_space=pltpu.VMEM),
        scratch_shapes=[
            pltpu.VMEM((blocks, 256, DH), BF16),
            pltpu.VMEM((blocks, 256, DH), BF16),
            pltpu.VMEM((blocks, DH, 256), F32),
            pltpu.VMEM((blocks, DH, 256), F32),
        ],
        compiler_params=pltpu.CompilerParams(vmem_limit_bytes=VMEM_BYTES),
        cost_estimate=pl.CostEstimate(flops=3 * 10**9, bytes_accessed=4 * 10**6, transcendentals=10**6),
        name="attend_backward",
    )(meta, packed, grad, exact, log_total)


class HeadSplit:
    def __init__(self, latent_len, rows):
        self.rows = rows
        self.meta = jnp.concatenate([lax.axis_index("dp").astype(jnp.int32)[None] % 2, latent_len])

    def forward(self, packed):
        self.packed = exchange(packed, "dp")
        out, self.exact, self.log_total = attend_forward(self.meta, self.packed)
        return exchange(out, "dp")

    def backward(self, grad, due):
        grad = exchange(grad, "dp")
        out = attend_backward(self.meta, self.packed, grad, self.exact, self.log_total)
        return exchange(gate(out, *due), "dp")


class Window:
    def __init__(self, latent_len, rows):
        self.rows = rows
        self.reach = (SEQ - 2) // rows + 1
        total = rows * lax.axis_size("dp")
        first = lax.axis_index("dp") * rows
        own = latent_index(latent_len, first, rows, total)
        ids = [
            latent_index(latent_len, first + offset * rows, rows, total)
            for offset in range(-self.reach, self.reach + 1)
        ]
        self.allowed = own[:, None] == jnp.concatenate(ids)[None, :]

    def from_behind(self, block, distance):
        devices = range(lax.axis_size("dp"))
        return lax.ppermute(
            block, "dp", [(i - distance, i) for i in devices if i - distance in devices]
        )

    def head_scores(self, query, key):
        raw = jnp.einsum("eq,ek->qk", query, key, preferred_element_type=F32) * SCALE
        return jnp.where(self.allowed, raw, NEGATIVE)

    def forward(self, packed):
        rows = self.rows
        split = packed.reshape(-1, 2, DH, rows * 5 // 2)
        query = jnp.concatenate([split[:, 0, :, 2 * rows :], split[:, 1, :, 2 * rows :]], axis=2)
        projected = jnp.stack([query, split[:, 0, :, :rows], split[:, 0, :, rows : 2 * rows]])
        key_value = projected[1:]
        pieces = [
            key_value if offset == 0 else self.from_behind(key_value, -offset)
            for offset in range(-self.reach, self.reach + 1)
        ]
        window = jnp.concatenate(pieces, axis=3)
        self.operands = (projected[0], window[0], window[1])

        def one(operands):
            query, key, value = operands
            scores = self.head_scores(query, key)
            largest = jnp.max(scores, axis=1, keepdims=True)
            weights = jnp.exp(scores - largest)
            totals = jnp.sum(weights, axis=1, keepdims=True)
            probs = (weights / totals).astype(BF16)
            mixed = jnp.einsum("qk,ek->eq", probs, value, preferred_element_type=F32)
            return mixed.astype(BF16), (largest + jnp.log(totals))[:, 0]

        out, self.log_total = lax.map(one, self.operands)
        out = out.reshape(-1, DH, 2, rows // 2).transpose(0, 2, 1, 3)
        return out.reshape(-1, DH, rows // 2)

    def backward(self, grad, due):
        rows, reach = self.rows, self.reach
        halves = grad.reshape(-1, 2, DH, rows // 2)
        grads = jnp.concatenate([halves[:, 0], halves[:, 1]], axis=2)

        def one(operands):
            query, key, value, grad, log_total = operands
            probs = jnp.exp(self.head_scores(query, key) - log_total[:, None])
            d_value = jnp.einsum("qk,eq->ek", probs.astype(BF16), grad, preferred_element_type=F32)
            d_probs = jnp.einsum("eq,ek->qk", grad, value, preferred_element_type=F32)
            inner = jnp.sum(probs * d_probs, axis=1, keepdims=True)
            d_scores = (probs * (d_probs - inner)).astype(BF16)
            d_query = jnp.einsum("qk,ek->eq", d_scores, key, preferred_element_type=F32) * SCALE
            d_key = jnp.einsum("qk,eq->ek", d_scores, query, preferred_element_type=F32) * SCALE
            return d_query, d_key, d_value

        d_query, d_key, d_value = lax.map(one, self.operands + (grads, self.log_total))
        d_window = jnp.stack([d_key, d_value])
        d_key_value = d_window[..., reach * rows : (reach + 1) * rows]
        for offset in range(-reach, reach + 1):
            if offset != 0:
                block = d_window[..., (offset + reach) * rows : (offset + reach + 1) * rows]
                d_key_value = d_key_value + self.from_behind(block, offset)
        wide = jnp.concatenate([d_key_value[0], d_key_value[1]], axis=2)
        wide = jnp.stack([wide, jnp.zeros_like(wide)], axis=1)
        halves = d_query.reshape(-1, DH, 2, rows // 2).transpose(0, 2, 1, 3)
        packed = jnp.concatenate([wide, halves], axis=3).astype(BF16)
        return packed.reshape(-1, DH, rows * 5 // 2)


META = 4


def vmem(count):
    return [pl.BlockSpec(memory_space=pltpu.VMEM)] * count


def call(body, name, meta, arrays, outs, scratch=(), anywhere=0, due=()):
    count = 1 + len(arrays)

    def kernel(*refs):
        body(*refs[:count], *refs[count + len(due) :])

    return pl.pallas_call(
        kernel,
        out_shape=tuple(jax.ShapeDtypeStruct(shape, kind) for shape, kind in outs),
        in_specs=[pl.BlockSpec(memory_space=pltpu.SMEM)]
        + [pl.BlockSpec(memory_space=pl.ANY)] * anywhere
        + vmem(len(arrays) - anywhere)
        + [pl.BlockSpec(memory_space=pl.ANY)] * len(due),
        out_specs=tuple(vmem(len(outs))),
        scratch_shapes=list(scratch),
        compiler_params=pltpu.CompilerParams(vmem_limit_bytes=VMEM_BYTES),
        cost_estimate=pl.CostEstimate(flops=1, bytes_accessed=1, transcendentals=0),
        name=name,
    )(meta, *arrays, *due)


def row_masks(meta_ref, latents, first, rows):
    place = first + lax.broadcasted_iota(jnp.int32, (rows, 1), 0)
    ids = jnp.zeros((rows, 1), jnp.int32)
    end = jnp.int32(0)
    for number in range(latents - 1):
        end = end + meta_ref[META + number]
        ids = ids + (place >= end).astype(jnp.int32)
    return [(ids == number).astype(F32) for number in range(latents)]


def rows_of(mod_ref, masks, feature):
    out = masks[0] * mod_ref[feature : feature + 1, :]
    for number in range(1, len(masks)):
        row = number * 6 + feature
        out = out + masks[number] * mod_ref[row : row + 1, :]
    return out


def latent_sums(out_ref, masks, values, feature, features):
    rounded = values.astype(BF16).astype(F32)
    for number, mask in enumerate(masks):
        row = number * features + feature
        out_ref[row : row + 1, :] = jnp.sum(mask * rounded, axis=0, keepdims=True)


def own_rows(meta_ref, ref, share):
    start = pl.multiple_of(meta_ref[2] * share, share)
    return ref[pl.ds(start, share), :].astype(F32)


def on_core(meta_ref, body, mine, other):
    @pl.when(meta_ref[0] == 0)
    def _():
        body(mine, other)

    @pl.when(meta_ref[0] != 0)
    def _():
        body(other, mine)


def place_rows(meta_ref, parts, whole, sems):
    block = parts[0].shape[0]
    copies = []
    for step, part in enumerate(parts):
        start = pl.multiple_of((meta_ref[3] ^ step) * block, 16)
        copies.append(
            pltpu.make_async_copy(part, whole.at[pl.ds(start, block), :], sems.at[step])
        )
    return copies


def place_pair(meta_ref, mine, other, first_ref, second_ref, sems):
    def body(first, second):
        copies = place_rows(meta_ref, first, first_ref, sems.at[0])
        copies += place_rows(meta_ref, second, second_ref, sems.at[1])
        for copy in copies:
            copy.start()
        for copy in copies:
            copy.wait()

    on_core(meta_ref, body, mine, other)


def project_kernel(latents, count, meta_ref, *refs):
    mine, other = refs[:count], refs[count : 2 * count]
    tokens_ref, cot_ref, mod_ref, bias_ref = refs[2 * count : 2 * count + 4]
    hidden_ref, d_mlp_ref, packed_ref, qk_ref, vp_ref, sems = refs[2 * count + 4 :]
    rows, width = tokens_ref.shape
    place_pair(meta_ref, mine, other, qk_ref, vp_ref, sems)
    masks = row_masks(meta_ref, latents, meta_ref[1], rows)
    unit, _ = normed(tokens_ref[...].astype(F32))
    hidden = unit * (1.0 + rows_of(mod_ref, masks, 1)) + rows_of(mod_ref, masks, 0)
    hidden_ref[...] = hidden.astype(BF16)
    d_mlp_ref[...] = (cot_ref[...].astype(F32) * rows_of(mod_ref, masks, 5)).astype(BF16)
    heads = packed_ref.shape[0] // 2
    features = heads * DH
    left = hidden_ref[...]
    both = jnp.dot(left, qk_ref[...], preferred_element_type=F32) + bias_ref[0:1, :]
    both = both.T
    value = jnp.dot(left, vp_ref[...], preferred_element_type=F32) + bias_ref[1:2, :]
    value = value.T
    for head in range(heads):
        start = head * DH
        query = both[start : start + DH].astype(BF16)
        key = both[features + start : features + start + DH].astype(BF16)
        val = value[start : start + DH].astype(BF16)
        for half in range(2):
            packed_ref[2 * head + half, :, :rows] = key
            packed_ref[2 * head + half, :, rows : 2 * rows] = val
            packed_ref[2 * head + half, :, 2 * rows :] = query[
                :, half * (rows // 2) : (half + 1) * (rows // 2)
            ]


def attend_out_kernel(meta_ref, parts_ref, vp_ref, part_ref, attended_ref):
    heads = parts_ref.shape[0] // 2
    rows = part_ref.shape[0]
    stacked = [jnp.zeros((heads * DH, rows), F32)]
    for head in range(heads):
        left = parts_ref[2 * head].astype(F32)
        right = parts_ref[2 * head + 1].astype(F32)
        stacked.append(jnp.concatenate([left, right], axis=1))
    attended_ref[...] = jnp.concatenate(stacked, axis=0).T.astype(BF16)
    part_ref[...] = lax.dot_general(
        attended_ref[...], vp_ref[...], (((1,), (1,)), ((), ())), preferred_element_type=F32
    ).astype(BF16)


def middle_kernel(
    latents, meta_ref, parts_ref, tokens_ref, mod_ref, bias_ref, sent_ref, attn_ref, mid_ref
):
    copies, share, width = parts_ref.shape
    masks = row_masks(meta_ref, latents, meta_ref[1] + meta_ref[2] * share, share)
    attn = bias_ref[...].astype(F32)
    for part in range(copies):
        attn = attn + parts_ref[part].astype(F32)
    attn_ref[...] = attn
    mid = own_rows(meta_ref, tokens_ref, share) + rows_of(mod_ref, masks, 2) * attn
    mid_ref[...] = mid
    unit, _ = normed(mid)
    hidden = unit * (1.0 + rows_of(mod_ref, masks, 4)) + rows_of(mod_ref, masks, 3)
    for part in range(copies):
        sent_ref[part] = hidden.astype(BF16)


def mlp_kernel(count, meta_ref, *refs):
    mine, other = refs[:count], refs[count : 2 * count]
    hidden_ref, d_mlp_ref, bias_ref = refs[2 * count : 2 * count + 3]
    d_two_ref, gelu_ref, d_pre_ref, d_bias_ref = refs[2 * count + 3 : 2 * count + 7]
    mlp_refs = refs[2 * count + 7 : -5]
    fc1_ref, fc2_ref, d_two_sum, mlp_sum, sems = refs[-5:]
    place_pair(meta_ref, mine, other, fc1_ref, fc2_ref, sems)
    d_two_sum[...] = jnp.zeros_like(d_two_sum)
    mlp_sum[...] = jnp.zeros_like(mlp_sum)
    tile = 384
    by_last = (((1,), (1,)), ((), ()))

    def step(number, carry):
        units = pl.ds(pl.multiple_of(number * tile, tile), tile)
        fc1, fc2 = fc1_ref[:, units], fc2_ref[:, units]
        pre = jnp.dot(hidden_ref[...], fc1, preferred_element_type=F32)
        gelu, slope = gelu_pair(pre + bias_ref[:, units].astype(F32))
        grad = jnp.dot(d_mlp_ref[...], fc2, preferred_element_type=F32)
        d_pre = (grad * slope).astype(BF16)
        gelu = gelu.astype(BF16)
        gelu_ref[:, units] = gelu
        d_pre_ref[:, units] = d_pre
        d_bias_ref[:, units] = jnp.sum(d_pre.astype(F32), axis=0, keepdims=True)
        d_two_sum[...] += lax.dot_general(d_pre, fc1, by_last, preferred_element_type=F32)
        mlp_sum[...] += lax.dot_general(gelu, fc2, by_last, preferred_element_type=F32)
        return carry

    lax.fori_loop(0, fc1_ref.shape[1] // tile, step, 0)
    d_two_ref[...] = d_two_sum[...].astype(BF16)
    share = mlp_refs[0].shape[0]
    for step, mlp_ref in enumerate(mlp_refs):
        start = pl.multiple_of((meta_ref[2] ^ step) * share, share)
        mlp_ref[...] = mlp_sum[pl.ds(start, share), :].astype(BF16)


def middle_back_kernel(
    latents, meta_ref, parts_ref, mid_in_ref, attn_ref, cot_ref, mod_ref, sent_ref, d_mid_ref, sums_ref
):
    copies, share, width = parts_ref.shape
    masks = row_masks(meta_ref, latents, meta_ref[1] + meta_ref[2] * share, share)
    d_hidden = parts_ref[0].astype(F32)
    for part in range(1, copies):
        d_hidden = d_hidden + parts_ref[part].astype(F32)
    unit, inverse = normed(mid_in_ref[...])
    d_mid = own_rows(meta_ref, cot_ref, share) + norm_back(
        unit, inverse, d_hidden * (1.0 + rows_of(mod_ref, masks, 4))
    )
    d_mid_ref[...] = d_mid
    d_attn = (d_mid * rows_of(mod_ref, masks, 2)).astype(BF16)
    for part in range(copies):
        sent_ref[part] = d_attn
    latent_sums(sums_ref, masks, d_mid * attn_ref[...], 0, 3)
    latent_sums(sums_ref, masks, d_hidden, 1, 3)
    latent_sums(sums_ref, masks, d_hidden * unit, 2, 3)


def result_kernel(
    latents, count, meta_ref, *refs
):
    parts = refs[:count]
    mid_ref, cot_ref, mod_ref, bias_ref, result_ref, sums_ref = refs[count:]
    share = result_ref.shape[0]
    masks = row_masks(meta_ref, latents, meta_ref[1] + meta_ref[2] * share, share)
    mlp = bias_ref[...].astype(F32)
    for part in parts:
        mlp = mlp + part[...].astype(F32)
    result_ref[...] = (mid_ref[...] + rows_of(mod_ref, masks, 5) * mlp).astype(BF16)
    latent_sums(sums_ref, masks, own_rows(meta_ref, cot_ref, share) * mlp, 0, 1)


def spread_kernel(meta_ref, d_attn_ref, vp_ref, packed_ref, d_bias_ref):
    grad = jnp.dot(d_attn_ref[...], vp_ref[...], preferred_element_type=F32).T
    half = grad.shape[1] // 2
    features = grad.shape[0] // 2
    for place in range(packed_ref.shape[0]):
        start = features + place // 2 * DH
        side = place % 2 * half
        packed_ref[place] = grad[start : start + DH, side : side + half].astype(BF16)
    d_bias_ref[...] = jnp.sum(d_attn_ref[...].astype(F32), axis=0, keepdims=True)


def unspread_kernel(meta_ref, parts_ref, qk_ref, vp_ref, d_one_ref, d_qk_ref, d_vp_ref):
    heads = parts_ref.shape[0] // 2
    rows = d_one_ref.shape[0]
    query, key, value = [], [], []
    for head in range(heads):
        left = parts_ref[2 * head].astype(F32)
        right = parts_ref[2 * head + 1].astype(F32)
        both = left[:, : 2 * rows] + right[:, : 2 * rows]
        key.append(both[:, :rows])
        value.append(both[:, rows:])
        query.append(jnp.concatenate([left[:, 2 * rows :], right[:, 2 * rows :]], axis=1))
    d_qk_ref[...] = jnp.concatenate(query + key, axis=0).T.astype(BF16)
    blank = jnp.zeros((heads * DH, rows), F32)
    d_vp_ref[...] = jnp.concatenate(value + [blank], axis=0).T.astype(BF16)
    tile = 384
    by_last = (((1,), (1,)), ((), ()))

    def step(number, carry):
        columns = pl.ds(pl.multiple_of(number * tile, tile), tile)
        total = lax.dot_general(d_qk_ref[...], qk_ref[columns, :], by_last, preferred_element_type=F32)
        total += lax.dot_general(d_vp_ref[...], vp_ref[columns, :], by_last, preferred_element_type=F32)
        d_one_ref[:, columns] = total.astype(BF16)
        return carry

    lax.fori_loop(0, qk_ref.shape[0] // tile, step, 0)


def weight_kernel(first_pairs, second_pairs, meta_ref, *refs):
    operands = 1 + max(max(pair) for pair in first_pairs + second_pairs)
    ins, outs, total = refs[:operands], refs[operands:-1], refs[-1]
    tile = 384

    def body(pairs):
        def step(number, carry):
            columns = pl.ds(pl.multiple_of(number * tile, tile), tile)
            block = jnp.zeros((tile, total.shape[1]), F32)
            for left, right in pairs:
                block += lax.dot_general(
                    ins[left][:, columns], ins[right][...], (((0,), (0,)), ((), ())),
                    preferred_element_type=F32,
                )
            total[columns, :] = block.astype(BF16)
            return carry

        lax.fori_loop(0, total.shape[0] // tile, step, 0)

    on_core(meta_ref, lambda pairs, _: body(pairs), first_pairs, second_pairs)
    rows = outs[0].shape[0]
    for step, out in enumerate(outs):
        start = pl.multiple_of((meta_ref[3] ^ step) * rows, 16)
        out[...] = total[pl.ds(start, rows), :]


def first_back_kernel(
    latents, meta_ref, parts_ref, tokens_ref, d_mid_ref, mod_ref, mid_sums_ref, last_sums_ref,
    grad_ref, sent_ref, first_sums,
):
    copies, share, width = parts_ref.shape
    masks = row_masks(meta_ref, latents, meta_ref[1] + meta_ref[2] * share, share)
    d_hidden = parts_ref[0].astype(F32)
    for part in range(1, copies):
        d_hidden = d_hidden + parts_ref[part].astype(F32)
    unit, inverse = normed(own_rows(meta_ref, tokens_ref, share))
    grad = d_mid_ref[...] + norm_back(unit, inverse, d_hidden * (1.0 + rows_of(mod_ref, masks, 1)))
    grad_ref[...] = grad.astype(BF16)
    latent_sums(first_sums, masks, d_hidden, 0, 2)
    latent_sums(first_sums, masks, d_hidden * unit, 1, 2)
    columns = width // copies
    for number in range(latents):
        for feature in range(6):
            if feature < 2:
                row = first_sums[number * 2 + feature : number * 2 + feature + 1, :]
            elif feature < 5:
                place = number * 3 + feature - 2
                row = mid_sums_ref[place : place + 1, :]
            else:
                row = last_sums_ref[number : number + 1, :]
            place = number * 6 + feature
            for part in range(copies):
                sent_ref[part, place : place + 1, :] = row[:, part * columns : (part + 1) * columns]


def latent_index(latent_len, first_row, row_count, token_total):
    positions = first_row + jnp.arange(row_count, dtype=jnp.int32)
    ends = jnp.cumsum(latent_len, dtype=jnp.int32)
    found = jnp.sum((positions[:, None] >= ends[None, :]).astype(jnp.int32), axis=1, dtype=jnp.int32)
    return jnp.where((positions >= 0) & (positions < token_total), found, -1)


def normed(values):
    average = jnp.mean(values, axis=-1, keepdims=True)
    centred = values - average
    spread = jnp.mean(centred * centred, axis=-1, keepdims=True)
    inverse = lax.rsqrt(spread + NORM_EPS)
    return centred * inverse, inverse


def norm_back(unit, inverse, grad):
    along = jnp.mean(grad * unit, axis=-1, keepdims=True)
    return inverse * (grad - jnp.mean(grad, axis=-1, keepdims=True) - unit * along)


def gelu_pair(value):
    root = math.sqrt(2.0 / math.pi)
    bend = jnp.tanh(root * (value + 0.044715 * value * value * value))
    slope = root * (1.0 + 3.0 * 0.044715 * value * value)
    gelu = 0.5 * value * (1.0 + bend)
    return gelu, 0.5 * (1.0 + bend) + 0.5 * value * (1.0 - bend * bend) * slope


def local(
    tokens,
    conditioning,
    latent_len,
    w_ada,
    b_ada,
    w_qkv,
    b_qv,
    w_proj,
    b_proj,
    w_fc1,
    b_fc1,
    w_fc2,
    b_fc2,
    cotangent,
):
    rows, width = tokens.shape
    share_width = w_qkv.shape[0]
    features = w_qkv.shape[2]
    units = w_fc1.shape[1]
    heads = features // DH
    latents = conditioning.shape[0]
    n_dp, n_tensor = lax.axis_size("dp"), lax.axis_size("tensor")
    my_dp, my_tensor = lax.axis_index("dp"), lax.axis_index("tensor")
    share = rows // n_tensor

    core = my_dp % 2
    qk = w_qkv[:, :2].reshape(share_width, 2 * features)
    vp = jnp.concatenate([w_qkv[:, 2], w_proj.T], axis=1)
    early_rows = pair_rows(qk, vp)

    cond = conditioning.astype(F32)
    sigmoid = 1.0 / (1.0 + jnp.exp(-cond))
    activated = (cond * sigmoid).astype(BF16)
    own_activated = lax.dynamic_slice_in_dim(activated, my_dp * share_width, share_width, 1)
    flat_ada = w_ada.reshape(share_width, 6 * features)
    mod_part = jnp.dot(own_activated, flat_ada, preferred_element_type=F32)
    mod_part = mod_part.reshape(latents * 6, features)
    mod_mine = jnp.sum(gather(mod_part, "dp", n_dp), axis=0)
    mod_mine = mod_mine + jnp.tile(b_ada.astype(F32), (latents, 1))
    few_chips = n_dp // 2 == 4
    early_rows = gate(early_rows, mod_mine)
    early_parts = chip_parts(early_rows) if few_chips else [gather_chips(early_rows)]
    modulation = gather(mod_mine, "tensor", n_tensor).transpose(1, 0, 2).reshape(6 * latents, width)

    mod_rows = modulation
    early_parts += [swap(part, "dp", 1) for part in early_parts]
    count = len(early_parts) // 2
    meta = jnp.stack([core, my_dp * rows, my_tensor, my_dp // 2]).astype(jnp.int32)
    meta = jnp.concatenate([meta, latent_len])
    place_meta = meta if few_chips else meta.at[3].set(0)
    by_last = (((1,), (1,)), ((), ()))
    by_token = (((0,), (0,)), ((), ()))
    bias = jnp.concatenate([b_qv[0], jnp.zeros_like(b_qv[0]), b_qv[1], jnp.zeros_like(b_qv[0])])
    hidden_one, d_mlp, packed, full_qk, full_vp = call(
        lambda *refs: project_kernel(latents, count, *refs),
        "project",
        place_meta,
        (*early_parts, tokens, cotangent, mod_rows, bias.astype(F32).reshape(2, -1)),
        (((rows, width), BF16), ((rows, width), BF16), ((2 * heads, DH, rows * 5 // 2), BF16))
        + (((width, 2 * features), BF16),) * 2,
        [pltpu.SemaphoreType.DMA((2, count))],
        2 * count,
    )
    late_rows = pair_rows(w_fc1, w_fc2.T)
    hidden_other = swap(hidden_one, "dp", 1)
    split = HeadSplit if 2 * heads == n_dp else Window
    attention = split(latent_len, rows)
    attended_parts = attention.forward(packed)
    late_rows = gate(late_rows, attended_parts)
    late_parts = chip_parts(late_rows)[:-1] if few_chips else [gather_chips(late_rows)]
    attn_part, attended = call(
        attend_out_kernel,
        "attend_out",
        meta,
        (attended_parts, full_vp),
        (((rows, width), BF16), ((rows, 2 * features), BF16)),
    )
    attn_parts = exchange_shares(attn_part, "tensor")
    hidden_blocks, attn_out, residual_mid = call(
        lambda *refs: middle_kernel(latents, *refs),
        "middle",
        meta,
        (attn_parts, tokens, mod_rows, b_proj.reshape(1, -1)),
        (((n_tensor, share, width), BF16), ((share, width), F32), ((share, width), F32)),
        due=late_parts[1:],
    )
    hidden_two = exchange(hidden_blocks, "tensor").reshape(rows, width)
    if few_chips:
        last_part = swap(gate(late_rows, attn_out), "dp", n_dp - 2)
        late_parts.append(gate(last_part, hidden_two))
    late_other = [swap(part, "dp", 1) for part in late_parts]

    d_two_part, gelu_out, d_pre, d_bias_fc1, *mlp_blocks = call(
        lambda *refs: mlp_kernel(count, *refs),
        "mlp",
        place_meta,
        (*late_parts, *late_other, hidden_two, d_mlp, b_fc1.reshape(1, -1)),
        (((rows, width), BF16), ((rows, units), BF16), ((rows, units), BF16), ((1, units), F32))
        + (((share, width), BF16),) * n_tensor,
        [pltpu.VMEM((width, units), BF16)] * 2
        + [pltpu.VMEM((rows, width), F32)] * 2
        + [pltpu.SemaphoreType.DMA((2, count))],
        2 * count,
    )
    d_two_parts = exchange_shares(d_two_part, "tensor")

    chips = n_dp // 2 if few_chips else 1
    left_other = swap(choose(core, d_mlp, hidden_two)[0], "dp", 1)
    right_other = swap(choose(core, gelu_out, d_pre)[0], "dp", 1)
    late_blocks = call(
        lambda *refs: weight_kernel([(0, 2), (4, 5)], [(1, 3), (4, 5)], *refs),
        "late_weights",
        place_meta,
        (hidden_two, d_mlp, d_pre, gelu_out, left_other, right_other),
        (((width // chips, units), BF16),) * chips,
        [pltpu.VMEM((width, units), BF16)],
    )
    late_grads = sum_chips(late_blocks[:-1]) if few_chips else sum_chips(late_blocks)

    d_attn_blocks, d_mid, mid_sums = call(
        lambda *refs: middle_back_kernel(latents, *refs),
        "middle_back",
        meta,
        (d_two_parts, residual_mid, attn_out, cotangent, mod_rows),
        (((n_tensor, share, width), BF16), ((share, width), F32), ((3 * latents, width), F32)),
        due=late_blocks,
    )
    d_attn = exchange(d_attn_blocks, "tensor").reshape(rows, width)

    d_spread, d_bias_proj = call(
        spread_kernel,
        "spread",
        meta,
        (d_attn, full_vp),
        (((2 * heads, DH, rows // 2), BF16), ((1, width), F32)),
        due=late_grads[1:],
    )
    mlp_parts = mlp_blocks[:1] + [
        swap(gate(block, d_spread), "tensor", step)
        for step, block in enumerate(mlp_blocks)
        if step
    ]
    d_attn_other = swap(d_attn, "dp", 1)
    attended_other = swap(attended, "dp", 1)
    d_packed = attention.backward(d_spread, mlp_parts[1:])
    result_own, last_sums = call(
        lambda *refs: result_kernel(latents, n_tensor, *refs),
        "result",
        meta,
        (*mlp_parts, residual_mid, cotangent, mod_rows, b_fc2.reshape(1, -1)),
        (((share, width), BF16), ((latents, width), F32)),
    )
    d_one_part, d_qk, d_vp = call(
        unspread_kernel,
        "unspread",
        meta,
        (d_packed, full_qk, full_vp),
        (((rows, width), BF16), ((rows, 2 * features), BF16), ((rows, 2 * features), BF16)),
    )
    d_one_parts = exchange_shares(d_one_part, "tensor")
    result = gather_beside(result_own, "tensor")

    if few_chips:
        late_grads.append(swap(gate(late_blocks[-1], d_one_part), "dp", n_dp - 2))
    right_other = swap(choose(core, d_vp, d_qk)[0], "dp", 1)
    early_blocks = call(
        lambda *refs: weight_kernel(
            [(0, 2), (5, 7)], [(0, 3), (1, 4), (5, 7), (6, 8)], *refs
        ),
        "early_weights",
        place_meta,
        (hidden_one, d_attn, d_qk, d_vp, attended, hidden_other, d_attn_other, right_other, attended_other),
        (((width // chips, 2 * features), BF16),) * chips,
        [pltpu.VMEM((width, 2 * features), BF16)],
    )
    early_grads = sum_chips(early_blocks)

    grad_own, d_mod_part = call(
        lambda *refs: first_back_kernel(latents, *refs),
        "first_back",
        meta,
        (d_one_parts, tokens, d_mid, mod_rows, mid_sums, last_sums),
        (((share, width), BF16), ((n_tensor, 6 * latents, features), F32)),
        [pltpu.VMEM((2 * latents, width), F32)],
        due=early_blocks,
    )
    bias_part = jnp.concatenate(
        [
            jnp.sum(d_mlp.astype(F32), axis=0),
            d_bias_proj[0],
            d_bias_fc1[0],
            jnp.sum(d_qk[:, :features].astype(F32), axis=0),
            jnp.sum(d_vp[:, :features].astype(F32), axis=0),
        ]
    )
    bias_rows = bias_part.reshape(-1, features)
    d_mod_mine = jnp.sum(exchange(d_mod_part, "tensor"), axis=0)
    grad_tokens = gather_beside(gate(grad_own, d_mod_mine), "tensor").astype(F32)
    sums = jnp.sum(gather(jnp.concatenate([d_mod_mine, bias_rows]), "dp", n_dp), axis=0)
    d_mod = sums[: 6 * latents].reshape(latents, 6 * features)
    bias_total = sums[6 * latents :].reshape(-1)
    grad_b_ada = jnp.sum(d_mod, axis=0).reshape(6, features)
    grad_w_ada = lax.dot_general(
        own_activated.astype(F32), d_mod, by_token, precision=lax.Precision.HIGHEST
    ).reshape(share_width, 6, features)
    high = d_mod.astype(BF16)
    low = (d_mod - high.astype(F32)).astype(BF16)
    d_active = lax.dot_general(
        jnp.concatenate([high, low]), flat_ada, by_last, preferred_element_type=F32
    )
    d_active = d_active[:latents] + d_active[latents:]
    d_active = gate(d_active, *early_grads[1:]) if few_chips else d_active
    d_active = gather(d_active, ("dp", "tensor"), n_dp * n_tensor)
    d_active = jnp.sum(d_active.reshape(n_dp, n_tensor, latents, share_width), axis=1)
    d_active = d_active.transpose(1, 0, 2).reshape(latents, width)
    grad_cond = d_active * (sigmoid * (1.0 + cond * (1.0 - sigmoid)))

    grad_fc1, grad_fc2 = finish_pair(late_grads)
    grad_qk, grad_vp = finish_pair(early_grads)
    grad_qkv = jnp.concatenate([grad_qk, grad_vp[:, :features]], axis=1)
    grad_qkv = grad_qkv.reshape(share_width, 3, features)

    return (
        result,
        grad_tokens,
        grad_cond,
        grad_w_ada,
        grad_b_ada,
        grad_qkv,
        bias_total[2 * width + units :].reshape(2, features),
        grad_vp[:, features:].T,
        bias_total[width : 2 * width],
        grad_fc1,
        bias_total[2 * width : 2 * width + units],
        grad_fc2.T,
        bias_total[:width],
    )


def solution(mesh):
    in_specs = (
        P("dp", None),
        P(),
        P(),
        P("dp", None, "tensor"),
        P(None, "tensor"),
        P("dp", None, "tensor"),
        P(None, "tensor"),
        P("tensor", "dp"),
        P(),
        P("dp", "tensor"),
        P("tensor"),
        P("tensor", "dp"),
        P(),
        P("dp", None),
    )
    out_specs = (
        P("dp", None),
        P("dp", None),
        P(),
        P("dp", None, "tensor"),
        P(None, "tensor"),
        P("dp", None, "tensor"),
        P(None, "tensor"),
        P("tensor", "dp"),
        P(),
        P("dp", "tensor"),
        P("tensor"),
        P("tensor", "dp"),
        P(),
    )
    return jax.shard_map(local, mesh=mesh, in_specs=in_specs, out_specs=out_specs, check_vma=False)
```

```python
import math

import jax
import jax.numpy as jnp
from jax import lax
from jax.experimental import pallas as pl
from jax.experimental.pallas import tpu as pltpu
from jax.sharding import PartitionSpec as P

DH = 72
SEQ = 1024
NORM_EPS = 1e-06
NEGATIVE = -1e30
SCALE = 1.0 / math.sqrt(DH)
VMEM_BYTES = 58 * 1024 * 1024
BF16 = jnp.bfloat16
F32 = jnp.float32


def swap(block, axis, bits):
    route = [(i, i ^ bits) for i in range(lax.axis_size(axis))]
    return lax.ppermute(block, axis, route)


def exchange(blocks, axis):
    return lax.all_to_all(blocks, axis, 0, 0, tiled=True)


def gather(block, axis, count):
    return exchange(jnp.broadcast_to(block[None], (count,) + block.shape), axis)


def gate_all(values, *others):
    anywhere = pl.BlockSpec(memory_space=pl.ANY)
    return pl.pallas_call(
        lambda *refs: None,
        out_shape=tuple(jax.ShapeDtypeStruct(value.shape, value.dtype) for value in values),
        in_specs=[anywhere] * (len(values) + len(others)),
        out_specs=(anywhere,) * len(values),
        input_output_aliases={place: place for place in range(len(values))},
        cost_estimate=pl.CostEstimate(flops=1, bytes_accessed=1, transcendentals=0),
        name="gate",
    )(*values, *others)


def gate(value, *others):
    return gate_all((value,), *others)[0]


def choose(core, first, second):
    return jnp.where(core == 0, first, second), jnp.where(core == 0, second, first)


def pair_rows(first, second):
    core = lax.axis_index("dp") % 2
    keep, send = choose(core, first, second)
    return jnp.concatenate(choose(core, keep, swap(send, "dp", 1)))


def chip_parts(rows):
    count = lax.axis_size("dp") // 2
    return [rows] + [swap(rows, "dp", 2 * step) for step in range(1, count)]


def gather_chips(rows):
    count = lax.axis_size("dp")
    groups = [list(range(core, count, 2)) for core in range(2)]
    return lax.all_gather(rows, "dp", axis=0, tiled=True, axis_index_groups=groups)


def sum_chips(blocks):
    if len(blocks) == 1:
        count, chip = lax.axis_size("dp") // 2, lax.axis_index("dp") // 2
        rows = blocks[0].reshape((count, -1) + blocks[0].shape[1:])
        blocks = [
            lax.dynamic_index_in_dim(rows, chip ^ step, 0, keepdims=False) for step in range(count)
        ]
    return [swap(block, "dp", 2 * step) if step else block for step, block in enumerate(blocks)]


def finish_pair(parts):
    core = lax.axis_index("dp") % 2
    rows = sum(part.astype(F32) for part in parts)
    half = rows.shape[0] // 2
    keep, send = choose(core, rows[:half], rows[half:])
    return choose(core, keep, swap(send, "dp", 1))


def in_order(parts, axis):
    me = lax.axis_index(axis)
    stacked = jnp.stack(parts)
    ordered = [
        lax.dynamic_index_in_dim(stacked, me ^ place, 0, keepdims=False) for place in range(len(parts))
    ]
    return jnp.concatenate(ordered)


def exchange_shares(partial, axis):
    count = lax.axis_size(axis)
    blocks = partial.reshape((count, partial.shape[0] // count) + partial.shape[1:])
    return exchange(blocks, axis)


def tile_range(meta_ref, latents, tile, core):
    lane = lax.broadcasted_iota(jnp.int32, (1, 256), 1)
    first = tile * 512 + core * 128
    last = first + 383
    place = first + lane + jnp.where(lane >= 128, 128, 0)
    begin = jnp.zeros((1, 256), jnp.int32)
    finish = jnp.zeros((1, 256), jnp.int32)
    low = jnp.int32(0)
    high = jnp.int32(0)
    start = jnp.int32(0)
    for number in range(latents):
        end = start + meta_ref[1 + number]
        inside = (place >= start) & (place < end)
        begin = jnp.where(inside, start, begin)
        finish = jnp.where(inside, end, finish)
        low = jnp.where((first >= start) & (first < end), start, low)
        high = jnp.where((last >= start) & (last < end), end, high)
        start = end
    return begin, finish, low // 256, (high + 255) // 256


def pair(ref, tile, start):
    left = ref[2 * tile, :, start : start + 128]
    right = ref[2 * tile + 1, :, start : start + 128]
    return jnp.concatenate([left, right], axis=1)


def key_mask(block, begin, finish):
    place = block * 256 + lax.broadcasted_iota(jnp.int32, (256, 256), 0)
    return (place >= begin) & (place < finish)


def forward_kernel(latents, meta_ref, packed_ref, out_ref, exact_ref, log_ref, keys, scores):
    blocks = packed_ref.shape[0]
    core = meta_ref[0]
    for block in range(blocks):
        keys[block] = packed_ref[block, :, :256].astype(F32).T.astype(BF16)
    for tile in range(blocks // 2):
        begin, finish, low, high = tile_range(meta_ref, latents, tile, core)
        query = pair(packed_ref, tile, 512)

        def score(block, largest):
            raw = jnp.dot(keys[block], query, preferred_element_type=F32) * SCALE
            raw = jnp.where(key_mask(block, begin, finish), raw, NEGATIVE)
            scores[block] = raw
            return jnp.maximum(largest, jnp.max(raw, axis=0, keepdims=True))

        largest = lax.fori_loop(low, high, score, jnp.full((1, 256), NEGATIVE, F32))

        def mix(block, carry):
            total, mixed = carry
            weights = jnp.exp(scores[block] - largest)
            total = total + jnp.sum(weights, axis=0, keepdims=True)
            values = packed_ref[block, :, 256:512]
            mixed = mixed + jnp.dot(values, weights.astype(BF16), preferred_element_type=F32)
            return total, mixed

        total, mixed = lax.fori_loop(
            low, high, mix, (jnp.zeros((1, 256), F32), jnp.zeros((DH, 256), F32))
        )
        mixed = mixed / total
        log_total = largest + jnp.log(total)
        for half in range(2):
            part = mixed[:, half * 128 : half * 128 + 128]
            exact_ref[2 * tile + half] = part
            out_ref[2 * tile + half] = part.astype(BF16)
            log_ref[2 * tile + half] = log_total[:, half * 128 : half * 128 + 128]


def backward_kernel(
    latents, meta_ref, packed_ref, grad_ref, exact_ref, log_ref, out_ref, keys, values, d_keys, d_values
):
    blocks = packed_ref.shape[0]
    core = meta_ref[0]
    for block in range(blocks):
        keys[block] = packed_ref[block, :, :256].astype(F32).T.astype(BF16)
        values[block] = packed_ref[block, :, 256:512].astype(F32).T.astype(BF16)
    d_keys[...] = jnp.zeros_like(d_keys)
    d_values[...] = jnp.zeros_like(d_values)
    by_query = (((1,), (1,)), ((), ()))
    for tile in range(blocks // 2):
        begin, finish, low, high = tile_range(meta_ref, latents, tile, core)
        query = pair(packed_ref, tile, 512)
        grad = pair(grad_ref, tile, 0)
        inner = jnp.sum(grad.astype(F32) * pair(exact_ref, tile, 0), axis=0, keepdims=True)
        log_total = pair(log_ref, tile, 0)

        def step(block, d_query):
            raw = jnp.dot(keys[block], query, preferred_element_type=F32) * SCALE
            probs = jnp.where(key_mask(block, begin, finish), jnp.exp(raw - log_total), 0.0)
            d_probs = jnp.dot(values[block], grad, preferred_element_type=F32)
            d_scores = (probs * (d_probs - inner)).astype(BF16)
            d_values[block] += lax.dot_general(
                grad, probs.astype(BF16), by_query, preferred_element_type=F32
            )
            d_keys[block] += lax.dot_general(query, d_scores, by_query, preferred_element_type=F32)
            key_rows = packed_ref[block, :, :256]
            return d_query + jnp.dot(key_rows, d_scores, preferred_element_type=F32)

        d_query = lax.fori_loop(low, high, step, jnp.zeros((DH, 256), F32)) * SCALE
        for half in range(2):
            part = d_query[:, half * 128 : half * 128 + 128]
            out_ref[2 * tile + half, :, 512:640] = part.astype(BF16)
    for block in range(blocks):
        out_ref[block, :, :256] = (d_keys[block] * SCALE).astype(BF16)
        out_ref[block, :, 256:512] = d_values[block].astype(BF16)


def attend_forward(meta, packed):
    blocks = packed.shape[0]
    shape = jax.ShapeDtypeStruct
    return pl.pallas_call(
        lambda *refs: forward_kernel(meta.shape[0] - 1, *refs),
        out_shape=(
            shape((blocks, DH, 128), BF16),
            shape((blocks, DH, 128), F32),
            shape((blocks, 1, 128), F32),
        ),
        in_specs=[
            pl.BlockSpec(memory_space=pltpu.SMEM),
            pl.BlockSpec(memory_space=pltpu.VMEM),
        ],
        out_specs=tuple([pl.BlockSpec(memory_space=pltpu.VMEM)] * 3),
        scratch_shapes=[
            pltpu.VMEM((blocks, 256, DH), BF16),
            pltpu.VMEM((blocks, 256, 256), F32),
        ],
        compiler_params=pltpu.CompilerParams(vmem_limit_bytes=VMEM_BYTES),
        cost_estimate=pl.CostEstimate(flops=10**9, bytes_accessed=4 * 10**6, transcendentals=10**6),
        name="attend_forward",
    )(meta, packed)


def attend_backward(meta, packed, grad, exact, log_total):
    blocks = packed.shape[0]
    return pl.pallas_call(
        lambda *refs: backward_kernel(meta.shape[0] - 1, *refs),
        out_shape=jax.ShapeDtypeStruct(packed.shape, BF16),
        in_specs=[pl.BlockSpec(memory_space=pltpu.SMEM)]
        + [pl.BlockSpec(memory_space=pltpu.VMEM)] * 4,
        out_specs=pl.BlockSpec(memory_space=pltpu.VMEM),
        scratch_shapes=[
            pltpu.VMEM((blocks, 256, DH), BF16),
            pltpu.VMEM((blocks, 256, DH), BF16),
            pltpu.VMEM((blocks, DH, 256), F32),
            pltpu.VMEM((blocks, DH, 256), F32),
        ],
        compiler_params=pltpu.CompilerParams(vmem_limit_bytes=VMEM_BYTES),
        cost_estimate=pl.CostEstimate(flops=3 * 10**9, bytes_accessed=4 * 10**6, transcendentals=10**6),
        name="attend_backward",
    )(meta, packed, grad, exact, log_total)


class HeadSplit:
    def __init__(self, latent_len, rows):
        self.rows = rows
        self.meta = jnp.concatenate([lax.axis_index("dp").astype(jnp.int32)[None] % 2, latent_len])

    def forward(self, packed):
        self.packed = exchange(packed, "dp")
        out, self.exact, self.log_total = attend_forward(self.meta, self.packed)
        return exchange(out, "dp")

    def backward(self, grad, due):
        grad = exchange(grad, "dp")
        out = attend_backward(self.meta, self.packed, grad, self.exact, self.log_total)
        return exchange(gate(out, *due), "dp")


class Window:
    def __init__(self, latent_len, rows):
        self.rows = rows
        self.reach = (SEQ - 2) // rows + 1
        total = rows * lax.axis_size("dp")
        first = lax.axis_index("dp") * rows
        own = latent_index(latent_len, first, rows, total)
        ids = [
            latent_index(latent_len, first + offset * rows, rows, total)
            for offset in range(-self.reach, self.reach + 1)
        ]
        self.allowed = own[:, None] == jnp.concatenate(ids)[None, :]

    def from_behind(self, block, distance):
        devices = range(lax.axis_size("dp"))
        return lax.ppermute(
            block, "dp", [(i - distance, i) for i in devices if i - distance in devices]
        )

    def head_scores(self, query, key):
        raw = jnp.einsum("eq,ek->qk", query, key, preferred_element_type=F32) * SCALE
        return jnp.where(self.allowed, raw, NEGATIVE)

    def forward(self, packed):
        rows = self.rows
        split = packed.reshape(-1, 2, DH, rows * 5 // 2)
        query = jnp.concatenate([split[:, 0, :, 2 * rows :], split[:, 1, :, 2 * rows :]], axis=2)
        projected = jnp.stack([query, split[:, 0, :, :rows], split[:, 0, :, rows : 2 * rows]])
        key_value = projected[1:]
        pieces = [
            key_value if offset == 0 else self.from_behind(key_value, -offset)
            for offset in range(-self.reach, self.reach + 1)
        ]
        window = jnp.concatenate(pieces, axis=3)
        self.operands = (projected[0], window[0], window[1])

        def one(operands):
            query, key, value = operands
            scores = self.head_scores(query, key)
            largest = jnp.max(scores, axis=1, keepdims=True)
            weights = jnp.exp(scores - largest)
            totals = jnp.sum(weights, axis=1, keepdims=True)
            probs = (weights / totals).astype(BF16)
            mixed = jnp.einsum("qk,ek->eq", probs, value, preferred_element_type=F32)
            return mixed.astype(BF16), (largest + jnp.log(totals))[:, 0]

        out, self.log_total = lax.map(one, self.operands)
        out = out.reshape(-1, DH, 2, rows // 2).transpose(0, 2, 1, 3)
        return out.reshape(-1, DH, rows // 2)

    def backward(self, grad, due):
        rows, reach = self.rows, self.reach
        halves = grad.reshape(-1, 2, DH, rows // 2)
        grads = jnp.concatenate([halves[:, 0], halves[:, 1]], axis=2)

        def one(operands):
            query, key, value, grad, log_total = operands
            probs = jnp.exp(self.head_scores(query, key) - log_total[:, None])
            d_value = jnp.einsum("qk,eq->ek", probs.astype(BF16), grad, preferred_element_type=F32)
            d_probs = jnp.einsum("eq,ek->qk", grad, value, preferred_element_type=F32)
            inner = jnp.sum(probs * d_probs, axis=1, keepdims=True)
            d_scores = (probs * (d_probs - inner)).astype(BF16)
            d_query = jnp.einsum("qk,ek->eq", d_scores, key, preferred_element_type=F32) * SCALE
            d_key = jnp.einsum("qk,eq->ek", d_scores, query, preferred_element_type=F32) * SCALE
            return d_query, d_key, d_value

        d_query, d_key, d_value = lax.map(one, self.operands + (grads, self.log_total))
        d_window = jnp.stack([d_key, d_value])
        d_key_value = d_window[..., reach * rows : (reach + 1) * rows]
        for offset in range(-reach, reach + 1):
            if offset != 0:
                block = d_window[..., (offset + reach) * rows : (offset + reach + 1) * rows]
                d_key_value = d_key_value + self.from_behind(block, offset)
        wide = jnp.concatenate([d_key_value[0], d_key_value[1]], axis=2)
        wide = jnp.stack([wide, jnp.zeros_like(wide)], axis=1)
        halves = d_query.reshape(-1, DH, 2, rows // 2).transpose(0, 2, 1, 3)
        packed = jnp.concatenate([wide, halves], axis=3).astype(BF16)
        return packed.reshape(-1, DH, rows * 5 // 2)


META = 4


def vmem(count):
    return [pl.BlockSpec(memory_space=pltpu.VMEM)] * count


def call(body, name, meta, arrays, outs, scratch=(), anywhere=0, due=()):
    count = 1 + len(arrays)

    def kernel(*refs):
        body(*refs[:count], *refs[count + len(due) :])

    return pl.pallas_call(
        kernel,
        out_shape=tuple(jax.ShapeDtypeStruct(shape, kind) for shape, kind in outs),
        in_specs=[pl.BlockSpec(memory_space=pltpu.SMEM)]
        + [pl.BlockSpec(memory_space=pl.ANY)] * anywhere
        + vmem(len(arrays) - anywhere)
        + [pl.BlockSpec(memory_space=pl.ANY)] * len(due),
        out_specs=tuple(vmem(len(outs))),
        scratch_shapes=list(scratch),
        compiler_params=pltpu.CompilerParams(vmem_limit_bytes=VMEM_BYTES),
        cost_estimate=pl.CostEstimate(flops=1, bytes_accessed=1, transcendentals=0),
        name=name,
    )(meta, *arrays, *due)


def row_masks(meta_ref, latents, first, rows):
    place = first + lax.broadcasted_iota(jnp.int32, (rows, 1), 0)
    ids = jnp.zeros((rows, 1), jnp.int32)
    end = jnp.int32(0)
    for number in range(latents - 1):
        end = end + meta_ref[META + number]
        ids = ids + (place >= end).astype(jnp.int32)
    return [(ids == number).astype(F32) for number in range(latents)]


def rows_of(mod_ref, masks, feature):
    out = masks[0] * mod_ref[feature : feature + 1, :]
    for number in range(1, len(masks)):
        row = number * 6 + feature
        out = out + masks[number] * mod_ref[row : row + 1, :]
    return out


def latent_sums(out_ref, masks, values, feature, features):
    rounded = values.astype(BF16).astype(F32)
    for number, mask in enumerate(masks):
        row = number * features + feature
        out_ref[row : row + 1, :] = jnp.sum(mask * rounded, axis=0, keepdims=True)


def own_rows(meta_ref, ref, share):
    start = pl.multiple_of(meta_ref[2] * share, share)
    return ref[pl.ds(start, share), :].astype(F32)


def on_core(meta_ref, body, mine, other):
    @pl.when(meta_ref[0] == 0)
    def _():
        body(mine, other)

    @pl.when(meta_ref[0] != 0)
    def _():
        body(other, mine)


def place_rows(meta_ref, parts, whole, sems):
    block = parts[0].shape[0]
    copies = []
    for step, part in enumerate(parts):
        start = pl.multiple_of((meta_ref[3] ^ step) * block, 16)
        copies.append(
            pltpu.make_async_copy(part, whole.at[pl.ds(start, block), :], sems.at[step])
        )
    return copies


def place_pair(meta_ref, mine, other, first_ref, second_ref, sems):
    def body(first, second):
        copies = place_rows(meta_ref, first, first_ref, sems.at[0])
        copies += place_rows(meta_ref, second, second_ref, sems.at[1])
        for copy in copies:
            copy.start()
        for copy in copies:
            copy.wait()

    on_core(meta_ref, body, mine, other)


def project_kernel(latents, count, meta_ref, *refs):
    mine, other = refs[:count], refs[count : 2 * count]
    tokens_ref, cot_ref, mod_ref, bias_ref = refs[2 * count : 2 * count + 4]
    hidden_ref, d_mlp_ref, packed_ref, qk_ref, vp_ref, d_bias_ref, sems = refs[2 * count + 4 :]
    rows, width = tokens_ref.shape
    place_pair(meta_ref, mine, other, qk_ref, vp_ref, sems)
    masks = row_masks(meta_ref, latents, meta_ref[1], rows)
    unit, _ = normed(tokens_ref[...].astype(F32))
    hidden = unit * (1.0 + rows_of(mod_ref, masks, 1)) + rows_of(mod_ref, masks, 0)
    hidden_ref[...] = hidden.astype(BF16)
    d_mlp = (cot_ref[...].astype(F32) * rows_of(mod_ref, masks, 5)).astype(BF16)
    d_mlp_ref[...] = d_mlp
    d_bias_ref[...] = jnp.sum(d_mlp.astype(F32), axis=0, keepdims=True)
    heads = packed_ref.shape[0] // 2
    features = heads * DH
    left = hidden_ref[...]
    both = jnp.dot(left, qk_ref[...], preferred_element_type=F32) + bias_ref[0:1, :]
    both = both.T
    value = jnp.dot(left, vp_ref[...], preferred_element_type=F32) + bias_ref[1:2, :]
    value = value.T
    for head in range(heads):
        start = head * DH
        query = both[start : start + DH].astype(BF16)
        key = both[features + start : features + start + DH].astype(BF16)
        val = value[start : start + DH].astype(BF16)
        for half in range(2):
            packed_ref[2 * head + half, :, :rows] = key
            packed_ref[2 * head + half, :, rows : 2 * rows] = val
            packed_ref[2 * head + half, :, 2 * rows :] = query[
                :, half * (rows // 2) : (half + 1) * (rows // 2)
            ]


def attend_out_kernel(meta_ref, parts_ref, vp_ref, part_ref, attended_ref):
    heads = parts_ref.shape[0] // 2
    rows = part_ref.shape[0]
    stacked = [jnp.zeros((heads * DH, rows), F32)]
    for head in range(heads):
        left = parts_ref[2 * head].astype(F32)
        right = parts_ref[2 * head + 1].astype(F32)
        stacked.append(jnp.concatenate([left, right], axis=1))
    attended_ref[...] = jnp.concatenate(stacked, axis=0).T.astype(BF16)
    part_ref[...] = lax.dot_general(
        attended_ref[...], vp_ref[...], (((1,), (1,)), ((), ())), preferred_element_type=F32
    ).astype(BF16)


def middle_kernel(
    latents, meta_ref, parts_ref, tokens_ref, mod_ref, bias_ref, sent_ref, attn_ref, mid_ref
):
    copies, share, width = parts_ref.shape
    masks = row_masks(meta_ref, latents, meta_ref[1] + meta_ref[2] * share, share)
    attn = bias_ref[...].astype(F32)
    for part in range(copies):
        attn = attn + parts_ref[part].astype(F32)
    attn_ref[...] = attn
    mid = own_rows(meta_ref, tokens_ref, share) + rows_of(mod_ref, masks, 2) * attn
    mid_ref[...] = mid
    unit, _ = normed(mid)
    hidden = unit * (1.0 + rows_of(mod_ref, masks, 4)) + rows_of(mod_ref, masks, 3)
    for part in range(copies):
        sent_ref[part] = hidden.astype(BF16)


def mlp_kernel(count, meta_ref, *refs):
    mine, other = refs[:count], refs[count : 2 * count]
    hidden_ref, d_mlp_ref, bias_ref = refs[2 * count : 2 * count + 3]
    d_two_ref, gelu_ref, d_pre_ref, d_bias_ref, left_ref, right_ref = refs[2 * count + 3 : 2 * count + 9]
    mlp_refs = refs[2 * count + 9 : -5]
    fc1_ref, fc2_ref, d_two_sum, mlp_sum, sems = refs[-5:]
    place_pair(meta_ref, mine, other, fc1_ref, fc2_ref, sems)
    d_two_sum[...] = jnp.zeros_like(d_two_sum)
    mlp_sum[...] = jnp.zeros_like(mlp_sum)
    tile = 384
    by_last = (((1,), (1,)), ((), ()))

    def step(number, carry):
        units = pl.ds(pl.multiple_of(number * tile, tile), tile)
        fc1, fc2 = fc1_ref[:, units], fc2_ref[:, units]
        pre = jnp.dot(hidden_ref[...], fc1, preferred_element_type=F32)
        gelu, slope = gelu_pair(pre + bias_ref[:, units].astype(F32))
        grad = jnp.dot(d_mlp_ref[...], fc2, preferred_element_type=F32)
        d_pre = (grad * slope).astype(BF16)
        gelu = gelu.astype(BF16)
        gelu_ref[:, units] = gelu
        d_pre_ref[:, units] = d_pre
        d_bias_ref[:, units] = jnp.sum(d_pre.astype(F32), axis=0, keepdims=True)
        d_two_sum[...] += lax.dot_general(d_pre, fc1, by_last, preferred_element_type=F32)
        mlp_sum[...] += lax.dot_general(gelu, fc2, by_last, preferred_element_type=F32)
        return carry

    lax.fori_loop(0, fc1_ref.shape[1] // tile, step, 0)
    d_two_ref[...] = d_two_sum[...].astype(BF16)
    def sent(left, right):
        left_ref[...] = left[0][...]
        right_ref[...] = left[1][...]

    on_core(meta_ref, sent, (d_mlp_ref, gelu_ref), (hidden_ref, d_pre_ref))
    share = mlp_refs[0].shape[0]
    for step, mlp_ref in enumerate(mlp_refs):
        start = pl.multiple_of((meta_ref[2] ^ step) * share, share)
        mlp_ref[...] = mlp_sum[pl.ds(start, share), :].astype(BF16)


def middle_back_kernel(
    latents, meta_ref, parts_ref, mid_in_ref, attn_ref, cot_ref, mod_ref, sent_ref, d_mid_ref, sums_ref
):
    copies, share, width = parts_ref.shape
    masks = row_masks(meta_ref, latents, meta_ref[1] + meta_ref[2] * share, share)
    d_hidden = parts_ref[0].astype(F32)
    for part in range(1, copies):
        d_hidden = d_hidden + parts_ref[part].astype(F32)
    unit, inverse = normed(mid_in_ref[...])
    d_mid = own_rows(meta_ref, cot_ref, share) + norm_back(
        unit, inverse, d_hidden * (1.0 + rows_of(mod_ref, masks, 4))
    )
    d_mid_ref[...] = d_mid
    d_attn = (d_mid * rows_of(mod_ref, masks, 2)).astype(BF16)
    for part in range(copies):
        sent_ref[part] = d_attn
    latent_sums(sums_ref, masks, d_mid * attn_ref[...], 0, 3)
    latent_sums(sums_ref, masks, d_hidden, 1, 3)
    latent_sums(sums_ref, masks, d_hidden * unit, 2, 3)


def result_kernel(
    latents, count, meta_ref, *refs
):
    parts = refs[:count]
    mid_ref, cot_ref, mod_ref, bias_ref, result_ref, sums_ref = refs[count:]
    share = result_ref.shape[0]
    masks = row_masks(meta_ref, latents, meta_ref[1] + meta_ref[2] * share, share)
    mlp = bias_ref[...].astype(F32)
    for part in parts:
        mlp = mlp + part[...].astype(F32)
    result_ref[...] = (mid_ref[...] + rows_of(mod_ref, masks, 5) * mlp).astype(BF16)
    latent_sums(sums_ref, masks, own_rows(meta_ref, cot_ref, share) * mlp, 0, 1)


def spread_kernel(meta_ref, d_attn_ref, vp_ref, packed_ref, d_bias_ref):
    grad = jnp.dot(d_attn_ref[...], vp_ref[...], preferred_element_type=F32).T
    half = grad.shape[1] // 2
    features = grad.shape[0] // 2
    for place in range(packed_ref.shape[0]):
        start = features + place // 2 * DH
        side = place % 2 * half
        packed_ref[place] = grad[start : start + DH, side : side + half].astype(BF16)
    d_bias_ref[...] = jnp.sum(d_attn_ref[...].astype(F32), axis=0, keepdims=True)


def unspread_kernel(
    meta_ref, parts_ref, qk_ref, vp_ref, d_one_ref, d_qk_ref, d_vp_ref, sent_ref, d_bias_ref
):
    heads = parts_ref.shape[0] // 2
    rows = d_one_ref.shape[0]
    query, key, value = [], [], []
    for head in range(heads):
        left = parts_ref[2 * head].astype(F32)
        right = parts_ref[2 * head + 1].astype(F32)
        both = left[:, : 2 * rows] + right[:, : 2 * rows]
        key.append(both[:, :rows])
        value.append(both[:, rows:])
        query.append(jnp.concatenate([left[:, 2 * rows :], right[:, 2 * rows :]], axis=1))
    d_qk_ref[...] = jnp.concatenate(query + key, axis=0).T.astype(BF16)
    blank = jnp.zeros((heads * DH, rows), F32)
    d_vp_ref[...] = jnp.concatenate(value + [blank], axis=0).T.astype(BF16)
    tile = 384
    by_last = (((1,), (1,)), ((), ()))

    def step(number, carry):
        columns = pl.ds(pl.multiple_of(number * tile, tile), tile)
        total = lax.dot_general(d_qk_ref[...], qk_ref[columns, :], by_last, preferred_element_type=F32)
        total += lax.dot_general(d_vp_ref[...], vp_ref[columns, :], by_last, preferred_element_type=F32)
        d_one_ref[:, columns] = total.astype(BF16)
        return carry

    lax.fori_loop(0, qk_ref.shape[0] // tile, step, 0)

    def sent(first, second):
        sent_ref[...] = first[...]

    on_core(meta_ref, sent, d_vp_ref, d_qk_ref)
    d_bias_ref[0:1, :] = jnp.sum(d_qk_ref[...].astype(F32), axis=0, keepdims=True)
    d_bias_ref[1:2, :] = jnp.sum(d_vp_ref[...].astype(F32), axis=0, keepdims=True)


def weight_kernel(first_pairs, second_pairs, meta_ref, *refs):
    operands = 1 + max(max(pair) for pair in first_pairs + second_pairs)
    ins, outs, total = refs[:operands], refs[operands:-1], refs[-1]
    tile = 384

    def body(pairs):
        def step(number, carry):
            columns = pl.ds(pl.multiple_of(number * tile, tile), tile)
            block = jnp.zeros((tile, total.shape[1]), F32)
            for left, right in pairs:
                block += lax.dot_general(
                    ins[left][:, columns], ins[right][...], (((0,), (0,)), ((), ())),
                    preferred_element_type=F32,
                )
            total[columns, :] = block.astype(BF16)
            return carry

        lax.fori_loop(0, total.shape[0] // tile, step, 0)

    on_core(meta_ref, lambda pairs, _: body(pairs), first_pairs, second_pairs)
    rows = outs[0].shape[0]
    for step, out in enumerate(outs):
        start = pl.multiple_of((meta_ref[3] ^ step) * rows, 16)
        out[...] = total[pl.ds(start, rows), :]


def first_back_kernel(
    latents, meta_ref, parts_ref, tokens_ref, d_mid_ref, mod_ref, mid_sums_ref, last_sums_ref,
    fc2_bias_ref, proj_bias_ref, fc1_bias_ref, qv_bias_ref, grad_ref, sent_ref, bias_ref, first_sums,
):
    copies, share, width = parts_ref.shape
    masks = row_masks(meta_ref, latents, meta_ref[1] + meta_ref[2] * share, share)
    d_hidden = parts_ref[0].astype(F32)
    for part in range(1, copies):
        d_hidden = d_hidden + parts_ref[part].astype(F32)
    unit, inverse = normed(own_rows(meta_ref, tokens_ref, share))
    grad = d_mid_ref[...] + norm_back(unit, inverse, d_hidden * (1.0 + rows_of(mod_ref, masks, 1)))
    grad_ref[...] = grad.astype(BF16)
    latent_sums(first_sums, masks, d_hidden, 0, 2)
    latent_sums(first_sums, masks, d_hidden * unit, 1, 2)
    columns = width // copies
    for number in range(latents):
        for feature in range(6):
            if feature < 2:
                row = first_sums[number * 2 + feature : number * 2 + feature + 1, :]
            elif feature < 5:
                place = number * 3 + feature - 2
                row = mid_sums_ref[place : place + 1, :]
            else:
                row = last_sums_ref[number : number + 1, :]
            place = number * 6 + feature
            for part in range(copies):
                sent_ref[part, place : place + 1, :] = row[:, part * columns : (part + 1) * columns]
    place = 0
    for ref in (fc2_bias_ref, proj_bias_ref, fc1_bias_ref):
        for start in range(0, ref.shape[1], columns):
            bias_ref[place : place + 1, :] = ref[:, start : start + columns]
            place += 1
    bias_ref[place : place + 2, :] = qv_bias_ref[:, :columns]


def latent_index(latent_len, first_row, row_count, token_total):
    positions = first_row + jnp.arange(row_count, dtype=jnp.int32)
    ends = jnp.cumsum(latent_len, dtype=jnp.int32)
    found = jnp.sum((positions[:, None] >= ends[None, :]).astype(jnp.int32), axis=1, dtype=jnp.int32)
    return jnp.where((positions >= 0) & (positions < token_total), found, -1)


def normed(values):
    average = jnp.mean(values, axis=-1, keepdims=True)
    centred = values - average
    spread = jnp.mean(centred * centred, axis=-1, keepdims=True)
    inverse = lax.rsqrt(spread + NORM_EPS)
    return centred * inverse, inverse


def norm_back(unit, inverse, grad):
    along = jnp.mean(grad * unit, axis=-1, keepdims=True)
    return inverse * (grad - jnp.mean(grad, axis=-1, keepdims=True) - unit * along)


def gelu_pair(value):
    root = math.sqrt(2.0 / math.pi)
    bend = jnp.tanh(root * (value + 0.044715 * value * value * value))
    slope = root * (1.0 + 3.0 * 0.044715 * value * value)
    gelu = 0.5 * value * (1.0 + bend)
    return gelu, 0.5 * (1.0 + bend) + 0.5 * value * (1.0 - bend * bend) * slope


def local(
    tokens,
    conditioning,
    latent_len,
    w_ada,
    b_ada,
    w_qkv,
    b_qv,
    w_proj,
    b_proj,
    w_fc1,
    b_fc1,
    w_fc2,
    b_fc2,
    cotangent,
):
    rows, width = tokens.shape
    share_width = w_qkv.shape[0]
    features = w_qkv.shape[2]
    units = w_fc1.shape[1]
    heads = features // DH
    latents = conditioning.shape[0]
    n_dp, n_tensor = lax.axis_size("dp"), lax.axis_size("tensor")
    my_dp, my_tensor = lax.axis_index("dp"), lax.axis_index("tensor")
    share = rows // n_tensor

    core = my_dp % 2
    qk = w_qkv[:, :2].reshape(share_width, 2 * features)
    vp = jnp.concatenate([w_qkv[:, 2], w_proj.T], axis=1)
    early_rows = pair_rows(qk, vp)

    cond = conditioning.astype(F32)
    sigmoid = 1.0 / (1.0 + jnp.exp(-cond))
    activated = (cond * sigmoid).astype(BF16)
    own_activated = lax.dynamic_slice_in_dim(activated, my_dp * share_width, share_width, 1)
    flat_ada = w_ada.reshape(share_width, 6 * features)
    mod_part = jnp.dot(own_activated, flat_ada, preferred_element_type=F32)
    mod_part = mod_part.reshape(latents * 6, features)
    mod_mine = jnp.sum(gather(mod_part, "dp", n_dp), axis=0)
    mod_mine = mod_mine + jnp.tile(b_ada.astype(F32), (latents, 1))
    few_chips = n_dp // 2 == 4
    early_rows = gate(early_rows, mod_mine)
    early_parts = chip_parts(early_rows) if few_chips else [gather_chips(early_rows)]
    modulation = gather(mod_mine, "tensor", n_tensor).transpose(1, 0, 2).reshape(6 * latents, width)

    mod_rows = modulation
    early_parts = list(gate_all(early_parts, modulation))
    early_parts += [swap(part, "dp", 1) for part in early_parts]
    count = len(early_parts) // 2
    meta = jnp.stack([core, my_dp * rows, my_tensor, my_dp // 2]).astype(jnp.int32)
    meta = jnp.concatenate([meta, latent_len])
    place_meta = meta if few_chips else meta.at[3].set(0)
    by_last = (((1,), (1,)), ((), ()))
    by_token = (((0,), (0,)), ((), ()))
    bias = jnp.concatenate([b_qv[0], jnp.zeros_like(b_qv[0]), b_qv[1], jnp.zeros_like(b_qv[0])])
    hidden_one, d_mlp, packed, full_qk, full_vp, d_bias_fc2 = call(
        lambda *refs: project_kernel(latents, count, *refs),
        "project",
        place_meta,
        (*early_parts, tokens, cotangent, mod_rows, bias.astype(F32).reshape(2, -1)),
        (((rows, width), BF16), ((rows, width), BF16), ((2 * heads, DH, rows * 5 // 2), BF16))
        + (((width, 2 * features), BF16),) * 2
        + (((1, width), F32),),
        [pltpu.SemaphoreType.DMA((2, count))],
        2 * count,
    )
    late_rows = pair_rows(w_fc1, w_fc2.T)
    hidden_other = swap(hidden_one, "dp", 1)
    split = HeadSplit if 2 * heads == n_dp else Window
    attention = split(latent_len, rows)
    attended_parts = attention.forward(packed)
    late_rows = gate(late_rows, attended_parts)
    late_parts = chip_parts(late_rows)[:-1] if few_chips else [gather_chips(late_rows)]
    attn_part, attended = call(
        attend_out_kernel,
        "attend_out",
        meta,
        (attended_parts, full_vp),
        (((rows, width), BF16), ((rows, 2 * features), BF16)),
    )
    attn_parts = exchange_shares(attn_part, "tensor")
    hidden_blocks, attn_out, residual_mid = call(
        lambda *refs: middle_kernel(latents, *refs),
        "middle",
        meta,
        (attn_parts, tokens, mod_rows, b_proj.reshape(1, -1)),
        (((n_tensor, share, width), BF16), ((share, width), F32), ((share, width), F32)),
        due=late_parts[1:],
    )
    hidden_two = exchange(hidden_blocks, "tensor").reshape(rows, width)
    if few_chips:
        last_part = swap(gate(late_rows, attn_out), "dp", n_dp - 2)
        late_parts.append(gate(last_part, hidden_two))
    late_other = [swap(part, "dp", 1) for part in late_parts]

    d_two_part, gelu_out, d_pre, d_bias_fc1, left_sent, right_sent, *mlp_blocks = call(
        lambda *refs: mlp_kernel(count, *refs),
        "mlp",
        place_meta,
        (*late_parts, *late_other, hidden_two, d_mlp, b_fc1.reshape(1, -1)),
        (((rows, width), BF16), ((rows, units), BF16), ((rows, units), BF16), ((1, units), F32))
        + (((rows, width), BF16), ((rows, units), BF16))
        + (((share, width), BF16),) * n_tensor,
        [pltpu.VMEM((width, units), BF16)] * 2
        + [pltpu.VMEM((rows, width), F32)] * 2
        + [pltpu.SemaphoreType.DMA((2, count))],
        2 * count,
    )
    d_two_parts = exchange_shares(d_two_part, "tensor")

    chips = n_dp // 2 if few_chips else 1
    left_other = swap(left_sent, "dp", 1)
    right_other = swap(right_sent, "dp", 1)
    late_blocks = call(
        lambda *refs: weight_kernel([(0, 2), (4, 5)], [(1, 3), (4, 5)], *refs),
        "late_weights",
        place_meta,
        (hidden_two, d_mlp, d_pre, gelu_out, left_other, right_other),
        (((width // chips, units), BF16),) * chips,
        [pltpu.VMEM((width, units), BF16)],
    )
    late_grads = sum_chips(late_blocks[:-1]) if few_chips else sum_chips(late_blocks)

    d_attn_blocks, d_mid, mid_sums = call(
        lambda *refs: middle_back_kernel(latents, *refs),
        "middle_back",
        meta,
        (d_two_parts, residual_mid, attn_out, cotangent, mod_rows),
        (((n_tensor, share, width), BF16), ((share, width), F32), ((3 * latents, width), F32)),
        due=late_blocks,
    )
    d_attn = exchange(d_attn_blocks, "tensor").reshape(rows, width)

    d_spread, d_bias_proj = call(
        spread_kernel,
        "spread",
        meta,
        (d_attn, full_vp),
        (((2 * heads, DH, rows // 2), BF16), ((1, width), F32)),
        due=late_grads[1:],
    )
    mlp_parts = mlp_blocks[:1] + [
        swap(gate(block, d_spread), "tensor", step)
        for step, block in enumerate(mlp_blocks)
        if step
    ]
    d_attn_other = swap(d_attn, "dp", 1)
    attended_other = swap(attended, "dp", 1)
    d_packed = attention.backward(d_spread, mlp_parts[1:])
    result_own, last_sums = call(
        lambda *refs: result_kernel(latents, n_tensor, *refs),
        "result",
        meta,
        (*mlp_parts, residual_mid, cotangent, mod_rows, b_fc2.reshape(1, -1)),
        (((share, width), BF16), ((latents, width), F32)),
    )
    result_parts = [result_own] + [swap(result_own, "tensor", bits) for bits in range(1, n_tensor)]
    d_one_part, d_qk, d_vp, d_sent, d_bias_qv = call(
        unspread_kernel,
        "unspread",
        meta,
        (d_packed, full_qk, full_vp),
        (((rows, width), BF16),)
        + (((rows, 2 * features), BF16),) * 3
        + (((2, 2 * features), F32),),
        due=result_parts[1:],
    )
    d_one_parts = exchange_shares(d_one_part, "tensor")
    result = in_order(result_parts, "tensor")

    grad_own, d_mod_part, bias_rows = call(
        lambda *refs: first_back_kernel(latents, *refs),
        "first_back",
        meta,
        (d_one_parts, tokens, d_mid, mod_rows, mid_sums, last_sums)
        + (d_bias_fc2, d_bias_proj, d_bias_fc1, d_bias_qv),
        (((share, width), BF16), ((n_tensor, 6 * latents, features), F32))
        + (((2 * (width // features) + units // features + 2, features), F32),),
        [pltpu.VMEM((2 * latents, width), F32)],
    )
    if few_chips:
        late_grads.append(swap(gate(late_blocks[-1], d_one_part), "dp", n_dp - 2))
    right_other = swap(gate(d_sent, d_one_parts), "dp", 1)
    early_blocks = call(
        lambda *refs: weight_kernel(
            [(0, 2), (5, 7)], [(0, 3), (1, 4), (5, 7), (6, 8)], *refs
        ),
        "early_weights",
        place_meta,
        (hidden_one, d_attn, d_qk, d_vp, attended, hidden_other, d_attn_other, right_other, attended_other),
        (((width // chips, 2 * features), BF16),) * chips,
        [pltpu.VMEM((width, 2 * features), BF16)],
        due=[d_mod_part],
    )
    early_grads = sum_chips(early_blocks)

    d_mod_mine = jnp.sum(gate(exchange(d_mod_part, "tensor"), early_blocks[-1]), axis=0)
    grad_own = gate(grad_own, d_mod_mine)
    grad_parts = [grad_own] + [swap(grad_own, "tensor", bits) for bits in range(1, n_tensor)]
    sums = gather(jnp.concatenate([d_mod_mine, bias_rows]), "dp", n_dp)
    sums = jnp.sum(gate(sums, *early_grads[1:]) if few_chips else sums, axis=0)
    grad_tokens = in_order(gate_all(grad_parts, sums), "tensor").astype(F32)
    d_mod = sums[: 6 * latents].reshape(latents, 6 * features)
    bias_total = sums[6 * latents :].reshape(-1)
    grad_b_ada = jnp.sum(d_mod, axis=0).reshape(6, features)
    grad_w_ada = lax.dot_general(
        own_activated.astype(F32), d_mod, by_token, precision=lax.Precision.HIGHEST
    ).reshape(share_width, 6, features)
    high = d_mod.astype(BF16)
    low = (d_mod - high.astype(F32)).astype(BF16)
    d_active = lax.dot_general(
        jnp.concatenate([high, low]), flat_ada, by_last, preferred_element_type=F32
    )
    d_active = d_active[:latents] + d_active[latents:]
    d_active = gather(d_active, ("dp", "tensor"), n_dp * n_tensor)
    d_active = jnp.sum(d_active.reshape(n_dp, n_tensor, latents, share_width), axis=1)
    d_active = d_active.transpose(1, 0, 2).reshape(latents, width)
    grad_cond = d_active * (sigmoid * (1.0 + cond * (1.0 - sigmoid)))

    grad_fc1, grad_fc2 = finish_pair(late_grads)
    grad_qk, grad_vp = finish_pair(early_grads)
    grad_qkv = jnp.concatenate([grad_qk, grad_vp[:, :features]], axis=1)
    grad_qkv = grad_qkv.reshape(share_width, 3, features)

    return (
        result,
        grad_tokens,
        grad_cond,
        grad_w_ada,
        grad_b_ada,
        grad_qkv,
        bias_total[2 * width + units :].reshape(2, features),
        grad_vp[:, features:].T,
        bias_total[width : 2 * width],
        grad_fc1,
        bias_total[2 * width : 2 * width + units],
        grad_fc2.T,
        bias_total[:width],
    )


def solution(mesh):
    in_specs = (
        P("dp", None),
        P(),
        P(),
        P("dp", None, "tensor"),
        P(None, "tensor"),
        P("dp", None, "tensor"),
        P(None, "tensor"),
        P("tensor", "dp"),
        P(),
        P("dp", "tensor"),
        P("tensor"),
        P("tensor", "dp"),
        P(),
        P("dp", None),
    )
    out_specs = (
        P("dp", None),
        P("dp", None),
        P(),
        P("dp", None, "tensor"),
        P(None, "tensor"),
        P("dp", None, "tensor"),
        P(None, "tensor"),
        P("tensor", "dp"),
        P(),
        P("dp", "tensor"),
        P("tensor"),
        P("tensor", "dp"),
        P(),
    )
    return jax.shard_map(local, mesh=mesh, in_specs=in_specs, out_specs=out_specs, check_vma=False)
```

```python
import math

import jax
import jax.numpy as jnp
from jax import lax
from jax.experimental import pallas as pl
from jax.experimental.pallas import tpu as pltpu
from jax.sharding import PartitionSpec as P

DH = 72
SEQ = 1024
NORM_EPS = 1e-06
NEGATIVE = -1e30
SCALE = 1.0 / math.sqrt(DH)
VMEM_BYTES = 58 * 1024 * 1024
BF16 = jnp.bfloat16
F32 = jnp.float32


def swap(block, axis, bits):
    route = [(i, i ^ bits) for i in range(lax.axis_size(axis))]
    return lax.ppermute(block, axis, route)


def exchange(blocks, axis):
    return lax.all_to_all(blocks, axis, 0, 0, tiled=True)


def gather(block, axis, count):
    return exchange(jnp.broadcast_to(block[None], (count,) + block.shape), axis)


def gate_all(values, *others):
    anywhere = pl.BlockSpec(memory_space=pl.ANY)
    return pl.pallas_call(
        lambda *refs: None,
        out_shape=tuple(jax.ShapeDtypeStruct(value.shape, value.dtype) for value in values),
        in_specs=[anywhere] * (len(values) + len(others)),
        out_specs=(anywhere,) * len(values),
        input_output_aliases={place: place for place in range(len(values))},
        cost_estimate=pl.CostEstimate(flops=1, bytes_accessed=1, transcendentals=0),
        name="gate",
    )(*values, *others)


def gate(value, *others):
    return gate_all((value,), *others)[0]


def choose(core, first, second):
    return jnp.where(core == 0, first, second), jnp.where(core == 0, second, first)


def pair_rows(first, second):
    core = lax.axis_index("dp") % 2
    keep, send = choose(core, first, second)
    return jnp.concatenate(choose(core, keep, swap(send, "dp", 1)))


def chip_parts(rows):
    count = lax.axis_size("dp") // 2
    return [rows] + [swap(rows, "dp", 2 * step) for step in range(1, count)]


def gather_chips(rows):
    count = lax.axis_size("dp")
    groups = [list(range(core, count, 2)) for core in range(2)]
    return lax.all_gather(rows, "dp", axis=0, tiled=True, axis_index_groups=groups)


def sum_chips(blocks):
    if len(blocks) == 1:
        count, chip = lax.axis_size("dp") // 2, lax.axis_index("dp") // 2
        rows = blocks[0].reshape((count, -1) + blocks[0].shape[1:])
        blocks = [
            lax.dynamic_index_in_dim(rows, chip ^ step, 0, keepdims=False) for step in range(count)
        ]
    return [swap(block, "dp", 2 * step) if step else block for step, block in enumerate(blocks)]


def finish_pair(parts):
    core = lax.axis_index("dp") % 2
    rows = sum(part.astype(F32) for part in parts)
    half = rows.shape[0] // 2
    keep, send = choose(core, rows[:half], rows[half:])
    return choose(core, keep, swap(send, "dp", 1))


def in_order(parts, axis):
    me = lax.axis_index(axis)
    stacked = jnp.stack(parts)
    ordered = [
        lax.dynamic_index_in_dim(stacked, me ^ place, 0, keepdims=False) for place in range(len(parts))
    ]
    return jnp.concatenate(ordered)


def exchange_shares(partial, axis):
    count = lax.axis_size(axis)
    blocks = partial.reshape((count, partial.shape[0] // count) + partial.shape[1:])
    return exchange(blocks, axis)


def tile_range(meta_ref, latents, tile, core):
    lane = lax.broadcasted_iota(jnp.int32, (1, 256), 1)
    first = tile * 512 + core * 128
    last = first + 383
    place = first + lane + jnp.where(lane >= 128, 128, 0)
    begin = jnp.zeros((1, 256), jnp.int32)
    finish = jnp.zeros((1, 256), jnp.int32)
    low = jnp.int32(0)
    high = jnp.int32(0)
    start = jnp.int32(0)
    for number in range(latents):
        end = start + meta_ref[1 + number]
        inside = (place >= start) & (place < end)
        begin = jnp.where(inside, start, begin)
        finish = jnp.where(inside, end, finish)
        low = jnp.where((first >= start) & (first < end), start, low)
        high = jnp.where((last >= start) & (last < end), end, high)
        start = end
    return begin, finish, low // 256, (high + 255) // 256


def pair(ref, tile, start):
    left = ref[2 * tile, :, start : start + 128]
    right = ref[2 * tile + 1, :, start : start + 128]
    return jnp.concatenate([left, right], axis=1)


def key_mask(block, begin, finish):
    place = block * 256 + lax.broadcasted_iota(jnp.int32, (256, 256), 0)
    return (place >= begin) & (place < finish)


def forward_kernel(latents, meta_ref, packed_ref, out_ref, exact_ref, log_ref, keys, scores):
    blocks = packed_ref.shape[0]
    core = meta_ref[0]
    for block in range(blocks):
        keys[block] = packed_ref[block, :, :256].astype(F32).T.astype(BF16)
    for tile in range(blocks // 2):
        begin, finish, low, high = tile_range(meta_ref, latents, tile, core)
        query = pair(packed_ref, tile, 512)

        def score(block, largest):
            raw = jnp.dot(keys[block], query, preferred_element_type=F32) * SCALE
            raw = jnp.where(key_mask(block, begin, finish), raw, NEGATIVE)
            scores[block] = raw
            return jnp.maximum(largest, jnp.max(raw, axis=0, keepdims=True))

        largest = lax.fori_loop(low, high, score, jnp.full((1, 256), NEGATIVE, F32))

        def mix(block, carry):
            total, mixed = carry
            weights = jnp.exp(scores[block] - largest)
            total = total + jnp.sum(weights, axis=0, keepdims=True)
            values = packed_ref[block, :, 256:512]
            mixed = mixed + jnp.dot(values, weights.astype(BF16), preferred_element_type=F32)
            return total, mixed

        total, mixed = lax.fori_loop(
            low, high, mix, (jnp.zeros((1, 256), F32), jnp.zeros((DH, 256), F32))
        )
        mixed = mixed / total
        log_total = largest + jnp.log(total)
        for half in range(2):
            part = mixed[:, half * 128 : half * 128 + 128]
            exact_ref[2 * tile + half] = part
            out_ref[2 * tile + half] = part.astype(BF16)
            log_ref[2 * tile + half] = log_total[:, half * 128 : half * 128 + 128]


def backward_kernel(
    latents, meta_ref, packed_ref, grad_ref, exact_ref, log_ref, out_ref, keys, values, d_keys, d_values
):
    blocks = packed_ref.shape[0]
    core = meta_ref[0]
    for block in range(blocks):
        keys[block] = packed_ref[block, :, :256].astype(F32).T.astype(BF16)
        values[block] = packed_ref[block, :, 256:512].astype(F32).T.astype(BF16)
    d_keys[...] = jnp.zeros_like(d_keys)
    d_values[...] = jnp.zeros_like(d_values)
    by_query = (((1,), (1,)), ((), ()))
    for tile in range(blocks // 2):
        begin, finish, low, high = tile_range(meta_ref, latents, tile, core)
        query = pair(packed_ref, tile, 512)
        grad = pair(grad_ref, tile, 0)
        inner = jnp.sum(grad.astype(F32) * pair(exact_ref, tile, 0), axis=0, keepdims=True)
        log_total = pair(log_ref, tile, 0)

        def step(block, d_query):
            raw = jnp.dot(keys[block], query, preferred_element_type=F32) * SCALE
            probs = jnp.where(key_mask(block, begin, finish), jnp.exp(raw - log_total), 0.0)
            d_probs = jnp.dot(values[block], grad, preferred_element_type=F32)
            d_scores = (probs * (d_probs - inner)).astype(BF16)
            d_values[block] += lax.dot_general(
                grad, probs.astype(BF16), by_query, preferred_element_type=F32
            )
            d_keys[block] += lax.dot_general(query, d_scores, by_query, preferred_element_type=F32)
            key_rows = packed_ref[block, :, :256]
            return d_query + jnp.dot(key_rows, d_scores, preferred_element_type=F32)

        d_query = lax.fori_loop(low, high, step, jnp.zeros((DH, 256), F32)) * SCALE
        for half in range(2):
            part = d_query[:, half * 128 : half * 128 + 128]
            out_ref[2 * tile + half, :, 512:640] = part.astype(BF16)
    for block in range(blocks):
        out_ref[block, :, :256] = (d_keys[block] * SCALE).astype(BF16)
        out_ref[block, :, 256:512] = d_values[block].astype(BF16)


def attend_forward(meta, packed):
    blocks = packed.shape[0]
    shape = jax.ShapeDtypeStruct
    return pl.pallas_call(
        lambda *refs: forward_kernel(meta.shape[0] - 1, *refs),
        out_shape=(
            shape((blocks, DH, 128), BF16),
            shape((blocks, DH, 128), F32),
            shape((blocks, 1, 128), F32),
        ),
        in_specs=[
            pl.BlockSpec(memory_space=pltpu.SMEM),
            pl.BlockSpec(memory_space=pltpu.VMEM),
        ],
        out_specs=tuple([pl.BlockSpec(memory_space=pltpu.VMEM)] * 3),
        scratch_shapes=[
            pltpu.VMEM((blocks, 256, DH), BF16),
            pltpu.VMEM((blocks, 256, 256), F32),
        ],
        compiler_params=pltpu.CompilerParams(vmem_limit_bytes=VMEM_BYTES),
        cost_estimate=pl.CostEstimate(flops=10**9, bytes_accessed=4 * 10**6, transcendentals=10**6),
        name="attend_forward",
    )(meta, packed)


def attend_backward(meta, packed, grad, exact, log_total):
    blocks = packed.shape[0]
    return pl.pallas_call(
        lambda *refs: backward_kernel(meta.shape[0] - 1, *refs),
        out_shape=jax.ShapeDtypeStruct(packed.shape, BF16),
        in_specs=[pl.BlockSpec(memory_space=pltpu.SMEM)]
        + [pl.BlockSpec(memory_space=pltpu.VMEM)] * 4,
        out_specs=pl.BlockSpec(memory_space=pltpu.VMEM),
        scratch_shapes=[
            pltpu.VMEM((blocks, 256, DH), BF16),
            pltpu.VMEM((blocks, 256, DH), BF16),
            pltpu.VMEM((blocks, DH, 256), F32),
            pltpu.VMEM((blocks, DH, 256), F32),
        ],
        compiler_params=pltpu.CompilerParams(vmem_limit_bytes=VMEM_BYTES),
        cost_estimate=pl.CostEstimate(flops=3 * 10**9, bytes_accessed=4 * 10**6, transcendentals=10**6),
        name="attend_backward",
    )(meta, packed, grad, exact, log_total)


class HeadSplit:
    def __init__(self, latent_len, rows):
        self.rows = rows
        self.meta = jnp.concatenate([lax.axis_index("dp").astype(jnp.int32)[None] % 2, latent_len])

    def forward(self, packed):
        self.packed = exchange(packed, "dp")
        out, self.exact, self.log_total = attend_forward(self.meta, self.packed)
        return exchange(out, "dp")

    def backward(self, grad, due):
        grad = exchange(grad, "dp")
        out = attend_backward(self.meta, self.packed, grad, self.exact, self.log_total)
        return exchange(gate(out, *due), "dp")


class Window:
    def __init__(self, latent_len, rows):
        self.rows = rows
        self.reach = (SEQ - 2) // rows + 1
        total = rows * lax.axis_size("dp")
        first = lax.axis_index("dp") * rows
        own = latent_index(latent_len, first, rows, total)
        ids = [
            latent_index(latent_len, first + offset * rows, rows, total)
            for offset in range(-self.reach, self.reach + 1)
        ]
        self.allowed = own[:, None] == jnp.concatenate(ids)[None, :]

    def from_behind(self, block, distance):
        devices = range(lax.axis_size("dp"))
        return lax.ppermute(
            block, "dp", [(i - distance, i) for i in devices if i - distance in devices]
        )

    def head_scores(self, query, key):
        raw = jnp.einsum("eq,ek->qk", query, key, preferred_element_type=F32) * SCALE
        return jnp.where(self.allowed, raw, NEGATIVE)

    def forward(self, packed):
        rows = self.rows
        split = packed.reshape(-1, 2, DH, rows * 5 // 2)
        query = jnp.concatenate([split[:, 0, :, 2 * rows :], split[:, 1, :, 2 * rows :]], axis=2)
        projected = jnp.stack([query, split[:, 0, :, :rows], split[:, 0, :, rows : 2 * rows]])
        key_value = projected[1:]
        pieces = [
            key_value if offset == 0 else self.from_behind(key_value, -offset)
            for offset in range(-self.reach, self.reach + 1)
        ]
        window = jnp.concatenate(pieces, axis=3)
        self.operands = (projected[0], window[0], window[1])

        def one(operands):
            query, key, value = operands
            scores = self.head_scores(query, key)
            largest = jnp.max(scores, axis=1, keepdims=True)
            weights = jnp.exp(scores - largest)
            totals = jnp.sum(weights, axis=1, keepdims=True)
            probs = (weights / totals).astype(BF16)
            mixed = jnp.einsum("qk,ek->eq", probs, value, preferred_element_type=F32)
            return mixed.astype(BF16), (largest + jnp.log(totals))[:, 0]

        out, self.log_total = lax.map(one, self.operands)
        out = out.reshape(-1, DH, 2, rows // 2).transpose(0, 2, 1, 3)
        return out.reshape(-1, DH, rows // 2)

    def backward(self, grad, due):
        rows, reach = self.rows, self.reach
        halves = grad.reshape(-1, 2, DH, rows // 2)
        grads = jnp.concatenate([halves[:, 0], halves[:, 1]], axis=2)

        def one(operands):
            query, key, value, grad, log_total = operands
            probs = jnp.exp(self.head_scores(query, key) - log_total[:, None])
            d_value = jnp.einsum("qk,eq->ek", probs.astype(BF16), grad, preferred_element_type=F32)
            d_probs = jnp.einsum("eq,ek->qk", grad, value, preferred_element_type=F32)
            inner = jnp.sum(probs * d_probs, axis=1, keepdims=True)
            d_scores = (probs * (d_probs - inner)).astype(BF16)
            d_query = jnp.einsum("qk,ek->eq", d_scores, key, preferred_element_type=F32) * SCALE
            d_key = jnp.einsum("qk,eq->ek", d_scores, query, preferred_element_type=F32) * SCALE
            return d_query, d_key, d_value

        d_query, d_key, d_value = lax.map(one, self.operands + (grads, self.log_total))
        d_window = jnp.stack([d_key, d_value])
        d_key_value = d_window[..., reach * rows : (reach + 1) * rows]
        for offset in range(-reach, reach + 1):
            if offset != 0:
                block = d_window[..., (offset + reach) * rows : (offset + reach + 1) * rows]
                d_key_value = d_key_value + self.from_behind(block, offset)
        wide = jnp.concatenate([d_key_value[0], d_key_value[1]], axis=2)
        wide = jnp.stack([wide, jnp.zeros_like(wide)], axis=1)
        halves = d_query.reshape(-1, DH, 2, rows // 2).transpose(0, 2, 1, 3)
        packed = jnp.concatenate([wide, halves], axis=3).astype(BF16)
        return packed.reshape(-1, DH, rows * 5 // 2)


META = 4


def vmem(count):
    return [pl.BlockSpec(memory_space=pltpu.VMEM)] * count


def call(body, name, meta, arrays, outs, scratch=(), anywhere=0, due=(), flops=1):
    count = 1 + len(arrays)

    def kernel(*refs):
        body(*refs[:count], *refs[count + len(due) :])

    return pl.pallas_call(
        kernel,
        out_shape=tuple(jax.ShapeDtypeStruct(shape, kind) for shape, kind in outs),
        in_specs=[pl.BlockSpec(memory_space=pltpu.SMEM)]
        + [pl.BlockSpec(memory_space=pl.ANY)] * anywhere
        + vmem(len(arrays) - anywhere)
        + [pl.BlockSpec(memory_space=pl.ANY)] * len(due),
        out_specs=tuple(vmem(len(outs))),
        scratch_shapes=list(scratch),
        compiler_params=pltpu.CompilerParams(vmem_limit_bytes=VMEM_BYTES),
        cost_estimate=pl.CostEstimate(flops=flops, bytes_accessed=1, transcendentals=0),
        name=name,
    )(meta, *arrays, *due)


def row_masks(meta_ref, latents, first, rows):
    place = first + lax.broadcasted_iota(jnp.int32, (rows, 1), 0)
    ids = jnp.zeros((rows, 1), jnp.int32)
    end = jnp.int32(0)
    for number in range(latents - 1):
        end = end + meta_ref[META + number]
        ids = ids + (place >= end).astype(jnp.int32)
    return [(ids == number).astype(F32) for number in range(latents)]


def rows_of(mod_ref, masks, feature):
    out = masks[0] * mod_ref[feature : feature + 1, :]
    for number in range(1, len(masks)):
        row = number * 6 + feature
        out = out + masks[number] * mod_ref[row : row + 1, :]
    return out


def latent_sums(out_ref, masks, values, feature, features):
    rounded = values.astype(BF16).astype(F32)
    for number, mask in enumerate(masks):
        row = number * features + feature
        out_ref[row : row + 1, :] = jnp.sum(mask * rounded, axis=0, keepdims=True)


def own_rows(meta_ref, ref, share):
    start = pl.multiple_of(meta_ref[2] * share, share)
    return ref[pl.ds(start, share), :].astype(F32)


def on_core(meta_ref, body, mine, other):
    @pl.when(meta_ref[0] == 0)
    def _():
        body(mine, other)

    @pl.when(meta_ref[0] != 0)
    def _():
        body(other, mine)


def place_rows(meta_ref, parts, whole, sems):
    block = parts[0].shape[0]
    copies = []
    for step, part in enumerate(parts):
        start = pl.multiple_of((meta_ref[3] ^ step) * block, 16)
        copies.append(
            pltpu.make_async_copy(part, whole.at[pl.ds(start, block), :], sems.at[step])
        )
    return copies


def place_pair(meta_ref, mine, other, first_ref, second_ref, sems):
    def body(first, second):
        copies = place_rows(meta_ref, first, first_ref, sems.at[0])
        copies += place_rows(meta_ref, second, second_ref, sems.at[1])
        for copy in copies:
            copy.start()
        for copy in copies:
            copy.wait()

    on_core(meta_ref, body, mine, other)


def project_kernel(latents, count, meta_ref, *refs):
    mine, other = refs[:count], refs[count : 2 * count]
    tokens_ref, cot_ref, mod_parts_ref, bias_ref = refs[2 * count : 2 * count + 4]
    hidden_ref, d_mlp_ref, packed_ref, qk_ref, vp_ref, d_bias_ref, mod_ref, sems = refs[2 * count + 4 :]
    rows, width = tokens_ref.shape
    place_pair(meta_ref, mine, other, qk_ref, vp_ref, sems)
    columns = mod_parts_ref.shape[2]
    pieces = width // columns
    for piece in range(pieces):
        total = mod_parts_ref[piece].astype(F32)
        for part in range(piece + pieces, mod_parts_ref.shape[0], pieces):
            total = total + mod_parts_ref[part].astype(F32)
        mod_ref[:, piece * columns : (piece + 1) * columns] = total
    masks = row_masks(meta_ref, latents, meta_ref[1], rows)
    unit, _ = normed(tokens_ref[...].astype(F32))
    hidden = unit * (1.0 + rows_of(mod_ref, masks, 1)) + rows_of(mod_ref, masks, 0)
    hidden_ref[...] = hidden.astype(BF16)
    d_mlp = (cot_ref[...].astype(F32) * rows_of(mod_ref, masks, 5)).astype(BF16)
    d_mlp_ref[...] = d_mlp
    d_bias_ref[...] = jnp.sum(d_mlp.astype(F32), axis=0, keepdims=True)
    heads = packed_ref.shape[0] // 2
    features = heads * DH
    left = hidden_ref[...]
    both = jnp.dot(left, qk_ref[...], preferred_element_type=F32) + bias_ref[0:1, :]
    both = both.T
    value = jnp.dot(left, vp_ref[...], preferred_element_type=F32) + bias_ref[1:2, :]
    value = value.T
    for head in range(heads):
        start = head * DH
        query = both[start : start + DH].astype(BF16)
        key = both[features + start : features + start + DH].astype(BF16)
        val = value[start : start + DH].astype(BF16)
        for half in range(2):
            packed_ref[2 * head + half, :, :rows] = key
            packed_ref[2 * head + half, :, rows : 2 * rows] = val
            packed_ref[2 * head + half, :, 2 * rows :] = query[
                :, half * (rows // 2) : (half + 1) * (rows // 2)
            ]


def attend_out_kernel(meta_ref, parts_ref, vp_ref, part_ref, attended_ref):
    heads = parts_ref.shape[0] // 2
    rows = part_ref.shape[0]
    stacked = [jnp.zeros((heads * DH, rows), F32)]
    for head in range(heads):
        left = parts_ref[2 * head].astype(F32)
        right = parts_ref[2 * head + 1].astype(F32)
        stacked.append(jnp.concatenate([left, right], axis=1))
    attended_ref[...] = jnp.concatenate(stacked, axis=0).T.astype(BF16)
    part_ref[...] = lax.dot_general(
        attended_ref[...], vp_ref[...], (((1,), (1,)), ((), ())), preferred_element_type=F32
    ).astype(BF16)


def middle_kernel(
    latents, meta_ref, parts_ref, tokens_ref, mod_ref, bias_ref, sent_ref, attn_ref, mid_ref
):
    copies, share, width = parts_ref.shape
    masks = row_masks(meta_ref, latents, meta_ref[1] + meta_ref[2] * share, share)
    attn = bias_ref[...].astype(F32)
    for part in range(copies):
        attn = attn + parts_ref[part].astype(F32)
    attn_ref[...] = attn
    mid = own_rows(meta_ref, tokens_ref, share) + rows_of(mod_ref, masks, 2) * attn
    mid_ref[...] = mid
    unit, _ = normed(mid)
    hidden = unit * (1.0 + rows_of(mod_ref, masks, 4)) + rows_of(mod_ref, masks, 3)
    for part in range(copies):
        sent_ref[part] = hidden.astype(BF16)


def mlp_kernel(count, meta_ref, *refs):
    mine, other = refs[:count], refs[count : 2 * count]
    hidden_ref, d_mlp_ref, bias_ref = refs[2 * count : 2 * count + 3]
    d_two_ref, gelu_ref, d_pre_ref, d_bias_ref, left_ref, right_ref = refs[2 * count + 3 : 2 * count + 9]
    mlp_refs = refs[2 * count + 9 : -5]
    fc1_ref, fc2_ref, d_two_sum, mlp_sum, sems = refs[-5:]
    place_pair(meta_ref, mine, other, fc1_ref, fc2_ref, sems)
    d_two_sum[...] = jnp.zeros_like(d_two_sum)
    mlp_sum[...] = jnp.zeros_like(mlp_sum)
    tile = 384
    by_last = (((1,), (1,)), ((), ()))

    def step(number, carry):
        units = pl.ds(pl.multiple_of(number * tile, tile), tile)
        fc1, fc2 = fc1_ref[:, units], fc2_ref[:, units]
        pre = jnp.dot(hidden_ref[...], fc1, preferred_element_type=F32)
        gelu, slope = gelu_pair(pre + bias_ref[:, units].astype(F32))
        grad = jnp.dot(d_mlp_ref[...], fc2, preferred_element_type=F32)
        d_pre = (grad * slope).astype(BF16)
        gelu = gelu.astype(BF16)
        gelu_ref[:, units] = gelu
        d_pre_ref[:, units] = d_pre
        d_bias_ref[:, units] = jnp.sum(d_pre.astype(F32), axis=0, keepdims=True)
        d_two_sum[...] += lax.dot_general(d_pre, fc1, by_last, preferred_element_type=F32)
        mlp_sum[...] += lax.dot_general(gelu, fc2, by_last, preferred_element_type=F32)
        return carry

    lax.fori_loop(0, fc1_ref.shape[1] // tile, step, 0)
    d_two_ref[...] = d_two_sum[...].astype(BF16)
    def sent(left, right):
        left_ref[...] = left[0][...]
        right_ref[...] = left[1][...]

    on_core(meta_ref, sent, (d_mlp_ref, gelu_ref), (hidden_ref, d_pre_ref))
    share = mlp_refs[0].shape[0]
    for step, mlp_ref in enumerate(mlp_refs):
        start = pl.multiple_of((meta_ref[2] ^ step) * share, share)
        mlp_ref[...] = mlp_sum[pl.ds(start, share), :].astype(BF16)


def middle_back_kernel(
    latents, meta_ref, parts_ref, mid_in_ref, attn_ref, cot_ref, mod_ref, sent_ref, d_mid_ref, sums_ref
):
    copies, share, width = parts_ref.shape
    masks = row_masks(meta_ref, latents, meta_ref[1] + meta_ref[2] * share, share)
    d_hidden = parts_ref[0].astype(F32)
    for part in range(1, copies):
        d_hidden = d_hidden + parts_ref[part].astype(F32)
    unit, inverse = normed(mid_in_ref[...])
    d_mid = own_rows(meta_ref, cot_ref, share) + norm_back(
        unit, inverse, d_hidden * (1.0 + rows_of(mod_ref, masks, 4))
    )
    d_mid_ref[...] = d_mid
    d_attn = (d_mid * rows_of(mod_ref, masks, 2)).astype(BF16)
    for part in range(copies):
        sent_ref[part] = d_attn
    latent_sums(sums_ref, masks, d_mid * attn_ref[...], 0, 3)
    latent_sums(sums_ref, masks, d_hidden, 1, 3)
    latent_sums(sums_ref, masks, d_hidden * unit, 2, 3)


def result_kernel(
    latents, count, meta_ref, *refs
):
    parts = refs[:count]
    mid_ref, cot_ref, mod_ref, bias_ref, result_ref, sums_ref = refs[count:]
    share = result_ref.shape[0]
    masks = row_masks(meta_ref, latents, meta_ref[1] + meta_ref[2] * share, share)
    mlp = bias_ref[...].astype(F32)
    for part in parts:
        mlp = mlp + part[...].astype(F32)
    result_ref[...] = (mid_ref[...] + rows_of(mod_ref, masks, 5) * mlp).astype(BF16)
    latent_sums(sums_ref, masks, own_rows(meta_ref, cot_ref, share) * mlp, 0, 1)


def spread_kernel(meta_ref, d_attn_ref, vp_ref, packed_ref, d_bias_ref):
    grad = jnp.dot(d_attn_ref[...], vp_ref[...], preferred_element_type=F32).T
    half = grad.shape[1] // 2
    features = grad.shape[0] // 2
    for place in range(packed_ref.shape[0]):
        start = features + place // 2 * DH
        side = place % 2 * half
        packed_ref[place] = grad[start : start + DH, side : side + half].astype(BF16)
    d_bias_ref[...] = jnp.sum(d_attn_ref[...].astype(F32), axis=0, keepdims=True)


def unspread_kernel(
    meta_ref, parts_ref, qk_ref, vp_ref, d_one_ref, d_qk_ref, d_vp_ref, sent_ref, d_bias_ref
):
    heads = parts_ref.shape[0] // 2
    rows = d_one_ref.shape[0]
    query, key, value = [], [], []
    for head in range(heads):
        left = parts_ref[2 * head].astype(F32)
        right = parts_ref[2 * head + 1].astype(F32)
        both = left[:, : 2 * rows] + right[:, : 2 * rows]
        key.append(both[:, :rows])
        value.append(both[:, rows:])
        query.append(jnp.concatenate([left[:, 2 * rows :], right[:, 2 * rows :]], axis=1))
    d_qk_ref[...] = jnp.concatenate(query + key, axis=0).T.astype(BF16)
    blank = jnp.zeros((heads * DH, rows), F32)
    d_vp_ref[...] = jnp.concatenate(value + [blank], axis=0).T.astype(BF16)
    tile = 384
    by_last = (((1,), (1,)), ((), ()))

    def step(number, carry):
        columns = pl.ds(pl.multiple_of(number * tile, tile), tile)
        total = lax.dot_general(d_qk_ref[...], qk_ref[columns, :], by_last, preferred_element_type=F32)
        total += lax.dot_general(d_vp_ref[...], vp_ref[columns, :], by_last, preferred_element_type=F32)
        d_one_ref[:, columns] = total.astype(BF16)
        return carry

    lax.fori_loop(0, qk_ref.shape[0] // tile, step, 0)

    def sent(first, second):
        sent_ref[...] = first[...]

    on_core(meta_ref, sent, d_vp_ref, d_qk_ref)
    d_bias_ref[0:1, :] = jnp.sum(d_qk_ref[...].astype(F32), axis=0, keepdims=True)
    d_bias_ref[1:2, :] = jnp.sum(d_vp_ref[...].astype(F32), axis=0, keepdims=True)


def weight_kernel(first_pairs, second_pairs, meta_ref, *refs):
    operands = 1 + max(max(pair) for pair in first_pairs + second_pairs)
    ins, outs, total = refs[:operands], refs[operands:-1], refs[-1]
    tile = 384

    def body(pairs):
        def step(number, carry):
            columns = pl.ds(pl.multiple_of(number * tile, tile), tile)
            block = jnp.zeros((tile, total.shape[1]), F32)
            for left, right in pairs:
                block += lax.dot_general(
                    ins[left][:, columns], ins[right][...], (((0,), (0,)), ((), ())),
                    preferred_element_type=F32,
                )
            total[columns, :] = block.astype(BF16)
            return carry

        lax.fori_loop(0, total.shape[0] // tile, step, 0)

    on_core(meta_ref, lambda pairs, _: body(pairs), first_pairs, second_pairs)
    rows = outs[0].shape[0]
    for step, out in enumerate(outs):
        start = pl.multiple_of((meta_ref[3] ^ step) * rows, 16)
        out[...] = total[pl.ds(start, rows), :]


def first_back_kernel(
    latents, meta_ref, parts_ref, tokens_ref, d_mid_ref, mod_ref, mid_sums_ref, last_sums_ref,
    fc2_bias_ref, proj_bias_ref, fc1_bias_ref, qv_bias_ref, grad_ref, sent_ref, bias_ref, first_sums,
):
    copies, share, width = parts_ref.shape
    masks = row_masks(meta_ref, latents, meta_ref[1] + meta_ref[2] * share, share)
    d_hidden = parts_ref[0].astype(F32)
    for part in range(1, copies):
        d_hidden = d_hidden + parts_ref[part].astype(F32)
    unit, inverse = normed(own_rows(meta_ref, tokens_ref, share))
    grad = d_mid_ref[...] + norm_back(unit, inverse, d_hidden * (1.0 + rows_of(mod_ref, masks, 1)))
    grad_ref[...] = grad.astype(BF16)
    latent_sums(first_sums, masks, d_hidden, 0, 2)
    latent_sums(first_sums, masks, d_hidden * unit, 1, 2)
    columns = width // copies
    for number in range(latents):
        for feature in range(6):
            if feature < 2:
                row = first_sums[number * 2 + feature : number * 2 + feature + 1, :]
            elif feature < 5:
                place = number * 3 + feature - 2
                row = mid_sums_ref[place : place + 1, :]
            else:
                row = last_sums_ref[number : number + 1, :]
            place = number * 6 + feature
            for part in range(copies):
                sent_ref[part, place : place + 1, :] = row[:, part * columns : (part + 1) * columns]
    place = 0
    for ref in (fc2_bias_ref, proj_bias_ref, fc1_bias_ref):
        for start in range(0, ref.shape[1], columns):
            bias_ref[place : place + 1, :] = ref[:, start : start + columns]
            place += 1
    bias_ref[place : place + 2, :] = qv_bias_ref[:, :columns]


def finish_kernel(
    latents, meta_ref, sums_ref, active_ref, w_ada_ref,
    w_grad_ref, b_grad_ref, d_active_ref, fc2_ref, proj_ref, fc1_ref, qv_ref, total_ref,
):
    total = sums_ref[0]
    for part in range(1, sums_ref.shape[0]):
        total = total + sums_ref[part]
    total_ref[...] = total
    by_last = (((1,), (1,)), ((), ()))
    d_active = jnp.zeros(d_active_ref.shape, F32)
    for feature in range(6):
        rows = [
            total_ref[number * 6 + feature : number * 6 + feature + 1, :] for number in range(latents)
        ]
        grad = active_ref[:, 0:1] * rows[0]
        bias = rows[0]
        for number in range(1, latents):
            grad = grad + active_ref[:, number : number + 1] * rows[number]
            bias = bias + rows[number]
        w_grad_ref[feature] = grad
        b_grad_ref[feature : feature + 1, :] = bias
        wide = jnp.concatenate(rows, axis=0)
        high = wide.astype(BF16)
        low = (wide - high.astype(F32)).astype(BF16)
        weight = w_ada_ref[feature]
        d_active += lax.dot_general(high, weight, by_last, preferred_element_type=F32)
        d_active += lax.dot_general(low, weight, by_last, preferred_element_type=F32)
    d_active_ref[...] = d_active
    columns = total_ref.shape[1]
    place = 6 * latents
    for ref in (fc2_ref, proj_ref, fc1_ref):
        for start in range(0, ref.shape[1], columns):
            ref[:, start : start + columns] = total_ref[place : place + 1, :]
            place += 1
    qv_ref[...] = total_ref[place : place + 2, :]


def latent_index(latent_len, first_row, row_count, token_total):
    positions = first_row + jnp.arange(row_count, dtype=jnp.int32)
    ends = jnp.cumsum(latent_len, dtype=jnp.int32)
    found = jnp.sum((positions[:, None] >= ends[None, :]).astype(jnp.int32), axis=1, dtype=jnp.int32)
    return jnp.where((positions >= 0) & (positions < token_total), found, -1)


def normed(values):
    average = jnp.mean(values, axis=-1, keepdims=True)
    centred = values - average
    spread = jnp.mean(centred * centred, axis=-1, keepdims=True)
    inverse = lax.rsqrt(spread + NORM_EPS)
    return centred * inverse, inverse


def norm_back(unit, inverse, grad):
    along = jnp.mean(grad * unit, axis=-1, keepdims=True)
    return inverse * (grad - jnp.mean(grad, axis=-1, keepdims=True) - unit * along)


def gelu_pair(value):
    root = math.sqrt(2.0 / math.pi)
    bend = jnp.tanh(root * (value + 0.044715 * value * value * value))
    slope = root * (1.0 + 3.0 * 0.044715 * value * value)
    gelu = 0.5 * value * (1.0 + bend)
    return gelu, 0.5 * (1.0 + bend) + 0.5 * value * (1.0 - bend * bend) * slope


def local(
    tokens,
    conditioning,
    latent_len,
    w_ada,
    b_ada,
    w_qkv,
    b_qv,
    w_proj,
    b_proj,
    w_fc1,
    b_fc1,
    w_fc2,
    b_fc2,
    cotangent,
):
    rows, width = tokens.shape
    share_width = w_qkv.shape[0]
    features = w_qkv.shape[2]
    units = w_fc1.shape[1]
    heads = features // DH
    latents = conditioning.shape[0]
    n_dp, n_tensor = lax.axis_size("dp"), lax.axis_size("tensor")
    my_dp, my_tensor = lax.axis_index("dp"), lax.axis_index("tensor")
    share = rows // n_tensor

    core = my_dp % 2
    qk = w_qkv[:, :2].reshape(share_width, 2 * features)
    vp = jnp.concatenate([w_qkv[:, 2], w_proj.T], axis=1)
    early_rows = pair_rows(qk, vp)

    cond = conditioning.astype(F32)
    sigmoid = 1.0 / (1.0 + jnp.exp(-cond))
    activated = (cond * sigmoid).astype(BF16)
    own_activated = lax.dynamic_slice_in_dim(activated, my_dp * share_width, share_width, 1)
    flat_ada = w_ada.reshape(share_width, 6 * features)
    mod_part = jnp.dot(own_activated, flat_ada, preferred_element_type=F32)
    mod_part = mod_part.reshape(latents * 6, features)
    bias_ada = jnp.tile(b_ada.astype(F32), (latents, 1))
    few_chips = n_dp // 2 == 4
    early_rows = gate(early_rows, mod_part)
    mod_mine = jnp.sum(gather(mod_part, "dp", n_dp), axis=0) + bias_ada
    mod_parts = gather(mod_mine, "tensor", n_tensor)
    early_parts = chip_parts(early_rows) if few_chips else [gather_chips(early_rows)]

    early_parts = list(gate_all(early_parts, mod_parts))
    early_parts += [swap(part, "dp", 1) for part in early_parts]
    count = len(early_parts) // 2
    meta = jnp.stack([core, my_dp * rows, my_tensor, my_dp // 2]).astype(jnp.int32)
    meta = jnp.concatenate([meta, latent_len])
    place_meta = meta if few_chips else meta.at[3].set(0)
    by_last = (((1,), (1,)), ((), ()))
    by_token = (((0,), (0,)), ((), ()))
    bias = jnp.concatenate([b_qv[0], jnp.zeros_like(b_qv[0]), b_qv[1], jnp.zeros_like(b_qv[0])])
    hidden_one, d_mlp, packed, full_qk, full_vp, d_bias_fc2, mod_rows = call(
        lambda *refs: project_kernel(latents, count, *refs),
        "project",
        place_meta,
        (*early_parts, tokens, cotangent, mod_parts, bias.astype(F32).reshape(2, -1)),
        (((rows, width), BF16), ((rows, width), BF16), ((2 * heads, DH, rows * 5 // 2), BF16))
        + (((width, 2 * features), BF16),) * 2
        + (((1, width), F32), ((6 * latents, width), F32)),
        [pltpu.SemaphoreType.DMA((2, count))],
        2 * count,
    )
    late_rows = pair_rows(w_fc1, w_fc2.T)
    hidden_other = swap(hidden_one, "dp", 1)
    split = HeadSplit if 2 * heads == n_dp else Window
    attention = split(latent_len, rows)
    attended_parts = attention.forward(packed)
    late_rows = gate(late_rows, attended_parts)
    late_parts = chip_parts(late_rows)[:-1] if few_chips else [gather_chips(late_rows)]
    attn_part, attended = call(
        attend_out_kernel,
        "attend_out",
        meta,
        (attended_parts, full_vp),
        (((rows, width), BF16), ((rows, 2 * features), BF16)),
    )
    attn_parts = exchange_shares(attn_part, "tensor")
    hidden_blocks, attn_out, residual_mid = call(
        lambda *refs: middle_kernel(latents, *refs),
        "middle",
        meta,
        (attn_parts, tokens, mod_rows, b_proj.reshape(1, -1)),
        (((n_tensor, share, width), BF16), ((share, width), F32), ((share, width), F32)),
        due=late_parts[1:],
    )
    hidden_two = exchange(hidden_blocks, "tensor").reshape(rows, width)
    if few_chips:
        last_part = swap(gate(late_rows, attn_out), "dp", n_dp - 2)
        late_parts.append(gate(last_part, hidden_two))
    late_other = [swap(part, "dp", 1) for part in late_parts]

    d_two_part, gelu_out, d_pre, d_bias_fc1, left_sent, right_sent, *mlp_blocks = call(
        lambda *refs: mlp_kernel(count, *refs),
        "mlp",
        place_meta,
        (*late_parts, *late_other, hidden_two, d_mlp, b_fc1.reshape(1, -1)),
        (((rows, width), BF16), ((rows, units), BF16), ((rows, units), BF16), ((1, units), F32))
        + (((rows, width), BF16), ((rows, units), BF16))
        + (((share, width), BF16),) * n_tensor,
        [pltpu.VMEM((width, units), BF16)] * 2
        + [pltpu.VMEM((rows, width), F32)] * 2
        + [pltpu.SemaphoreType.DMA((2, count))],
        2 * count,
    )
    d_two_parts = exchange_shares(d_two_part, "tensor")

    chips = n_dp // 2 if few_chips else 1
    left_other = swap(left_sent, "dp", 1)
    right_other = swap(right_sent, "dp", 1)
    late_blocks = call(
        lambda *refs: weight_kernel([(0, 2), (4, 5)], [(1, 3), (4, 5)], *refs),
        "late_weights",
        place_meta,
        (hidden_two, d_mlp, d_pre, gelu_out, left_other, right_other),
        (((width // chips, units), BF16),) * chips,
        [pltpu.VMEM((width, units), BF16)],
    )
    late_grads = sum_chips(late_blocks[:-1]) if few_chips else sum_chips(late_blocks)

    d_attn_blocks, d_mid, mid_sums = call(
        lambda *refs: middle_back_kernel(latents, *refs),
        "middle_back",
        meta,
        (d_two_parts, residual_mid, attn_out, cotangent, mod_rows),
        (((n_tensor, share, width), BF16), ((share, width), F32), ((3 * latents, width), F32)),
        due=late_blocks,
    )
    d_attn = exchange(d_attn_blocks, "tensor").reshape(rows, width)

    d_spread, d_bias_proj = call(
        spread_kernel,
        "spread",
        meta,
        (d_attn, full_vp),
        (((2 * heads, DH, rows // 2), BF16), ((1, width), F32)),
        due=late_grads[1:],
    )
    mlp_parts = mlp_blocks[:1] + [
        swap(gate(block, d_spread), "tensor", step)
        for step, block in enumerate(mlp_blocks)
        if step
    ]
    d_attn_other = swap(d_attn, "dp", 1)
    attended_other = swap(attended, "dp", 1)
    d_packed = attention.backward(d_spread, mlp_parts[1:])
    result_own, last_sums = call(
        lambda *refs: result_kernel(latents, n_tensor, *refs),
        "result",
        meta,
        (*mlp_parts, residual_mid, cotangent, mod_rows, b_fc2.reshape(1, -1)),
        (((share, width), BF16), ((latents, width), F32)),
    )
    d_one_part, d_qk, d_vp, d_sent, d_bias_qv = call(
        unspread_kernel,
        "unspread",
        meta,
        (d_packed, full_qk, full_vp),
        (((rows, width), BF16),)
        + (((rows, 2 * features), BF16),) * 3
        + (((2, 2 * features), F32),),
        flops=2 * 10**10,
    )
    result_parts = [result_own] + [swap(result_own, "tensor", bits) for bits in range(1, n_tensor)]
    d_one_part = gate(d_one_part, *result_parts[1:])
    d_one_parts = exchange_shares(d_one_part, "tensor")

    if few_chips:
        late_grads.append(swap(gate(late_blocks[-1], d_one_part), "dp", n_dp - 2))
    right_other = swap(d_sent, "dp", 1)
    early_blocks = call(
        lambda *refs: weight_kernel(
            [(0, 2), (5, 7)], [(0, 3), (1, 4), (5, 7), (6, 8)], *refs
        ),
        "early_weights",
        place_meta,
        (hidden_one, d_attn, d_qk, d_vp, attended, hidden_other, d_attn_other, right_other, attended_other),
        (((width // chips, 2 * features), BF16),) * chips,
        [pltpu.VMEM((width, 2 * features), BF16)],
    )
    grad_own, d_mod_part, bias_rows = call(
        lambda *refs: first_back_kernel(latents, *refs),
        "first_back",
        meta,
        (d_one_parts, tokens, d_mid, mod_rows, mid_sums, last_sums)
        + (d_bias_fc2, d_bias_proj, d_bias_fc1, d_bias_qv),
        (((share, width), BF16), ((n_tensor, 6 * latents, features), F32))
        + (((2 * (width // features) + units // features + 2, features), F32),),
        [pltpu.VMEM((2 * latents, width), F32)],
        due=early_blocks,
    )
    early_grads = sum_chips(gate_all(early_blocks, d_mod_part))
    d_mod_mine = exchange(d_mod_part, "tensor")
    d_mod_mine = jnp.sum(gate(d_mod_mine, *early_grads[1:3]) if few_chips else d_mod_mine, axis=0)
    grad_own = gate(grad_own, d_mod_mine)
    grad_parts = [grad_own] + [swap(grad_own, "tensor", bits) for bits in range(1, n_tensor)]
    sums = gather(jnp.concatenate([d_mod_mine, bias_rows]), "dp", n_dp)
    sums = gate(sums, early_grads[3]) if few_chips else sums
    grad_tokens = in_order(gate_all(grad_parts, sums), "tensor").astype(F32)
    result = in_order(gate_all(result_parts, sums), "tensor")
    grad_w_ada, grad_b_ada, d_active, sum_b_fc2, sum_b_proj, sum_b_fc1, sum_b_qv = call(
        lambda *refs: finish_kernel(latents, *refs),
        "finish",
        meta,
        (sums, own_activated.astype(F32).T, w_ada.transpose(1, 0, 2)),
        (((6, share_width, features), F32), ((6, features), F32), ((latents, share_width), F32))
        + (((1, width), F32), ((1, width), F32), ((1, units), F32), ((2, features), F32)),
        [pltpu.VMEM(sums.shape[1:], F32)],
    )
    d_active = gather(d_active, ("dp", "tensor"), n_dp * n_tensor)
    d_active = jnp.sum(d_active.reshape(n_dp, n_tensor, latents, share_width), axis=1)
    d_active = d_active.transpose(1, 0, 2).reshape(latents, width)
    grad_cond = d_active * (sigmoid * (1.0 + cond * (1.0 - sigmoid)))

    grad_fc1, grad_fc2 = finish_pair(late_grads)
    grad_qk, grad_vp = finish_pair(early_grads)
    grad_qkv = jnp.concatenate([grad_qk, grad_vp[:, :features]], axis=1)
    grad_qkv = grad_qkv.reshape(share_width, 3, features)

    return (
        result,
        grad_tokens,
        grad_cond,
        grad_w_ada.transpose(1, 0, 2),
        grad_b_ada,
        grad_qkv,
        sum_b_qv,
        grad_vp[:, features:].T,
        sum_b_proj[0],
        grad_fc1,
        sum_b_fc1[0],
        grad_fc2.T,
        sum_b_fc2[0],
    )


def solution(mesh):
    in_specs = (
        P("dp", None),
        P(),
        P(),
        P("dp", None, "tensor"),
        P(None, "tensor"),
        P("dp", None, "tensor"),
        P(None, "tensor"),
        P("tensor", "dp"),
        P(),
        P("dp", "tensor"),
        P("tensor"),
        P("tensor", "dp"),
        P(),
        P("dp", None),
    )
    out_specs = (
        P("dp", None),
        P("dp", None),
        P(),
        P("dp", None, "tensor"),
        P(None, "tensor"),
        P("dp", None, "tensor"),
        P(None, "tensor"),
        P("tensor", "dp"),
        P(),
        P("dp", "tensor"),
        P("tensor"),
        P("tensor", "dp"),
        P(),
    )
    return jax.shard_map(local, mesh=mesh, in_specs=in_specs, out_specs=out_specs, check_vma=False)
```

```python
import math

import jax
import jax.numpy as jnp
from jax import lax
from jax.experimental import pallas as pl
from jax.experimental.pallas import tpu as pltpu
from jax.sharding import PartitionSpec as P

DH = 72
SEQ = 1024
NORM_EPS = 1e-06
NEGATIVE = -1e30
SCALE = 1.0 / math.sqrt(DH)
VMEM_BYTES = 58 * 1024 * 1024
BF16 = jnp.bfloat16
F32 = jnp.float32


def swap(block, axis, bits):
    route = [(i, i ^ bits) for i in range(lax.axis_size(axis))]
    return lax.ppermute(block, axis, route)


def exchange(blocks, axis):
    return lax.all_to_all(blocks, axis, 0, 0, tiled=True)


def gather(block, axis, count):
    return exchange(jnp.broadcast_to(block[None], (count,) + block.shape), axis)


def gate_all(values, *others):
    anywhere = pl.BlockSpec(memory_space=pl.ANY)
    return pl.pallas_call(
        lambda *refs: None,
        out_shape=tuple(jax.ShapeDtypeStruct(value.shape, value.dtype) for value in values),
        in_specs=[anywhere] * (len(values) + len(others)),
        out_specs=(anywhere,) * len(values),
        input_output_aliases={place: place for place in range(len(values))},
        cost_estimate=pl.CostEstimate(flops=1, bytes_accessed=1, transcendentals=0),
        name="gate",
    )(*values, *others)


def gate(value, *others):
    return gate_all((value,), *others)[0]


def choose(core, first, second):
    return jnp.where(core == 0, first, second), jnp.where(core == 0, second, first)


def pair_rows(first, second):
    core = lax.axis_index("dp") % 2
    keep, send = choose(core, first, second)
    return jnp.concatenate(choose(core, keep, swap(send, "dp", 1)))


def chip_parts(rows):
    count = lax.axis_size("dp") // 2
    return [rows] + [swap(rows, "dp", 2 * step) for step in range(1, count)]


def gather_chips(rows):
    count = lax.axis_size("dp")
    groups = [list(range(core, count, 2)) for core in range(2)]
    return lax.all_gather(rows, "dp", axis=0, tiled=True, axis_index_groups=groups)


def sum_chips(blocks):
    if len(blocks) == 1:
        count, chip = lax.axis_size("dp") // 2, lax.axis_index("dp") // 2
        rows = blocks[0].reshape((count, -1) + blocks[0].shape[1:])
        blocks = [
            lax.dynamic_index_in_dim(rows, chip ^ step, 0, keepdims=False) for step in range(count)
        ]
    return [swap(block, "dp", 2 * step) if step else block for step, block in enumerate(blocks)]


def finish_pair(parts):
    core = lax.axis_index("dp") % 2
    rows = sum(part.astype(F32) for part in parts)
    half = rows.shape[0] // 2
    keep, send = choose(core, rows[:half], rows[half:])
    return choose(core, keep, swap(send, "dp", 1))


def exchange_shares(partial, axis):
    count = lax.axis_size(axis)
    blocks = partial.reshape((count, partial.shape[0] // count) + partial.shape[1:])
    return exchange(blocks, axis)


def tile_range(meta_ref, latents, tile, core):
    lane = lax.broadcasted_iota(jnp.int32, (1, 256), 1)
    first = tile * 512 + core * 128
    last = first + 383
    place = first + lane + jnp.where(lane >= 128, 128, 0)
    begin = jnp.zeros((1, 256), jnp.int32)
    finish = jnp.zeros((1, 256), jnp.int32)
    low = jnp.int32(0)
    high = jnp.int32(0)
    start = jnp.int32(0)
    for number in range(latents):
        end = start + meta_ref[1 + number]
        inside = (place >= start) & (place < end)
        begin = jnp.where(inside, start, begin)
        finish = jnp.where(inside, end, finish)
        low = jnp.where((first >= start) & (first < end), start, low)
        high = jnp.where((last >= start) & (last < end), end, high)
        start = end
    return begin, finish, low // 256, (high + 255) // 256


def pair(ref, tile, start):
    left = ref[2 * tile, :, start : start + 128]
    right = ref[2 * tile + 1, :, start : start + 128]
    return jnp.concatenate([left, right], axis=1)


def key_mask(block, begin, finish):
    place = block * 256 + lax.broadcasted_iota(jnp.int32, (256, 256), 0)
    return (place >= begin) & (place < finish)


def forward_kernel(latents, meta_ref, packed_ref, out_ref, exact_ref, log_ref, keys, scores):
    blocks = packed_ref.shape[0]
    core = meta_ref[0]
    for block in range(blocks):
        keys[block] = packed_ref[block, :, :256].astype(F32).T.astype(BF16)
    for tile in range(blocks // 2):
        begin, finish, low, high = tile_range(meta_ref, latents, tile, core)
        query = pair(packed_ref, tile, 512)

        def score(block, largest):
            raw = jnp.dot(keys[block], query, preferred_element_type=F32) * SCALE
            raw = jnp.where(key_mask(block, begin, finish), raw, NEGATIVE)
            scores[block] = raw
            return jnp.maximum(largest, jnp.max(raw, axis=0, keepdims=True))

        largest = lax.fori_loop(low, high, score, jnp.full((1, 256), NEGATIVE, F32))

        def mix(block, carry):
            total, mixed = carry
            weights = jnp.exp(scores[block] - largest)
            total = total + jnp.sum(weights, axis=0, keepdims=True)
            values = packed_ref[block, :, 256:512]
            mixed = mixed + jnp.dot(values, weights.astype(BF16), preferred_element_type=F32)
            return total, mixed

        total, mixed = lax.fori_loop(
            low, high, mix, (jnp.zeros((1, 256), F32), jnp.zeros((DH, 256), F32))
        )
        mixed = mixed / total
        log_total = largest + jnp.log(total)
        for half in range(2):
            part = mixed[:, half * 128 : half * 128 + 128]
            exact_ref[2 * tile + half] = part
            out_ref[2 * tile + half] = part.astype(BF16)
            log_ref[2 * tile + half] = log_total[:, half * 128 : half * 128 + 128]


def backward_kernel(
    latents, meta_ref, packed_ref, grad_ref, exact_ref, log_ref, out_ref, keys, values, d_keys, d_values
):
    blocks = packed_ref.shape[0]
    core = meta_ref[0]
    for block in range(blocks):
        keys[block] = packed_ref[block, :, :256].astype(F32).T.astype(BF16)
        values[block] = packed_ref[block, :, 256:512].astype(F32).T.astype(BF16)
    d_keys[...] = jnp.zeros_like(d_keys)
    d_values[...] = jnp.zeros_like(d_values)
    by_query = (((1,), (1,)), ((), ()))
    for tile in range(blocks // 2):
        begin, finish, low, high = tile_range(meta_ref, latents, tile, core)
        query = pair(packed_ref, tile, 512)
        grad = pair(grad_ref, tile, 0)
        inner = jnp.sum(grad.astype(F32) * pair(exact_ref, tile, 0), axis=0, keepdims=True)
        log_total = pair(log_ref, tile, 0)

        def step(block, d_query):
            raw = jnp.dot(keys[block], query, preferred_element_type=F32) * SCALE
            probs = jnp.where(key_mask(block, begin, finish), jnp.exp(raw - log_total), 0.0)
            d_probs = jnp.dot(values[block], grad, preferred_element_type=F32)
            d_scores = (probs * (d_probs - inner)).astype(BF16)
            d_values[block] += lax.dot_general(
                grad, probs.astype(BF16), by_query, preferred_element_type=F32
            )
            d_keys[block] += lax.dot_general(query, d_scores, by_query, preferred_element_type=F32)
            key_rows = packed_ref[block, :, :256]
            return d_query + jnp.dot(key_rows, d_scores, preferred_element_type=F32)

        d_query = lax.fori_loop(low, high, step, jnp.zeros((DH, 256), F32)) * SCALE
        for half in range(2):
            part = d_query[:, half * 128 : half * 128 + 128]
            out_ref[2 * tile + half, :, 512:640] = part.astype(BF16)
    for block in range(blocks):
        out_ref[block, :, :256] = (d_keys[block] * SCALE).astype(BF16)
        out_ref[block, :, 256:512] = d_values[block].astype(BF16)


def attend_forward(meta, packed):
    blocks = packed.shape[0]
    shape = jax.ShapeDtypeStruct
    return pl.pallas_call(
        lambda *refs: forward_kernel(meta.shape[0] - 1, *refs),
        out_shape=(
            shape((blocks, DH, 128), BF16),
            shape((blocks, DH, 128), F32),
            shape((blocks, 1, 128), F32),
        ),
        in_specs=[
            pl.BlockSpec(memory_space=pltpu.SMEM),
            pl.BlockSpec(memory_space=pltpu.VMEM),
        ],
        out_specs=tuple([pl.BlockSpec(memory_space=pltpu.VMEM)] * 3),
        scratch_shapes=[
            pltpu.VMEM((blocks, 256, DH), BF16),
            pltpu.VMEM((blocks, 256, 256), F32),
        ],
        compiler_params=pltpu.CompilerParams(vmem_limit_bytes=VMEM_BYTES),
        cost_estimate=pl.CostEstimate(flops=10**9, bytes_accessed=4 * 10**6, transcendentals=10**6),
        name="attend_forward",
    )(meta, packed)


def attend_backward(meta, packed, grad, exact, log_total):
    blocks = packed.shape[0]
    return pl.pallas_call(
        lambda *refs: backward_kernel(meta.shape[0] - 1, *refs),
        out_shape=jax.ShapeDtypeStruct(packed.shape, BF16),
        in_specs=[pl.BlockSpec(memory_space=pltpu.SMEM)]
        + [pl.BlockSpec(memory_space=pltpu.VMEM)] * 4,
        out_specs=pl.BlockSpec(memory_space=pltpu.VMEM),
        scratch_shapes=[
            pltpu.VMEM((blocks, 256, DH), BF16),
            pltpu.VMEM((blocks, 256, DH), BF16),
            pltpu.VMEM((blocks, DH, 256), F32),
            pltpu.VMEM((blocks, DH, 256), F32),
        ],
        compiler_params=pltpu.CompilerParams(vmem_limit_bytes=VMEM_BYTES),
        cost_estimate=pl.CostEstimate(flops=3 * 10**9, bytes_accessed=4 * 10**6, transcendentals=10**6),
        name="attend_backward",
    )(meta, packed, grad, exact, log_total)


class HeadSplit:
    def __init__(self, latent_len, rows):
        self.rows = rows
        self.meta = jnp.concatenate([lax.axis_index("dp").astype(jnp.int32)[None] % 2, latent_len])

    def forward(self, packed):
        self.packed = exchange(packed, "dp")
        out, self.exact, self.log_total = attend_forward(self.meta, self.packed)
        return exchange(out, "dp")

    def backward(self, grad, due, beside):
        grad = exchange(grad, "dp")
        beside = swap(gate(beside, grad), "dp", lax.axis_size("dp") - 2)
        out = attend_backward(self.meta, self.packed, grad, self.exact, self.log_total)
        return exchange(gate(out, beside, *due), "dp"), beside


class Window:
    def __init__(self, latent_len, rows):
        self.rows = rows
        self.reach = (SEQ - 2) // rows + 1
        total = rows * lax.axis_size("dp")
        first = lax.axis_index("dp") * rows
        own = latent_index(latent_len, first, rows, total)
        ids = [
            latent_index(latent_len, first + offset * rows, rows, total)
            for offset in range(-self.reach, self.reach + 1)
        ]
        self.allowed = own[:, None] == jnp.concatenate(ids)[None, :]

    def from_behind(self, block, distance):
        devices = range(lax.axis_size("dp"))
        return lax.ppermute(
            block, "dp", [(i - distance, i) for i in devices if i - distance in devices]
        )

    def head_scores(self, query, key):
        raw = jnp.einsum("eq,ek->qk", query, key, preferred_element_type=F32) * SCALE
        return jnp.where(self.allowed, raw, NEGATIVE)

    def forward(self, packed):
        rows = self.rows
        split = packed.reshape(-1, 2, DH, rows * 5 // 2)
        query = jnp.concatenate([split[:, 0, :, 2 * rows :], split[:, 1, :, 2 * rows :]], axis=2)
        projected = jnp.stack([query, split[:, 0, :, :rows], split[:, 0, :, rows : 2 * rows]])
        key_value = projected[1:]
        pieces = [
            key_value if offset == 0 else self.from_behind(key_value, -offset)
            for offset in range(-self.reach, self.reach + 1)
        ]
        window = jnp.concatenate(pieces, axis=3)
        self.operands = (projected[0], window[0], window[1])

        def one(operands):
            query, key, value = operands
            scores = self.head_scores(query, key)
            largest = jnp.max(scores, axis=1, keepdims=True)
            weights = jnp.exp(scores - largest)
            totals = jnp.sum(weights, axis=1, keepdims=True)
            probs = (weights / totals).astype(BF16)
            mixed = jnp.einsum("qk,ek->eq", probs, value, preferred_element_type=F32)
            return mixed.astype(BF16), (largest + jnp.log(totals))[:, 0]

        out, self.log_total = lax.map(one, self.operands)
        out = out.reshape(-1, DH, 2, rows // 2).transpose(0, 2, 1, 3)
        return out.reshape(-1, DH, rows // 2)

    def backward(self, grad, due, beside):
        rows, reach = self.rows, self.reach
        halves = grad.reshape(-1, 2, DH, rows // 2)
        grads = jnp.concatenate([halves[:, 0], halves[:, 1]], axis=2)

        def one(operands):
            query, key, value, grad, log_total = operands
            probs = jnp.exp(self.head_scores(query, key) - log_total[:, None])
            d_value = jnp.einsum("qk,eq->ek", probs.astype(BF16), grad, preferred_element_type=F32)
            d_probs = jnp.einsum("eq,ek->qk", grad, value, preferred_element_type=F32)
            inner = jnp.sum(probs * d_probs, axis=1, keepdims=True)
            d_scores = (probs * (d_probs - inner)).astype(BF16)
            d_query = jnp.einsum("qk,ek->eq", d_scores, key, preferred_element_type=F32) * SCALE
            d_key = jnp.einsum("qk,eq->ek", d_scores, query, preferred_element_type=F32) * SCALE
            return d_query, d_key, d_value

        d_query, d_key, d_value = lax.map(one, self.operands + (grads, self.log_total))
        d_window = jnp.stack([d_key, d_value])
        d_key_value = d_window[..., reach * rows : (reach + 1) * rows]
        for offset in range(-reach, reach + 1):
            if offset != 0:
                block = d_window[..., (offset + reach) * rows : (offset + reach + 1) * rows]
                d_key_value = d_key_value + self.from_behind(block, offset)
        wide = jnp.concatenate([d_key_value[0], d_key_value[1]], axis=2)
        wide = jnp.stack([wide, jnp.zeros_like(wide)], axis=1)
        halves = d_query.reshape(-1, DH, 2, rows // 2).transpose(0, 2, 1, 3)
        packed = jnp.concatenate([wide, halves], axis=3).astype(BF16)
        return packed.reshape(-1, DH, rows * 5 // 2), beside


META = 4


def vmem(count):
    return [pl.BlockSpec(memory_space=pltpu.VMEM)] * count


def call(body, name, meta, arrays, outs, scratch=(), anywhere=0, due=(), flops=1):
    count = 1 + len(arrays)

    def kernel(*refs):
        body(*refs[:count], *refs[count + len(due) :])

    return pl.pallas_call(
        kernel,
        out_shape=tuple(jax.ShapeDtypeStruct(shape, kind) for shape, kind in outs),
        in_specs=[pl.BlockSpec(memory_space=pltpu.SMEM)]
        + [pl.BlockSpec(memory_space=pl.ANY)] * anywhere
        + vmem(len(arrays) - anywhere)
        + [pl.BlockSpec(memory_space=pl.ANY)] * len(due),
        out_specs=tuple(vmem(len(outs))),
        scratch_shapes=list(scratch),
        compiler_params=pltpu.CompilerParams(vmem_limit_bytes=VMEM_BYTES),
        cost_estimate=pl.CostEstimate(flops=flops, bytes_accessed=1, transcendentals=0),
        name=name,
    )(meta, *arrays, *due)


def row_masks(meta_ref, latents, first, rows):
    place = first + lax.broadcasted_iota(jnp.int32, (rows, 1), 0)
    ids = jnp.zeros((rows, 1), jnp.int32)
    end = jnp.int32(0)
    for number in range(latents - 1):
        end = end + meta_ref[META + number]
        ids = ids + (place >= end).astype(jnp.int32)
    return [(ids == number).astype(F32) for number in range(latents)]


def rows_of(mod_ref, masks, feature):
    out = masks[0] * mod_ref[feature : feature + 1, :]
    for number in range(1, len(masks)):
        row = number * 6 + feature
        out = out + masks[number] * mod_ref[row : row + 1, :]
    return out


def latent_sums(out_ref, masks, values, feature, features):
    rounded = values.astype(BF16).astype(F32)
    for number, mask in enumerate(masks):
        row = number * features + feature
        out_ref[row : row + 1, :] = jnp.sum(mask * rounded, axis=0, keepdims=True)


def own_rows(meta_ref, ref, share):
    start = pl.multiple_of(meta_ref[2] * share, share)
    return ref[pl.ds(start, share), :].astype(F32)


def on_core(meta_ref, body, mine, other):
    @pl.when(meta_ref[0] == 0)
    def _():
        body(mine, other)

    @pl.when(meta_ref[0] != 0)
    def _():
        body(other, mine)


def place_rows(meta_ref, parts, whole, sems):
    block = parts[0].shape[0]
    copies = []
    for step, part in enumerate(parts):
        start = pl.multiple_of((meta_ref[3] ^ step) * block, 16)
        copies.append(
            pltpu.make_async_copy(part, whole.at[pl.ds(start, block), :], sems.at[step])
        )
    return copies


def place_pair(meta_ref, mine, other, first_ref, second_ref, sems):
    def body(first, second):
        copies = place_rows(meta_ref, first, first_ref, sems.at[0])
        copies += place_rows(meta_ref, second, second_ref, sems.at[1])
        for copy in copies:
            copy.start()
        for copy in copies:
            copy.wait()

    on_core(meta_ref, body, mine, other)


def project_kernel(latents, count, meta_ref, *refs):
    mine, other = refs[:count], refs[count : 2 * count]
    tokens_ref, cot_ref, mod_parts_ref, bias_ref = refs[2 * count : 2 * count + 4]
    hidden_ref, d_mlp_ref, packed_ref, qk_ref, vp_ref, d_bias_ref, mod_ref, sems = refs[2 * count + 4 :]
    rows, width = tokens_ref.shape
    place_pair(meta_ref, mine, other, qk_ref, vp_ref, sems)
    columns = mod_parts_ref.shape[2]
    pieces = width // columns
    for piece in range(pieces):
        total = mod_parts_ref[piece].astype(F32)
        for part in range(piece + pieces, mod_parts_ref.shape[0], pieces):
            total = total + mod_parts_ref[part].astype(F32)
        mod_ref[:, piece * columns : (piece + 1) * columns] = total
    masks = row_masks(meta_ref, latents, meta_ref[1], rows)
    unit, _ = normed(tokens_ref[...].astype(F32))
    hidden = unit * (1.0 + rows_of(mod_ref, masks, 1)) + rows_of(mod_ref, masks, 0)
    hidden_ref[...] = hidden.astype(BF16)
    d_mlp = (cot_ref[...].astype(F32) * rows_of(mod_ref, masks, 5)).astype(BF16)
    d_mlp_ref[...] = d_mlp
    d_bias_ref[...] = jnp.sum(d_mlp.astype(F32), axis=0, keepdims=True)
    heads = packed_ref.shape[0] // 2
    features = heads * DH
    left = hidden_ref[...]
    both = jnp.dot(left, qk_ref[...], preferred_element_type=F32) + bias_ref[0:1, :]
    both = both.T
    value = jnp.dot(left, vp_ref[...], preferred_element_type=F32) + bias_ref[1:2, :]
    value = value.T
    for head in range(heads):
        start = head * DH
        query = both[start : start + DH].astype(BF16)
        key = both[features + start : features + start + DH].astype(BF16)
        val = value[start : start + DH].astype(BF16)
        for half in range(2):
            packed_ref[2 * head + half, :, :rows] = key
            packed_ref[2 * head + half, :, rows : 2 * rows] = val
            packed_ref[2 * head + half, :, 2 * rows :] = query[
                :, half * (rows // 2) : (half + 1) * (rows // 2)
            ]


def attend_out_kernel(meta_ref, parts_ref, vp_ref, part_ref, attended_ref):
    heads = parts_ref.shape[0] // 2
    rows = part_ref.shape[0]
    stacked = [jnp.zeros((heads * DH, rows), F32)]
    for head in range(heads):
        left = parts_ref[2 * head].astype(F32)
        right = parts_ref[2 * head + 1].astype(F32)
        stacked.append(jnp.concatenate([left, right], axis=1))
    attended_ref[...] = jnp.concatenate(stacked, axis=0).T.astype(BF16)
    part_ref[...] = lax.dot_general(
        attended_ref[...], vp_ref[...], (((1,), (1,)), ((), ())), preferred_element_type=F32
    ).astype(BF16)


def middle_kernel(
    latents, meta_ref, parts_ref, tokens_ref, mod_ref, bias_ref, sent_ref, attn_ref, mid_ref
):
    copies, share, width = parts_ref.shape
    masks = row_masks(meta_ref, latents, meta_ref[1] + meta_ref[2] * share, share)
    attn = bias_ref[...].astype(F32)
    for part in range(copies):
        attn = attn + parts_ref[part].astype(F32)
    attn_ref[...] = attn
    mid = own_rows(meta_ref, tokens_ref, share) + rows_of(mod_ref, masks, 2) * attn
    mid_ref[...] = mid
    unit, _ = normed(mid)
    hidden = unit * (1.0 + rows_of(mod_ref, masks, 4)) + rows_of(mod_ref, masks, 3)
    for part in range(copies):
        sent_ref[part] = hidden.astype(BF16)


def mlp_kernel(count, meta_ref, *refs):
    mine, other = refs[:count], refs[count : 2 * count]
    hidden_ref, d_mlp_ref, bias_ref = refs[2 * count : 2 * count + 3]
    d_two_ref, gelu_ref, d_pre_ref, d_bias_ref, left_ref, right_ref = refs[2 * count + 3 : 2 * count + 9]
    mlp_refs = refs[2 * count + 9 : -5]
    fc1_ref, fc2_ref, d_two_sum, mlp_sum, sems = refs[-5:]
    place_pair(meta_ref, mine, other, fc1_ref, fc2_ref, sems)
    d_two_sum[...] = jnp.zeros_like(d_two_sum)
    mlp_sum[...] = jnp.zeros_like(mlp_sum)
    tile = 384
    by_last = (((1,), (1,)), ((), ()))

    def step(number, carry):
        units = pl.ds(pl.multiple_of(number * tile, tile), tile)
        fc1, fc2 = fc1_ref[:, units], fc2_ref[:, units]
        pre = jnp.dot(hidden_ref[...], fc1, preferred_element_type=F32)
        gelu, slope = gelu_pair(pre + bias_ref[:, units].astype(F32))
        grad = jnp.dot(d_mlp_ref[...], fc2, preferred_element_type=F32)
        d_pre = (grad * slope).astype(BF16)
        gelu = gelu.astype(BF16)
        gelu_ref[:, units] = gelu
        d_pre_ref[:, units] = d_pre
        d_bias_ref[:, units] = jnp.sum(d_pre.astype(F32), axis=0, keepdims=True)
        d_two_sum[...] += lax.dot_general(d_pre, fc1, by_last, preferred_element_type=F32)
        mlp_sum[...] += lax.dot_general(gelu, fc2, by_last, preferred_element_type=F32)
        return carry

    lax.fori_loop(0, fc1_ref.shape[1] // tile, step, 0)
    d_two_ref[...] = d_two_sum[...].astype(BF16)
    def sent(left, right):
        left_ref[...] = left[0][...]
        right_ref[...] = left[1][...]

    on_core(meta_ref, sent, (d_mlp_ref, gelu_ref), (hidden_ref, d_pre_ref))
    share = mlp_refs[0].shape[0]
    for step, mlp_ref in enumerate(mlp_refs):
        start = pl.multiple_of((meta_ref[2] ^ step) * share, share)
        mlp_ref[...] = mlp_sum[pl.ds(start, share), :].astype(BF16)


def middle_back_kernel(
    latents, meta_ref, parts_ref, mid_in_ref, attn_ref, cot_ref, mod_ref, sent_ref, d_mid_ref, sums_ref
):
    copies, share, width = parts_ref.shape
    masks = row_masks(meta_ref, latents, meta_ref[1] + meta_ref[2] * share, share)
    d_hidden = parts_ref[0].astype(F32)
    for part in range(1, copies):
        d_hidden = d_hidden + parts_ref[part].astype(F32)
    unit, inverse = normed(mid_in_ref[...])
    d_mid = own_rows(meta_ref, cot_ref, share) + norm_back(
        unit, inverse, d_hidden * (1.0 + rows_of(mod_ref, masks, 4))
    )
    d_mid_ref[...] = d_mid
    d_attn = (d_mid * rows_of(mod_ref, masks, 2)).astype(BF16)
    for part in range(copies):
        sent_ref[part] = d_attn
    latent_sums(sums_ref, masks, d_mid * attn_ref[...], 0, 3)
    latent_sums(sums_ref, masks, d_hidden, 1, 3)
    latent_sums(sums_ref, masks, d_hidden * unit, 2, 3)


def result_kernel(
    latents, count, meta_ref, *refs
):
    parts = refs[:count]
    mid_ref, cot_ref, mod_ref, bias_ref, result_ref, sums_ref = refs[count:]
    share = result_ref.shape[0]
    masks = row_masks(meta_ref, latents, meta_ref[1] + meta_ref[2] * share, share)
    mlp = bias_ref[...].astype(F32)
    for part in parts:
        mlp = mlp + part[...].astype(F32)
    result_ref[...] = (mid_ref[...] + rows_of(mod_ref, masks, 5) * mlp).astype(BF16)
    latent_sums(sums_ref, masks, own_rows(meta_ref, cot_ref, share) * mlp, 0, 1)


def spread_kernel(meta_ref, d_attn_ref, vp_ref, packed_ref, d_bias_ref):
    grad = jnp.dot(d_attn_ref[...], vp_ref[...], preferred_element_type=F32).T
    half = grad.shape[1] // 2
    features = grad.shape[0] // 2
    for place in range(packed_ref.shape[0]):
        start = features + place // 2 * DH
        side = place % 2 * half
        packed_ref[place] = grad[start : start + DH, side : side + half].astype(BF16)
    d_bias_ref[...] = jnp.sum(d_attn_ref[...].astype(F32), axis=0, keepdims=True)


def unspread_kernel(
    meta_ref, parts_ref, qk_ref, vp_ref, d_one_ref, d_qk_ref, d_vp_ref, sent_ref, d_bias_ref
):
    heads = parts_ref.shape[0] // 2
    rows = d_one_ref.shape[0]
    query, key, value = [], [], []
    for head in range(heads):
        left = parts_ref[2 * head].astype(F32)
        right = parts_ref[2 * head + 1].astype(F32)
        both = left[:, : 2 * rows] + right[:, : 2 * rows]
        key.append(both[:, :rows])
        value.append(both[:, rows:])
        query.append(jnp.concatenate([left[:, 2 * rows :], right[:, 2 * rows :]], axis=1))
    d_qk_ref[...] = jnp.concatenate(query + key, axis=0).T.astype(BF16)
    blank = jnp.zeros((heads * DH, rows), F32)
    d_vp_ref[...] = jnp.concatenate(value + [blank], axis=0).T.astype(BF16)
    tile = 384
    by_last = (((1,), (1,)), ((), ()))

    def step(number, carry):
        columns = pl.ds(pl.multiple_of(number * tile, tile), tile)
        total = lax.dot_general(d_qk_ref[...], qk_ref[columns, :], by_last, preferred_element_type=F32)
        total += lax.dot_general(d_vp_ref[...], vp_ref[columns, :], by_last, preferred_element_type=F32)
        d_one_ref[:, columns] = total.astype(BF16)
        return carry

    lax.fori_loop(0, qk_ref.shape[0] // tile, step, 0)

    def sent(first, second):
        sent_ref[...] = first[...]

    on_core(meta_ref, sent, d_vp_ref, d_qk_ref)
    d_bias_ref[0:1, :] = jnp.sum(d_qk_ref[...].astype(F32), axis=0, keepdims=True)
    d_bias_ref[1:2, :] = jnp.sum(d_vp_ref[...].astype(F32), axis=0, keepdims=True)


def weight_kernel(first_pairs, second_pairs, meta_ref, *refs):
    operands = 1 + max(max(pair) for pair in first_pairs + second_pairs)
    ins, outs, total = refs[:operands], refs[operands:-1], refs[-1]
    tile = 384

    def body(pairs):
        def step(number, carry):
            columns = pl.ds(pl.multiple_of(number * tile, tile), tile)
            block = jnp.zeros((tile, total.shape[1]), F32)
            for left, right in pairs:
                block += lax.dot_general(
                    ins[left][:, columns], ins[right][...], (((0,), (0,)), ((), ())),
                    preferred_element_type=F32,
                )
            total[columns, :] = block.astype(BF16)
            return carry

        lax.fori_loop(0, total.shape[0] // tile, step, 0)

    on_core(meta_ref, lambda pairs, _: body(pairs), first_pairs, second_pairs)
    rows = outs[0].shape[0]
    for step, out in enumerate(outs):
        start = pl.multiple_of((meta_ref[3] ^ step) * rows, 16)
        out[...] = total[pl.ds(start, rows), :]


def first_back_kernel(
    latents, meta_ref, parts_ref, tokens_ref, d_mid_ref, mod_ref, mid_sums_ref, last_sums_ref,
    fc2_bias_ref, proj_bias_ref, fc1_bias_ref, qv_bias_ref, grad_ref, sent_ref, bias_ref, first_sums,
):
    copies, share, width = parts_ref.shape
    masks = row_masks(meta_ref, latents, meta_ref[1] + meta_ref[2] * share, share)
    d_hidden = parts_ref[0].astype(F32)
    for part in range(1, copies):
        d_hidden = d_hidden + parts_ref[part].astype(F32)
    unit, inverse = normed(own_rows(meta_ref, tokens_ref, share))
    grad = d_mid_ref[...] + norm_back(unit, inverse, d_hidden * (1.0 + rows_of(mod_ref, masks, 1)))
    grad_ref[...] = grad.astype(BF16)
    latent_sums(first_sums, masks, d_hidden, 0, 2)
    latent_sums(first_sums, masks, d_hidden * unit, 1, 2)
    columns = width // copies
    for number in range(latents):
        for feature in range(6):
            if feature < 2:
                row = first_sums[number * 2 + feature : number * 2 + feature + 1, :]
            elif feature < 5:
                place = number * 3 + feature - 2
                row = mid_sums_ref[place : place + 1, :]
            else:
                row = last_sums_ref[number : number + 1, :]
            place = number * 6 + feature
            for part in range(copies):
                sent_ref[part, place : place + 1, :] = row[:, part * columns : (part + 1) * columns]
    place = 0
    for ref in (fc2_bias_ref, proj_bias_ref, fc1_bias_ref):
        for start in range(0, ref.shape[1], columns):
            bias_ref[place : place + 1, :] = ref[:, start : start + columns]
            place += 1
    bias_ref[place : place + 2, :] = qv_bias_ref[:, :columns]


def order_kernel(count, meta_ref, *refs):
    result_ref, grad_ref = refs[2 * count :]
    share = refs[0].shape[0]
    for step in range(count):
        start = pl.multiple_of((meta_ref[2] ^ step) * share, share)
        result_ref[pl.ds(start, share), :] = refs[step][...]
        grad_ref[pl.ds(start, share), :] = refs[count + step][...].astype(F32)


def finish_kernel(
    latents, meta_ref, sums_ref, active_ref, w_ada_ref,
    w_grad_ref, b_grad_ref, d_active_ref, fc2_ref, proj_ref, fc1_ref, qv_ref, total_ref,
):
    total = sums_ref[0]
    for part in range(1, sums_ref.shape[0]):
        total = total + sums_ref[part]
    total_ref[...] = total
    by_last = (((1,), (1,)), ((), ()))
    d_active = jnp.zeros(d_active_ref.shape, F32)
    for feature in range(6):
        rows = [
            total_ref[number * 6 + feature : number * 6 + feature + 1, :] for number in range(latents)
        ]
        grad = active_ref[:, 0:1] * rows[0]
        bias = rows[0]
        for number in range(1, latents):
            grad = grad + active_ref[:, number : number + 1] * rows[number]
            bias = bias + rows[number]
        w_grad_ref[feature] = grad
        b_grad_ref[feature : feature + 1, :] = bias
        wide = jnp.concatenate(rows, axis=0)
        high = wide.astype(BF16)
        low = (wide - high.astype(F32)).astype(BF16)
        weight = w_ada_ref[feature]
        d_active += lax.dot_general(high, weight, by_last, preferred_element_type=F32)
        d_active += lax.dot_general(low, weight, by_last, preferred_element_type=F32)
    d_active_ref[...] = d_active
    columns = total_ref.shape[1]
    place = 6 * latents
    for ref in (fc2_ref, proj_ref, fc1_ref):
        for start in range(0, ref.shape[1], columns):
            ref[:, start : start + columns] = total_ref[place : place + 1, :]
            place += 1
    qv_ref[...] = total_ref[place : place + 2, :]


def latent_index(latent_len, first_row, row_count, token_total):
    positions = first_row + jnp.arange(row_count, dtype=jnp.int32)
    ends = jnp.cumsum(latent_len, dtype=jnp.int32)
    found = jnp.sum((positions[:, None] >= ends[None, :]).astype(jnp.int32), axis=1, dtype=jnp.int32)
    return jnp.where((positions >= 0) & (positions < token_total), found, -1)


def normed(values):
    average = jnp.mean(values, axis=-1, keepdims=True)
    centred = values - average
    spread = jnp.mean(centred * centred, axis=-1, keepdims=True)
    inverse = lax.rsqrt(spread + NORM_EPS)
    return centred * inverse, inverse


def norm_back(unit, inverse, grad):
    along = jnp.mean(grad * unit, axis=-1, keepdims=True)
    return inverse * (grad - jnp.mean(grad, axis=-1, keepdims=True) - unit * along)


def gelu_pair(value):
    root = math.sqrt(2.0 / math.pi)
    bend = jnp.tanh(root * (value + 0.044715 * value * value * value))
    slope = root * (1.0 + 3.0 * 0.044715 * value * value)
    gelu = 0.5 * value * (1.0 + bend)
    return gelu, 0.5 * (1.0 + bend) + 0.5 * value * (1.0 - bend * bend) * slope


def local(
    tokens,
    conditioning,
    latent_len,
    w_ada,
    b_ada,
    w_qkv,
    b_qv,
    w_proj,
    b_proj,
    w_fc1,
    b_fc1,
    w_fc2,
    b_fc2,
    cotangent,
):
    rows, width = tokens.shape
    share_width = w_qkv.shape[0]
    features = w_qkv.shape[2]
    units = w_fc1.shape[1]
    heads = features // DH
    latents = conditioning.shape[0]
    n_dp, n_tensor = lax.axis_size("dp"), lax.axis_size("tensor")
    my_dp, my_tensor = lax.axis_index("dp"), lax.axis_index("tensor")
    share = rows // n_tensor

    core = my_dp % 2
    qk = w_qkv[:, :2].reshape(share_width, 2 * features)
    vp = jnp.concatenate([w_qkv[:, 2], w_proj.T], axis=1)
    early_rows = pair_rows(qk, vp)

    cond = conditioning.astype(F32)
    sigmoid = 1.0 / (1.0 + jnp.exp(-cond))
    activated = (cond * sigmoid).astype(BF16)
    own_activated = lax.dynamic_slice_in_dim(activated, my_dp * share_width, share_width, 1)
    flat_ada = w_ada.reshape(share_width, 6 * features)
    mod_part = jnp.dot(own_activated, flat_ada, preferred_element_type=F32)
    mod_part = mod_part.reshape(latents * 6, features)
    bias_ada = jnp.tile(b_ada.astype(F32), (latents, 1))
    few_chips = n_dp // 2 == 4
    mod_mine = jnp.sum(gather(mod_part, "dp", n_dp), axis=0) + bias_ada
    early_rows = gate(early_rows, mod_mine)
    mod_parts = gather(mod_mine, "tensor", n_tensor)
    early_parts = chip_parts(early_rows) if few_chips else [gather_chips(early_rows)]

    early_parts = list(gate_all(early_parts, mod_parts))
    early_parts += [swap(part, "dp", 1) for part in early_parts]
    count = len(early_parts) // 2
    meta = jnp.stack([core, my_dp * rows, my_tensor, my_dp // 2]).astype(jnp.int32)
    meta = jnp.concatenate([meta, latent_len])
    place_meta = meta if few_chips else meta.at[3].set(0)
    by_last = (((1,), (1,)), ((), ()))
    by_token = (((0,), (0,)), ((), ()))
    bias = jnp.concatenate([b_qv[0], jnp.zeros_like(b_qv[0]), b_qv[1], jnp.zeros_like(b_qv[0])])
    hidden_one, d_mlp, packed, full_qk, full_vp, d_bias_fc2, mod_rows = call(
        lambda *refs: project_kernel(latents, count, *refs),
        "project",
        place_meta,
        (*early_parts, tokens, cotangent, mod_parts, bias.astype(F32).reshape(2, -1)),
        (((rows, width), BF16), ((rows, width), BF16), ((2 * heads, DH, rows * 5 // 2), BF16))
        + (((width, 2 * features), BF16),) * 2
        + (((1, width), F32), ((6 * latents, width), F32)),
        [pltpu.SemaphoreType.DMA((2, count))],
        2 * count,
    )
    late_rows = pair_rows(w_fc1, w_fc2.T)
    hidden_other = swap(hidden_one, "dp", 1)
    split = HeadSplit if 2 * heads == n_dp else Window
    attention = split(latent_len, rows)
    attended_parts = attention.forward(packed)
    late_rows = gate(late_rows, attended_parts)
    late_parts = chip_parts(late_rows)[:-1] if few_chips else [gather_chips(late_rows)]
    attn_part, attended = call(
        attend_out_kernel,
        "attend_out",
        meta,
        (attended_parts, full_vp),
        (((rows, width), BF16), ((rows, 2 * features), BF16)),
    )
    attn_parts = exchange_shares(attn_part, "tensor")
    hidden_blocks, attn_out, residual_mid = call(
        lambda *refs: middle_kernel(latents, *refs),
        "middle",
        meta,
        (attn_parts, tokens, mod_rows, b_proj.reshape(1, -1)),
        (((n_tensor, share, width), BF16), ((share, width), F32), ((share, width), F32)),
        due=late_parts[1:],
    )
    hidden_two = exchange(hidden_blocks, "tensor").reshape(rows, width)
    if few_chips:
        last_part = swap(gate(late_rows, attn_out), "dp", n_dp - 2)
        late_parts.append(gate(last_part, hidden_two))
    late_other = [swap(part, "dp", 1) for part in late_parts]

    d_two_part, gelu_out, d_pre, d_bias_fc1, left_sent, right_sent, *mlp_blocks = call(
        lambda *refs: mlp_kernel(count, *refs),
        "mlp",
        place_meta,
        (*late_parts, *late_other, hidden_two, d_mlp, b_fc1.reshape(1, -1)),
        (((rows, width), BF16), ((rows, units), BF16), ((rows, units), BF16), ((1, units), F32))
        + (((rows, width), BF16), ((rows, units), BF16))
        + (((share, width), BF16),) * n_tensor,
        [pltpu.VMEM((width, units), BF16)] * 2
        + [pltpu.VMEM((rows, width), F32)] * 2
        + [pltpu.SemaphoreType.DMA((2, count))],
        2 * count,
    )
    d_two_parts = exchange_shares(d_two_part, "tensor")

    chips = n_dp // 2 if few_chips else 1
    left_other = swap(left_sent, "dp", 1)
    right_other = swap(right_sent, "dp", 1)
    late_blocks = call(
        lambda *refs: weight_kernel([(0, 2), (4, 5)], [(1, 3), (4, 5)], *refs),
        "late_weights",
        place_meta,
        (hidden_two, d_mlp, d_pre, gelu_out, left_other, right_other),
        (((width // chips, units), BF16),) * chips,
        [pltpu.VMEM((width, units), BF16)],
    )
    late_grads = sum_chips(late_blocks[:-1]) if few_chips else sum_chips(late_blocks)

    d_attn_blocks, d_mid, mid_sums = call(
        lambda *refs: middle_back_kernel(latents, *refs),
        "middle_back",
        meta,
        (d_two_parts, residual_mid, attn_out, cotangent, mod_rows),
        (((n_tensor, share, width), BF16), ((share, width), F32), ((3 * latents, width), F32)),
        due=late_blocks,
    )
    d_attn = exchange(d_attn_blocks, "tensor").reshape(rows, width)

    d_spread, d_bias_proj = call(
        spread_kernel,
        "spread",
        meta,
        (d_attn, full_vp),
        (((2 * heads, DH, rows // 2), BF16), ((1, width), F32)),
        due=late_grads[1:],
    )
    mlp_parts = mlp_blocks[:1] + [
        swap(gate(block, d_spread), "tensor", step)
        for step, block in enumerate(mlp_blocks)
        if step
    ]
    d_attn_other = swap(d_attn, "dp", 1)
    attended_other = swap(attended, "dp", 1)
    d_packed, last_grad = attention.backward(d_spread, mlp_parts[1:], late_blocks[-1])
    result_own, last_sums = call(
        lambda *refs: result_kernel(latents, n_tensor, *refs),
        "result",
        meta,
        (*mlp_parts, residual_mid, cotangent, mod_rows, b_fc2.reshape(1, -1)),
        (((share, width), BF16), ((latents, width), F32)),
    )
    d_one_part, d_qk, d_vp, d_sent, d_bias_qv = call(
        unspread_kernel,
        "unspread",
        meta,
        (d_packed, full_qk, full_vp),
        (((rows, width), BF16),)
        + (((rows, 2 * features), BF16),) * 3
        + (((2, 2 * features), F32),),
        flops=2 * 10**10,
    )
    result_parts = [result_own] + [swap(result_own, "tensor", bits) for bits in range(1, n_tensor)]
    d_one_part = gate(d_one_part, *result_parts[1:])
    d_one_parts = exchange_shares(d_one_part, "tensor")

    if few_chips:
        late_grads.append(last_grad)
    right_other = swap(d_sent, "dp", 1)
    early_blocks = call(
        lambda *refs: weight_kernel(
            [(0, 2), (5, 7)], [(0, 3), (1, 4), (5, 7), (6, 8)], *refs
        ),
        "early_weights",
        place_meta,
        (hidden_one, d_attn, d_qk, d_vp, attended, hidden_other, d_attn_other, right_other, attended_other),
        (((width // chips, 2 * features), BF16),) * chips,
        [pltpu.VMEM((width, 2 * features), BF16)],
    )
    early_grads = sum_chips(early_blocks[:3] if few_chips else early_blocks)

    grad_own, d_mod_part, bias_rows = call(
        lambda *refs: first_back_kernel(latents, *refs),
        "first_back",
        meta,
        (d_one_parts, tokens, d_mid, mod_rows, mid_sums, last_sums)
        + (d_bias_fc2, d_bias_proj, d_bias_fc1, d_bias_qv),
        (((share, width), BF16), ((n_tensor, 6 * latents, features), F32))
        + (((2 * (width // features) + units // features + 2, features), F32),),
        [pltpu.VMEM((2 * latents, width), F32)],
        due=early_grads[1:3],
    )
    if few_chips:
        last_block = gate(early_blocks[3], d_mod_part)
        early_grads.append(swap(last_block, "dp", n_dp - 2))
    d_mod_mine = jnp.sum(exchange(d_mod_part, "tensor"), axis=0)
    d_mod_rows = jnp.concatenate([d_mod_mine, bias_rows])
    d_mod_rows = gate(jnp.broadcast_to(d_mod_rows[None], (n_dp,) + d_mod_rows.shape))
    grad_own = gate(grad_own, d_mod_rows)
    grad_parts = [grad_own] + [swap(grad_own, "tensor", bits) for bits in range(1, n_tensor)]
    sums = exchange(d_mod_rows, "dp")
    sums = gate(sums, early_grads[3]) if few_chips else sums
    grad_parts = gate_all(grad_parts, sums)
    result, grad_tokens = call(
        lambda *refs: order_kernel(n_tensor, *refs),
        "order",
        meta,
        (*result_parts, *grad_parts),
        (((rows, width), BF16), ((rows, width), F32)),
    )
    grad_w_ada, grad_b_ada, d_active, sum_b_fc2, sum_b_proj, sum_b_fc1, sum_b_qv = call(
        lambda *refs: finish_kernel(latents, *refs),
        "finish",
        meta,
        (sums, own_activated.astype(F32).T, w_ada.transpose(1, 0, 2)),
        (((6, share_width, features), F32), ((6, features), F32), ((latents, share_width), F32))
        + (((1, width), F32), ((1, width), F32), ((1, units), F32), ((2, features), F32)),
        [pltpu.VMEM(sums.shape[1:], F32)],
    )
    d_active = gather(d_active, ("dp", "tensor"), n_dp * n_tensor)
    d_active = jnp.sum(d_active.reshape(n_dp, n_tensor, latents, share_width), axis=1)
    d_active = d_active.transpose(1, 0, 2).reshape(latents, width)
    grad_cond = d_active * (sigmoid * (1.0 + cond * (1.0 - sigmoid)))

    grad_fc1, grad_fc2 = finish_pair(late_grads)
    grad_qk, grad_vp = finish_pair(early_grads)
    grad_qkv = jnp.concatenate([grad_qk, grad_vp[:, :features]], axis=1)
    grad_qkv = grad_qkv.reshape(share_width, 3, features)

    return (
        result,
        grad_tokens,
        grad_cond,
        grad_w_ada.transpose(1, 0, 2),
        grad_b_ada,
        grad_qkv,
        sum_b_qv,
        grad_vp[:, features:].T,
        sum_b_proj.reshape(width),
        grad_fc1,
        sum_b_fc1.reshape(units),
        grad_fc2.T,
        sum_b_fc2.reshape(width),
    )


def solution(mesh):
    in_specs = (
        P("dp", None),
        P(),
        P(),
        P("dp", None, "tensor"),
        P(None, "tensor"),
        P("dp", None, "tensor"),
        P(None, "tensor"),
        P("tensor", "dp"),
        P(),
        P("dp", "tensor"),
        P("tensor"),
        P("tensor", "dp"),
        P(),
        P("dp", None),
    )
    out_specs = (
        P("dp", None),
        P("dp", None),
        P(),
        P("dp", None, "tensor"),
        P(None, "tensor"),
        P("dp", None, "tensor"),
        P(None, "tensor"),
        P("tensor", "dp"),
        P(),
        P("dp", "tensor"),
        P("tensor"),
        P("tensor", "dp"),
        P(),
    )
    return jax.shard_map(local, mesh=mesh, in_specs=in_specs, out_specs=out_specs, check_vma=False)
```

```python
import math

import jax
import jax.numpy as jnp
from jax import lax
from jax.experimental import pallas as pl
from jax.experimental.pallas import tpu as pltpu
from jax.sharding import PartitionSpec as P

DH = 72
SEQ = 1024
NORM_EPS = 1e-06
NEGATIVE = -1e30
SCALE = 1.0 / math.sqrt(DH)
VMEM_BYTES = 64 * 1024 * 1024
BF16 = jnp.bfloat16
F32 = jnp.float32


def swap(block, axis, bits):
    route = [(i, i ^ bits) for i in range(lax.axis_size(axis))]
    return lax.ppermute(block, axis, route)


def exchange(blocks, axis):
    return lax.all_to_all(blocks, axis, 0, 0, tiled=True)


def gather(block, axis, count):
    return exchange(jnp.broadcast_to(block[None], (count,) + block.shape), axis)


def gate_all(values, *others):
    anywhere = pl.BlockSpec(memory_space=pl.ANY)
    return pl.pallas_call(
        lambda *refs: None,
        out_shape=tuple(jax.ShapeDtypeStruct(value.shape, value.dtype) for value in values),
        in_specs=[anywhere] * (len(values) + len(others)),
        out_specs=(anywhere,) * len(values),
        input_output_aliases={place: place for place in range(len(values))},
        cost_estimate=pl.CostEstimate(flops=1, bytes_accessed=1, transcendentals=0),
        name="gate",
    )(*values, *others)


def gate(value, *others):
    return gate_all((value,), *others)[0]


def choose(core, first, second):
    return jnp.where(core == 0, first, second), jnp.where(core == 0, second, first)


def pair_rows(first, second):
    core = lax.axis_index("dp") % 2
    keep, send = choose(core, first, second)
    return jnp.concatenate(choose(core, keep, swap(send, "dp", 1)))


def chip_parts(rows):
    count = lax.axis_size("dp") // 2
    return [rows] + [swap(rows, "dp", 2 * step) for step in range(1, count)]


def gather_chips(rows):
    count = lax.axis_size("dp")
    groups = [list(range(core, count, 2)) for core in range(2)]
    return lax.all_gather(rows, "dp", axis=0, tiled=True, axis_index_groups=groups)


def sum_chips(blocks):
    if len(blocks) == 1:
        count, chip = lax.axis_size("dp") // 2, lax.axis_index("dp") // 2
        rows = blocks[0].reshape((count, -1) + blocks[0].shape[1:])
        blocks = [
            lax.dynamic_index_in_dim(rows, chip ^ step, 0, keepdims=False) for step in range(count)
        ]
    return [swap(block, "dp", 2 * step) if step else block for step, block in enumerate(blocks)]


def finish_pair(parts):
    core = lax.axis_index("dp") % 2
    rows = sum(part.astype(F32) for part in parts)
    half = rows.shape[0] // 2
    keep, send = choose(core, rows[:half], rows[half:])
    return choose(core, keep, swap(send, "dp", 1))


def exchange_shares(partial, axis):
    count = lax.axis_size(axis)
    blocks = partial.reshape((count, partial.shape[0] // count) + partial.shape[1:])
    return exchange(blocks, axis)


def tile_range(meta_ref, latents, tile, core):
    lane = lax.broadcasted_iota(jnp.int32, (1, 256), 1)
    first = tile * 512 + core * 128
    last = first + 383
    place = first + lane + jnp.where(lane >= 128, 128, 0)
    begin = jnp.zeros((1, 256), jnp.int32)
    finish = jnp.zeros((1, 256), jnp.int32)
    low = jnp.int32(0)
    high = jnp.int32(0)
    start = jnp.int32(0)
    for number in range(latents):
        end = start + meta_ref[1 + number]
        inside = (place >= start) & (place < end)
        begin = jnp.where(inside, start, begin)
        finish = jnp.where(inside, end, finish)
        low = jnp.where((first >= start) & (first < end), start, low)
        high = jnp.where((last >= start) & (last < end), end, high)
        start = end
    return begin, finish, low // 256, (high + 255) // 256


def pair(ref, tile, start):
    left = ref[2 * tile, :, start : start + 128]
    right = ref[2 * tile + 1, :, start : start + 128]
    return jnp.concatenate([left, right], axis=1)


def key_mask(block, begin, finish):
    place = block * 256 + lax.broadcasted_iota(jnp.int32, (256, 256), 0)
    return (place >= begin) & (place < finish)


def forward_kernel(latents, meta_ref, packed_ref, out_ref, exact_ref, log_ref, keys, scores):
    blocks = packed_ref.shape[0]
    core = meta_ref[0]
    for block in range(blocks):
        keys[block] = packed_ref[block, :, :256].astype(F32).T.astype(BF16)
    for tile in range(blocks // 2):
        begin, finish, low, high = tile_range(meta_ref, latents, tile, core)
        query = pair(packed_ref, tile, 512)

        def score(block, largest):
            raw = jnp.dot(keys[block], query, preferred_element_type=F32) * SCALE
            raw = jnp.where(key_mask(block, begin, finish), raw, NEGATIVE)
            scores[block] = raw
            return jnp.maximum(largest, jnp.max(raw, axis=0, keepdims=True))

        largest = lax.fori_loop(low, high, score, jnp.full((1, 256), NEGATIVE, F32))

        def mix(block, carry):
            total, mixed = carry
            weights = jnp.exp(scores[block] - largest)
            total = total + jnp.sum(weights, axis=0, keepdims=True)
            values = packed_ref[block, :, 256:512]
            mixed = mixed + jnp.dot(values, weights.astype(BF16), preferred_element_type=F32)
            return total, mixed

        total, mixed = lax.fori_loop(
            low, high, mix, (jnp.zeros((1, 256), F32), jnp.zeros((DH, 256), F32))
        )
        mixed = mixed / total
        log_total = largest + jnp.log(total)
        for half in range(2):
            part = mixed[:, half * 128 : half * 128 + 128]
            exact_ref[2 * tile + half] = part
            out_ref[2 * tile + half] = part.astype(BF16)
            log_ref[2 * tile + half] = log_total[:, half * 128 : half * 128 + 128]


def backward_kernel(
    latents, meta_ref, packed_ref, grad_ref, exact_ref, log_ref, out_ref, keys, values, d_keys, d_values
):
    blocks = packed_ref.shape[0]
    core = meta_ref[0]
    for block in range(blocks):
        keys[block] = packed_ref[block, :, :256].astype(F32).T.astype(BF16)
        values[block] = packed_ref[block, :, 256:512].astype(F32).T.astype(BF16)
    d_keys[...] = jnp.zeros_like(d_keys)
    d_values[...] = jnp.zeros_like(d_values)
    by_query = (((1,), (1,)), ((), ()))
    for tile in range(blocks // 2):
        begin, finish, low, high = tile_range(meta_ref, latents, tile, core)
        query = pair(packed_ref, tile, 512)
        grad = pair(grad_ref, tile, 0)
        inner = jnp.sum(grad.astype(F32) * pair(exact_ref, tile, 0), axis=0, keepdims=True)
        log_total = pair(log_ref, tile, 0)

        def step(block, d_query):
            raw = jnp.dot(keys[block], query, preferred_element_type=F32) * SCALE
            probs = jnp.where(key_mask(block, begin, finish), jnp.exp(raw - log_total), 0.0)
            d_probs = jnp.dot(values[block], grad, preferred_element_type=F32)
            d_scores = (probs * (d_probs - inner)).astype(BF16)
            d_values[block] += lax.dot_general(
                grad, probs.astype(BF16), by_query, preferred_element_type=F32
            )
            d_keys[block] += lax.dot_general(query, d_scores, by_query, preferred_element_type=F32)
            key_rows = packed_ref[block, :, :256]
            return d_query + jnp.dot(key_rows, d_scores, preferred_element_type=F32)

        d_query = lax.fori_loop(low, high, step, jnp.zeros((DH, 256), F32)) * SCALE
        for half in range(2):
            part = d_query[:, half * 128 : half * 128 + 128]
            out_ref[2 * tile + half, :, 512:640] = part.astype(BF16)
    for block in range(blocks):
        out_ref[block, :, :256] = (d_keys[block] * SCALE).astype(BF16)
        out_ref[block, :, 256:512] = d_values[block].astype(BF16)


def attend_forward(meta, packed):
    blocks = packed.shape[0]
    shape = jax.ShapeDtypeStruct
    return pl.pallas_call(
        lambda *refs: forward_kernel(meta.shape[0] - 1, *refs),
        out_shape=(
            shape((blocks, DH, 128), BF16),
            shape((blocks, DH, 128), F32),
            shape((blocks, 1, 128), F32),
        ),
        in_specs=[
            pl.BlockSpec(memory_space=pltpu.SMEM),
            pl.BlockSpec(memory_space=pltpu.VMEM),
        ],
        out_specs=tuple([pl.BlockSpec(memory_space=pltpu.VMEM)] * 3),
        scratch_shapes=[
            pltpu.VMEM((blocks, 256, DH), BF16),
            pltpu.VMEM((blocks, 256, 256), F32),
        ],
        compiler_params=pltpu.CompilerParams(vmem_limit_bytes=VMEM_BYTES),
        cost_estimate=pl.CostEstimate(flops=10**9, bytes_accessed=4 * 10**6, transcendentals=10**6),
        name="attend_forward",
    )(meta, packed)


def attend_backward(meta, packed, grad, exact, log_total):
    blocks = packed.shape[0]
    return pl.pallas_call(
        lambda *refs: backward_kernel(meta.shape[0] - 1, *refs),
        out_shape=jax.ShapeDtypeStruct(packed.shape, BF16),
        in_specs=[pl.BlockSpec(memory_space=pltpu.SMEM)]
        + [pl.BlockSpec(memory_space=pltpu.VMEM)] * 4,
        out_specs=pl.BlockSpec(memory_space=pltpu.VMEM),
        scratch_shapes=[
            pltpu.VMEM((blocks, 256, DH), BF16),
            pltpu.VMEM((blocks, 256, DH), BF16),
            pltpu.VMEM((blocks, DH, 256), F32),
            pltpu.VMEM((blocks, DH, 256), F32),
        ],
        compiler_params=pltpu.CompilerParams(vmem_limit_bytes=VMEM_BYTES),
        cost_estimate=pl.CostEstimate(flops=3 * 10**9, bytes_accessed=4 * 10**6, transcendentals=10**6),
        name="attend_backward",
    )(meta, packed, grad, exact, log_total)


class HeadSplit:
    def __init__(self, latent_len, rows):
        self.rows = rows
        self.meta = jnp.concatenate([lax.axis_index("dp").astype(jnp.int32)[None] % 2, latent_len])

    def forward(self, packed):
        self.packed = exchange(packed, "dp")
        out, self.exact, self.log_total = attend_forward(self.meta, self.packed)
        return exchange(out, "dp")

    def backward(self, grad, due, beside):
        grad = exchange(grad, "dp")
        beside = swap(gate(beside, grad), "dp", lax.axis_size("dp") - 2)
        out = attend_backward(self.meta, self.packed, grad, self.exact, self.log_total)
        return exchange(gate(out, beside, *due), "dp"), beside


class Window:
    def __init__(self, latent_len, rows):
        self.rows = rows
        self.reach = (SEQ - 2) // rows + 1
        total = rows * lax.axis_size("dp")
        first = lax.axis_index("dp") * rows
        own = latent_index(latent_len, first, rows, total)
        ids = [
            latent_index(latent_len, first + offset * rows, rows, total)
            for offset in range(-self.reach, self.reach + 1)
        ]
        self.allowed = own[:, None] == jnp.concatenate(ids)[None, :]

    def from_behind(self, block, distance):
        devices = range(lax.axis_size("dp"))
        return lax.ppermute(
            block, "dp", [(i - distance, i) for i in devices if i - distance in devices]
        )

    def head_scores(self, query, key):
        raw = jnp.einsum("eq,ek->qk", query, key, preferred_element_type=F32) * SCALE
        return jnp.where(self.allowed, raw, NEGATIVE)

    def forward(self, packed):
        rows = self.rows
        split = packed.reshape(-1, 2, DH, rows * 5 // 2)
        query = jnp.concatenate([split[:, 0, :, 2 * rows :], split[:, 1, :, 2 * rows :]], axis=2)
        projected = jnp.stack([query, split[:, 0, :, :rows], split[:, 0, :, rows : 2 * rows]])
        key_value = projected[1:]
        pieces = [
            key_value if offset == 0 else self.from_behind(key_value, -offset)
            for offset in range(-self.reach, self.reach + 1)
        ]
        window = jnp.concatenate(pieces, axis=3)
        self.operands = (projected[0], window[0], window[1])

        def one(operands):
            query, key, value = operands
            scores = self.head_scores(query, key)
            largest = jnp.max(scores, axis=1, keepdims=True)
            weights = jnp.exp(scores - largest)
            totals = jnp.sum(weights, axis=1, keepdims=True)
            probs = (weights / totals).astype(BF16)
            mixed = jnp.einsum("qk,ek->eq", probs, value, preferred_element_type=F32)
            return mixed.astype(BF16), (largest + jnp.log(totals))[:, 0]

        out, self.log_total = lax.map(one, self.operands)
        out = out.reshape(-1, DH, 2, rows // 2).transpose(0, 2, 1, 3)
        return out.reshape(-1, DH, rows // 2)

    def backward(self, grad, due, beside):
        rows, reach = self.rows, self.reach
        halves = grad.reshape(-1, 2, DH, rows // 2)
        grads = jnp.concatenate([halves[:, 0], halves[:, 1]], axis=2)

        def one(operands):
            query, key, value, grad, log_total = operands
            probs = jnp.exp(self.head_scores(query, key) - log_total[:, None])
            d_value = jnp.einsum("qk,eq->ek", probs.astype(BF16), grad, preferred_element_type=F32)
            d_probs = jnp.einsum("eq,ek->qk", grad, value, preferred_element_type=F32)
            inner = jnp.sum(probs * d_probs, axis=1, keepdims=True)
            d_scores = (probs * (d_probs - inner)).astype(BF16)
            d_query = jnp.einsum("qk,ek->eq", d_scores, key, preferred_element_type=F32) * SCALE
            d_key = jnp.einsum("qk,eq->ek", d_scores, query, preferred_element_type=F32) * SCALE
            return d_query, d_key, d_value

        d_query, d_key, d_value = lax.map(one, self.operands + (grads, self.log_total))
        d_window = jnp.stack([d_key, d_value])
        d_key_value = d_window[..., reach * rows : (reach + 1) * rows]
        for offset in range(-reach, reach + 1):
            if offset != 0:
                block = d_window[..., (offset + reach) * rows : (offset + reach + 1) * rows]
                d_key_value = d_key_value + self.from_behind(block, offset)
        wide = jnp.concatenate([d_key_value[0], d_key_value[1]], axis=2)
        wide = jnp.stack([wide, jnp.zeros_like(wide)], axis=1)
        halves = d_query.reshape(-1, DH, 2, rows // 2).transpose(0, 2, 1, 3)
        packed = jnp.concatenate([wide, halves], axis=3).astype(BF16)
        return packed.reshape(-1, DH, rows * 5 // 2), beside


META = 4


def vmem(count):
    return [pl.BlockSpec(memory_space=pltpu.VMEM)] * count


def call(body, name, meta, arrays, outs, scratch=(), anywhere=0, due=(), flops=1):
    count = 1 + len(arrays)

    def kernel(*refs):
        body(*refs[:count], *refs[count + len(due) :])

    return pl.pallas_call(
        kernel,
        out_shape=tuple(jax.ShapeDtypeStruct(shape, kind) for shape, kind in outs),
        in_specs=[pl.BlockSpec(memory_space=pltpu.SMEM)]
        + [pl.BlockSpec(memory_space=pl.ANY)] * anywhere
        + vmem(len(arrays) - anywhere)
        + [pl.BlockSpec(memory_space=pl.ANY)] * len(due),
        out_specs=tuple(vmem(len(outs))),
        scratch_shapes=list(scratch),
        compiler_params=pltpu.CompilerParams(vmem_limit_bytes=VMEM_BYTES),
        cost_estimate=pl.CostEstimate(flops=flops, bytes_accessed=1, transcendentals=0),
        name=name,
    )(meta, *arrays, *due)


def row_masks(meta_ref, latents, first, rows):
    place = first + lax.broadcasted_iota(jnp.int32, (rows, 1), 0)
    ids = jnp.zeros((rows, 1), jnp.int32)
    end = jnp.int32(0)
    for number in range(latents - 1):
        end = end + meta_ref[META + number]
        ids = ids + (place >= end).astype(jnp.int32)
    return [(ids == number).astype(F32) for number in range(latents)]


def rows_of(mod_ref, masks, feature):
    out = masks[0] * mod_ref[feature : feature + 1, :]
    for number in range(1, len(masks)):
        row = number * 6 + feature
        out = out + masks[number] * mod_ref[row : row + 1, :]
    return out


def latent_sums(out_ref, masks, values, feature, features):
    rounded = values.astype(BF16).astype(F32)
    for number, mask in enumerate(masks):
        row = number * features + feature
        out_ref[row : row + 1, :] = jnp.sum(mask * rounded, axis=0, keepdims=True)


def own_rows(meta_ref, ref, share):
    start = pl.multiple_of(meta_ref[2] * share, share)
    return ref[pl.ds(start, share), :].astype(F32)


def on_core(meta_ref, body, mine, other):
    @pl.when(meta_ref[0] == 0)
    def _():
        body(mine, other)

    @pl.when(meta_ref[0] != 0)
    def _():
        body(other, mine)


def place_rows(meta_ref, parts, whole, sems):
    block = parts[0].shape[0]
    copies = []
    for step, part in enumerate(parts):
        start = pl.multiple_of((meta_ref[3] ^ step) * block, 16)
        copies.append(
            pltpu.make_async_copy(part, whole.at[pl.ds(start, block), :], sems.at[step])
        )
    return copies


def place_pair(meta_ref, mine, other, first_ref, second_ref, sems):
    def body(first, second):
        copies = place_rows(meta_ref, first, first_ref, sems.at[0])
        copies += place_rows(meta_ref, second, second_ref, sems.at[1])
        for copy in copies:
            copy.start()
        for copy in copies:
            copy.wait()

    on_core(meta_ref, body, mine, other)


def project_kernel(latents, count, meta_ref, *refs):
    mine, other = refs[:count], refs[count : 2 * count]
    tokens_ref, cot_ref, mod_parts_ref, bias_ref = refs[2 * count : 2 * count + 4]
    hidden_ref, d_mlp_ref, packed_ref, qk_ref, vp_ref, d_bias_ref, mod_ref, sems = refs[2 * count + 4 :]
    rows, width = tokens_ref.shape
    place_pair(meta_ref, mine, other, qk_ref, vp_ref, sems)
    columns = mod_parts_ref.shape[2]
    pieces = width // columns
    for piece in range(pieces):
        total = mod_parts_ref[piece].astype(F32)
        for part in range(piece + pieces, mod_parts_ref.shape[0], pieces):
            total = total + mod_parts_ref[part].astype(F32)
        mod_ref[:, piece * columns : (piece + 1) * columns] = total
    masks = row_masks(meta_ref, latents, meta_ref[1], rows)
    unit, _ = normed(tokens_ref[...].astype(F32))
    hidden = unit * (1.0 + rows_of(mod_ref, masks, 1)) + rows_of(mod_ref, masks, 0)
    hidden_ref[...] = hidden.astype(BF16)
    d_mlp = (cot_ref[...].astype(F32) * rows_of(mod_ref, masks, 5)).astype(BF16)
    d_mlp_ref[...] = d_mlp
    d_bias_ref[...] = jnp.sum(d_mlp.astype(F32), axis=0, keepdims=True)
    heads = packed_ref.shape[0] // 2
    features = heads * DH
    left = hidden_ref[...]
    both = jnp.dot(left, qk_ref[...], preferred_element_type=F32) + bias_ref[0:1, :]
    both = both.T
    value = jnp.dot(left, vp_ref[...], preferred_element_type=F32) + bias_ref[1:2, :]
    value = value.T
    for head in range(heads):
        start = head * DH
        query = both[start : start + DH].astype(BF16)
        key = both[features + start : features + start + DH].astype(BF16)
        val = value[start : start + DH].astype(BF16)
        for half in range(2):
            packed_ref[2 * head + half, :, :rows] = key
            packed_ref[2 * head + half, :, rows : 2 * rows] = val
            packed_ref[2 * head + half, :, 2 * rows :] = query[
                :, half * (rows // 2) : (half + 1) * (rows // 2)
            ]


def attend_out_kernel(meta_ref, parts_ref, vp_ref, part_ref, attended_ref):
    heads = parts_ref.shape[0] // 2
    rows = part_ref.shape[0]
    stacked = [jnp.zeros((heads * DH, rows), F32)]
    for head in range(heads):
        left = parts_ref[2 * head].astype(F32)
        right = parts_ref[2 * head + 1].astype(F32)
        stacked.append(jnp.concatenate([left, right], axis=1))
    attended_ref[...] = jnp.concatenate(stacked, axis=0).T.astype(BF16)
    part_ref[...] = lax.dot_general(
        attended_ref[...], vp_ref[...], (((1,), (1,)), ((), ())), preferred_element_type=F32
    ).astype(BF16)


def middle_kernel(
    latents, meta_ref, parts_ref, tokens_ref, mod_ref, bias_ref, sent_ref, attn_ref, mid_ref
):
    copies, share, width = parts_ref.shape
    masks = row_masks(meta_ref, latents, meta_ref[1] + meta_ref[2] * share, share)
    attn = bias_ref[...].astype(F32)
    for part in range(copies):
        attn = attn + parts_ref[part].astype(F32)
    attn_ref[...] = attn
    mid = own_rows(meta_ref, tokens_ref, share) + rows_of(mod_ref, masks, 2) * attn
    mid_ref[...] = mid
    unit, _ = normed(mid)
    hidden = unit * (1.0 + rows_of(mod_ref, masks, 4)) + rows_of(mod_ref, masks, 3)
    for part in range(copies):
        sent_ref[part] = hidden.astype(BF16)


def mlp_kernel(count, meta_ref, *refs):
    mine, other = refs[:count], refs[count : 2 * count]
    hidden_ref, d_mlp_ref, bias_ref = refs[2 * count : 2 * count + 3]
    d_two_ref, gelu_ref, d_pre_ref, d_bias_ref, left_ref, right_ref = refs[2 * count + 3 : 2 * count + 9]
    mlp_refs = refs[2 * count + 9 : -5]
    fc1_ref, fc2_ref, d_two_sum, mlp_sum, sems = refs[-5:]
    place_pair(meta_ref, mine, other, fc1_ref, fc2_ref, sems)
    d_two_sum[...] = jnp.zeros_like(d_two_sum)
    mlp_sum[...] = jnp.zeros_like(mlp_sum)
    tile = 384
    by_last = (((1,), (1,)), ((), ()))

    def step(number, carry):
        units = pl.ds(pl.multiple_of(number * tile, tile), tile)
        fc1, fc2 = fc1_ref[:, units], fc2_ref[:, units]
        pre = jnp.dot(hidden_ref[...], fc1, preferred_element_type=F32)
        gelu, slope = gelu_pair(pre + bias_ref[:, units].astype(F32))
        grad = jnp.dot(d_mlp_ref[...], fc2, preferred_element_type=F32)
        d_pre = (grad * slope).astype(BF16)
        gelu = gelu.astype(BF16)
        gelu_ref[:, units] = gelu
        d_pre_ref[:, units] = d_pre
        d_bias_ref[:, units] = jnp.sum(d_pre.astype(F32), axis=0, keepdims=True)
        d_two_sum[...] += lax.dot_general(d_pre, fc1, by_last, preferred_element_type=F32)
        mlp_sum[...] += lax.dot_general(gelu, fc2, by_last, preferred_element_type=F32)
        return carry

    lax.fori_loop(0, fc1_ref.shape[1] // tile, step, 0)
    d_two_ref[...] = d_two_sum[...].astype(BF16)
    def sent(left, right):
        left_ref[...] = left[0][...]
        right_ref[...] = left[1][...]

    on_core(meta_ref, sent, (d_mlp_ref, gelu_ref), (hidden_ref, d_pre_ref))
    share = mlp_refs[0].shape[0]
    for step, mlp_ref in enumerate(mlp_refs):
        start = pl.multiple_of((meta_ref[2] ^ step) * share, share)
        mlp_ref[...] = mlp_sum[pl.ds(start, share), :].astype(BF16)


def middle_back_kernel(
    latents, meta_ref, parts_ref, mid_in_ref, attn_ref, cot_ref, mod_ref, sent_ref, d_mid_ref, sums_ref
):
    copies, share, width = parts_ref.shape
    masks = row_masks(meta_ref, latents, meta_ref[1] + meta_ref[2] * share, share)
    d_hidden = parts_ref[0].astype(F32)
    for part in range(1, copies):
        d_hidden = d_hidden + parts_ref[part].astype(F32)
    unit, inverse = normed(mid_in_ref[...])
    d_mid = own_rows(meta_ref, cot_ref, share) + norm_back(
        unit, inverse, d_hidden * (1.0 + rows_of(mod_ref, masks, 4))
    )
    d_mid_ref[...] = d_mid
    d_attn = (d_mid * rows_of(mod_ref, masks, 2)).astype(BF16)
    for part in range(copies):
        sent_ref[part] = d_attn
    latent_sums(sums_ref, masks, d_mid * attn_ref[...], 0, 3)
    latent_sums(sums_ref, masks, d_hidden, 1, 3)
    latent_sums(sums_ref, masks, d_hidden * unit, 2, 3)


def result_kernel(
    latents, count, meta_ref, *refs
):
    parts = refs[:count]
    mid_ref, cot_ref, mod_ref, bias_ref, result_ref, sums_ref = refs[count:]
    share = result_ref.shape[0]
    masks = row_masks(meta_ref, latents, meta_ref[1] + meta_ref[2] * share, share)
    mlp = bias_ref[...].astype(F32)
    for part in parts:
        mlp = mlp + part[...].astype(F32)
    result_ref[...] = (mid_ref[...] + rows_of(mod_ref, masks, 5) * mlp).astype(BF16)
    latent_sums(sums_ref, masks, own_rows(meta_ref, cot_ref, share) * mlp, 0, 1)


def spread_kernel(meta_ref, d_attn_ref, vp_ref, packed_ref, d_bias_ref):
    grad = jnp.dot(d_attn_ref[...], vp_ref[...], preferred_element_type=F32).T
    half = grad.shape[1] // 2
    features = grad.shape[0] // 2
    for place in range(packed_ref.shape[0]):
        start = features + place // 2 * DH
        side = place % 2 * half
        packed_ref[place] = grad[start : start + DH, side : side + half].astype(BF16)
    d_bias_ref[...] = jnp.sum(d_attn_ref[...].astype(F32), axis=0, keepdims=True)


def unspread_kernel(
    meta_ref, parts_ref, qk_ref, vp_ref, d_one_ref, d_qk_ref, d_vp_ref, sent_ref, d_bias_ref
):
    heads = parts_ref.shape[0] // 2
    rows = d_one_ref.shape[0]
    query, key, value = [], [], []
    for head in range(heads):
        left = parts_ref[2 * head].astype(F32)
        right = parts_ref[2 * head + 1].astype(F32)
        both = left[:, : 2 * rows] + right[:, : 2 * rows]
        key.append(both[:, :rows])
        value.append(both[:, rows:])
        query.append(jnp.concatenate([left[:, 2 * rows :], right[:, 2 * rows :]], axis=1))
    d_qk_ref[...] = jnp.concatenate(query + key, axis=0).T.astype(BF16)
    blank = jnp.zeros((heads * DH, rows), F32)
    d_vp_ref[...] = jnp.concatenate(value + [blank], axis=0).T.astype(BF16)
    tile = 384
    by_last = (((1,), (1,)), ((), ()))

    def step(number, carry):
        columns = pl.ds(pl.multiple_of(number * tile, tile), tile)
        total = lax.dot_general(d_qk_ref[...], qk_ref[columns, :], by_last, preferred_element_type=F32)
        total += lax.dot_general(d_vp_ref[...], vp_ref[columns, :], by_last, preferred_element_type=F32)
        d_one_ref[:, columns] = total.astype(BF16)
        return carry

    lax.fori_loop(0, qk_ref.shape[0] // tile, step, 0)

    def sent(first, second):
        sent_ref[...] = first[...]

    on_core(meta_ref, sent, d_vp_ref, d_qk_ref)
    d_bias_ref[0:1, :] = jnp.sum(d_qk_ref[...].astype(F32), axis=0, keepdims=True)
    d_bias_ref[1:2, :] = jnp.sum(d_vp_ref[...].astype(F32), axis=0, keepdims=True)


def weight_kernel(first_pairs, second_pairs, meta_ref, *refs):
    operands = 1 + max(max(pair) for pair in first_pairs + second_pairs)
    ins, outs, total = refs[:operands], refs[operands:-1], refs[-1]
    tile = 384

    def body(pairs):
        def step(number, carry):
            columns = pl.ds(pl.multiple_of(number * tile, tile), tile)
            block = jnp.zeros((tile, total.shape[1]), F32)
            for left, right in pairs:
                block += lax.dot_general(
                    ins[left][:, columns], ins[right][...], (((0,), (0,)), ((), ())),
                    preferred_element_type=F32,
                )
            total[columns, :] = block.astype(BF16)
            return carry

        lax.fori_loop(0, total.shape[0] // tile, step, 0)

    on_core(meta_ref, lambda pairs, _: body(pairs), first_pairs, second_pairs)
    rows = outs[0].shape[0]
    for step, out in enumerate(outs):
        start = pl.multiple_of((meta_ref[3] ^ step) * rows, 16)
        out[...] = total[pl.ds(start, rows), :]


def first_back_kernel(
    latents, meta_ref, parts_ref, tokens_ref, d_mid_ref, mod_ref, mid_sums_ref, last_sums_ref,
    fc2_bias_ref, proj_bias_ref, fc1_bias_ref, qv_bias_ref, grad_ref, sent_ref, bias_ref, first_sums,
):
    copies, share, width = parts_ref.shape
    masks = row_masks(meta_ref, latents, meta_ref[1] + meta_ref[2] * share, share)
    d_hidden = parts_ref[0].astype(F32)
    for part in range(1, copies):
        d_hidden = d_hidden + parts_ref[part].astype(F32)
    unit, inverse = normed(own_rows(meta_ref, tokens_ref, share))
    grad = d_mid_ref[...] + norm_back(unit, inverse, d_hidden * (1.0 + rows_of(mod_ref, masks, 1)))
    grad_ref[...] = grad.astype(BF16)
    latent_sums(first_sums, masks, d_hidden, 0, 2)
    latent_sums(first_sums, masks, d_hidden * unit, 1, 2)
    columns = width // copies
    for number in range(latents):
        for feature in range(6):
            if feature < 2:
                row = first_sums[number * 2 + feature : number * 2 + feature + 1, :]
            elif feature < 5:
                place = number * 3 + feature - 2
                row = mid_sums_ref[place : place + 1, :]
            else:
                row = last_sums_ref[number : number + 1, :]
            place = number * 6 + feature
            for part in range(copies):
                sent_ref[part, place : place + 1, :] = row[:, part * columns : (part + 1) * columns]
    place = 0
    for ref in (fc2_bias_ref, proj_bias_ref, fc1_bias_ref):
        for start in range(0, ref.shape[1], columns):
            bias_ref[place : place + 1, :] = ref[:, start : start + columns]
            place += 1
    bias_ref[place : place + 2, :] = qv_bias_ref[:, :columns]


def order_kernel(count, meta_ref, *refs):
    result_ref, grad_ref = refs[2 * count :]
    share = refs[0].shape[0]
    for step in range(count):
        start = pl.multiple_of((meta_ref[2] ^ step) * share, share)
        result_ref[pl.ds(start, share), :] = refs[step][...]
        grad_ref[pl.ds(start, share), :] = refs[count + step][...].astype(F32)


def finish_kernel(
    latents, meta_ref, sums_ref, active_ref, w_ada_ref,
    w_grad_ref, b_grad_ref, d_active_ref, fc2_ref, proj_ref, fc1_ref, qv_ref, total_ref,
):
    total = sums_ref[0]
    for part in range(1, sums_ref.shape[0]):
        total = total + sums_ref[part]
    total_ref[...] = total
    by_last = (((1,), (1,)), ((), ()))
    d_active = jnp.zeros(d_active_ref.shape, F32)
    for feature in range(6):
        rows = [
            total_ref[number * 6 + feature : number * 6 + feature + 1, :] for number in range(latents)
        ]
        grad = active_ref[:, 0:1] * rows[0]
        bias = rows[0]
        for number in range(1, latents):
            grad = grad + active_ref[:, number : number + 1] * rows[number]
            bias = bias + rows[number]
        w_grad_ref[feature] = grad
        b_grad_ref[feature : feature + 1, :] = bias
        wide = jnp.concatenate(rows, axis=0)
        high = wide.astype(BF16)
        low = (wide - high.astype(F32)).astype(BF16)
        weight = w_ada_ref[feature]
        d_active += lax.dot_general(high, weight, by_last, preferred_element_type=F32)
        d_active += lax.dot_general(low, weight, by_last, preferred_element_type=F32)
    d_active_ref[...] = d_active
    columns = total_ref.shape[1]
    place = 6 * latents
    for ref in (fc2_ref, proj_ref, fc1_ref):
        for start in range(0, ref.shape[1], columns):
            ref[:, start : start + columns] = total_ref[place : place + 1, :]
            place += 1
    qv_ref[...] = total_ref[place : place + 2, :]


def latent_index(latent_len, first_row, row_count, token_total):
    positions = first_row + jnp.arange(row_count, dtype=jnp.int32)
    ends = jnp.cumsum(latent_len, dtype=jnp.int32)
    found = jnp.sum((positions[:, None] >= ends[None, :]).astype(jnp.int32), axis=1, dtype=jnp.int32)
    return jnp.where((positions >= 0) & (positions < token_total), found, -1)


def normed(values):
    average = jnp.mean(values, axis=-1, keepdims=True)
    centred = values - average
    spread = jnp.mean(centred * centred, axis=-1, keepdims=True)
    inverse = lax.rsqrt(spread + NORM_EPS)
    return centred * inverse, inverse


def norm_back(unit, inverse, grad):
    along = jnp.mean(grad * unit, axis=-1, keepdims=True)
    return inverse * (grad - jnp.mean(grad, axis=-1, keepdims=True) - unit * along)


def gelu_pair(value):
    root = math.sqrt(2.0 / math.pi)
    bend = jnp.tanh(root * (value + 0.044715 * value * value * value))
    slope = root * (1.0 + 3.0 * 0.044715 * value * value)
    gelu = 0.5 * value * (1.0 + bend)
    return gelu, 0.5 * (1.0 + bend) + 0.5 * value * (1.0 - bend * bend) * slope


def local(
    tokens,
    conditioning,
    latent_len,
    w_ada,
    b_ada,
    w_qkv,
    b_qv,
    w_proj,
    b_proj,
    w_fc1,
    b_fc1,
    w_fc2,
    b_fc2,
    cotangent,
):
    rows, width = tokens.shape
    share_width = w_qkv.shape[0]
    features = w_qkv.shape[2]
    units = w_fc1.shape[1]
    heads = features // DH
    latents = conditioning.shape[0]
    n_dp, n_tensor = lax.axis_size("dp"), lax.axis_size("tensor")
    my_dp, my_tensor = lax.axis_index("dp"), lax.axis_index("tensor")
    share = rows // n_tensor

    core = my_dp % 2
    qk = w_qkv[:, :2].reshape(share_width, 2 * features)
    vp = jnp.concatenate([w_qkv[:, 2], w_proj.T], axis=1)
    early_rows = pair_rows(qk, vp)

    cond = conditioning.astype(F32)
    sigmoid = 1.0 / (1.0 + jnp.exp(-cond))
    activated = (cond * sigmoid).astype(BF16)
    own_activated = lax.dynamic_slice_in_dim(activated, my_dp * share_width, share_width, 1)
    flat_ada = w_ada.reshape(share_width, 6 * features)
    mod_part = jnp.dot(own_activated, flat_ada, preferred_element_type=F32)
    mod_part = mod_part.reshape(latents * 6, features)
    bias_ada = jnp.tile(b_ada.astype(F32), (latents, 1))
    few_chips = n_dp // 2 == 4
    if few_chips:
        mod_part = mod_part + jnp.where(my_dp == 0, bias_ada, 0.0)
        mod_wide = gather(mod_part, "tensor", n_tensor)
        mod_parts = gather(mod_wide, "dp", n_dp).reshape((-1,) + mod_part.shape)
    else:
        mod_wide = jnp.sum(gather(mod_part, "dp", n_dp), axis=0) + bias_ada
        mod_parts = gather(mod_wide, "tensor", n_tensor)
    early_parts = chip_parts(early_rows) if few_chips else [gather_chips(early_rows)]

    early_parts = list(gate_all(early_parts, mod_wide))
    early_parts += [swap(part, "dp", 1) for part in early_parts]
    count = len(early_parts) // 2
    meta = jnp.stack([core, my_dp * rows, my_tensor, my_dp // 2]).astype(jnp.int32)
    meta = jnp.concatenate([meta, latent_len])
    place_meta = meta if few_chips else meta.at[3].set(0)
    by_last = (((1,), (1,)), ((), ()))
    by_token = (((0,), (0,)), ((), ()))
    bias = jnp.concatenate([b_qv[0], jnp.zeros_like(b_qv[0]), b_qv[1], jnp.zeros_like(b_qv[0])])
    hidden_one, d_mlp, packed, full_qk, full_vp, d_bias_fc2, mod_rows = call(
        lambda *refs: project_kernel(latents, count, *refs),
        "project",
        place_meta,
        (*early_parts, tokens, cotangent, mod_parts, bias.astype(F32).reshape(2, -1)),
        (((rows, width), BF16), ((rows, width), BF16), ((2 * heads, DH, rows * 5 // 2), BF16))
        + (((width, 2 * features), BF16),) * 2
        + (((1, width), F32), ((6 * latents, width), F32)),
        [pltpu.SemaphoreType.DMA((2, count))],
        2 * count,
    )
    late_rows = pair_rows(w_fc1, w_fc2.T)
    hidden_other = swap(hidden_one, "dp", 1)
    split = HeadSplit if 2 * heads == n_dp else Window
    attention = split(latent_len, rows)
    attended_parts = attention.forward(packed)
    late_rows = gate(late_rows, attended_parts)
    late_parts = chip_parts(late_rows)[:-1] if few_chips else [gather_chips(late_rows)]
    attn_part, attended = call(
        attend_out_kernel,
        "attend_out",
        meta,
        (attended_parts, full_vp),
        (((rows, width), BF16), ((rows, 2 * features), BF16)),
    )
    attn_parts = exchange_shares(attn_part, "tensor")
    hidden_blocks, attn_out, residual_mid = call(
        lambda *refs: middle_kernel(latents, *refs),
        "middle",
        meta,
        (attn_parts, tokens, mod_rows, b_proj.reshape(1, -1)),
        (((n_tensor, share, width), BF16), ((share, width), F32), ((share, width), F32)),
        due=late_parts[1:],
    )
    hidden_two = exchange(hidden_blocks, "tensor").reshape(rows, width)
    if few_chips:
        last_part = swap(gate(late_rows, attn_out), "dp", n_dp - 2)
        late_parts.append(gate(last_part, hidden_two))
    late_other = [swap(part, "dp", 1) for part in late_parts]

    d_two_part, gelu_out, d_pre, d_bias_fc1, left_sent, right_sent, *mlp_blocks = call(
        lambda *refs: mlp_kernel(count, *refs),
        "mlp",
        place_meta,
        (*late_parts, *late_other, hidden_two, d_mlp, b_fc1.reshape(1, -1)),
        (((rows, width), BF16), ((rows, units), BF16), ((rows, units), BF16), ((1, units), F32))
        + (((rows, width), BF16), ((rows, units), BF16))
        + (((share, width), BF16),) * n_tensor,
        [pltpu.VMEM((width, units), BF16)] * 2
        + [pltpu.VMEM((rows, width), F32)] * 2
        + [pltpu.SemaphoreType.DMA((2, count))],
        2 * count,
    )
    d_two_parts = exchange_shares(d_two_part, "tensor")

    chips = n_dp // 2 if few_chips else 1
    left_other = swap(left_sent, "dp", 1)
    right_other = swap(right_sent, "dp", 1)
    late_blocks = call(
        lambda *refs: weight_kernel([(0, 2), (4, 5)], [(1, 3), (4, 5)], *refs),
        "late_weights",
        place_meta,
        (hidden_two, d_mlp, d_pre, gelu_out, left_other, right_other),
        (((width // chips, units), BF16),) * chips,
        [pltpu.VMEM((width, units), BF16)],
    )
    late_grads = sum_chips(late_blocks[:-1]) if few_chips else sum_chips(late_blocks)

    d_attn_blocks, d_mid, mid_sums = call(
        lambda *refs: middle_back_kernel(latents, *refs),
        "middle_back",
        meta,
        (d_two_parts, residual_mid, attn_out, cotangent, mod_rows),
        (((n_tensor, share, width), BF16), ((share, width), F32), ((3 * latents, width), F32)),
        due=late_blocks,
    )
    d_attn = exchange(d_attn_blocks, "tensor").reshape(rows, width)

    d_spread, d_bias_proj = call(
        spread_kernel,
        "spread",
        meta,
        (d_attn, full_vp),
        (((2 * heads, DH, rows // 2), BF16), ((1, width), F32)),
        due=late_grads[1:],
    )
    mlp_parts = mlp_blocks[:1] + [
        swap(gate(block, d_spread), "tensor", step)
        for step, block in enumerate(mlp_blocks)
        if step
    ]
    d_attn_other = swap(d_attn, "dp", 1)
    attended_other = swap(attended, "dp", 1)
    d_packed, last_grad = attention.backward(d_spread, mlp_parts[1:], late_blocks[-1])
    result_own, last_sums = call(
        lambda *refs: result_kernel(latents, n_tensor, *refs),
        "result",
        meta,
        (*mlp_parts, residual_mid, cotangent, mod_rows, b_fc2.reshape(1, -1)),
        (((share, width), BF16), ((latents, width), F32)),
    )
    d_one_part, d_qk, d_vp, d_sent, d_bias_qv = call(
        unspread_kernel,
        "unspread",
        meta,
        (d_packed, full_qk, full_vp),
        (((rows, width), BF16),)
        + (((rows, 2 * features), BF16),) * 3
        + (((2, 2 * features), F32),),
        flops=2 * 10**10,
    )
    result_parts = [result_own] + [swap(result_own, "tensor", bits) for bits in range(1, n_tensor)]
    d_one_part = gate(d_one_part, *result_parts[1:])
    d_one_parts = exchange_shares(d_one_part, "tensor")

    if few_chips:
        late_grads.append(last_grad)
    right_other = swap(d_sent, "dp", 1)
    early_blocks = call(
        lambda *refs: weight_kernel(
            [(0, 2), (5, 7)], [(0, 3), (1, 4), (5, 7), (6, 8)], *refs
        ),
        "early_weights",
        place_meta,
        (hidden_one, d_attn, d_qk, d_vp, attended, hidden_other, d_attn_other, right_other, attended_other),
        (((width // chips, 2 * features), BF16),) * chips,
        [pltpu.VMEM((width, 2 * features), BF16)],
    )
    early_grads = sum_chips(early_blocks[:3] if few_chips else early_blocks)

    grad_own, d_mod_part, bias_rows = call(
        lambda *refs: first_back_kernel(latents, *refs),
        "first_back",
        meta,
        (d_one_parts, tokens, d_mid, mod_rows, mid_sums, last_sums)
        + (d_bias_fc2, d_bias_proj, d_bias_fc1, d_bias_qv),
        (((share, width), BF16), ((n_tensor, 6 * latents, features), F32))
        + (((2 * (width // features) + units // features + 2, features), F32),),
        [pltpu.VMEM((2 * latents, width), F32)],
        due=early_grads[1:3],
    )
    if few_chips:
        last_block = gate(early_blocks[3], d_mod_part)
        early_grads.append(swap(last_block, "dp", n_dp - 2))
    d_mod_mine = jnp.sum(exchange(d_mod_part, "tensor"), axis=0)
    d_mod_rows = jnp.concatenate([d_mod_mine, bias_rows])
    d_mod_rows = gate(jnp.broadcast_to(d_mod_rows[None], (n_dp,) + d_mod_rows.shape))
    grad_own = gate(grad_own, d_mod_rows)
    grad_parts = [grad_own] + [swap(grad_own, "tensor", bits) for bits in range(1, n_tensor)]
    sums = exchange(d_mod_rows, "dp")
    sums = gate(sums, early_grads[3]) if few_chips else sums
    grad_parts = gate_all(grad_parts, sums)
    result, grad_tokens = call(
        lambda *refs: order_kernel(n_tensor, *refs),
        "order",
        meta,
        (*result_parts, *grad_parts),
        (((rows, width), BF16), ((rows, width), F32)),
    )
    grad_w_ada, grad_b_ada, d_active, sum_b_fc2, sum_b_proj, sum_b_fc1, sum_b_qv = call(
        lambda *refs: finish_kernel(latents, *refs),
        "finish",
        meta,
        (sums, own_activated.astype(F32).T, w_ada.transpose(1, 0, 2)),
        (((6, share_width, features), F32), ((6, features), F32), ((latents, share_width), F32))
        + (((1, width), F32), ((1, width), F32), ((1, units), F32), ((2, features), F32)),
        [pltpu.VMEM(sums.shape[1:], F32)],
    )
    d_active = gather(d_active, ("dp", "tensor"), n_dp * n_tensor)
    d_active = jnp.sum(d_active.reshape(n_dp, n_tensor, latents, share_width), axis=1)
    d_active = d_active.transpose(1, 0, 2).reshape(latents, width)
    grad_cond = d_active * (sigmoid * (1.0 + cond * (1.0 - sigmoid)))

    grad_fc1, grad_fc2 = finish_pair(late_grads)
    grad_qk, grad_vp = finish_pair(early_grads)
    grad_qkv = jnp.concatenate([grad_qk, grad_vp[:, :features]], axis=1)
    grad_qkv = grad_qkv.reshape(share_width, 3, features)

    return (
        result,
        grad_tokens,
        grad_cond,
        grad_w_ada.transpose(1, 0, 2),
        grad_b_ada,
        grad_qkv,
        sum_b_qv,
        grad_vp[:, features:].T,
        sum_b_proj.reshape(width),
        grad_fc1,
        sum_b_fc1.reshape(units),
        grad_fc2.T,
        sum_b_fc2.reshape(width),
    )


def solution(mesh):
    in_specs = (
        P("dp", None),
        P(),
        P(),
        P("dp", None, "tensor"),
        P(None, "tensor"),
        P("dp", None, "tensor"),
        P(None, "tensor"),
        P("tensor", "dp"),
        P(),
        P("dp", "tensor"),
        P("tensor"),
        P("tensor", "dp"),
        P(),
        P("dp", None),
    )
    out_specs = (
        P("dp", None),
        P("dp", None),
        P(),
        P("dp", None, "tensor"),
        P(None, "tensor"),
        P("dp", None, "tensor"),
        P(None, "tensor"),
        P("tensor", "dp"),
        P(),
        P("dp", "tensor"),
        P("tensor"),
        P("tensor", "dp"),
        P(),
    )
    return jax.shard_map(local, mesh=mesh, in_specs=in_specs, out_specs=out_specs, check_vma=False)
```

```python
import math

import jax
import jax.numpy as jnp
from jax import lax
from jax.experimental import pallas as pl
from jax.experimental.pallas import tpu as pltpu
from jax.sharding import PartitionSpec as P

DH = 72
SEQ = 1024
STEP = 512
NORM_EPS = 1e-06
NEGATIVE = -1e30
SCALE = 1.0 / math.sqrt(DH)
VMEM_BYTES = 255 * 256 * 1024
BF16 = jnp.bfloat16
F32 = jnp.float32


def swap(block, axis, bits):
    route = [(i, i ^ bits) for i in range(lax.axis_size(axis))]
    return lax.ppermute(block, axis, route)


def exchange(blocks, axis):
    return lax.all_to_all(blocks, axis, 0, 0, tiled=True)


def gather(block, axis, count):
    return exchange(jnp.broadcast_to(block[None], (count,) + block.shape), axis)


def gate_all(values, *others):
    anywhere = pl.BlockSpec(memory_space=pl.ANY)
    return pl.pallas_call(
        lambda *refs: None,
        out_shape=tuple(jax.ShapeDtypeStruct(value.shape, value.dtype) for value in values),
        in_specs=[anywhere] * (len(values) + len(others)),
        out_specs=(anywhere,) * len(values),
        input_output_aliases={place: place for place in range(len(values))},
        cost_estimate=pl.CostEstimate(flops=1, bytes_accessed=1, transcendentals=0),
        name="gate",
    )(*values, *others)


def gate(value, *others):
    return gate_all((value,), *others)[0]


def choose(core, first, second):
    return jnp.where(core == 0, first, second), jnp.where(core == 0, second, first)


def pair_rows(first, second):
    core = lax.axis_index("dp") % 2
    keep, send = choose(core, first, second)
    return jnp.concatenate(choose(core, keep, swap(send, "dp", 1)))


def chip_parts(rows):
    count = lax.axis_size("dp") // 2
    return [rows] + [swap(rows, "dp", 2 * step) for step in range(1, count)]


def gather_chips(rows):
    count = lax.axis_size("dp")
    groups = [list(range(core, count, 2)) for core in range(2)]
    return lax.all_gather(rows, "dp", axis=0, tiled=True, axis_index_groups=groups)


def sum_chips(blocks):
    if len(blocks) == 1:
        count, chip = lax.axis_size("dp") // 2, lax.axis_index("dp") // 2
        rows = blocks[0].reshape((count, -1) + blocks[0].shape[1:])
        blocks = [
            lax.dynamic_index_in_dim(rows, chip ^ step, 0, keepdims=False) for step in range(count)
        ]
    return [swap(block, "dp", 2 * step) if step else block for step, block in enumerate(blocks)]


def finish_pair(parts):
    core = lax.axis_index("dp") % 2
    rows = sum(part.astype(F32) for part in parts)
    half = rows.shape[0] // 2
    keep, send = choose(core, rows[:half], rows[half:])
    return choose(core, keep, swap(send, "dp", 1))


def exchange_shares(partial, axis):
    count = lax.axis_size(axis)
    blocks = partial.reshape((count, partial.shape[0] // count) + partial.shape[1:])
    return exchange(blocks, axis)


def tile_range(meta_ref, latents, tile, core):
    lane = lax.broadcasted_iota(jnp.int32, (1, 256), 1)
    first = tile * 512 + core * 128
    last = first + 383
    place = first + lane + jnp.where(lane >= 128, 128, 0)
    begin = jnp.zeros((1, 256), jnp.int32)
    finish = jnp.zeros((1, 256), jnp.int32)
    low = jnp.int32(0)
    high = jnp.int32(0)
    start = jnp.int32(0)
    for number in range(latents):
        end = start + meta_ref[1 + number]
        inside = (place >= start) & (place < end)
        begin = jnp.where(inside, start, begin)
        finish = jnp.where(inside, end, finish)
        low = jnp.where((first >= start) & (first < end), start, low)
        high = jnp.where((last >= start) & (last < end), end, high)
        start = end
    return begin, finish, low // STEP, (high + STEP - 1) // STEP


def pair(ref, tile, start):
    left = ref[2 * tile, :, start : start + 128]
    right = ref[2 * tile + 1, :, start : start + 128]
    return jnp.concatenate([left, right], axis=1)


def wide(packed_ref, block, start):
    left = packed_ref[2 * block, :, start : start + 256]
    right = packed_ref[2 * block + 1, :, start : start + 256]
    return jnp.concatenate([left, right], axis=1)


def key_mask(block, begin, finish):
    place = block * STEP + lax.broadcasted_iota(jnp.int32, (STEP, 256), 0)
    return (place >= begin) & (place < finish)


def forward_kernel(latents, meta_ref, packed_ref, out_ref, exact_ref, log_ref, keys, scores):
    blocks = packed_ref.shape[0]
    core = meta_ref[0]
    for block in range(blocks // 2):
        keys[block] = wide(packed_ref, block, 0).astype(F32).T.astype(BF16)
    for tile in range(blocks // 2):
        begin, finish, low, high = tile_range(meta_ref, latents, tile, core)
        query = pair(packed_ref, tile, 512)

        def score(block, largest):
            raw = jnp.dot(keys[block], query, preferred_element_type=F32) * SCALE
            raw = jnp.where(key_mask(block, begin, finish), raw, NEGATIVE)
            scores[block] = raw
            return jnp.maximum(largest, jnp.max(raw, axis=0, keepdims=True))

        largest = lax.fori_loop(low, high, score, jnp.full((1, 256), NEGATIVE, F32))

        def mix(block, carry):
            total, mixed = carry
            weights = jnp.exp(scores[block] - largest)
            total = total + jnp.sum(weights, axis=0, keepdims=True)
            values = wide(packed_ref, block, 256)
            mixed = mixed + jnp.dot(values, weights.astype(BF16), preferred_element_type=F32)
            return total, mixed

        total, mixed = lax.fori_loop(
            low, high, mix, (jnp.zeros((1, 256), F32), jnp.zeros((DH, 256), F32))
        )
        mixed = mixed / total
        log_total = largest + jnp.log(total)
        for half in range(2):
            part = mixed[:, half * 128 : half * 128 + 128]
            exact_ref[2 * tile + half] = part
            out_ref[2 * tile + half] = part.astype(BF16)
            log_ref[2 * tile + half] = log_total[:, half * 128 : half * 128 + 128]


def backward_kernel(
    latents, meta_ref, packed_ref, grad_ref, exact_ref, log_ref, out_ref, keys, values, d_keys, d_values
):
    blocks = packed_ref.shape[0]
    core = meta_ref[0]
    for block in range(blocks // 2):
        keys[block] = wide(packed_ref, block, 0).astype(F32).T.astype(BF16)
        values[block] = wide(packed_ref, block, 256).astype(F32).T.astype(BF16)
    d_keys[...] = jnp.zeros_like(d_keys)
    d_values[...] = jnp.zeros_like(d_values)
    by_query = (((1,), (1,)), ((), ()))
    for tile in range(blocks // 2):
        begin, finish, low, high = tile_range(meta_ref, latents, tile, core)
        query = pair(packed_ref, tile, 512)
        grad = pair(grad_ref, tile, 0)
        inner = jnp.sum(grad.astype(F32) * pair(exact_ref, tile, 0), axis=0, keepdims=True)
        log_total = pair(log_ref, tile, 0)

        def step(block, d_query):
            raw = jnp.dot(keys[block], query, preferred_element_type=F32) * SCALE
            probs = jnp.where(key_mask(block, begin, finish), jnp.exp(raw - log_total), 0.0)
            d_probs = jnp.dot(values[block], grad, preferred_element_type=F32)
            d_scores = (probs * (d_probs - inner)).astype(BF16)
            d_values[block] += lax.dot_general(
                grad, probs.astype(BF16), by_query, preferred_element_type=F32
            )
            d_keys[block] += lax.dot_general(query, d_scores, by_query, preferred_element_type=F32)
            key_rows = wide(packed_ref, block, 0)
            return d_query + jnp.dot(key_rows, d_scores, preferred_element_type=F32)

        d_query = lax.fori_loop(low, high, step, jnp.zeros((DH, 256), F32)) * SCALE
        for half in range(2):
            part = d_query[:, half * 128 : half * 128 + 128]
            out_ref[2 * tile + half, :, 512:640] = part.astype(BF16)
    for block in range(blocks):
        half = slice(block % 2 * 256, block % 2 * 256 + 256)
        out_ref[block, :, :256] = (d_keys[block // 2, :, half] * SCALE).astype(BF16)
        out_ref[block, :, 256:512] = d_values[block // 2, :, half].astype(BF16)


def attend_forward(meta, packed):
    blocks = packed.shape[0]
    shape = jax.ShapeDtypeStruct
    return pl.pallas_call(
        lambda *refs: forward_kernel(meta.shape[0] - 1, *refs),
        out_shape=(
            shape((blocks, DH, 128), BF16),
            shape((blocks, DH, 128), F32),
            shape((blocks, 1, 128), F32),
        ),
        in_specs=[
            pl.BlockSpec(memory_space=pltpu.SMEM),
            pl.BlockSpec(memory_space=pltpu.VMEM),
        ],
        out_specs=tuple([pl.BlockSpec(memory_space=pltpu.VMEM)] * 3),
        scratch_shapes=[
            pltpu.VMEM((blocks // 2, STEP, DH), BF16),
            pltpu.VMEM((blocks // 2, STEP, 256), F32),
        ],
        compiler_params=pltpu.CompilerParams(vmem_limit_bytes=VMEM_BYTES),
        cost_estimate=pl.CostEstimate(flops=10**9, bytes_accessed=4 * 10**6, transcendentals=10**6),
        name="attend_forward",
    )(meta, packed)


def attend_backward(meta, packed, grad, exact, log_total):
    blocks = packed.shape[0]
    return pl.pallas_call(
        lambda *refs: backward_kernel(meta.shape[0] - 1, *refs),
        out_shape=jax.ShapeDtypeStruct(packed.shape, BF16),
        in_specs=[pl.BlockSpec(memory_space=pltpu.SMEM)]
        + [pl.BlockSpec(memory_space=pltpu.VMEM)] * 4,
        out_specs=pl.BlockSpec(memory_space=pltpu.VMEM),
        scratch_shapes=[
            pltpu.VMEM((blocks // 2, STEP, DH), BF16),
            pltpu.VMEM((blocks // 2, STEP, DH), BF16),
            pltpu.VMEM((blocks // 2, DH, STEP), F32),
            pltpu.VMEM((blocks // 2, DH, STEP), F32),
        ],
        compiler_params=pltpu.CompilerParams(vmem_limit_bytes=VMEM_BYTES),
        cost_estimate=pl.CostEstimate(flops=3 * 10**9, bytes_accessed=4 * 10**6, transcendentals=10**6),
        name="attend_backward",
    )(meta, packed, grad, exact, log_total)


class HeadSplit:
    def __init__(self, latent_len, rows):
        self.rows = rows
        self.meta = jnp.concatenate([lax.axis_index("dp").astype(jnp.int32)[None] % 2, latent_len])

    def forward(self, packed):
        self.packed = exchange(packed, "dp")
        out, self.exact, self.log_total = attend_forward(self.meta, self.packed)
        return exchange(out, "dp")

    def backward(self, grad, due, beside):
        grad = exchange(grad, "dp")
        beside = swap(gate(beside, grad), "dp", lax.axis_size("dp") - 2)
        out = attend_backward(self.meta, self.packed, grad, self.exact, self.log_total)
        return exchange(gate(out, beside, *due), "dp"), beside


class Window:
    def __init__(self, latent_len, rows):
        self.rows = rows
        self.reach = (SEQ - 2) // rows + 1
        total = rows * lax.axis_size("dp")
        first = lax.axis_index("dp") * rows
        own = latent_index(latent_len, first, rows, total)
        ids = [
            latent_index(latent_len, first + offset * rows, rows, total)
            for offset in range(-self.reach, self.reach + 1)
        ]
        self.allowed = own[:, None] == jnp.concatenate(ids)[None, :]

    def from_behind(self, block, distance):
        devices = range(lax.axis_size("dp"))
        return lax.ppermute(
            block, "dp", [(i - distance, i) for i in devices if i - distance in devices]
        )

    def head_scores(self, query, key):
        raw = jnp.einsum("eq,ek->qk", query, key, preferred_element_type=F32) * SCALE
        return jnp.where(self.allowed, raw, NEGATIVE)

    def forward(self, packed):
        rows = self.rows
        split = packed.reshape(-1, 2, DH, rows * 5 // 2)
        query = jnp.concatenate([split[:, 0, :, 2 * rows :], split[:, 1, :, 2 * rows :]], axis=2)
        projected = jnp.stack([query, split[:, 0, :, :rows], split[:, 0, :, rows : 2 * rows]])
        key_value = projected[1:]
        pieces = [
            key_value if offset == 0 else self.from_behind(key_value, -offset)
            for offset in range(-self.reach, self.reach + 1)
        ]
        window = jnp.concatenate(pieces, axis=3)
        self.operands = (projected[0], window[0], window[1])

        def one(operands):
            query, key, value = operands
            scores = self.head_scores(query, key)
            largest = jnp.max(scores, axis=1, keepdims=True)
            weights = jnp.exp(scores - largest)
            totals = jnp.sum(weights, axis=1, keepdims=True)
            probs = (weights / totals).astype(BF16)
            mixed = jnp.einsum("qk,ek->eq", probs, value, preferred_element_type=F32)
            return mixed.astype(BF16), (largest + jnp.log(totals))[:, 0]

        out, self.log_total = lax.map(one, self.operands)
        out = out.reshape(-1, DH, 2, rows // 2).transpose(0, 2, 1, 3)
        return out.reshape(-1, DH, rows // 2)

    def backward(self, grad, due, beside):
        rows, reach = self.rows, self.reach
        halves = grad.reshape(-1, 2, DH, rows // 2)
        grads = jnp.concatenate([halves[:, 0], halves[:, 1]], axis=2)

        def one(operands):
            query, key, value, grad, log_total = operands
            probs = jnp.exp(self.head_scores(query, key) - log_total[:, None])
            d_value = jnp.einsum("qk,eq->ek", probs.astype(BF16), grad, preferred_element_type=F32)
            d_probs = jnp.einsum("eq,ek->qk", grad, value, preferred_element_type=F32)
            inner = jnp.sum(probs * d_probs, axis=1, keepdims=True)
            d_scores = (probs * (d_probs - inner)).astype(BF16)
            d_query = jnp.einsum("qk,ek->eq", d_scores, key, preferred_element_type=F32) * SCALE
            d_key = jnp.einsum("qk,eq->ek", d_scores, query, preferred_element_type=F32) * SCALE
            return d_query, d_key, d_value

        d_query, d_key, d_value = lax.map(one, self.operands + (grads, self.log_total))
        d_window = jnp.stack([d_key, d_value])
        d_key_value = d_window[..., reach * rows : (reach + 1) * rows]
        for offset in range(-reach, reach + 1):
            if offset != 0:
                block = d_window[..., (offset + reach) * rows : (offset + reach + 1) * rows]
                d_key_value = d_key_value + self.from_behind(block, offset)
        wide = jnp.concatenate([d_key_value[0], d_key_value[1]], axis=2)
        wide = jnp.stack([wide, jnp.zeros_like(wide)], axis=1)
        halves = d_query.reshape(-1, DH, 2, rows // 2).transpose(0, 2, 1, 3)
        packed = jnp.concatenate([wide, halves], axis=3).astype(BF16)
        return packed.reshape(-1, DH, rows * 5 // 2), beside


META = 4


def vmem(count):
    return [pl.BlockSpec(memory_space=pltpu.VMEM)] * count


def call(body, name, meta, arrays, outs, scratch=(), anywhere=0, due=(), flops=1):
    count = 1 + len(arrays)

    def kernel(*refs):
        body(*refs[:count], *refs[count + len(due) :])

    return pl.pallas_call(
        kernel,
        out_shape=tuple(jax.ShapeDtypeStruct(shape, kind) for shape, kind in outs),
        in_specs=[pl.BlockSpec(memory_space=pltpu.SMEM)]
        + [pl.BlockSpec(memory_space=pl.ANY)] * anywhere
        + vmem(len(arrays) - anywhere)
        + [pl.BlockSpec(memory_space=pl.ANY)] * len(due),
        out_specs=tuple(vmem(len(outs))),
        scratch_shapes=list(scratch),
        compiler_params=pltpu.CompilerParams(vmem_limit_bytes=VMEM_BYTES),
        cost_estimate=pl.CostEstimate(flops=flops, bytes_accessed=1, transcendentals=0),
        name=name,
    )(meta, *arrays, *due)


def row_masks(meta_ref, latents, first, rows):
    place = first + lax.broadcasted_iota(jnp.int32, (rows, 1), 0)
    ids = jnp.zeros((rows, 1), jnp.int32)
    end = jnp.int32(0)
    for number in range(latents - 1):
        end = end + meta_ref[META + number]
        ids = ids + (place >= end).astype(jnp.int32)
    return [(ids == number).astype(F32) for number in range(latents)]


def rows_of(mod_ref, masks, feature):
    out = masks[0] * mod_ref[feature : feature + 1, :]
    for number in range(1, len(masks)):
        row = number * 6 + feature
        out = out + masks[number] * mod_ref[row : row + 1, :]
    return out


def latent_sums(out_ref, masks, values, feature, features):
    rounded = values.astype(BF16).astype(F32)
    for number, mask in enumerate(masks):
        row = number * features + feature
        out_ref[row : row + 1, :] = jnp.sum(mask * rounded, axis=0, keepdims=True)


def own_rows(meta_ref, ref, share):
    start = pl.multiple_of(meta_ref[2] * share, share)
    return ref[pl.ds(start, share), :].astype(F32)


def on_core(meta_ref, body, mine, other):
    @pl.when(meta_ref[0] == 0)
    def _():
        body(mine, other)

    @pl.when(meta_ref[0] != 0)
    def _():
        body(other, mine)


def place_rows(meta_ref, parts, whole, sems):
    block = parts[0].shape[0]
    copies = []
    for step, part in enumerate(parts):
        start = pl.multiple_of((meta_ref[3] ^ step) * block, 16)
        copies.append(
            pltpu.make_async_copy(part, whole.at[pl.ds(start, block), :], sems.at[step])
        )
    return copies


def place_pair(meta_ref, mine, other, first_ref, second_ref, sems):
    def body(first, second):
        copies = place_rows(meta_ref, first, first_ref, sems.at[0])
        copies += place_rows(meta_ref, second, second_ref, sems.at[1])
        for copy in copies:
            copy.start()
        for copy in copies:
            copy.wait()

    on_core(meta_ref, body, mine, other)


def project_kernel(latents, count, meta_ref, *refs):
    mine, other = refs[:count], refs[count : 2 * count]
    tokens_ref, cot_ref, mod_parts_ref, bias_ref = refs[2 * count : 2 * count + 4]
    hidden_ref, d_mlp_ref, packed_ref, qk_ref, vp_ref, d_bias_ref, mod_ref, sems = refs[2 * count + 4 :]
    rows, width = tokens_ref.shape
    place_pair(meta_ref, mine, other, qk_ref, vp_ref, sems)
    columns = mod_parts_ref.shape[2]
    pieces = width // columns
    for piece in range(pieces):
        total = mod_parts_ref[piece].astype(F32)
        for part in range(piece + pieces, mod_parts_ref.shape[0], pieces):
            total = total + mod_parts_ref[part].astype(F32)
        mod_ref[:, piece * columns : (piece + 1) * columns] = total
    masks = row_masks(meta_ref, latents, meta_ref[1], rows)
    unit, _ = normed(tokens_ref[...].astype(F32))
    hidden = unit * (1.0 + rows_of(mod_ref, masks, 1)) + rows_of(mod_ref, masks, 0)
    hidden_ref[...] = hidden.astype(BF16)
    d_mlp = (cot_ref[...].astype(F32) * rows_of(mod_ref, masks, 5)).astype(BF16)
    d_mlp_ref[...] = d_mlp
    d_bias_ref[...] = jnp.sum(d_mlp.astype(F32), axis=0, keepdims=True)
    heads = packed_ref.shape[0] // 2
    features = heads * DH
    left = hidden_ref[...]
    both = jnp.dot(left, qk_ref[...], preferred_element_type=F32) + bias_ref[0:1, :]
    both = both.T
    value = jnp.dot(left, vp_ref[...], preferred_element_type=F32) + bias_ref[1:2, :]
    value = value.T
    for head in range(heads):
        start = head * DH
        query = both[start : start + DH].astype(BF16)
        key = both[features + start : features + start + DH].astype(BF16)
        val = value[start : start + DH].astype(BF16)
        for half in range(2):
            packed_ref[2 * head + half, :, :rows] = key
            packed_ref[2 * head + half, :, rows : 2 * rows] = val
            packed_ref[2 * head + half, :, 2 * rows :] = query[
                :, half * (rows // 2) : (half + 1) * (rows // 2)
            ]


def attend_out_kernel(meta_ref, parts_ref, vp_ref, part_ref, attended_ref):
    heads = parts_ref.shape[0] // 2
    rows = part_ref.shape[0]
    stacked = [jnp.zeros((heads * DH, rows), F32)]
    for head in range(heads):
        left = parts_ref[2 * head].astype(F32)
        right = parts_ref[2 * head + 1].astype(F32)
        stacked.append(jnp.concatenate([left, right], axis=1))
    attended_ref[...] = jnp.concatenate(stacked, axis=0).T.astype(BF16)
    part_ref[...] = lax.dot_general(
        attended_ref[...], vp_ref[...], (((1,), (1,)), ((), ())), preferred_element_type=F32
    ).astype(BF16)


def middle_kernel(
    latents, meta_ref, parts_ref, tokens_ref, mod_ref, bias_ref, sent_ref, attn_ref, mid_ref
):
    copies, share, width = parts_ref.shape
    masks = row_masks(meta_ref, latents, meta_ref[1] + meta_ref[2] * share, share)
    attn = bias_ref[...].astype(F32)
    for part in range(copies):
        attn = attn + parts_ref[part].astype(F32)
    attn_ref[...] = attn
    mid = own_rows(meta_ref, tokens_ref, share) + rows_of(mod_ref, masks, 2) * attn
    mid_ref[...] = mid
    unit, _ = normed(mid)
    hidden = unit * (1.0 + rows_of(mod_ref, masks, 4)) + rows_of(mod_ref, masks, 3)
    for part in range(copies):
        sent_ref[part] = hidden.astype(BF16)


def mlp_kernel(count, meta_ref, *refs):
    mine, other = refs[:count], refs[count : 2 * count]
    hidden_ref, d_mlp_ref, bias_ref = refs[2 * count : 2 * count + 3]
    d_two_ref, gelu_ref, d_pre_ref, d_bias_ref, left_ref, right_ref = refs[2 * count + 3 : 2 * count + 9]
    mlp_refs = refs[2 * count + 9 : -5]
    fc1_ref, fc2_ref, d_two_sum, mlp_sum, sems = refs[-5:]
    place_pair(meta_ref, mine, other, fc1_ref, fc2_ref, sems)
    d_two_sum[...] = jnp.zeros_like(d_two_sum)
    mlp_sum[...] = jnp.zeros_like(mlp_sum)
    tile = 384
    by_last = (((1,), (1,)), ((), ()))

    def step(number, carry):
        units = pl.ds(pl.multiple_of(number * tile, tile), tile)
        fc1, fc2 = fc1_ref[:, units], fc2_ref[:, units]
        pre = jnp.dot(hidden_ref[...], fc1, preferred_element_type=F32)
        gelu, slope = gelu_pair(pre + bias_ref[:, units].astype(F32))
        grad = jnp.dot(d_mlp_ref[...], fc2, preferred_element_type=F32)
        d_pre = (grad * slope).astype(BF16)
        gelu = gelu.astype(BF16)
        gelu_ref[:, units] = gelu
        d_pre_ref[:, units] = d_pre
        d_bias_ref[:, units] = jnp.sum(d_pre.astype(F32), axis=0, keepdims=True)
        d_two_sum[...] += lax.dot_general(d_pre, fc1, by_last, preferred_element_type=F32)
        mlp_sum[...] += lax.dot_general(gelu, fc2, by_last, preferred_element_type=F32)
        return carry

    lax.fori_loop(0, fc1_ref.shape[1] // tile, step, 0)
    d_two_ref[...] = d_two_sum[...].astype(BF16)
    def sent(left, right):
        left_ref[...] = left[0][...]
        right_ref[...] = left[1][...]

    on_core(meta_ref, sent, (d_mlp_ref, gelu_ref), (hidden_ref, d_pre_ref))
    share = mlp_refs[0].shape[0]
    for step, mlp_ref in enumerate(mlp_refs):
        start = pl.multiple_of((meta_ref[2] ^ step) * share, share)
        mlp_ref[...] = mlp_sum[pl.ds(start, share), :].astype(BF16)


def middle_back_kernel(
    latents, meta_ref, parts_ref, mid_in_ref, attn_ref, cot_ref, mod_ref, sent_ref, d_mid_ref, sums_ref
):
    copies, share, width = parts_ref.shape
    masks = row_masks(meta_ref, latents, meta_ref[1] + meta_ref[2] * share, share)
    d_hidden = parts_ref[0].astype(F32)
    for part in range(1, copies):
        d_hidden = d_hidden + parts_ref[part].astype(F32)
    unit, inverse = normed(mid_in_ref[...])
    d_mid = own_rows(meta_ref, cot_ref, share) + norm_back(
        unit, inverse, d_hidden * (1.0 + rows_of(mod_ref, masks, 4))
    )
    d_mid_ref[...] = d_mid
    d_attn = (d_mid * rows_of(mod_ref, masks, 2)).astype(BF16)
    for part in range(copies):
        sent_ref[part] = d_attn
    latent_sums(sums_ref, masks, d_mid * attn_ref[...], 0, 3)
    latent_sums(sums_ref, masks, d_hidden, 1, 3)
    latent_sums(sums_ref, masks, d_hidden * unit, 2, 3)


def result_kernel(
    latents, count, meta_ref, *refs
):
    parts = refs[:count]
    mid_ref, cot_ref, mod_ref, bias_ref, result_ref, sums_ref = refs[count:]
    share = result_ref.shape[0]
    masks = row_masks(meta_ref, latents, meta_ref[1] + meta_ref[2] * share, share)
    mlp = bias_ref[...].astype(F32)
    for part in parts:
        mlp = mlp + part[...].astype(F32)
    result_ref[...] = (mid_ref[...] + rows_of(mod_ref, masks, 5) * mlp).astype(BF16)
    latent_sums(sums_ref, masks, own_rows(meta_ref, cot_ref, share) * mlp, 0, 1)


def spread_kernel(meta_ref, d_attn_ref, vp_ref, packed_ref, d_bias_ref):
    grad = jnp.dot(d_attn_ref[...], vp_ref[...], preferred_element_type=F32).T
    half = grad.shape[1] // 2
    features = grad.shape[0] // 2
    for place in range(packed_ref.shape[0]):
        start = features + place // 2 * DH
        side = place % 2 * half
        packed_ref[place] = grad[start : start + DH, side : side + half].astype(BF16)
    d_bias_ref[...] = jnp.sum(d_attn_ref[...].astype(F32), axis=0, keepdims=True)


def unspread_kernel(
    meta_ref, parts_ref, qk_ref, vp_ref, d_one_ref, d_qk_ref, d_vp_ref, sent_ref, d_bias_ref
):
    heads = parts_ref.shape[0] // 2
    rows = d_one_ref.shape[0]
    query, key, value = [], [], []
    for head in range(heads):
        left = parts_ref[2 * head].astype(F32)
        right = parts_ref[2 * head + 1].astype(F32)
        both = left[:, : 2 * rows] + right[:, : 2 * rows]
        key.append(both[:, :rows])
        value.append(both[:, rows:])
        query.append(jnp.concatenate([left[:, 2 * rows :], right[:, 2 * rows :]], axis=1))
    d_qk_ref[...] = jnp.concatenate(query + key, axis=0).T.astype(BF16)
    blank = jnp.zeros((heads * DH, rows), F32)
    d_vp_ref[...] = jnp.concatenate(value + [blank], axis=0).T.astype(BF16)
    tile = 384
    by_last = (((1,), (1,)), ((), ()))

    def step(number, carry):
        columns = pl.ds(pl.multiple_of(number * tile, tile), tile)
        total = lax.dot_general(d_qk_ref[...], qk_ref[columns, :], by_last, preferred_element_type=F32)
        total += lax.dot_general(d_vp_ref[...], vp_ref[columns, :], by_last, preferred_element_type=F32)
        d_one_ref[:, columns] = total.astype(BF16)
        return carry

    lax.fori_loop(0, qk_ref.shape[0] // tile, step, 0)

    def sent(first, second):
        sent_ref[...] = first[...]

    on_core(meta_ref, sent, d_vp_ref, d_qk_ref)
    d_bias_ref[0:1, :] = jnp.sum(d_qk_ref[...].astype(F32), axis=0, keepdims=True)
    d_bias_ref[1:2, :] = jnp.sum(d_vp_ref[...].astype(F32), axis=0, keepdims=True)


def weight_kernel(first_pairs, second_pairs, meta_ref, *refs):
    operands = 1 + max(max(pair) for pair in first_pairs + second_pairs)
    ins, outs, total = refs[:operands], refs[operands:-1], refs[-1]
    tile = 384

    def body(pairs):
        def step(number, carry):
            columns = pl.ds(pl.multiple_of(number * tile, tile), tile)
            block = jnp.zeros((tile, total.shape[1]), F32)
            for left, right in pairs:
                block += lax.dot_general(
                    ins[left][:, columns], ins[right][...], (((0,), (0,)), ((), ())),
                    preferred_element_type=F32,
                )
            total[columns, :] = block.astype(BF16)
            return carry

        lax.fori_loop(0, total.shape[0] // tile, step, 0)

    on_core(meta_ref, lambda pairs, _: body(pairs), first_pairs, second_pairs)
    rows = outs[0].shape[0]
    for step, out in enumerate(outs):
        start = pl.multiple_of((meta_ref[3] ^ step) * rows, 16)
        out[...] = total[pl.ds(start, rows), :]


def first_back_kernel(
    latents, meta_ref, parts_ref, tokens_ref, d_mid_ref, mod_ref, mid_sums_ref, last_sums_ref,
    fc2_bias_ref, proj_bias_ref, fc1_bias_ref, qv_bias_ref, grad_ref, sent_ref, bias_ref, first_sums,
):
    copies, share, width = parts_ref.shape
    masks = row_masks(meta_ref, latents, meta_ref[1] + meta_ref[2] * share, share)
    d_hidden = parts_ref[0].astype(F32)
    for part in range(1, copies):
        d_hidden = d_hidden + parts_ref[part].astype(F32)
    unit, inverse = normed(own_rows(meta_ref, tokens_ref, share))
    grad = d_mid_ref[...] + norm_back(unit, inverse, d_hidden * (1.0 + rows_of(mod_ref, masks, 1)))
    grad_ref[...] = grad.astype(BF16)
    latent_sums(first_sums, masks, d_hidden, 0, 2)
    latent_sums(first_sums, masks, d_hidden * unit, 1, 2)
    columns = width // copies
    for number in range(latents):
        for feature in range(6):
            if feature < 2:
                row = first_sums[number * 2 + feature : number * 2 + feature + 1, :]
            elif feature < 5:
                place = number * 3 + feature - 2
                row = mid_sums_ref[place : place + 1, :]
            else:
                row = last_sums_ref[number : number + 1, :]
            place = number * 6 + feature
            for part in range(copies):
                sent_ref[part, place : place + 1, :] = row[:, part * columns : (part + 1) * columns]
    place = 0
    for ref in (fc2_bias_ref, proj_bias_ref, fc1_bias_ref):
        for start in range(0, ref.shape[1], columns):
            bias_ref[place : place + 1, :] = ref[:, start : start + columns]
            place += 1
    bias_ref[place : place + 2, :] = qv_bias_ref[:, :columns]


def order_kernel(count, meta_ref, *refs):
    result_ref, grad_ref = refs[2 * count :]
    share = refs[0].shape[0]
    for step in range(count):
        start = pl.multiple_of((meta_ref[2] ^ step) * share, share)
        result_ref[pl.ds(start, share), :] = refs[step][...]
        grad_ref[pl.ds(start, share), :] = refs[count + step][...].astype(F32)


def finish_kernel(
    latents, meta_ref, sums_ref, active_ref, w_ada_ref,
    w_grad_ref, b_grad_ref, d_active_ref, fc2_ref, proj_ref, fc1_ref, qv_ref, total_ref,
):
    total = sums_ref[0]
    for part in range(1, sums_ref.shape[0]):
        total = total + sums_ref[part]
    total_ref[...] = total
    by_last = (((1,), (1,)), ((), ()))
    d_active = jnp.zeros(d_active_ref.shape, F32)
    for feature in range(6):
        rows = [
            total_ref[number * 6 + feature : number * 6 + feature + 1, :] for number in range(latents)
        ]
        grad = active_ref[:, 0:1] * rows[0]
        bias = rows[0]
        for number in range(1, latents):
            grad = grad + active_ref[:, number : number + 1] * rows[number]
            bias = bias + rows[number]
        w_grad_ref[feature] = grad
        b_grad_ref[feature : feature + 1, :] = bias
        wide = jnp.concatenate(rows, axis=0)
        high = wide.astype(BF16)
        low = (wide - high.astype(F32)).astype(BF16)
        weight = w_ada_ref[feature]
        d_active += lax.dot_general(high, weight, by_last, preferred_element_type=F32)
        d_active += lax.dot_general(low, weight, by_last, preferred_element_type=F32)
    d_active_ref[...] = d_active
    columns = total_ref.shape[1]
    place = 6 * latents
    for ref in (fc2_ref, proj_ref, fc1_ref):
        for start in range(0, ref.shape[1], columns):
            ref[:, start : start + columns] = total_ref[place : place + 1, :]
            place += 1
    qv_ref[...] = total_ref[place : place + 2, :]


def latent_index(latent_len, first_row, row_count, token_total):
    positions = first_row + jnp.arange(row_count, dtype=jnp.int32)
    ends = jnp.cumsum(latent_len, dtype=jnp.int32)
    found = jnp.sum((positions[:, None] >= ends[None, :]).astype(jnp.int32), axis=1, dtype=jnp.int32)
    return jnp.where((positions >= 0) & (positions < token_total), found, -1)


def normed(values):
    average = jnp.mean(values, axis=-1, keepdims=True)
    centred = values - average
    spread = jnp.mean(centred * centred, axis=-1, keepdims=True)
    inverse = lax.rsqrt(spread + NORM_EPS)
    return centred * inverse, inverse


def norm_back(unit, inverse, grad):
    along = jnp.mean(grad * unit, axis=-1, keepdims=True)
    return inverse * (grad - jnp.mean(grad, axis=-1, keepdims=True) - unit * along)


def gelu_pair(value):
    root = math.sqrt(2.0 / math.pi)
    bend = jnp.tanh(root * (value + 0.044715 * value * value * value))
    slope = root * (1.0 + 3.0 * 0.044715 * value * value)
    gelu = 0.5 * value * (1.0 + bend)
    return gelu, 0.5 * (1.0 + bend) + 0.5 * value * (1.0 - bend * bend) * slope


def local(
    tokens,
    conditioning,
    latent_len,
    w_ada,
    b_ada,
    w_qkv,
    b_qv,
    w_proj,
    b_proj,
    w_fc1,
    b_fc1,
    w_fc2,
    b_fc2,
    cotangent,
):
    rows, width = tokens.shape
    share_width = w_qkv.shape[0]
    features = w_qkv.shape[2]
    units = w_fc1.shape[1]
    heads = features // DH
    latents = conditioning.shape[0]
    n_dp, n_tensor = lax.axis_size("dp"), lax.axis_size("tensor")
    my_dp, my_tensor = lax.axis_index("dp"), lax.axis_index("tensor")
    share = rows // n_tensor

    core = my_dp % 2
    qk = w_qkv[:, :2].reshape(share_width, 2 * features)
    vp = jnp.concatenate([w_qkv[:, 2], w_proj.T], axis=1)
    early_rows = pair_rows(qk, vp)

    cond = conditioning.astype(F32)
    sigmoid = 1.0 / (1.0 + jnp.exp(-cond))
    activated = (cond * sigmoid).astype(BF16)
    own_activated = lax.dynamic_slice_in_dim(activated, my_dp * share_width, share_width, 1)
    flat_ada = w_ada.reshape(share_width, 6 * features)
    mod_part = jnp.dot(own_activated, flat_ada, preferred_element_type=F32)
    mod_part = mod_part.reshape(latents * 6, features)
    bias_ada = jnp.tile(b_ada.astype(F32), (latents, 1))
    few_chips = n_dp // 2 == 4
    if few_chips:
        mod_part = gate(mod_part + jnp.where(my_dp == 0, bias_ada, 0.0), early_rows)
        mod_wide = gather(mod_part, "tensor", n_tensor)
        mod_parts = gather(mod_wide, "dp", n_dp).reshape((-1,) + mod_part.shape)
    else:
        mod_wide = jnp.sum(gather(mod_part, "dp", n_dp), axis=0) + bias_ada
        mod_parts = gather(mod_wide, "tensor", n_tensor)
    early_parts = chip_parts(early_rows) if few_chips else [gather_chips(early_rows)]

    early_parts = list(gate_all(early_parts, mod_wide))
    early_parts += [swap(part, "dp", 1) for part in early_parts]
    count = len(early_parts) // 2
    meta = jnp.stack([core, my_dp * rows, my_tensor, my_dp // 2]).astype(jnp.int32)
    meta = jnp.concatenate([meta, latent_len])
    place_meta = meta if few_chips else meta.at[3].set(0)
    by_last = (((1,), (1,)), ((), ()))
    by_token = (((0,), (0,)), ((), ()))
    bias = jnp.concatenate([b_qv[0], jnp.zeros_like(b_qv[0]), b_qv[1], jnp.zeros_like(b_qv[0])])
    hidden_one, d_mlp, packed, full_qk, full_vp, d_bias_fc2, mod_rows = call(
        lambda *refs: project_kernel(latents, count, *refs),
        "project",
        place_meta,
        (*early_parts, tokens, cotangent, mod_parts, bias.astype(F32).reshape(2, -1)),
        (((rows, width), BF16), ((rows, width), BF16), ((2 * heads, DH, rows * 5 // 2), BF16))
        + (((width, 2 * features), BF16),) * 2
        + (((1, width), F32), ((6 * latents, width), F32)),
        [pltpu.SemaphoreType.DMA((2, count))],
        2 * count,
    )
    late_rows = pair_rows(w_fc1, w_fc2.T)
    hidden_other = swap(hidden_one, "dp", 1)
    split = HeadSplit if 2 * heads == n_dp else Window
    attention = split(latent_len, rows)
    attended_parts = attention.forward(packed)
    late_rows = gate(late_rows, attended_parts)
    late_parts = chip_parts(late_rows)[:-1] if few_chips else [gather_chips(late_rows)]
    attn_part, attended = call(
        attend_out_kernel,
        "attend_out",
        meta,
        (attended_parts, full_vp),
        (((rows, width), BF16), ((rows, 2 * features), BF16)),
    )
    attn_parts = exchange_shares(attn_part, "tensor")
    hidden_blocks, attn_out, residual_mid = call(
        lambda *refs: middle_kernel(latents, *refs),
        "middle",
        meta,
        (attn_parts, tokens, mod_rows, b_proj.reshape(1, -1)),
        (((n_tensor, share, width), BF16), ((share, width), F32), ((share, width), F32)),
        due=late_parts[1:],
    )
    hidden_two = exchange(hidden_blocks, "tensor").reshape(rows, width)
    if few_chips:
        last_part = swap(gate(late_rows, attn_out), "dp", n_dp - 2)
        late_parts.append(gate(last_part, hidden_two))
    late_other = [swap(part, "dp", 1) for part in late_parts]

    d_two_part, gelu_out, d_pre, d_bias_fc1, left_sent, right_sent, *mlp_blocks = call(
        lambda *refs: mlp_kernel(count, *refs),
        "mlp",
        place_meta,
        (*late_parts, *late_other, hidden_two, d_mlp, b_fc1.reshape(1, -1)),
        (((rows, width), BF16), ((rows, units), BF16), ((rows, units), BF16), ((1, units), F32))
        + (((rows, width), BF16), ((rows, units), BF16))
        + (((share, width), BF16),) * n_tensor,
        [pltpu.VMEM((width, units), BF16)] * 2
        + [pltpu.VMEM((rows, width), F32)] * 2
        + [pltpu.SemaphoreType.DMA((2, count))],
        2 * count,
    )
    d_two_parts = exchange_shares(d_two_part, "tensor")

    chips = n_dp // 2 if few_chips else 1
    left_other = swap(left_sent, "dp", 1)
    right_other = swap(right_sent, "dp", 1)
    late_blocks = call(
        lambda *refs: weight_kernel([(0, 2), (4, 5)], [(1, 3), (4, 5)], *refs),
        "late_weights",
        place_meta,
        (hidden_two, d_mlp, d_pre, gelu_out, left_other, right_other),
        (((width // chips, units), BF16),) * chips,
        [pltpu.VMEM((width, units), BF16)],
    )
    late_grads = sum_chips(late_blocks[:-1]) if few_chips else sum_chips(late_blocks)

    d_attn_blocks, d_mid, mid_sums = call(
        lambda *refs: middle_back_kernel(latents, *refs),
        "middle_back",
        meta,
        (d_two_parts, residual_mid, attn_out, cotangent, mod_rows),
        (((n_tensor, share, width), BF16), ((share, width), F32), ((3 * latents, width), F32)),
        due=late_blocks,
    )
    d_attn = exchange(d_attn_blocks, "tensor").reshape(rows, width)

    d_spread, d_bias_proj = call(
        spread_kernel,
        "spread",
        meta,
        (d_attn, full_vp),
        (((2 * heads, DH, rows // 2), BF16), ((1, width), F32)),
        due=late_grads[1:],
    )
    mlp_parts = mlp_blocks[:1] + [
        swap(gate(block, d_spread), "tensor", step)
        for step, block in enumerate(mlp_blocks)
        if step
    ]
    d_attn_other = swap(d_attn, "dp", 1)
    attended_other = swap(attended, "dp", 1)
    d_packed, last_grad = attention.backward(d_spread, mlp_parts[1:], late_blocks[-1])
    result_own, last_sums = call(
        lambda *refs: result_kernel(latents, n_tensor, *refs),
        "result",
        meta,
        (*mlp_parts, residual_mid, cotangent, mod_rows, b_fc2.reshape(1, -1)),
        (((share, width), BF16), ((latents, width), F32)),
    )
    d_one_part, d_qk, d_vp, d_sent, d_bias_qv = call(
        unspread_kernel,
        "unspread",
        meta,
        (d_packed, full_qk, full_vp),
        (((rows, width), BF16),)
        + (((rows, 2 * features), BF16),) * 3
        + (((2, 2 * features), F32),),
        flops=2 * 10**10,
    )
    result_parts = [result_own] + [swap(result_own, "tensor", bits) for bits in range(1, n_tensor)]
    d_one_part = gate(d_one_part, *result_parts[1:])
    d_one_parts = exchange_shares(d_one_part, "tensor")

    if few_chips:
        late_grads.append(last_grad)
    right_other = swap(d_sent, "dp", 1)
    early_blocks = call(
        lambda *refs: weight_kernel(
            [(0, 2), (5, 7)], [(0, 3), (1, 4), (5, 7), (6, 8)], *refs
        ),
        "early_weights",
        place_meta,
        (hidden_one, d_attn, d_qk, d_vp, attended, hidden_other, d_attn_other, right_other, attended_other),
        (((width // chips, 2 * features), BF16),) * chips,
        [pltpu.VMEM((width, 2 * features), BF16)],
    )
    early_grads = sum_chips(early_blocks[:3] if few_chips else early_blocks)

    grad_own, d_mod_part, bias_rows = call(
        lambda *refs: first_back_kernel(latents, *refs),
        "first_back",
        meta,
        (d_one_parts, tokens, d_mid, mod_rows, mid_sums, last_sums)
        + (d_bias_fc2, d_bias_proj, d_bias_fc1, d_bias_qv),
        (((share, width), BF16), ((n_tensor, 6 * latents, features), F32))
        + (((2 * (width // features) + units // features + 2, features), F32),),
        [pltpu.VMEM((2 * latents, width), F32)],
        due=early_grads[1:3],
    )
    if few_chips:
        last_block = gate(early_blocks[3], d_mod_part)
        early_grads.append(swap(last_block, "dp", n_dp - 2))
    d_mod_mine = jnp.sum(exchange(d_mod_part, "tensor"), axis=0)
    d_mod_rows = jnp.concatenate([d_mod_mine, bias_rows])
    d_mod_rows = gate(jnp.broadcast_to(d_mod_rows[None], (n_dp,) + d_mod_rows.shape))
    grad_own = gate(grad_own, d_mod_rows)
    grad_parts = [grad_own] + [swap(grad_own, "tensor", bits) for bits in range(1, n_tensor)]
    sums = exchange(d_mod_rows, "dp")
    sums = gate(sums, early_grads[3]) if few_chips else sums
    grad_parts = gate_all(grad_parts, sums)
    result, grad_tokens = call(
        lambda *refs: order_kernel(n_tensor, *refs),
        "order",
        meta,
        (*result_parts, *grad_parts),
        (((rows, width), BF16), ((rows, width), F32)),
    )
    grad_w_ada, grad_b_ada, d_active, sum_b_fc2, sum_b_proj, sum_b_fc1, sum_b_qv = call(
        lambda *refs: finish_kernel(latents, *refs),
        "finish",
        meta,
        (sums, own_activated.astype(F32).T, w_ada.transpose(1, 0, 2)),
        (((6, share_width, features), F32), ((6, features), F32), ((latents, share_width), F32))
        + (((1, width), F32), ((1, width), F32), ((1, units), F32), ((2, features), F32)),
        [pltpu.VMEM(sums.shape[1:], F32)],
    )
    d_active = gather(d_active, ("dp", "tensor"), n_dp * n_tensor)
    d_active = jnp.sum(d_active.reshape(n_dp, n_tensor, latents, share_width), axis=1)
    d_active = d_active.transpose(1, 0, 2).reshape(latents, width)
    grad_cond = d_active * (sigmoid * (1.0 + cond * (1.0 - sigmoid)))

    grad_fc1, grad_fc2 = finish_pair(late_grads)
    grad_qk, grad_vp = finish_pair(early_grads)
    grad_qkv = jnp.concatenate([grad_qk, grad_vp[:, :features]], axis=1)
    grad_qkv = grad_qkv.reshape(share_width, 3, features)

    return (
        result,
        grad_tokens,
        grad_cond,
        grad_w_ada.transpose(1, 0, 2),
        grad_b_ada,
        grad_qkv,
        sum_b_qv,
        grad_vp[:, features:].T,
        sum_b_proj.reshape(width),
        grad_fc1,
        sum_b_fc1.reshape(units),
        grad_fc2.T,
        sum_b_fc2.reshape(width),
    )


def solution(mesh):
    in_specs = (
        P("dp", None),
        P(),
        P(),
        P("dp", None, "tensor"),
        P(None, "tensor"),
        P("dp", None, "tensor"),
        P(None, "tensor"),
        P("tensor", "dp"),
        P(),
        P("dp", "tensor"),
        P("tensor"),
        P("tensor", "dp"),
        P(),
        P("dp", None),
    )
    out_specs = (
        P("dp", None),
        P("dp", None),
        P(),
        P("dp", None, "tensor"),
        P(None, "tensor"),
        P("dp", None, "tensor"),
        P(None, "tensor"),
        P("tensor", "dp"),
        P(),
        P("dp", "tensor"),
        P("tensor"),
        P("tensor", "dp"),
        P(),
    )
    return jax.shard_map(local, mesh=mesh, in_specs=in_specs, out_specs=out_specs, check_vma=False)
```

```python
import math

import jax
import jax.numpy as jnp
from jax import lax
from jax.experimental import pallas as pl
from jax.experimental.pallas import tpu as pltpu
from jax.sharding import PartitionSpec as P

DH = 72
SEQ = 1024
STEP = 512
NORM_EPS = 1e-06
NEGATIVE = -1e30
SCALE = 1.0 / math.sqrt(DH)
VMEM_BYTES = 255 * 256 * 1024
BF16 = jnp.bfloat16
F32 = jnp.float32


def swap(block, axis, bits):
    route = [(i, i ^ bits) for i in range(lax.axis_size(axis))]
    return lax.ppermute(block, axis, route)


def exchange(blocks, axis):
    return lax.all_to_all(blocks, axis, 0, 0, tiled=True)


def gather(block, axis, count):
    return exchange(jnp.broadcast_to(block[None], (count,) + block.shape), axis)


def gate_all(values, *others):
    anywhere = pl.BlockSpec(memory_space=pl.ANY)
    return pl.pallas_call(
        lambda *refs: None,
        out_shape=tuple(jax.ShapeDtypeStruct(value.shape, value.dtype) for value in values),
        in_specs=[anywhere] * (len(values) + len(others)),
        out_specs=(anywhere,) * len(values),
        input_output_aliases={place: place for place in range(len(values))},
        cost_estimate=pl.CostEstimate(flops=1, bytes_accessed=1, transcendentals=0),
        name="gate",
    )(*values, *others)


def gate(value, *others):
    return gate_all((value,), *others)[0]


def choose(core, first, second):
    return jnp.where(core == 0, first, second), jnp.where(core == 0, second, first)


def pair_rows(first, second):
    core = lax.axis_index("dp") % 2
    keep, send = choose(core, first, second)
    return jnp.concatenate(choose(core, keep, swap(send, "dp", 1)))


def chip_parts(rows):
    count = lax.axis_size("dp") // 2
    return [rows] + [swap(rows, "dp", 2 * step) for step in range(1, count)]


def gather_chips(rows):
    count = lax.axis_size("dp")
    groups = [list(range(core, count, 2)) for core in range(2)]
    return lax.all_gather(rows, "dp", axis=0, tiled=True, axis_index_groups=groups)


def sum_chips(blocks):
    if len(blocks) == 1:
        count, chip = lax.axis_size("dp") // 2, lax.axis_index("dp") // 2
        rows = blocks[0].reshape((count, -1) + blocks[0].shape[1:])
        blocks = [
            lax.dynamic_index_in_dim(rows, chip ^ step, 0, keepdims=False) for step in range(count)
        ]
    return [swap(block, "dp", 2 * step) if step else block for step, block in enumerate(blocks)]


def finish_pair(parts):
    core = lax.axis_index("dp") % 2
    rows = sum(part.astype(F32) for part in parts)
    half = rows.shape[0] // 2
    keep, send = choose(core, rows[:half], rows[half:])
    return choose(core, keep, swap(send, "dp", 1))


def exchange_shares(partial, axis):
    count = lax.axis_size(axis)
    blocks = partial.reshape((count, partial.shape[0] // count) + partial.shape[1:])
    return exchange(blocks, axis)


def tile_range(meta_ref, latents, tile, core):
    lane = lax.broadcasted_iota(jnp.int32, (1, 256), 1)
    first = tile * 512 + core * 128
    last = first + 383
    place = first + lane + jnp.where(lane >= 128, 128, 0)
    begin = jnp.zeros((1, 256), jnp.int32)
    finish = jnp.zeros((1, 256), jnp.int32)
    low = jnp.int32(0)
    high = jnp.int32(0)
    start = jnp.int32(0)
    for number in range(latents):
        end = start + meta_ref[1 + number]
        inside = (place >= start) & (place < end)
        begin = jnp.where(inside, start, begin)
        finish = jnp.where(inside, end, finish)
        low = jnp.where((first >= start) & (first < end), start, low)
        high = jnp.where((last >= start) & (last < end), end, high)
        start = end
    return begin, finish, low // STEP, (high + STEP - 1) // STEP


def pair(ref, tile, start):
    left = ref[2 * tile, :, start : start + 128]
    right = ref[2 * tile + 1, :, start : start + 128]
    return jnp.concatenate([left, right], axis=1)


def wide(packed_ref, block, start):
    left = packed_ref[2 * block, :, start : start + 256]
    right = packed_ref[2 * block + 1, :, start : start + 256]
    return jnp.concatenate([left, right], axis=1)


def key_mask(block, begin, finish):
    place = block * STEP + lax.broadcasted_iota(jnp.int32, (STEP, 256), 0)
    return (place >= begin) & (place < finish)


def forward_kernel(latents, meta_ref, packed_ref, out_ref, exact_ref, log_ref, keys, scores):
    blocks = packed_ref.shape[0]
    core = meta_ref[0]
    for block in range(blocks // 2):
        keys[block] = wide(packed_ref, block, 0).astype(F32).T.astype(BF16)
    for tile in range(blocks // 2):
        begin, finish, low, high = tile_range(meta_ref, latents, tile, core)
        query = pair(packed_ref, tile, 512)

        def score(block, largest):
            raw = jnp.dot(keys[block], query, preferred_element_type=F32) * SCALE
            raw = jnp.where(key_mask(block, begin, finish), raw, NEGATIVE)
            scores[block] = raw
            return jnp.maximum(largest, jnp.max(raw, axis=0, keepdims=True))

        largest = lax.fori_loop(low, high, score, jnp.full((1, 256), NEGATIVE, F32))

        def mix(block, carry):
            total, mixed = carry
            weights = jnp.exp(scores[block] - largest)
            total = total + jnp.sum(weights, axis=0, keepdims=True)
            values = wide(packed_ref, block, 256)
            mixed = mixed + jnp.dot(values, weights.astype(BF16), preferred_element_type=F32)
            return total, mixed

        total, mixed = lax.fori_loop(
            low, high, mix, (jnp.zeros((1, 256), F32), jnp.zeros((DH, 256), F32))
        )
        mixed = mixed / total
        log_total = largest + jnp.log(total)
        for half in range(2):
            part = mixed[:, half * 128 : half * 128 + 128]
            exact_ref[2 * tile + half] = part
            out_ref[2 * tile + half] = part.astype(BF16)
            log_ref[2 * tile + half] = log_total[:, half * 128 : half * 128 + 128]


def backward_kernel(
    latents, meta_ref, packed_ref, grad_ref, exact_ref, log_ref, out_ref, keys, values, d_keys, d_values
):
    blocks = packed_ref.shape[0]
    core = meta_ref[0]
    for block in range(blocks // 2):
        keys[block] = wide(packed_ref, block, 0).astype(F32).T.astype(BF16)
        values[block] = wide(packed_ref, block, 256).astype(F32).T.astype(BF16)
    d_keys[...] = jnp.zeros_like(d_keys)
    d_values[...] = jnp.zeros_like(d_values)
    by_query = (((1,), (1,)), ((), ()))
    for tile in range(blocks // 2):
        begin, finish, low, high = tile_range(meta_ref, latents, tile, core)
        query = pair(packed_ref, tile, 512)
        grad = pair(grad_ref, tile, 0)
        inner = jnp.sum(grad.astype(F32) * pair(exact_ref, tile, 0), axis=0, keepdims=True)
        log_total = pair(log_ref, tile, 0)

        def step(block, d_query):
            raw = jnp.dot(keys[block], query, preferred_element_type=F32) * SCALE
            probs = jnp.where(key_mask(block, begin, finish), jnp.exp(raw - log_total), 0.0)
            d_probs = jnp.dot(values[block], grad, preferred_element_type=F32)
            d_scores = (probs * (d_probs - inner)).astype(BF16)
            d_values[block] += lax.dot_general(
                grad, probs.astype(BF16), by_query, preferred_element_type=F32
            )
            d_keys[block] += lax.dot_general(query, d_scores, by_query, preferred_element_type=F32)
            key_rows = wide(packed_ref, block, 0)
            return d_query + jnp.dot(key_rows, d_scores, preferred_element_type=F32)

        d_query = lax.fori_loop(low, high, step, jnp.zeros((DH, 256), F32)) * SCALE
        for half in range(2):
            part = d_query[:, half * 128 : half * 128 + 128]
            out_ref[2 * tile + half, :, 512:640] = part.astype(BF16)
    for block in range(blocks):
        half = slice(block % 2 * 256, block % 2 * 256 + 256)
        out_ref[block, :, :256] = (d_keys[block // 2, :, half] * SCALE).astype(BF16)
        out_ref[block, :, 256:512] = d_values[block // 2, :, half].astype(BF16)


def attend_forward(meta, packed):
    blocks = packed.shape[0]
    shape = jax.ShapeDtypeStruct
    return pl.pallas_call(
        lambda *refs: forward_kernel(meta.shape[0] - 1, *refs),
        out_shape=(
            shape((blocks, DH, 128), BF16),
            shape((blocks, DH, 128), F32),
            shape((blocks, 1, 128), F32),
        ),
        in_specs=[
            pl.BlockSpec(memory_space=pltpu.SMEM),
            pl.BlockSpec(memory_space=pltpu.VMEM),
        ],
        out_specs=tuple([pl.BlockSpec(memory_space=pltpu.VMEM)] * 3),
        scratch_shapes=[
            pltpu.VMEM((blocks // 2, STEP, DH), BF16),
            pltpu.VMEM((blocks // 2, STEP, 256), F32),
        ],
        compiler_params=pltpu.CompilerParams(vmem_limit_bytes=VMEM_BYTES),
        cost_estimate=pl.CostEstimate(flops=10**9, bytes_accessed=4 * 10**6, transcendentals=10**6),
        name="attend_forward",
    )(meta, packed)


def attend_backward(meta, packed, grad, exact, log_total):
    blocks = packed.shape[0]
    return pl.pallas_call(
        lambda *refs: backward_kernel(meta.shape[0] - 1, *refs),
        out_shape=jax.ShapeDtypeStruct(packed.shape, BF16),
        in_specs=[pl.BlockSpec(memory_space=pltpu.SMEM)]
        + [pl.BlockSpec(memory_space=pltpu.VMEM)] * 4,
        out_specs=pl.BlockSpec(memory_space=pltpu.VMEM),
        scratch_shapes=[
            pltpu.VMEM((blocks // 2, STEP, DH), BF16),
            pltpu.VMEM((blocks // 2, STEP, DH), BF16),
            pltpu.VMEM((blocks // 2, DH, STEP), F32),
            pltpu.VMEM((blocks // 2, DH, STEP), F32),
        ],
        compiler_params=pltpu.CompilerParams(vmem_limit_bytes=VMEM_BYTES),
        cost_estimate=pl.CostEstimate(flops=1, bytes_accessed=1, transcendentals=0),
        name="attend_backward",
    )(meta, packed, grad, exact, log_total)


class HeadSplit:
    def __init__(self, latent_len, rows):
        self.rows = rows
        self.meta = jnp.concatenate([lax.axis_index("dp").astype(jnp.int32)[None] % 2, latent_len])

    def forward(self, packed):
        self.packed = exchange(packed, "dp")
        out, self.exact, self.log_total = attend_forward(self.meta, self.packed)
        return exchange(out, "dp")

    def backward(self, grad, due, beside):
        beside = swap(gate(beside, grad), "dp", lax.axis_size("dp") - 2)
        grad = exchange(grad, "dp")
        out = attend_backward(self.meta, self.packed, grad, self.exact, self.log_total)
        return exchange(gate(out, beside, *due), "dp"), beside


class Window:
    def __init__(self, latent_len, rows):
        self.rows = rows
        self.reach = (SEQ - 2) // rows + 1
        total = rows * lax.axis_size("dp")
        first = lax.axis_index("dp") * rows
        own = latent_index(latent_len, first, rows, total)
        ids = [
            latent_index(latent_len, first + offset * rows, rows, total)
            for offset in range(-self.reach, self.reach + 1)
        ]
        self.allowed = own[:, None] == jnp.concatenate(ids)[None, :]

    def from_behind(self, block, distance):
        devices = range(lax.axis_size("dp"))
        return lax.ppermute(
            block, "dp", [(i - distance, i) for i in devices if i - distance in devices]
        )

    def head_scores(self, query, key):
        raw = jnp.einsum("eq,ek->qk", query, key, preferred_element_type=F32) * SCALE
        return jnp.where(self.allowed, raw, NEGATIVE)

    def forward(self, packed):
        rows = self.rows
        split = packed.reshape(-1, 2, DH, rows * 5 // 2)
        query = jnp.concatenate([split[:, 0, :, 2 * rows :], split[:, 1, :, 2 * rows :]], axis=2)
        projected = jnp.stack([query, split[:, 0, :, :rows], split[:, 0, :, rows : 2 * rows]])
        key_value = projected[1:]
        pieces = [
            key_value if offset == 0 else self.from_behind(key_value, -offset)
            for offset in range(-self.reach, self.reach + 1)
        ]
        window = jnp.concatenate(pieces, axis=3)
        self.operands = (projected[0], window[0], window[1])

        def one(operands):
            query, key, value = operands
            scores = self.head_scores(query, key)
            largest = jnp.max(scores, axis=1, keepdims=True)
            weights = jnp.exp(scores - largest)
            totals = jnp.sum(weights, axis=1, keepdims=True)
            probs = (weights / totals).astype(BF16)
            mixed = jnp.einsum("qk,ek->eq", probs, value, preferred_element_type=F32)
            return mixed.astype(BF16), (largest + jnp.log(totals))[:, 0]

        out, self.log_total = lax.map(one, self.operands)
        out = out.reshape(-1, DH, 2, rows // 2).transpose(0, 2, 1, 3)
        return out.reshape(-1, DH, rows // 2)

    def backward(self, grad, due, beside):
        rows, reach = self.rows, self.reach
        halves = grad.reshape(-1, 2, DH, rows // 2)
        grads = jnp.concatenate([halves[:, 0], halves[:, 1]], axis=2)

        def one(operands):
            query, key, value, grad, log_total = operands
            probs = jnp.exp(self.head_scores(query, key) - log_total[:, None])
            d_value = jnp.einsum("qk,eq->ek", probs.astype(BF16), grad, preferred_element_type=F32)
            d_probs = jnp.einsum("eq,ek->qk", grad, value, preferred_element_type=F32)
            inner = jnp.sum(probs * d_probs, axis=1, keepdims=True)
            d_scores = (probs * (d_probs - inner)).astype(BF16)
            d_query = jnp.einsum("qk,ek->eq", d_scores, key, preferred_element_type=F32) * SCALE
            d_key = jnp.einsum("qk,eq->ek", d_scores, query, preferred_element_type=F32) * SCALE
            return d_query, d_key, d_value

        d_query, d_key, d_value = lax.map(one, self.operands + (grads, self.log_total))
        d_window = jnp.stack([d_key, d_value])
        d_key_value = d_window[..., reach * rows : (reach + 1) * rows]
        for offset in range(-reach, reach + 1):
            if offset != 0:
                block = d_window[..., (offset + reach) * rows : (offset + reach + 1) * rows]
                d_key_value = d_key_value + self.from_behind(block, offset)
        wide = jnp.concatenate([d_key_value[0], d_key_value[1]], axis=2)
        wide = jnp.stack([wide, jnp.zeros_like(wide)], axis=1)
        halves = d_query.reshape(-1, DH, 2, rows // 2).transpose(0, 2, 1, 3)
        packed = jnp.concatenate([wide, halves], axis=3).astype(BF16)
        return packed.reshape(-1, DH, rows * 5 // 2), beside


META = 4


def vmem(count):
    return [pl.BlockSpec(memory_space=pltpu.VMEM)] * count


def call(body, name, meta, arrays, outs, scratch=(), anywhere=0, due=(), flops=1):
    count = 1 + len(arrays)

    def kernel(*refs):
        body(*refs[:count], *refs[count + len(due) :])

    return pl.pallas_call(
        kernel,
        out_shape=tuple(jax.ShapeDtypeStruct(shape, kind) for shape, kind in outs),
        in_specs=[pl.BlockSpec(memory_space=pltpu.SMEM)]
        + [pl.BlockSpec(memory_space=pl.ANY)] * anywhere
        + vmem(len(arrays) - anywhere)
        + [pl.BlockSpec(memory_space=pl.ANY)] * len(due),
        out_specs=tuple(vmem(len(outs))),
        scratch_shapes=list(scratch),
        compiler_params=pltpu.CompilerParams(vmem_limit_bytes=VMEM_BYTES),
        cost_estimate=pl.CostEstimate(flops=flops, bytes_accessed=1, transcendentals=0),
        name=name,
    )(meta, *arrays, *due)


def row_masks(meta_ref, latents, first, rows):
    place = first + lax.broadcasted_iota(jnp.int32, (rows, 1), 0)
    ids = jnp.zeros((rows, 1), jnp.int32)
    end = jnp.int32(0)
    for number in range(latents - 1):
        end = end + meta_ref[META + number]
        ids = ids + (place >= end).astype(jnp.int32)
    return [(ids == number).astype(F32) for number in range(latents)]


def rows_of(mod_ref, masks, feature):
    out = masks[0] * mod_ref[feature : feature + 1, :]
    for number in range(1, len(masks)):
        row = number * 6 + feature
        out = out + masks[number] * mod_ref[row : row + 1, :]
    return out


def latent_sums(out_ref, masks, values, feature, features):
    rounded = values.astype(BF16).astype(F32)
    for number, mask in enumerate(masks):
        row = number * features + feature
        out_ref[row : row + 1, :] = jnp.sum(mask * rounded, axis=0, keepdims=True)


def own_rows(meta_ref, ref, share):
    start = pl.multiple_of(meta_ref[2] * share, share)
    return ref[pl.ds(start, share), :].astype(F32)


def on_core(meta_ref, body, mine, other):
    @pl.when(meta_ref[0] == 0)
    def _():
        body(mine, other)

    @pl.when(meta_ref[0] != 0)
    def _():
        body(other, mine)


def place_rows(meta_ref, parts, whole, sems):
    block = parts[0].shape[0]
    copies = []
    for step, part in enumerate(parts):
        start = pl.multiple_of((meta_ref[3] ^ step) * block, 16)
        copies.append(
            pltpu.make_async_copy(part, whole.at[pl.ds(start, block), :], sems.at[step])
        )
    return copies


def place_pair(meta_ref, mine, other, first_ref, second_ref, sems):
    def body(first, second):
        copies = place_rows(meta_ref, first, first_ref, sems.at[0])
        copies += place_rows(meta_ref, second, second_ref, sems.at[1])
        for copy in copies:
            copy.start()
        for copy in copies:
            copy.wait()

    on_core(meta_ref, body, mine, other)


def project_kernel(latents, count, meta_ref, *refs):
    mine, other = refs[:count], refs[count : 2 * count]
    tokens_ref, cot_ref, mod_parts_ref, bias_ref = refs[2 * count : 2 * count + 4]
    hidden_ref, d_mlp_ref, packed_ref, qk_ref, vp_ref, d_bias_ref, mod_ref, sems = refs[2 * count + 4 :]
    rows, width = tokens_ref.shape
    place_pair(meta_ref, mine, other, qk_ref, vp_ref, sems)
    columns = mod_parts_ref.shape[2]
    pieces = width // columns
    for piece in range(pieces):
        total = mod_parts_ref[piece].astype(F32)
        for part in range(piece + pieces, mod_parts_ref.shape[0], pieces):
            total = total + mod_parts_ref[part].astype(F32)
        mod_ref[:, piece * columns : (piece + 1) * columns] = total
    masks = row_masks(meta_ref, latents, meta_ref[1], rows)
    unit, _ = normed(tokens_ref[...].astype(F32))
    hidden = unit * (1.0 + rows_of(mod_ref, masks, 1)) + rows_of(mod_ref, masks, 0)
    hidden_ref[...] = hidden.astype(BF16)
    d_mlp = (cot_ref[...].astype(F32) * rows_of(mod_ref, masks, 5)).astype(BF16)
    d_mlp_ref[...] = d_mlp
    d_bias_ref[...] = jnp.sum(d_mlp.astype(F32), axis=0, keepdims=True)
    heads = packed_ref.shape[0] // 2
    features = heads * DH
    left = hidden_ref[...]
    both = jnp.dot(left, qk_ref[...], preferred_element_type=F32) + bias_ref[0:1, :]
    both = both.T
    value = jnp.dot(left, vp_ref[...], preferred_element_type=F32) + bias_ref[1:2, :]
    value = value.T
    for head in range(heads):
        start = head * DH
        query = both[start : start + DH].astype(BF16)
        key = both[features + start : features + start + DH].astype(BF16)
        val = value[start : start + DH].astype(BF16)
        for half in range(2):
            packed_ref[2 * head + half, :, :rows] = key
            packed_ref[2 * head + half, :, rows : 2 * rows] = val
            packed_ref[2 * head + half, :, 2 * rows :] = query[
                :, half * (rows // 2) : (half + 1) * (rows // 2)
            ]


def attend_out_kernel(meta_ref, parts_ref, vp_ref, part_ref, attended_ref):
    heads = parts_ref.shape[0] // 2
    rows = part_ref.shape[0]
    stacked = [jnp.zeros((heads * DH, rows), F32)]
    for head in range(heads):
        left = parts_ref[2 * head].astype(F32)
        right = parts_ref[2 * head + 1].astype(F32)
        stacked.append(jnp.concatenate([left, right], axis=1))
    attended_ref[...] = jnp.concatenate(stacked, axis=0).T.astype(BF16)
    part_ref[...] = lax.dot_general(
        attended_ref[...], vp_ref[...], (((1,), (1,)), ((), ())), preferred_element_type=F32
    ).astype(BF16)


def middle_kernel(
    latents, meta_ref, parts_ref, tokens_ref, mod_ref, bias_ref, sent_ref, attn_ref, mid_ref
):
    copies, share, width = parts_ref.shape
    masks = row_masks(meta_ref, latents, meta_ref[1] + meta_ref[2] * share, share)
    attn = bias_ref[...].astype(F32)
    for part in range(copies):
        attn = attn + parts_ref[part].astype(F32)
    attn_ref[...] = attn
    mid = own_rows(meta_ref, tokens_ref, share) + rows_of(mod_ref, masks, 2) * attn
    mid_ref[...] = mid
    unit, _ = normed(mid)
    hidden = unit * (1.0 + rows_of(mod_ref, masks, 4)) + rows_of(mod_ref, masks, 3)
    for part in range(copies):
        sent_ref[part] = hidden.astype(BF16)


def mlp_kernel(count, meta_ref, *refs):
    mine, other = refs[:count], refs[count : 2 * count]
    hidden_ref, d_mlp_ref, bias_ref = refs[2 * count : 2 * count + 3]
    d_two_ref, gelu_ref, d_pre_ref, d_bias_ref, left_ref, right_ref = refs[2 * count + 3 : 2 * count + 9]
    mlp_refs = refs[2 * count + 9 : -5]
    fc1_ref, fc2_ref, d_two_sum, mlp_sum, sems = refs[-5:]
    place_pair(meta_ref, mine, other, fc1_ref, fc2_ref, sems)
    d_two_sum[...] = jnp.zeros_like(d_two_sum)
    mlp_sum[...] = jnp.zeros_like(mlp_sum)
    tile = 384
    by_last = (((1,), (1,)), ((), ()))

    def step(number, carry):
        units = pl.ds(pl.multiple_of(number * tile, tile), tile)
        fc1, fc2 = fc1_ref[:, units], fc2_ref[:, units]
        pre = jnp.dot(hidden_ref[...], fc1, preferred_element_type=F32)
        gelu, slope = gelu_pair(pre + bias_ref[:, units].astype(F32))
        grad = jnp.dot(d_mlp_ref[...], fc2, preferred_element_type=F32)
        d_pre = (grad * slope).astype(BF16)
        gelu = gelu.astype(BF16)
        gelu_ref[:, units] = gelu
        d_pre_ref[:, units] = d_pre
        d_bias_ref[:, units] = jnp.sum(d_pre.astype(F32), axis=0, keepdims=True)
        d_two_sum[...] += lax.dot_general(d_pre, fc1, by_last, preferred_element_type=F32)
        mlp_sum[...] += lax.dot_general(gelu, fc2, by_last, preferred_element_type=F32)
        return carry

    lax.fori_loop(0, fc1_ref.shape[1] // tile, step, 0)
    d_two_ref[...] = d_two_sum[...].astype(BF16)
    def sent(left, right):
        left_ref[...] = left[0][...]
        right_ref[...] = left[1][...]

    on_core(meta_ref, sent, (d_mlp_ref, gelu_ref), (hidden_ref, d_pre_ref))
    share = mlp_refs[0].shape[0]
    for step, mlp_ref in enumerate(mlp_refs):
        start = pl.multiple_of((meta_ref[2] ^ step) * share, share)
        mlp_ref[...] = mlp_sum[pl.ds(start, share), :].astype(BF16)


def middle_back_kernel(
    latents, meta_ref, parts_ref, mid_in_ref, attn_ref, cot_ref, mod_ref, sent_ref, d_mid_ref, sums_ref
):
    copies, share, width = parts_ref.shape
    masks = row_masks(meta_ref, latents, meta_ref[1] + meta_ref[2] * share, share)
    d_hidden = parts_ref[0].astype(F32)
    for part in range(1, copies):
        d_hidden = d_hidden + parts_ref[part].astype(F32)
    unit, inverse = normed(mid_in_ref[...])
    d_mid = own_rows(meta_ref, cot_ref, share) + norm_back(
        unit, inverse, d_hidden * (1.0 + rows_of(mod_ref, masks, 4))
    )
    d_mid_ref[...] = d_mid
    d_attn = (d_mid * rows_of(mod_ref, masks, 2)).astype(BF16)
    for part in range(copies):
        sent_ref[part] = d_attn
    latent_sums(sums_ref, masks, d_mid * attn_ref[...], 0, 3)
    latent_sums(sums_ref, masks, d_hidden, 1, 3)
    latent_sums(sums_ref, masks, d_hidden * unit, 2, 3)


def result_kernel(
    latents, count, meta_ref, *refs
):
    parts = refs[:count]
    mid_ref, cot_ref, mod_ref, bias_ref, result_ref, sums_ref = refs[count:]
    share = result_ref.shape[0]
    masks = row_masks(meta_ref, latents, meta_ref[1] + meta_ref[2] * share, share)
    mlp = bias_ref[...].astype(F32)
    for part in parts:
        mlp = mlp + part[...].astype(F32)
    result_ref[...] = (mid_ref[...] + rows_of(mod_ref, masks, 5) * mlp).astype(BF16)
    latent_sums(sums_ref, masks, own_rows(meta_ref, cot_ref, share) * mlp, 0, 1)


def spread_kernel(meta_ref, d_attn_ref, vp_ref, packed_ref, d_bias_ref):
    grad = jnp.dot(d_attn_ref[...], vp_ref[...], preferred_element_type=F32).T
    half = grad.shape[1] // 2
    features = grad.shape[0] // 2
    for place in range(packed_ref.shape[0]):
        start = features + place // 2 * DH
        side = place % 2 * half
        packed_ref[place] = grad[start : start + DH, side : side + half].astype(BF16)
    d_bias_ref[...] = jnp.sum(d_attn_ref[...].astype(F32), axis=0, keepdims=True)


def unspread_kernel(
    meta_ref, parts_ref, qk_ref, vp_ref, d_one_ref, d_qk_ref, d_vp_ref, sent_ref, d_bias_ref
):
    heads = parts_ref.shape[0] // 2
    rows = d_one_ref.shape[0]
    query, key, value = [], [], []
    for head in range(heads):
        left = parts_ref[2 * head].astype(F32)
        right = parts_ref[2 * head + 1].astype(F32)
        both = left[:, : 2 * rows] + right[:, : 2 * rows]
        key.append(both[:, :rows])
        value.append(both[:, rows:])
        query.append(jnp.concatenate([left[:, 2 * rows :], right[:, 2 * rows :]], axis=1))
    d_qk_ref[...] = jnp.concatenate(query + key, axis=0).T.astype(BF16)
    blank = jnp.zeros((heads * DH, rows), F32)
    d_vp_ref[...] = jnp.concatenate(value + [blank], axis=0).T.astype(BF16)
    tile = 384
    by_last = (((1,), (1,)), ((), ()))

    def step(number, carry):
        columns = pl.ds(pl.multiple_of(number * tile, tile), tile)
        total = lax.dot_general(d_qk_ref[...], qk_ref[columns, :], by_last, preferred_element_type=F32)
        total += lax.dot_general(d_vp_ref[...], vp_ref[columns, :], by_last, preferred_element_type=F32)
        d_one_ref[:, columns] = total.astype(BF16)
        return carry

    lax.fori_loop(0, qk_ref.shape[0] // tile, step, 0)

    def sent(first, second):
        sent_ref[...] = first[...]

    on_core(meta_ref, sent, d_vp_ref, d_qk_ref)
    d_bias_ref[0:1, :] = jnp.sum(d_qk_ref[...].astype(F32), axis=0, keepdims=True)
    d_bias_ref[1:2, :] = jnp.sum(d_vp_ref[...].astype(F32), axis=0, keepdims=True)


def weight_kernel(first_pairs, second_pairs, meta_ref, *refs):
    operands = 1 + max(max(pair) for pair in first_pairs + second_pairs)
    ins, outs, total = refs[:operands], refs[operands:-1], refs[-1]
    tile = 384

    def body(pairs):
        def step(number, carry):
            columns = pl.ds(pl.multiple_of(number * tile, tile), tile)
            block = jnp.zeros((tile, total.shape[1]), F32)
            for left, right in pairs:
                block += lax.dot_general(
                    ins[left][:, columns], ins[right][...], (((0,), (0,)), ((), ())),
                    preferred_element_type=F32,
                )
            total[columns, :] = block.astype(BF16)
            return carry

        lax.fori_loop(0, total.shape[0] // tile, step, 0)

    on_core(meta_ref, lambda pairs, _: body(pairs), first_pairs, second_pairs)
    rows = outs[0].shape[0]
    for step, out in enumerate(outs):
        start = pl.multiple_of((meta_ref[3] ^ step) * rows, 16)
        out[...] = total[pl.ds(start, rows), :]


def first_back_kernel(
    latents, meta_ref, parts_ref, tokens_ref, d_mid_ref, mod_ref, mid_sums_ref, last_sums_ref,
    fc2_bias_ref, proj_bias_ref, fc1_bias_ref, qv_bias_ref, grad_ref, sent_ref, bias_ref, first_sums,
):
    copies, share, width = parts_ref.shape
    masks = row_masks(meta_ref, latents, meta_ref[1] + meta_ref[2] * share, share)
    d_hidden = parts_ref[0].astype(F32)
    for part in range(1, copies):
        d_hidden = d_hidden + parts_ref[part].astype(F32)
    unit, inverse = normed(own_rows(meta_ref, tokens_ref, share))
    grad = d_mid_ref[...] + norm_back(unit, inverse, d_hidden * (1.0 + rows_of(mod_ref, masks, 1)))
    grad_ref[...] = grad.astype(BF16)
    latent_sums(first_sums, masks, d_hidden, 0, 2)
    latent_sums(first_sums, masks, d_hidden * unit, 1, 2)
    columns = width // copies
    for number in range(latents):
        for feature in range(6):
            if feature < 2:
                row = first_sums[number * 2 + feature : number * 2 + feature + 1, :]
            elif feature < 5:
                place = number * 3 + feature - 2
                row = mid_sums_ref[place : place + 1, :]
            else:
                row = last_sums_ref[number : number + 1, :]
            place = number * 6 + feature
            for part in range(copies):
                sent_ref[part, place : place + 1, :] = row[:, part * columns : (part + 1) * columns]
    place = 0
    for ref in (fc2_bias_ref, proj_bias_ref, fc1_bias_ref):
        for start in range(0, ref.shape[1], columns):
            bias_ref[place : place + 1, :] = ref[:, start : start + columns]
            place += 1
    bias_ref[place : place + 2, :] = qv_bias_ref[:, :columns]


def order_kernel(count, meta_ref, *refs):
    result_ref, grad_ref = refs[2 * count :]
    share = refs[0].shape[0]
    for step in range(count):
        start = pl.multiple_of((meta_ref[2] ^ step) * share, share)
        result_ref[pl.ds(start, share), :] = refs[step][...]
        grad_ref[pl.ds(start, share), :] = refs[count + step][...].astype(F32)


def finish_kernel(
    latents, meta_ref, sums_ref, active_ref, w_ada_ref,
    w_grad_ref, b_grad_ref, d_active_ref, fc2_ref, proj_ref, fc1_ref, qv_ref, total_ref,
):
    total = sums_ref[0]
    for part in range(1, sums_ref.shape[0]):
        total = total + sums_ref[part]
    total_ref[...] = total
    by_last = (((1,), (1,)), ((), ()))
    d_active = jnp.zeros(d_active_ref.shape, F32)
    for feature in range(6):
        rows = [
            total_ref[number * 6 + feature : number * 6 + feature + 1, :] for number in range(latents)
        ]
        grad = active_ref[:, 0:1] * rows[0]
        bias = rows[0]
        for number in range(1, latents):
            grad = grad + active_ref[:, number : number + 1] * rows[number]
            bias = bias + rows[number]
        w_grad_ref[feature] = grad
        b_grad_ref[feature : feature + 1, :] = bias
        wide = jnp.concatenate(rows, axis=0)
        high = wide.astype(BF16)
        low = (wide - high.astype(F32)).astype(BF16)
        weight = w_ada_ref[feature]
        d_active += lax.dot_general(high, weight, by_last, preferred_element_type=F32)
        d_active += lax.dot_general(low, weight, by_last, preferred_element_type=F32)
    d_active_ref[...] = d_active
    columns = total_ref.shape[1]
    place = 6 * latents
    for ref in (fc2_ref, proj_ref, fc1_ref):
        for start in range(0, ref.shape[1], columns):
            ref[:, start : start + columns] = total_ref[place : place + 1, :]
            place += 1
    qv_ref[...] = total_ref[place : place + 2, :]


def latent_index(latent_len, first_row, row_count, token_total):
    positions = first_row + jnp.arange(row_count, dtype=jnp.int32)
    ends = jnp.cumsum(latent_len, dtype=jnp.int32)
    found = jnp.sum((positions[:, None] >= ends[None, :]).astype(jnp.int32), axis=1, dtype=jnp.int32)
    return jnp.where((positions >= 0) & (positions < token_total), found, -1)


def normed(values):
    average = jnp.mean(values, axis=-1, keepdims=True)
    centred = values - average
    spread = jnp.mean(centred * centred, axis=-1, keepdims=True)
    inverse = lax.rsqrt(spread + NORM_EPS)
    return centred * inverse, inverse


def norm_back(unit, inverse, grad):
    along = jnp.mean(grad * unit, axis=-1, keepdims=True)
    return inverse * (grad - jnp.mean(grad, axis=-1, keepdims=True) - unit * along)


def gelu_pair(value):
    root = math.sqrt(2.0 / math.pi)
    bend = jnp.tanh(root * (value + 0.044715 * value * value * value))
    slope = root * (1.0 + 3.0 * 0.044715 * value * value)
    gelu = 0.5 * value * (1.0 + bend)
    return gelu, 0.5 * (1.0 + bend) + 0.5 * value * (1.0 - bend * bend) * slope


def local(
    tokens,
    conditioning,
    latent_len,
    w_ada,
    b_ada,
    w_qkv,
    b_qv,
    w_proj,
    b_proj,
    w_fc1,
    b_fc1,
    w_fc2,
    b_fc2,
    cotangent,
):
    rows, width = tokens.shape
    share_width = w_qkv.shape[0]
    features = w_qkv.shape[2]
    units = w_fc1.shape[1]
    heads = features // DH
    latents = conditioning.shape[0]
    n_dp, n_tensor = lax.axis_size("dp"), lax.axis_size("tensor")
    my_dp, my_tensor = lax.axis_index("dp"), lax.axis_index("tensor")
    share = rows // n_tensor

    core = my_dp % 2
    qk = w_qkv[:, :2].reshape(share_width, 2 * features)
    vp = jnp.concatenate([w_qkv[:, 2], w_proj.T], axis=1)
    early_rows = pair_rows(qk, vp)

    cond = conditioning.astype(F32)
    sigmoid = 1.0 / (1.0 + jnp.exp(-cond))
    activated = (cond * sigmoid).astype(BF16)
    own_activated = lax.dynamic_slice_in_dim(activated, my_dp * share_width, share_width, 1)
    flat_ada = w_ada.reshape(share_width, 6 * features)
    mod_part = jnp.dot(own_activated, flat_ada, preferred_element_type=F32)
    mod_part = mod_part.reshape(latents * 6, features)
    bias_ada = jnp.tile(b_ada.astype(F32), (latents, 1))
    few_chips = n_dp // 2 == 4
    mod_sent = gate(jnp.broadcast_to(mod_part[None], (n_dp,) + mod_part.shape))
    early_rows = gate(early_rows, mod_sent)
    mod_mine = jnp.sum(exchange(mod_sent, "dp"), axis=0) + bias_ada
    mod_parts = gather(mod_mine, "tensor", n_tensor)
    early_parts = chip_parts(early_rows) if few_chips else [gather_chips(early_rows)]

    early_parts = list(gate_all(early_parts, mod_parts))
    early_parts += [swap(part, "dp", 1) for part in early_parts]
    count = len(early_parts) // 2
    meta = jnp.stack([core, my_dp * rows, my_tensor, my_dp // 2]).astype(jnp.int32)
    meta = jnp.concatenate([meta, latent_len])
    place_meta = meta if few_chips else meta.at[3].set(0)
    by_last = (((1,), (1,)), ((), ()))
    by_token = (((0,), (0,)), ((), ()))
    bias = jnp.concatenate([b_qv[0], jnp.zeros_like(b_qv[0]), b_qv[1], jnp.zeros_like(b_qv[0])])
    hidden_one, d_mlp, packed, full_qk, full_vp, d_bias_fc2, mod_rows = call(
        lambda *refs: project_kernel(latents, count, *refs),
        "project",
        place_meta,
        (*early_parts, tokens, cotangent, mod_parts, bias.astype(F32).reshape(2, -1)),
        (((rows, width), BF16), ((rows, width), BF16), ((2 * heads, DH, rows * 5 // 2), BF16))
        + (((width, 2 * features), BF16),) * 2
        + (((1, width), F32), ((6 * latents, width), F32)),
        [pltpu.SemaphoreType.DMA((2, count))],
        2 * count,
    )
    late_rows = pair_rows(w_fc1, w_fc2.T)
    hidden_other = swap(hidden_one, "dp", 1)
    split = HeadSplit if 2 * heads == n_dp else Window
    attention = split(latent_len, rows)
    attended_parts = attention.forward(packed)
    late_rows = gate(late_rows, attended_parts)
    late_parts = chip_parts(late_rows)[:-1] if few_chips else [gather_chips(late_rows)]
    attn_part, attended = call(
        attend_out_kernel,
        "attend_out",
        meta,
        (attended_parts, full_vp),
        (((rows, width), BF16), ((rows, 2 * features), BF16)),
    )
    attn_parts = exchange_shares(attn_part, "tensor")
    hidden_blocks, attn_out, residual_mid = call(
        lambda *refs: middle_kernel(latents, *refs),
        "middle",
        meta,
        (attn_parts, tokens, mod_rows, b_proj.reshape(1, -1)),
        (((n_tensor, share, width), BF16), ((share, width), F32), ((share, width), F32)),
        due=late_parts[1:],
    )
    hidden_two = exchange(hidden_blocks, "tensor").reshape(rows, width)
    if few_chips:
        last_part = swap(gate(late_rows, attn_out), "dp", n_dp - 2)
        late_parts.append(gate(last_part, hidden_two))
    late_other = [swap(part, "dp", 1) for part in late_parts]

    d_two_part, gelu_out, d_pre, d_bias_fc1, left_sent, right_sent, *mlp_blocks = call(
        lambda *refs: mlp_kernel(count, *refs),
        "mlp",
        place_meta,
        (*late_parts, *late_other, hidden_two, d_mlp, b_fc1.reshape(1, -1)),
        (((rows, width), BF16), ((rows, units), BF16), ((rows, units), BF16), ((1, units), F32))
        + (((rows, width), BF16), ((rows, units), BF16))
        + (((share, width), BF16),) * n_tensor,
        [pltpu.VMEM((width, units), BF16)] * 2
        + [pltpu.VMEM((rows, width), F32)] * 2
        + [pltpu.SemaphoreType.DMA((2, count))],
        2 * count,
    )
    d_two_parts = exchange_shares(d_two_part, "tensor")

    chips = n_dp // 2 if few_chips else 1
    left_other = swap(left_sent, "dp", 1)
    right_other = swap(right_sent, "dp", 1)
    late_blocks = call(
        lambda *refs: weight_kernel([(0, 2), (4, 5)], [(1, 3), (4, 5)], *refs),
        "late_weights",
        place_meta,
        (hidden_two, d_mlp, d_pre, gelu_out, left_other, right_other),
        (((width // chips, units), BF16),) * chips,
        [pltpu.VMEM((width, units), BF16)],
    )
    late_grads = sum_chips(late_blocks[:-1]) if few_chips else sum_chips(late_blocks)

    d_attn_blocks, d_mid, mid_sums = call(
        lambda *refs: middle_back_kernel(latents, *refs),
        "middle_back",
        meta,
        (d_two_parts, residual_mid, attn_out, cotangent, mod_rows),
        (((n_tensor, share, width), BF16), ((share, width), F32), ((3 * latents, width), F32)),
        due=late_blocks,
    )
    d_attn = exchange(d_attn_blocks, "tensor").reshape(rows, width)

    d_spread, d_bias_proj = call(
        spread_kernel,
        "spread",
        meta,
        (d_attn, full_vp),
        (((2 * heads, DH, rows // 2), BF16), ((1, width), F32)),
        due=late_grads[1:],
    )
    mlp_parts = mlp_blocks[:1] + [
        swap(gate(block, d_spread), "tensor", step)
        for step, block in enumerate(mlp_blocks)
        if step
    ]
    d_attn_other = swap(d_attn, "dp", 1)
    attended_other = swap(attended, "dp", 1)
    d_packed, last_grad = attention.backward(d_spread, mlp_parts[1:], late_blocks[-1])
    result_own, last_sums = call(
        lambda *refs: result_kernel(latents, n_tensor, *refs),
        "result",
        meta,
        (*mlp_parts, residual_mid, cotangent, mod_rows, b_fc2.reshape(1, -1)),
        (((share, width), BF16), ((latents, width), F32)),
    )
    d_one_part, d_qk, d_vp, d_sent, d_bias_qv = call(
        unspread_kernel,
        "unspread",
        meta,
        (d_packed, full_qk, full_vp),
        (((rows, width), BF16),)
        + (((rows, 2 * features), BF16),) * 3
        + (((2, 2 * features), F32),),
        flops=2 * 10**10,
    )
    result_parts = [result_own] + [swap(result_own, "tensor", bits) for bits in range(1, n_tensor)]
    d_one_part = gate(d_one_part, *result_parts[1:])
    d_one_parts = exchange_shares(d_one_part, "tensor")

    if few_chips:
        late_grads.append(last_grad)
    right_other = swap(d_sent, "dp", 1)
    early_blocks = call(
        lambda *refs: weight_kernel(
            [(0, 2), (5, 7)], [(0, 3), (1, 4), (5, 7), (6, 8)], *refs
        ),
        "early_weights",
        place_meta,
        (hidden_one, d_attn, d_qk, d_vp, attended, hidden_other, d_attn_other, right_other, attended_other),
        (((width // chips, 2 * features), BF16),) * chips,
        [pltpu.VMEM((width, 2 * features), BF16)],
    )
    early_grads = sum_chips(early_blocks[:3] if few_chips else early_blocks)

    grad_own, d_mod_part, bias_rows = call(
        lambda *refs: first_back_kernel(latents, *refs),
        "first_back",
        meta,
        (d_one_parts, tokens, d_mid, mod_rows, mid_sums, last_sums)
        + (d_bias_fc2, d_bias_proj, d_bias_fc1, d_bias_qv),
        (((share, width), BF16), ((n_tensor, 6 * latents, features), F32))
        + (((2 * (width // features) + units // features + 2, features), F32),),
        [pltpu.VMEM((2 * latents, width), F32)],
        due=early_grads[1:3],
    )
    if few_chips:
        last_block = gate(early_blocks[3], d_mod_part)
        early_grads.append(swap(last_block, "dp", n_dp - 2))
    d_mod_mine = jnp.sum(exchange(d_mod_part, "tensor"), axis=0)
    d_mod_rows = jnp.concatenate([d_mod_mine, bias_rows])
    d_mod_rows = gate(jnp.broadcast_to(d_mod_rows[None], (n_dp,) + d_mod_rows.shape))
    grad_own = gate(grad_own, d_mod_rows)
    grad_parts = [grad_own] + [swap(grad_own, "tensor", bits) for bits in range(1, n_tensor)]
    sums = exchange(d_mod_rows, "dp")
    sums = gate(sums, early_grads[3]) if few_chips else sums
    grad_parts = gate_all(grad_parts, sums)
    result, grad_tokens = call(
        lambda *refs: order_kernel(n_tensor, *refs),
        "order",
        meta,
        (*result_parts, *grad_parts),
        (((rows, width), BF16), ((rows, width), F32)),
    )
    grad_w_ada, grad_b_ada, d_active, sum_b_fc2, sum_b_proj, sum_b_fc1, sum_b_qv = call(
        lambda *refs: finish_kernel(latents, *refs),
        "finish",
        meta,
        (sums, own_activated.astype(F32).T, w_ada.transpose(1, 0, 2)),
        (((6, share_width, features), F32), ((6, features), F32), ((latents, share_width), F32))
        + (((1, width), F32), ((1, width), F32), ((1, units), F32), ((2, features), F32)),
        [pltpu.VMEM(sums.shape[1:], F32)],
    )
    d_active = gather(d_active, ("dp", "tensor"), n_dp * n_tensor)
    d_active = jnp.sum(d_active.reshape(n_dp, n_tensor, latents, share_width), axis=1)
    d_active = d_active.transpose(1, 0, 2).reshape(latents, width)
    grad_cond = d_active * (sigmoid * (1.0 + cond * (1.0 - sigmoid)))

    grad_fc1, grad_fc2 = finish_pair(late_grads)
    grad_qk, grad_vp = finish_pair(early_grads)
    grad_qkv = jnp.concatenate([grad_qk, grad_vp[:, :features]], axis=1)
    grad_qkv = grad_qkv.reshape(share_width, 3, features)

    return (
        result,
        grad_tokens,
        grad_cond,
        grad_w_ada.transpose(1, 0, 2),
        grad_b_ada,
        grad_qkv,
        sum_b_qv,
        grad_vp[:, features:].T,
        sum_b_proj.reshape(width),
        grad_fc1,
        sum_b_fc1.reshape(units),
        grad_fc2.T,
        sum_b_fc2.reshape(width),
    )


def solution(mesh):
    in_specs = (
        P("dp", None),
        P(),
        P(),
        P("dp", None, "tensor"),
        P(None, "tensor"),
        P("dp", None, "tensor"),
        P(None, "tensor"),
        P("tensor", "dp"),
        P(),
        P("dp", "tensor"),
        P("tensor"),
        P("tensor", "dp"),
        P(),
        P("dp", None),
    )
    out_specs = (
        P("dp", None),
        P("dp", None),
        P(),
        P("dp", None, "tensor"),
        P(None, "tensor"),
        P("dp", None, "tensor"),
        P(None, "tensor"),
        P("tensor", "dp"),
        P(),
        P("dp", "tensor"),
        P("tensor"),
        P("tensor", "dp"),
        P(),
    )
    return jax.shard_map(local, mesh=mesh, in_specs=in_specs, out_specs=out_specs, check_vma=False)
```

```python
import math

import jax
import jax.numpy as jnp
from jax import lax
from jax.experimental import pallas as pl
from jax.experimental.pallas import tpu as pltpu
from jax.sharding import PartitionSpec as P

DH = 72
SEQ = 1024
STEP = 512
NORM_EPS = 1e-06
NEGATIVE = -1e30
SCALE = 1.0 / math.sqrt(DH)
VMEM_BYTES = 255 * 256 * 1024
BF16 = jnp.bfloat16
F32 = jnp.float32


def swap(block, axis, bits):
    route = [(i, i ^ bits) for i in range(lax.axis_size(axis))]
    return lax.ppermute(block, axis, route)


def exchange(blocks, axis):
    return lax.all_to_all(blocks, axis, 0, 0, tiled=True)


def gather(block, axis, count):
    return exchange(jnp.broadcast_to(block[None], (count,) + block.shape), axis)


def gate_all(values, *others):
    anywhere = pl.BlockSpec(memory_space=pl.ANY)
    return pl.pallas_call(
        lambda *refs: None,
        out_shape=tuple(jax.ShapeDtypeStruct(value.shape, value.dtype) for value in values),
        in_specs=[anywhere] * (len(values) + len(others)),
        out_specs=(anywhere,) * len(values),
        input_output_aliases={place: place for place in range(len(values))},
        cost_estimate=pl.CostEstimate(flops=1, bytes_accessed=1, transcendentals=0),
        name="gate",
    )(*values, *others)


def gate(value, *others):
    return gate_all((value,), *others)[0]


def choose(core, first, second):
    return jnp.where(core == 0, first, second), jnp.where(core == 0, second, first)


def pair_rows(first, second):
    core = lax.axis_index("dp") % 2
    keep, send = choose(core, first, second)
    return jnp.concatenate(choose(core, keep, swap(send, "dp", 1)))


def chip_parts(rows):
    count = lax.axis_size("dp") // 2
    return [rows] + [swap(rows, "dp", 2 * step) for step in range(1, count)]


def gather_chips(rows):
    count = lax.axis_size("dp")
    groups = [list(range(core, count, 2)) for core in range(2)]
    return lax.all_gather(rows, "dp", axis=0, tiled=True, axis_index_groups=groups)


def sum_chips(blocks):
    if len(blocks) == 1:
        count, chip = lax.axis_size("dp") // 2, lax.axis_index("dp") // 2
        rows = blocks[0].reshape((count, -1) + blocks[0].shape[1:])
        blocks = [
            lax.dynamic_index_in_dim(rows, chip ^ step, 0, keepdims=False) for step in range(count)
        ]
    return [swap(block, "dp", 2 * step) if step else block for step, block in enumerate(blocks)]


def finish_pair(parts):
    core = lax.axis_index("dp") % 2
    rows = sum(part.astype(F32) for part in parts)
    half = rows.shape[0] // 2
    keep, send = choose(core, rows[:half], rows[half:])
    return choose(core, keep, swap(send, "dp", 1))


def exchange_shares(partial, axis):
    count = lax.axis_size(axis)
    blocks = partial.reshape((count, partial.shape[0] // count) + partial.shape[1:])
    return exchange(blocks, axis)


def tile_range(meta_ref, latents, tile, core):
    lane = lax.broadcasted_iota(jnp.int32, (1, 256), 1)
    first = tile * 512 + core * 128
    last = first + 383
    place = first + lane + jnp.where(lane >= 128, 128, 0)
    begin = jnp.zeros((1, 256), jnp.int32)
    finish = jnp.zeros((1, 256), jnp.int32)
    low = jnp.int32(0)
    high = jnp.int32(0)
    start = jnp.int32(0)
    for number in range(latents):
        end = start + meta_ref[1 + number]
        inside = (place >= start) & (place < end)
        begin = jnp.where(inside, start, begin)
        finish = jnp.where(inside, end, finish)
        low = jnp.where((first >= start) & (first < end), start, low)
        high = jnp.where((last >= start) & (last < end), end, high)
        start = end
    return begin, finish, low // STEP, (high + STEP - 1) // STEP


def pair(ref, tile, start):
    left = ref[2 * tile, :, start : start + 128]
    right = ref[2 * tile + 1, :, start : start + 128]
    return jnp.concatenate([left, right], axis=1)


def wide(packed_ref, block, start):
    left = packed_ref[2 * block, :, start : start + 256]
    right = packed_ref[2 * block + 1, :, start : start + 256]
    return jnp.concatenate([left, right], axis=1)


def key_mask(block, begin, finish):
    place = block * STEP + lax.broadcasted_iota(jnp.int32, (STEP, 256), 0)
    return (place >= begin) & (place < finish)


def forward_kernel(latents, meta_ref, packed_ref, out_ref, exact_ref, log_ref, keys, scores):
    blocks = packed_ref.shape[0]
    core = meta_ref[0]
    for block in range(blocks // 2):
        keys[block] = wide(packed_ref, block, 0).astype(F32).T.astype(BF16)
    for tile in range(blocks // 2):
        begin, finish, low, high = tile_range(meta_ref, latents, tile, core)
        query = pair(packed_ref, tile, 512)

        def score(block, largest):
            raw = jnp.dot(keys[block], query, preferred_element_type=F32) * SCALE
            raw = jnp.where(key_mask(block, begin, finish), raw, NEGATIVE)
            scores[block] = raw
            return jnp.maximum(largest, jnp.max(raw, axis=0, keepdims=True))

        largest = lax.fori_loop(low, high, score, jnp.full((1, 256), NEGATIVE, F32))

        def mix(block, carry):
            total, mixed = carry
            weights = jnp.exp(scores[block] - largest)
            total = total + jnp.sum(weights, axis=0, keepdims=True)
            values = wide(packed_ref, block, 256)
            mixed = mixed + jnp.dot(values, weights.astype(BF16), preferred_element_type=F32)
            return total, mixed

        total, mixed = lax.fori_loop(
            low, high, mix, (jnp.zeros((1, 256), F32), jnp.zeros((DH, 256), F32))
        )
        mixed = mixed / total
        log_total = largest + jnp.log(total)
        for half in range(2):
            part = mixed[:, half * 128 : half * 128 + 128]
            exact_ref[2 * tile + half] = part
            out_ref[2 * tile + half] = part.astype(BF16)
            log_ref[2 * tile + half] = log_total[:, half * 128 : half * 128 + 128]


def backward_kernel(
    latents, meta_ref, packed_ref, grad_ref, exact_ref, log_ref, out_ref, keys, values, d_keys, d_values
):
    blocks = packed_ref.shape[0]
    core = meta_ref[0]
    for block in range(blocks // 2):
        keys[block] = wide(packed_ref, block, 0).astype(F32).T.astype(BF16)
        values[block] = wide(packed_ref, block, 256).astype(F32).T.astype(BF16)
    d_keys[...] = jnp.zeros_like(d_keys)
    d_values[...] = jnp.zeros_like(d_values)
    by_query = (((1,), (1,)), ((), ()))
    for tile in range(blocks // 2):
        begin, finish, low, high = tile_range(meta_ref, latents, tile, core)
        query = pair(packed_ref, tile, 512)
        grad = pair(grad_ref, tile, 0)
        inner = jnp.sum(grad.astype(F32) * pair(exact_ref, tile, 0), axis=0, keepdims=True)
        log_total = pair(log_ref, tile, 0)

        def step(block, d_query):
            raw = jnp.dot(keys[block], query, preferred_element_type=F32) * SCALE
            probs = jnp.where(key_mask(block, begin, finish), jnp.exp(raw - log_total), 0.0)
            d_probs = jnp.dot(values[block], grad, preferred_element_type=F32)
            d_scores = (probs * (d_probs - inner)).astype(BF16)
            d_values[block] += lax.dot_general(
                grad, probs.astype(BF16), by_query, preferred_element_type=F32
            )
            d_keys[block] += lax.dot_general(query, d_scores, by_query, preferred_element_type=F32)
            key_rows = wide(packed_ref, block, 0)
            return d_query + jnp.dot(key_rows, d_scores, preferred_element_type=F32)

        d_query = lax.fori_loop(low, high, step, jnp.zeros((DH, 256), F32)) * SCALE
        for half in range(2):
            part = d_query[:, half * 128 : half * 128 + 128]
            out_ref[2 * tile + half, :, 512:640] = part.astype(BF16)
    for block in range(blocks):
        half = slice(block % 2 * 256, block % 2 * 256 + 256)
        out_ref[block, :, :256] = (d_keys[block // 2, :, half] * SCALE).astype(BF16)
        out_ref[block, :, 256:512] = d_values[block // 2, :, half].astype(BF16)


def attend_forward(meta, packed):
    blocks = packed.shape[0]
    shape = jax.ShapeDtypeStruct
    return pl.pallas_call(
        lambda *refs: forward_kernel(meta.shape[0] - 1, *refs),
        out_shape=(
            shape((blocks, DH, 128), BF16),
            shape((blocks, DH, 128), F32),
            shape((blocks, 1, 128), F32),
        ),
        in_specs=[
            pl.BlockSpec(memory_space=pltpu.SMEM),
            pl.BlockSpec(memory_space=pltpu.VMEM),
        ],
        out_specs=tuple([pl.BlockSpec(memory_space=pltpu.VMEM)] * 3),
        scratch_shapes=[
            pltpu.VMEM((blocks // 2, STEP, DH), BF16),
            pltpu.VMEM((blocks // 2, STEP, 256), F32),
        ],
        compiler_params=pltpu.CompilerParams(vmem_limit_bytes=VMEM_BYTES),
        cost_estimate=pl.CostEstimate(flops=10**9, bytes_accessed=4 * 10**6, transcendentals=10**6),
        name="attend_forward",
    )(meta, packed)


def attend_backward(meta, packed, grad, exact, log_total):
    blocks = packed.shape[0]
    return pl.pallas_call(
        lambda *refs: backward_kernel(meta.shape[0] - 1, *refs),
        out_shape=jax.ShapeDtypeStruct(packed.shape, BF16),
        in_specs=[pl.BlockSpec(memory_space=pltpu.SMEM)]
        + [pl.BlockSpec(memory_space=pltpu.VMEM)] * 4,
        out_specs=pl.BlockSpec(memory_space=pltpu.VMEM),
        scratch_shapes=[
            pltpu.VMEM((blocks // 2, STEP, DH), BF16),
            pltpu.VMEM((blocks // 2, STEP, DH), BF16),
            pltpu.VMEM((blocks // 2, DH, STEP), F32),
            pltpu.VMEM((blocks // 2, DH, STEP), F32),
        ],
        compiler_params=pltpu.CompilerParams(vmem_limit_bytes=VMEM_BYTES),
        cost_estimate=pl.CostEstimate(flops=1, bytes_accessed=1, transcendentals=0),
        name="attend_backward",
    )(meta, packed, grad, exact, log_total)


class HeadSplit:
    def __init__(self, latent_len, rows):
        self.rows = rows
        self.meta = jnp.concatenate([lax.axis_index("dp").astype(jnp.int32)[None] % 2, latent_len])

    def forward(self, packed):
        self.packed = exchange(packed, "dp")
        out, self.exact, self.log_total = attend_forward(self.meta, self.packed)
        return exchange(out, "dp")

    def backward(self, grad, due, beside):
        beside = swap(gate(beside, grad), "dp", lax.axis_size("dp") - 2)
        grad = exchange(grad, "dp")
        out = attend_backward(self.meta, self.packed, grad, self.exact, self.log_total)
        return exchange(gate(out, beside, *due), "dp"), beside


class Window:
    def __init__(self, latent_len, rows):
        self.rows = rows
        self.reach = (SEQ - 2) // rows + 1
        total = rows * lax.axis_size("dp")
        first = lax.axis_index("dp") * rows
        own = latent_index(latent_len, first, rows, total)
        ids = [
            latent_index(latent_len, first + offset * rows, rows, total)
            for offset in range(-self.reach, self.reach + 1)
        ]
        self.allowed = own[:, None] == jnp.concatenate(ids)[None, :]

    def from_behind(self, block, distance):
        devices = range(lax.axis_size("dp"))
        return lax.ppermute(
            block, "dp", [(i - distance, i) for i in devices if i - distance in devices]
        )

    def head_scores(self, query, key):
        raw = jnp.einsum("eq,ek->qk", query, key, preferred_element_type=F32) * SCALE
        return jnp.where(self.allowed, raw, NEGATIVE)

    def forward(self, packed):
        rows = self.rows
        split = packed.reshape(-1, 2, DH, rows * 5 // 2)
        query = jnp.concatenate([split[:, 0, :, 2 * rows :], split[:, 1, :, 2 * rows :]], axis=2)
        projected = jnp.stack([query, split[:, 0, :, :rows], split[:, 0, :, rows : 2 * rows]])
        key_value = projected[1:]
        pieces = [
            key_value if offset == 0 else self.from_behind(key_value, -offset)
            for offset in range(-self.reach, self.reach + 1)
        ]
        window = jnp.concatenate(pieces, axis=3)
        self.operands = (projected[0], window[0], window[1])

        def one(operands):
            query, key, value = operands
            scores = self.head_scores(query, key)
            largest = jnp.max(scores, axis=1, keepdims=True)
            weights = jnp.exp(scores - largest)
            totals = jnp.sum(weights, axis=1, keepdims=True)
            probs = (weights / totals).astype(BF16)
            mixed = jnp.einsum("qk,ek->eq", probs, value, preferred_element_type=F32)
            return mixed.astype(BF16), (largest + jnp.log(totals))[:, 0]

        out, self.log_total = lax.map(one, self.operands)
        out = out.reshape(-1, DH, 2, rows // 2).transpose(0, 2, 1, 3)
        return out.reshape(-1, DH, rows // 2)

    def backward(self, grad, due, beside):
        rows, reach = self.rows, self.reach
        halves = grad.reshape(-1, 2, DH, rows // 2)
        grads = jnp.concatenate([halves[:, 0], halves[:, 1]], axis=2)

        def one(operands):
            query, key, value, grad, log_total = operands
            probs = jnp.exp(self.head_scores(query, key) - log_total[:, None])
            d_value = jnp.einsum("qk,eq->ek", probs.astype(BF16), grad, preferred_element_type=F32)
            d_probs = jnp.einsum("eq,ek->qk", grad, value, preferred_element_type=F32)
            inner = jnp.sum(probs * d_probs, axis=1, keepdims=True)
            d_scores = (probs * (d_probs - inner)).astype(BF16)
            d_query = jnp.einsum("qk,ek->eq", d_scores, key, preferred_element_type=F32) * SCALE
            d_key = jnp.einsum("qk,eq->ek", d_scores, query, preferred_element_type=F32) * SCALE
            return d_query, d_key, d_value

        d_query, d_key, d_value = lax.map(one, self.operands + (grads, self.log_total))
        d_window = jnp.stack([d_key, d_value])
        d_key_value = d_window[..., reach * rows : (reach + 1) * rows]
        for offset in range(-reach, reach + 1):
            if offset != 0:
                block = d_window[..., (offset + reach) * rows : (offset + reach + 1) * rows]
                d_key_value = d_key_value + self.from_behind(block, offset)
        wide = jnp.concatenate([d_key_value[0], d_key_value[1]], axis=2)
        wide = jnp.stack([wide, jnp.zeros_like(wide)], axis=1)
        halves = d_query.reshape(-1, DH, 2, rows // 2).transpose(0, 2, 1, 3)
        packed = jnp.concatenate([wide, halves], axis=3).astype(BF16)
        return packed.reshape(-1, DH, rows * 5 // 2), beside


META = 4


def vmem(count):
    return [pl.BlockSpec(memory_space=pltpu.VMEM)] * count


def call(body, name, meta, arrays, outs, scratch=(), anywhere=0, due=(), flops=1):
    count = 1 + len(arrays)

    def kernel(*refs):
        body(*refs[:count], *refs[count + len(due) :])

    return pl.pallas_call(
        kernel,
        out_shape=tuple(jax.ShapeDtypeStruct(shape, kind) for shape, kind in outs),
        in_specs=[pl.BlockSpec(memory_space=pltpu.SMEM)]
        + [pl.BlockSpec(memory_space=pl.ANY)] * anywhere
        + vmem(len(arrays) - anywhere)
        + [pl.BlockSpec(memory_space=pl.ANY)] * len(due),
        out_specs=tuple(vmem(len(outs))),
        scratch_shapes=list(scratch),
        compiler_params=pltpu.CompilerParams(vmem_limit_bytes=VMEM_BYTES),
        cost_estimate=pl.CostEstimate(flops=flops, bytes_accessed=1, transcendentals=0),
        name=name,
    )(meta, *arrays, *due)


def row_masks(meta_ref, latents, first, rows):
    place = first + lax.broadcasted_iota(jnp.int32, (rows, 1), 0)
    ids = jnp.zeros((rows, 1), jnp.int32)
    end = jnp.int32(0)
    for number in range(latents - 1):
        end = end + meta_ref[META + number]
        ids = ids + (place >= end).astype(jnp.int32)
    return [(ids == number).astype(F32) for number in range(latents)]


def rows_of(mod_ref, masks, feature):
    out = masks[0] * mod_ref[feature : feature + 1, :]
    for number in range(1, len(masks)):
        row = number * 6 + feature
        out = out + masks[number] * mod_ref[row : row + 1, :]
    return out


def latent_sums(out_ref, masks, values, feature, features):
    rounded = values.astype(BF16).astype(F32)
    for number, mask in enumerate(masks):
        row = number * features + feature
        out_ref[row : row + 1, :] = jnp.sum(mask * rounded, axis=0, keepdims=True)


def own_rows(meta_ref, ref, share):
    start = pl.multiple_of(meta_ref[2] * share, share)
    return ref[pl.ds(start, share), :].astype(F32)


def on_core(meta_ref, body, mine, other):
    @pl.when(meta_ref[0] == 0)
    def _():
        body(mine, other)

    @pl.when(meta_ref[0] != 0)
    def _():
        body(other, mine)


def place_rows(meta_ref, parts, whole, sems):
    block = parts[0].shape[0]
    copies = []
    for step, part in enumerate(parts):
        start = pl.multiple_of((meta_ref[3] ^ step) * block, 16)
        copies.append(
            pltpu.make_async_copy(part, whole.at[pl.ds(start, block), :], sems.at[step])
        )
    return copies


def place_pair(meta_ref, mine, other, first_ref, second_ref, sems):
    def body(first, second):
        copies = place_rows(meta_ref, first, first_ref, sems.at[0])
        copies += place_rows(meta_ref, second, second_ref, sems.at[1])
        for copy in copies:
            copy.start()
        for copy in copies:
            copy.wait()

    on_core(meta_ref, body, mine, other)


def project_kernel(latents, count, meta_ref, *refs):
    mine, other = refs[:count], refs[count : 2 * count]
    tokens_ref, cot_ref, mod_parts_ref, bias_ref = refs[2 * count : 2 * count + 4]
    hidden_ref, d_mlp_ref, packed_ref, qk_ref, vp_ref, d_bias_ref, mod_ref, sems = refs[2 * count + 4 :]
    rows, width = tokens_ref.shape
    place_pair(meta_ref, mine, other, qk_ref, vp_ref, sems)
    columns = mod_parts_ref.shape[2]
    pieces = width // columns
    for piece in range(pieces):
        total = mod_parts_ref[piece].astype(F32)
        for part in range(piece + pieces, mod_parts_ref.shape[0], pieces):
            total = total + mod_parts_ref[part].astype(F32)
        mod_ref[:, piece * columns : (piece + 1) * columns] = total
    masks = row_masks(meta_ref, latents, meta_ref[1], rows)
    unit, _ = normed(tokens_ref[...].astype(F32))
    hidden = unit * (1.0 + rows_of(mod_ref, masks, 1)) + rows_of(mod_ref, masks, 0)
    hidden_ref[...] = hidden.astype(BF16)
    d_mlp = (cot_ref[...].astype(F32) * rows_of(mod_ref, masks, 5)).astype(BF16)
    d_mlp_ref[...] = d_mlp
    d_bias_ref[...] = jnp.sum(d_mlp.astype(F32), axis=0, keepdims=True)
    heads = packed_ref.shape[0] // 2
    features = heads * DH
    left = hidden_ref[...]
    both = jnp.dot(left, qk_ref[...], preferred_element_type=F32) + bias_ref[0:1, :]
    both = both.T
    value = jnp.dot(left, vp_ref[...], preferred_element_type=F32) + bias_ref[1:2, :]
    value = value.T
    for head in range(heads):
        start = head * DH
        query = both[start : start + DH].astype(BF16)
        key = both[features + start : features + start + DH].astype(BF16)
        val = value[start : start + DH].astype(BF16)
        for half in range(2):
            packed_ref[2 * head + half, :, :rows] = key
            packed_ref[2 * head + half, :, rows : 2 * rows] = val
            packed_ref[2 * head + half, :, 2 * rows :] = query[
                :, half * (rows // 2) : (half + 1) * (rows // 2)
            ]


def attend_out_kernel(meta_ref, parts_ref, vp_ref, part_ref, attended_ref):
    heads = parts_ref.shape[0] // 2
    rows = part_ref.shape[0]
    stacked = [jnp.zeros((heads * DH, rows), F32)]
    for head in range(heads):
        left = parts_ref[2 * head].astype(F32)
        right = parts_ref[2 * head + 1].astype(F32)
        stacked.append(jnp.concatenate([left, right], axis=1))
    attended_ref[...] = jnp.concatenate(stacked, axis=0).T.astype(BF16)
    part_ref[...] = lax.dot_general(
        attended_ref[...], vp_ref[...], (((1,), (1,)), ((), ())), preferred_element_type=F32
    ).astype(BF16)


def middle_kernel(
    latents, meta_ref, parts_ref, tokens_ref, mod_ref, bias_ref, sent_ref, attn_ref, mid_ref
):
    copies, share, width = parts_ref.shape
    masks = row_masks(meta_ref, latents, meta_ref[1] + meta_ref[2] * share, share)
    attn = bias_ref[...].astype(F32)
    for part in range(copies):
        attn = attn + parts_ref[part].astype(F32)
    attn_ref[...] = attn
    mid = own_rows(meta_ref, tokens_ref, share) + rows_of(mod_ref, masks, 2) * attn
    mid_ref[...] = mid
    unit, _ = normed(mid)
    hidden = unit * (1.0 + rows_of(mod_ref, masks, 4)) + rows_of(mod_ref, masks, 3)
    for part in range(copies):
        sent_ref[part] = hidden.astype(BF16)


def mlp_kernel(count, meta_ref, *refs):
    mine, other = refs[:count], refs[count : 2 * count]
    hidden_ref, d_mlp_ref, bias_ref = refs[2 * count : 2 * count + 3]
    d_two_ref, gelu_ref, d_pre_ref, d_bias_ref, left_ref, right_ref = refs[2 * count + 3 : 2 * count + 9]
    mlp_refs = refs[2 * count + 9 : -5]
    fc1_ref, fc2_ref, d_two_sum, mlp_sum, sems = refs[-5:]
    place_pair(meta_ref, mine, other, fc1_ref, fc2_ref, sems)
    d_two_sum[...] = jnp.zeros_like(d_two_sum)
    mlp_sum[...] = jnp.zeros_like(mlp_sum)
    tile = 384
    by_last = (((1,), (1,)), ((), ()))

    def step(number, carry):
        units = pl.ds(pl.multiple_of(number * tile, tile), tile)
        fc1, fc2 = fc1_ref[:, units], fc2_ref[:, units]
        pre = jnp.dot(hidden_ref[...], fc1, preferred_element_type=F32)
        gelu, slope = gelu_pair(pre + bias_ref[:, units].astype(F32))
        grad = jnp.dot(d_mlp_ref[...], fc2, preferred_element_type=F32)
        d_pre = (grad * slope).astype(BF16)
        gelu = gelu.astype(BF16)
        gelu_ref[:, units] = gelu
        d_pre_ref[:, units] = d_pre
        d_bias_ref[:, units] = jnp.sum(d_pre.astype(F32), axis=0, keepdims=True)
        d_two_sum[...] += lax.dot_general(d_pre, fc1, by_last, preferred_element_type=F32)
        mlp_sum[...] += lax.dot_general(gelu, fc2, by_last, preferred_element_type=F32)
        return carry

    lax.fori_loop(0, fc1_ref.shape[1] // tile, step, 0)
    d_two_ref[...] = d_two_sum[...].astype(BF16)
    def sent(left, right):
        left_ref[...] = left[0][...]
        right_ref[...] = left[1][...]

    on_core(meta_ref, sent, (d_mlp_ref, gelu_ref), (hidden_ref, d_pre_ref))
    share = mlp_refs[0].shape[0]
    for step, mlp_ref in enumerate(mlp_refs):
        start = pl.multiple_of((meta_ref[2] ^ step) * share, share)
        mlp_ref[...] = mlp_sum[pl.ds(start, share), :].astype(BF16)


def middle_back_kernel(
    latents, meta_ref, parts_ref, mid_in_ref, attn_ref, cot_ref, mod_ref, sent_ref, d_mid_ref, sums_ref
):
    copies, share, width = parts_ref.shape
    masks = row_masks(meta_ref, latents, meta_ref[1] + meta_ref[2] * share, share)
    d_hidden = parts_ref[0].astype(F32)
    for part in range(1, copies):
        d_hidden = d_hidden + parts_ref[part].astype(F32)
    unit, inverse = normed(mid_in_ref[...])
    d_mid = own_rows(meta_ref, cot_ref, share) + norm_back(
        unit, inverse, d_hidden * (1.0 + rows_of(mod_ref, masks, 4))
    )
    d_mid_ref[...] = d_mid
    d_attn = (d_mid * rows_of(mod_ref, masks, 2)).astype(BF16)
    for part in range(copies):
        sent_ref[part] = d_attn
    latent_sums(sums_ref, masks, d_mid * attn_ref[...], 0, 3)
    latent_sums(sums_ref, masks, d_hidden, 1, 3)
    latent_sums(sums_ref, masks, d_hidden * unit, 2, 3)


def result_kernel(
    latents, count, meta_ref, *refs
):
    parts = refs[:count]
    mid_ref, cot_ref, mod_ref, bias_ref, result_ref, sums_ref = refs[count:]
    share = result_ref.shape[0]
    masks = row_masks(meta_ref, latents, meta_ref[1] + meta_ref[2] * share, share)
    mlp = bias_ref[...].astype(F32)
    for part in parts:
        mlp = mlp + part[...].astype(F32)
    result_ref[...] = (mid_ref[...] + rows_of(mod_ref, masks, 5) * mlp).astype(BF16)
    latent_sums(sums_ref, masks, own_rows(meta_ref, cot_ref, share) * mlp, 0, 1)


def spread_kernel(meta_ref, d_attn_ref, vp_ref, packed_ref, d_bias_ref):
    grad = jnp.dot(d_attn_ref[...], vp_ref[...], preferred_element_type=F32).T
    half = grad.shape[1] // 2
    features = grad.shape[0] // 2
    for place in range(packed_ref.shape[0]):
        start = features + place // 2 * DH
        side = place % 2 * half
        packed_ref[place] = grad[start : start + DH, side : side + half].astype(BF16)
    d_bias_ref[...] = jnp.sum(d_attn_ref[...].astype(F32), axis=0, keepdims=True)


def unspread_kernel(
    meta_ref, parts_ref, qk_ref, vp_ref, d_one_ref, d_qk_ref, d_vp_ref, sent_ref, d_bias_ref
):
    heads = parts_ref.shape[0] // 2
    rows = d_one_ref.shape[0]
    query, key, value = [], [], []
    for head in range(heads):
        left = parts_ref[2 * head].astype(F32)
        right = parts_ref[2 * head + 1].astype(F32)
        both = left[:, : 2 * rows] + right[:, : 2 * rows]
        key.append(both[:, :rows])
        value.append(both[:, rows:])
        query.append(jnp.concatenate([left[:, 2 * rows :], right[:, 2 * rows :]], axis=1))
    d_qk_ref[...] = jnp.concatenate(query + key, axis=0).T.astype(BF16)
    blank = jnp.zeros((heads * DH, rows), F32)
    d_vp_ref[...] = jnp.concatenate(value + [blank], axis=0).T.astype(BF16)
    tile = 384
    by_last = (((1,), (1,)), ((), ()))

    def step(number, carry):
        columns = pl.ds(pl.multiple_of(number * tile, tile), tile)
        total = lax.dot_general(d_qk_ref[...], qk_ref[columns, :], by_last, preferred_element_type=F32)
        total += lax.dot_general(d_vp_ref[...], vp_ref[columns, :], by_last, preferred_element_type=F32)
        d_one_ref[:, columns] = total.astype(BF16)
        return carry

    lax.fori_loop(0, qk_ref.shape[0] // tile, step, 0)

    def sent(first, second):
        sent_ref[...] = first[...]

    on_core(meta_ref, sent, d_vp_ref, d_qk_ref)
    d_bias_ref[0:1, :] = jnp.sum(d_qk_ref[...].astype(F32), axis=0, keepdims=True)
    d_bias_ref[1:2, :] = jnp.sum(d_vp_ref[...].astype(F32), axis=0, keepdims=True)


def weight_kernel(first_pairs, second_pairs, meta_ref, *refs):
    operands = 1 + max(max(pair) for pair in first_pairs + second_pairs)
    ins, outs, total = refs[:operands], refs[operands:-1], refs[-1]
    tile = 384

    def body(pairs):
        def step(number, carry):
            columns = pl.ds(pl.multiple_of(number * tile, tile), tile)
            block = jnp.zeros((tile, total.shape[1]), F32)
            for left, right in pairs:
                block += lax.dot_general(
                    ins[left][:, columns], ins[right][...], (((0,), (0,)), ((), ())),
                    preferred_element_type=F32,
                )
            total[columns, :] = block.astype(BF16)
            return carry

        lax.fori_loop(0, total.shape[0] // tile, step, 0)

    on_core(meta_ref, lambda pairs, _: body(pairs), first_pairs, second_pairs)
    rows = outs[0].shape[0]
    for step, out in enumerate(outs):
        start = pl.multiple_of((meta_ref[3] ^ step) * rows, 16)
        out[...] = total[pl.ds(start, rows), :]


def first_back_kernel(
    latents, meta_ref, parts_ref, tokens_ref, d_mid_ref, mod_ref, mid_sums_ref, last_sums_ref,
    fc2_bias_ref, proj_bias_ref, fc1_bias_ref, qv_bias_ref, grad_ref, sent_ref, bias_ref, first_sums,
):
    copies, share, width = parts_ref.shape
    masks = row_masks(meta_ref, latents, meta_ref[1] + meta_ref[2] * share, share)
    d_hidden = parts_ref[0].astype(F32)
    for part in range(1, copies):
        d_hidden = d_hidden + parts_ref[part].astype(F32)
    unit, inverse = normed(own_rows(meta_ref, tokens_ref, share))
    grad = d_mid_ref[...] + norm_back(unit, inverse, d_hidden * (1.0 + rows_of(mod_ref, masks, 1)))
    grad_ref[...] = grad.astype(BF16)
    latent_sums(first_sums, masks, d_hidden, 0, 2)
    latent_sums(first_sums, masks, d_hidden * unit, 1, 2)
    columns = width // copies
    for number in range(latents):
        for feature in range(6):
            if feature < 2:
                row = first_sums[number * 2 + feature : number * 2 + feature + 1, :]
            elif feature < 5:
                place = number * 3 + feature - 2
                row = mid_sums_ref[place : place + 1, :]
            else:
                row = last_sums_ref[number : number + 1, :]
            place = number * 6 + feature
            for part in range(copies):
                sent_ref[part, place : place + 1, :] = row[:, part * columns : (part + 1) * columns]
    place = 0
    for ref in (fc2_bias_ref, proj_bias_ref, fc1_bias_ref):
        for start in range(0, ref.shape[1], columns):
            bias_ref[place : place + 1, :] = ref[:, start : start + columns]
            place += 1
    bias_ref[place : place + 2, :] = qv_bias_ref[:, :columns]


def order_kernel(count, meta_ref, *refs):
    result_ref, grad_ref = refs[2 * count :]
    share = refs[0].shape[0]
    for step in range(count):
        start = pl.multiple_of((meta_ref[2] ^ step) * share, share)
        result_ref[pl.ds(start, share), :] = refs[step][...]
        grad_ref[pl.ds(start, share), :] = refs[count + step][...].astype(F32)


def finish_kernel(
    latents, meta_ref, sums_ref, active_ref, w_ada_ref,
    w_grad_ref, b_grad_ref, d_active_ref, fc2_ref, proj_ref, fc1_ref, qv_ref, total_ref,
):
    total = sums_ref[0]
    for part in range(1, sums_ref.shape[0]):
        total = total + sums_ref[part]
    total_ref[...] = total
    by_last = (((1,), (1,)), ((), ()))
    d_active = jnp.zeros(d_active_ref.shape, F32)
    for feature in range(6):
        rows = [
            total_ref[number * 6 + feature : number * 6 + feature + 1, :] for number in range(latents)
        ]
        grad = active_ref[:, 0:1] * rows[0]
        bias = rows[0]
        for number in range(1, latents):
            grad = grad + active_ref[:, number : number + 1] * rows[number]
            bias = bias + rows[number]
        w_grad_ref[feature] = grad
        b_grad_ref[feature : feature + 1, :] = bias
        wide = jnp.concatenate(rows, axis=0)
        high = wide.astype(BF16)
        low = (wide - high.astype(F32)).astype(BF16)
        weight = w_ada_ref[feature]
        d_active += lax.dot_general(high, weight, by_last, preferred_element_type=F32)
        d_active += lax.dot_general(low, weight, by_last, preferred_element_type=F32)
    d_active_ref[...] = d_active
    columns = total_ref.shape[1]
    place = 6 * latents
    for ref in (fc2_ref, proj_ref, fc1_ref):
        for start in range(0, ref.shape[1], columns):
            ref[:, start : start + columns] = total_ref[place : place + 1, :]
            place += 1
    qv_ref[...] = total_ref[place : place + 2, :]


def latent_index(latent_len, first_row, row_count, token_total):
    positions = first_row + jnp.arange(row_count, dtype=jnp.int32)
    ends = jnp.cumsum(latent_len, dtype=jnp.int32)
    found = jnp.sum((positions[:, None] >= ends[None, :]).astype(jnp.int32), axis=1, dtype=jnp.int32)
    return jnp.where((positions >= 0) & (positions < token_total), found, -1)


def normed(values):
    average = jnp.mean(values, axis=-1, keepdims=True)
    centred = values - average
    spread = jnp.mean(centred * centred, axis=-1, keepdims=True)
    inverse = lax.rsqrt(spread + NORM_EPS)
    return centred * inverse, inverse


def norm_back(unit, inverse, grad):
    along = jnp.mean(grad * unit, axis=-1, keepdims=True)
    return inverse * (grad - jnp.mean(grad, axis=-1, keepdims=True) - unit * along)


def gelu_pair(value):
    root = math.sqrt(2.0 / math.pi)
    bend = jnp.tanh(root * (value + 0.044715 * value * value * value))
    slope = root * (1.0 + 3.0 * 0.044715 * value * value)
    gelu = 0.5 * value * (1.0 + bend)
    return gelu, 0.5 * (1.0 + bend) + 0.5 * value * (1.0 - bend * bend) * slope


def local(
    tokens,
    conditioning,
    latent_len,
    w_ada,
    b_ada,
    w_qkv,
    b_qv,
    w_proj,
    b_proj,
    w_fc1,
    b_fc1,
    w_fc2,
    b_fc2,
    cotangent,
):
    rows, width = tokens.shape
    share_width = w_qkv.shape[0]
    features = w_qkv.shape[2]
    units = w_fc1.shape[1]
    heads = features // DH
    latents = conditioning.shape[0]
    n_dp, n_tensor = lax.axis_size("dp"), lax.axis_size("tensor")
    my_dp, my_tensor = lax.axis_index("dp"), lax.axis_index("tensor")
    share = rows // n_tensor

    core = my_dp % 2
    qk = w_qkv[:, :2].reshape(share_width, 2 * features)
    vp = jnp.concatenate([w_qkv[:, 2], w_proj.T], axis=1)
    early_rows = pair_rows(qk, vp)

    cond = conditioning.astype(F32)
    sigmoid = 1.0 / (1.0 + jnp.exp(-cond))
    activated = (cond * sigmoid).astype(BF16)
    own_activated = lax.dynamic_slice_in_dim(activated, my_dp * share_width, share_width, 1)
    flat_ada = w_ada.reshape(share_width, 6 * features)
    mod_part = jnp.dot(own_activated, flat_ada, preferred_element_type=F32)
    mod_part = mod_part.reshape(latents * 6, features)
    bias_ada = jnp.tile(b_ada.astype(F32), (latents, 1))
    few_chips = n_dp // 2 == 4
    mod_mine = jnp.sum(gather(mod_part, "dp", n_dp), axis=0) + bias_ada
    early_rows = gate(early_rows, mod_mine)
    mod_parts = gather(mod_mine, "tensor", n_tensor)
    early_parts = chip_parts(early_rows) if few_chips else [gather_chips(early_rows)]

    early_parts = list(gate_all(early_parts, mod_parts))
    early_parts += [swap(part, "dp", 1) for part in early_parts]
    count = len(early_parts) // 2
    meta = jnp.stack([core, my_dp * rows, my_tensor, my_dp // 2]).astype(jnp.int32)
    meta = jnp.concatenate([meta, latent_len])
    place_meta = meta if few_chips else meta.at[3].set(0)
    by_last = (((1,), (1,)), ((), ()))
    by_token = (((0,), (0,)), ((), ()))
    bias = jnp.concatenate([b_qv[0], jnp.zeros_like(b_qv[0]), b_qv[1], jnp.zeros_like(b_qv[0])])
    hidden_one, d_mlp, packed, full_qk, full_vp, d_bias_fc2, mod_rows = call(
        lambda *refs: project_kernel(latents, count, *refs),
        "project",
        place_meta,
        (*early_parts, tokens, cotangent, mod_parts, bias.astype(F32).reshape(2, -1)),
        (((rows, width), BF16), ((rows, width), BF16), ((2 * heads, DH, rows * 5 // 2), BF16))
        + (((width, 2 * features), BF16),) * 2
        + (((1, width), F32), ((6 * latents, width), F32)),
        [pltpu.SemaphoreType.DMA((2, count))],
        2 * count,
    )
    late_rows = pair_rows(w_fc1, w_fc2.T)
    hidden_other = swap(hidden_one, "dp", 1)
    split = HeadSplit if 2 * heads == n_dp else Window
    attention = split(latent_len, rows)
    attended_parts = attention.forward(packed)
    late_rows = gate(late_rows, attended_parts)
    late_parts = chip_parts(late_rows)[:-1] if few_chips else [gather_chips(late_rows)]
    attn_part, attended = call(
        attend_out_kernel,
        "attend_out",
        meta,
        (attended_parts, full_vp),
        (((rows, width), BF16), ((rows, 2 * features), BF16)),
    )
    attn_parts = exchange_shares(attn_part, "tensor")
    hidden_blocks, attn_out, residual_mid = call(
        lambda *refs: middle_kernel(latents, *refs),
        "middle",
        meta,
        (attn_parts, tokens, mod_rows, b_proj.reshape(1, -1)),
        (((n_tensor, share, width), BF16), ((share, width), F32), ((share, width), F32)),
        due=late_parts[1:],
    )
    hidden_two = exchange(hidden_blocks, "tensor").reshape(rows, width)
    if few_chips:
        last_part = swap(gate(late_rows, attn_out), "dp", n_dp - 2)
        late_parts.append(gate(last_part, hidden_two))
    late_other = [swap(part, "dp", 1) for part in late_parts]

    d_two_part, gelu_out, d_pre, d_bias_fc1, left_sent, right_sent, *mlp_blocks = call(
        lambda *refs: mlp_kernel(count, *refs),
        "mlp",
        place_meta,
        (*late_parts, *late_other, hidden_two, d_mlp, b_fc1.reshape(1, -1)),
        (((rows, width), BF16), ((rows, units), BF16), ((rows, units), BF16), ((1, units), F32))
        + (((rows, width), BF16), ((rows, units), BF16))
        + (((share, width), BF16),) * n_tensor,
        [pltpu.VMEM((width, units), BF16)] * 2
        + [pltpu.VMEM((rows, width), F32)] * 2
        + [pltpu.SemaphoreType.DMA((2, count))],
        2 * count,
    )
    d_two_parts = exchange_shares(d_two_part, "tensor")

    chips = n_dp // 2 if few_chips else 1
    left_other = swap(left_sent, "dp", 1)
    right_other = swap(right_sent, "dp", 1)
    late_blocks = call(
        lambda *refs: weight_kernel([(0, 2), (4, 5)], [(1, 3), (4, 5)], *refs),
        "late_weights",
        place_meta,
        (hidden_two, d_mlp, d_pre, gelu_out, left_other, right_other),
        (((width // chips, units), BF16),) * chips,
        [pltpu.VMEM((width, units), BF16)],
    )
    late_grads = sum_chips(late_blocks[:-1]) if few_chips else sum_chips(late_blocks)

    d_attn_blocks, d_mid, mid_sums = call(
        lambda *refs: middle_back_kernel(latents, *refs),
        "middle_back",
        meta,
        (d_two_parts, residual_mid, attn_out, cotangent, mod_rows),
        (((n_tensor, share, width), BF16), ((share, width), F32), ((3 * latents, width), F32)),
        due=late_blocks,
    )
    d_attn = exchange(d_attn_blocks, "tensor").reshape(rows, width)

    d_spread, d_bias_proj = call(
        spread_kernel,
        "spread",
        meta,
        (d_attn, full_vp),
        (((2 * heads, DH, rows // 2), BF16), ((1, width), F32)),
        due=late_grads[1:],
    )
    mlp_parts = mlp_blocks[:1] + [
        swap(gate(block, d_spread), "tensor", step)
        for step, block in enumerate(mlp_blocks)
        if step
    ]
    d_attn_other = swap(d_attn, "dp", 1)
    attended_other = swap(attended, "dp", 1)
    d_packed, last_grad = attention.backward(d_spread, mlp_parts[1:], late_blocks[-1])
    result_own, last_sums = call(
        lambda *refs: result_kernel(latents, n_tensor, *refs),
        "result",
        meta,
        (*mlp_parts, residual_mid, cotangent, mod_rows, b_fc2.reshape(1, -1)),
        (((share, width), BF16), ((latents, width), F32)),
    )
    d_one_part, d_qk, d_vp, d_sent, d_bias_qv = call(
        unspread_kernel,
        "unspread",
        meta,
        (d_packed, full_qk, full_vp),
        (((rows, width), BF16),)
        + (((rows, 2 * features), BF16),) * 3
        + (((2, 2 * features), F32),),
        flops=2 * 10**10,
    )
    result_parts = [result_own] + [swap(result_own, "tensor", bits) for bits in range(1, n_tensor)]
    d_one_part = gate(d_one_part, *result_parts[1:])
    d_one_parts = exchange_shares(d_one_part, "tensor")

    if few_chips:
        late_grads.append(last_grad)
    right_other = swap(d_sent, "dp", 1)
    early_blocks = call(
        lambda *refs: weight_kernel(
            [(0, 2), (5, 7)], [(0, 3), (1, 4), (5, 7), (6, 8)], *refs
        ),
        "early_weights",
        place_meta,
        (hidden_one, d_attn, d_qk, d_vp, attended, hidden_other, d_attn_other, right_other, attended_other),
        (((width // chips, 2 * features), BF16),) * chips,
        [pltpu.VMEM((width, 2 * features), BF16)],
    )
    early_grads = sum_chips(early_blocks[:3] if few_chips else early_blocks)

    grad_own, d_mod_part, bias_rows = call(
        lambda *refs: first_back_kernel(latents, *refs),
        "first_back",
        meta,
        (d_one_parts, tokens, d_mid, mod_rows, mid_sums, last_sums)
        + (d_bias_fc2, d_bias_proj, d_bias_fc1, d_bias_qv),
        (((share, width), BF16), ((n_tensor, 6 * latents, features), F32))
        + (((2 * (width // features) + units // features + 2, features), F32),),
        [pltpu.VMEM((2 * latents, width), F32)],
        due=early_grads[1:3],
    )
    if few_chips:
        last_block = gate(early_blocks[3], d_mod_part)
        early_grads.append(swap(last_block, "dp", n_dp - 2))
    d_mod_mine = jnp.sum(exchange(d_mod_part, "tensor"), axis=0)
    d_mod_rows = jnp.concatenate([d_mod_mine, bias_rows])
    d_mod_rows = gate(jnp.broadcast_to(d_mod_rows[None], (n_dp,) + d_mod_rows.shape))
    grad_own = gate(grad_own, d_mod_rows)
    grad_parts = [grad_own] + [swap(grad_own, "tensor", bits) for bits in range(1, n_tensor)]
    sums = exchange(d_mod_rows, "dp")
    sums = gate(sums, early_grads[3]) if few_chips else sums
    grad_parts = gate_all(grad_parts, sums)
    result, grad_tokens = call(
        lambda *refs: order_kernel(n_tensor, *refs),
        "order",
        meta,
        (*result_parts, *grad_parts),
        (((rows, width), BF16), ((rows, width), F32)),
    )
    grad_w_ada, grad_b_ada, d_active, sum_b_fc2, sum_b_proj, sum_b_fc1, sum_b_qv = call(
        lambda *refs: finish_kernel(latents, *refs),
        "finish",
        meta,
        (sums, own_activated.astype(F32).T, w_ada.transpose(1, 0, 2)),
        (((6, share_width, features), F32), ((6, features), F32), ((latents, share_width), F32))
        + (((1, width), F32), ((1, width), F32), ((1, units), F32), ((2, features), F32)),
        [pltpu.VMEM(sums.shape[1:], F32)],
    )
    d_active = gather(d_active, ("dp", "tensor"), n_dp * n_tensor)
    d_active = jnp.sum(d_active.reshape(n_dp, n_tensor, latents, share_width), axis=1)
    d_active = d_active.transpose(1, 0, 2).reshape(latents, width)
    grad_cond = d_active * (sigmoid * (1.0 + cond * (1.0 - sigmoid)))

    grad_fc1, grad_fc2 = finish_pair(late_grads)
    grad_qk, grad_vp = finish_pair(early_grads)
    grad_qkv = jnp.concatenate([grad_qk, grad_vp[:, :features]], axis=1)
    grad_qkv = grad_qkv.reshape(share_width, 3, features)

    return (
        result,
        grad_tokens,
        grad_cond,
        grad_w_ada.transpose(1, 0, 2),
        grad_b_ada,
        grad_qkv,
        sum_b_qv,
        grad_vp[:, features:].T,
        sum_b_proj.reshape(width),
        grad_fc1,
        sum_b_fc1.reshape(units),
        grad_fc2.T,
        sum_b_fc2.reshape(width),
    )


def solution(mesh):
    in_specs = (
        P("dp", None),
        P(),
        P(),
        P("dp", None, "tensor"),
        P(None, "tensor"),
        P("dp", None, "tensor"),
        P(None, "tensor"),
        P("tensor", "dp"),
        P(),
        P("dp", "tensor"),
        P("tensor"),
        P("tensor", "dp"),
        P(),
        P("dp", None),
    )
    out_specs = (
        P("dp", None),
        P("dp", None),
        P(),
        P("dp", None, "tensor"),
        P(None, "tensor"),
        P("dp", None, "tensor"),
        P(None, "tensor"),
        P("tensor", "dp"),
        P(),
        P("dp", "tensor"),
        P("tensor"),
        P("tensor", "dp"),
        P(),
    )
    return jax.shard_map(local, mesh=mesh, in_specs=in_specs, out_specs=out_specs, check_vma=False)
```
